32 devices in a mesh: shard: 2 (over x), rep: 16 (over z, y, core).
Axes of the slice: x: 2, y: 2, z: 4, core: 2. Of those that a mesh axis runs over, the one named last changes fastest.
Arguments:
- hidden: bfloat16 [4, 2048, 768], P('shard', 'rep'), may hold values from -6 to 6
- encoded: bfloat16 [4, 512, 768], P('shard', 'rep'), may hold values from -6 to 6
- out_grad: bfloat16 [4, 2048, 768], P('shard', 'rep'), may hold values from -6 to 6
- self_query: float32 [768, 768], P('shard'), may hold values from -0.078125 to 0.078125
- self_key: float32 [768, 768], P('shard'), may hold values from -0.078125 to 0.078125
- self_value: float32 [768, 768], P('shard'), may hold values from -0.21875 to 0.21875
- self_out: float32 [768, 768], P('shard'), may hold values from -1.25 to 1.25
- cross_query: float32 [768, 768], P('shard'), may hold values from -0.078125 to 0.078125
- cross_key: float32 [768, 768], P('shard'), may hold values from -0.078125 to 0.078125
- cross_value: float32 [768, 768], P('shard'), may hold values from -0.21875 to 0.21875
- cross_out: float32 [768, 768], P('shard'), may hold values from -0.625 to 0.625
- ffn_gate: float32 [768, 2048], P('shard'), may hold values from -0.21875 to 0.21875
- ffn_up: float32 [768, 2048], P('shard'), may hold values from -0.21875 to 0.21875
- ffn_down: float32 [2048, 768], P('shard'), may hold values from -0.125 to 0.125
- gain_self: float32 [768], P('shard'), may hold values from 0.5 to 1.5
- gain_cross: float32 [768], P('shard'), may hold values from 0.5 to 1.5
- gain_ffn: float32 [768], P('shard'), may hold values from 0.5 to 1.5
- bias_table: float32 [32, 12], P('shard'), may hold values from -4 to 4
- buckets: int32 [2048], replicated, may hold values from 0 to 31, as said below
Outputs:
- output: bfloat16 [4, 2048, 768], P('shard', 'rep')
- hidden_grad: bfloat16 [4, 2048, 768], P('shard', 'rep')
- encoded_grad: bfloat16 [4, 512, 768], P('shard', 'rep')
- self_query_grad: float32 [768, 768], P('shard')
- self_key_grad: float32 [768, 768], P('shard')
- self_value_grad: float32 [768, 768], P('shard')
- self_out_grad: float32 [768, 768], P('shard')
- cross_query_grad: float32 [768, 768], P('shard')
- cross_key_grad: float32 [768, 768], P('shard')
- cross_value_grad: float32 [768, 768], P('shard')
- cross_out_grad: float32 [768, 768], P('shard')
- ffn_gate_grad: float32 [768, 2048], P('shard')
- ffn_up_grad: float32 [768, 2048], P('shard')
- ffn_down_grad: float32 [2048, 768], P('shard')
- gain_self_grad: float32 [768], P('shard')
- gain_cross_grad: float32 [768], P('shard')
- gain_ffn_grad: float32 [768], P('shard')
- bias_table_grad: float32 [32, 12], P('shard')
The draws below stay inside these ranges and needn't reach their ends.
Inputs may be any that keep to these rules, and one draw needn't show every extreme that they name: buckets[d] is a relabelling, by a permutation of the 32 buckets, of T5's causal relative position bucket of distance d with 32 buckets and max distance 128: distances below 16 have buckets of their own, distances up to 127 are spaced logarithmically over the other buckets, and every distance of 128 or more falls in the same bucket as 127.
All inputs are finite; a program needn't handle non-finite values.
Results may differ from the reference program's by a relative error of at most 0.03.
Values may be sent and summed in bfloat16 or wider, within the bound.
A program may use at most 256 MiB of HBM per device.

```python
import math
import jax
import jax.numpy as jnp
import numpy as np
from jax import lax

D = 768
H = 12
DH = 64
FF = 2048
NB = 32
ENC = 512
LEN = 2048
BATCH = 4


def t5_table(count, length):
    exact = count // 2
    table = np.zeros((length,), dtype=np.int64)
    for dist in range(length):
        if dist < exact:
            table[dist] = dist
        else:
            spaced = exact + int(math.log(dist / exact) / math.log(128.0 / exact) * (count - exact))
            table[dist] = min(spaced, count - 1)
    return table


def draw_buckets(key, part):
    table = jnp.asarray(t5_table(NB, LEN).astype(np.int32))
    relabel = jax.random.permutation(jax.random.fold_in(key, 7), NB).astype(jnp.int32)
    return jnp.take(relabel, table).astype(jnp.int32)


def levels(rng, extent, pieces, low, largest):
    def one(position, shards_of):
        heights = jax.random.uniform(jax.random.fold_in(jax.random.fold_in(rng, 6), position), (shards_of,), jnp.float32, low / len(pieces), largest / len(pieces))
        return jnp.repeat(jnp.exp(heights), extent[position] // shards_of).reshape((-1,) + (1,) * (len(extent) - position - 1))

    loudness = one(*pieces[0])
    for cut in pieces[1:]:
        loudness = loudness * one(*cut)
    return loudness


def bell_draw(key, shape, scale, limit, cuts=(), kind=jnp.bfloat16):
    values = scale * jax.random.normal(key, shape, jnp.float32)
    if cuts:
        values = values * levels(key, shape, cuts, -0.22, 0.18)
    return jnp.clip(values, -limit, limit).astype(kind)


def setup_inputs(seed: int = 0) -> dict:
    key_list = jax.random.split(jax.random.key(seed), 20)
    hidden = bell_draw(key_list[0], (BATCH, LEN, D), 1.0, 6.0, ((0, 2), (1, 16)))
    encoded = bell_draw(key_list[1], (BATCH, ENC, D), 1.0, 6.0, ((0, 2), (1, 16)))
    out_grad = bell_draw(key_list[2], (BATCH, LEN, D), 1.0, 6.0, ((0, 2), (1, 16)))
    self_query = bell_draw(key_list[3], (D, D), (8 * D) ** -0.5, 0.078125, ((0, 2),), jnp.float32)
    self_key = bell_draw(key_list[4], (D, D), (8 * D) ** -0.5, 0.078125, ((0, 2),), jnp.float32)
    self_value = bell_draw(key_list[5], (D, D), D ** -0.5, 0.21875, ((0, 2),), jnp.float32)
    self_out = bell_draw(key_list[6], (D, D), (D // 36) ** -0.5, 1.25, ((0, 2),), jnp.float32)
    cross_query = bell_draw(key_list[7], (D, D), (8 * D) ** -0.5, 0.078125, ((0, 2),), jnp.float32)
    cross_key = bell_draw(key_list[8], (D, D), (8 * D) ** -0.5, 0.078125, ((0, 2),), jnp.float32)
    cross_value = bell_draw(key_list[9], (D, D), D ** -0.5, 0.21875, ((0, 2),), jnp.float32)
    cross_out = bell_draw(key_list[10], (D, D), (D // 9) ** -0.5, 0.625, ((0, 2),), jnp.float32)
    ffn_gate = bell_draw(key_list[11], (D, FF), D ** -0.5, 0.21875, ((0, 2),), jnp.float32)
    ffn_up = bell_draw(key_list[12], (D, FF), D ** -0.5, 0.21875, ((0, 2),), jnp.float32)
    ffn_down = bell_draw(key_list[13], (FF, D), FF ** -0.5, 0.125, ((0, 2),), jnp.float32)
    gain_self = jnp.clip(1.0 + 0.1 * jax.random.normal(key_list[14], (D,), jnp.float32), 0.5, 1.5)
    gain_cross = jnp.clip(1.0 + 0.1 * jax.random.normal(key_list[15], (D,), jnp.float32), 0.5, 1.5)
    gain_ffn = jnp.clip(1.0 + 0.1 * jax.random.normal(key_list[16], (D,), jnp.float32), 0.5, 1.5)
    bias_table = bell_draw(key_list[17], (NB, H), 1.0, 4.0, ((0, 2),), jnp.float32)
    buckets = draw_buckets(jax.random.fold_in(key_list[19], 71), 0)
    return {"hidden": hidden, "encoded": encoded, "out_grad": out_grad, "self_query": self_query, "self_key": self_key, "self_value": self_value, "self_out": self_out, "cross_query": cross_query, "cross_key": cross_key, "cross_value": cross_value, "cross_out": cross_out, "ffn_gate": ffn_gate, "ffn_up": ffn_up, "ffn_down": ffn_down, "gain_self": gain_self, "gain_cross": gain_cross, "gain_ffn": gain_ffn, "bias_table": bias_table, "buckets": buckets}


@jax.custom_vjp
def low(v):
    return lax.optimization_barrier(v.astype(jnp.bfloat16)).astype(jnp.float32)

@jax.custom_vjp
def low_back(v):
    return v

def low_keep(v):
    return (low(v), None)

def low_pass(kept, grad):
    return (grad,)

def back_keep(v):
    return (v, None)

def back_low(kept, grad):
    return (low(grad),)
low.defvjp(low_keep, low_pass)
low_back.defvjp(back_keep, back_low)
EPS = 1e-06
HIGH = lax.Precision.HIGHEST

def normalize(rows, gain):
    return rows * lax.rsqrt(lax.optimization_barrier(jnp.mean(rows * rows, axis=-1, keepdims=True)) + EPS) * gain

def project(left, right):
    return jnp.dot(left, right, precision=HIGH)

def rounded(value):
    return low_back(low(value))

def self_attention(queries, keys, values, table, buckets):
    block_rows = min(512, LEN)
    key_pos = jnp.arange(LEN, dtype=jnp.int32)

    def one_block(item):
        query_block, start = item
        query_pos = start + jnp.arange(block_rows, dtype=jnp.int32)
        offsets = query_pos[:, None] - key_pos[None, :]
        valid = (offsets >= 0)[None]
        picked = jnp.take(buckets, jnp.clip(offsets, 0, LEN - 1).astype(jnp.int32))
        bias = jnp.transpose(jnp.take(table, picked, axis=0), (2, 0, 1))
        scores = low_back(jnp.einsum('qhd,khd->hqk', query_block, keys, precision=HIGH) + bias)
        expo = jnp.where(valid, jnp.exp(jnp.where(valid, scores, 0.0)), 0.0)
        total = lax.optimization_barrier(jnp.sum(expo, axis=-1))
        summed = jnp.einsum('hqk,khd->qhd', low(expo), values, precision=HIGH)
        return summed / jnp.transpose(total)[:, :, None]
    starts = (jnp.arange(LEN // block_rows) * block_rows).astype(jnp.int32)
    blocks = lax.map(jax.checkpoint(one_block), (queries.reshape(LEN // block_rows, block_rows, H, DH), starts))
    return blocks.reshape(LEN, H * DH)

def cross_attention(queries, keys, values):
    block_rows = min(512, LEN)

    def one_block(query_block):
        scores = low_back(jnp.einsum('qhd,khd->hqk', query_block, keys, precision=HIGH))
        expo = jnp.exp(scores)
        total = lax.optimization_barrier(jnp.sum(expo, axis=-1))
        summed = jnp.einsum('hqk,khd->qhd', low(expo), values, precision=HIGH)
        return summed / jnp.transpose(total)[:, :, None]
    blocks = lax.map(jax.checkpoint(one_block), queries.reshape(LEN // block_rows, block_rows, H, DH))
    return blocks.reshape(LEN, H * DH)

def layer(inputs, enc, params, buckets):
    w_query, w_key, w_value, w_out, c_query, c_key, c_value, c_out, w_gate, w_up, w_down, g_self, g_cross, g_ffn, w_table = tuple((low(part) for part in params))
    normed1 = low(normalize(inputs, g_self))
    queries = rounded(project(normed1, w_query))
    keys = rounded(project(normed1, w_key))
    values = rounded(project(normed1, w_value))
    attn = rounded(self_attention(queries.reshape(LEN, H, DH), keys.reshape(LEN, H, DH), values.reshape(LEN, H, DH), w_table, buckets))
    resid1 = inputs + low_back(project(attn, w_out))
    normed2 = low(normalize(resid1, g_cross))
    cross_q = rounded(project(normed2, c_query))
    enc_keys = rounded(project(enc, c_key))
    enc_values = rounded(project(enc, c_value))
    cross_attn = rounded(cross_attention(cross_q.reshape(LEN, H, DH), enc_keys.reshape(ENC, H, DH), enc_values.reshape(ENC, H, DH)))
    resid2 = resid1 + low_back(project(cross_attn, c_out))
    normed3 = low(normalize(resid2, g_ffn))
    gate = low_back(project(normed3, w_gate))
    upper = low_back(project(normed3, w_up))
    inner = rounded(jax.nn.gelu(gate, approximate=True) * upper)
    return resid2 + low_back(project(inner, w_down))

def reference(hidden, encoded, out_grad, self_query, self_key, self_value, self_out, cross_query, cross_key, cross_value, cross_out, ffn_gate, ffn_up, ffn_down, gain_self, gain_cross, gain_ffn, bias_table, buckets):
    params = (self_query, self_key, self_value, self_out, cross_query, cross_key, cross_value, cross_out, ffn_gate, ffn_up, ffn_down, gain_self, gain_cross, gain_ffn, bias_table)

    def step(totals, item):
        inputs, enc, grad = item

        def forward_one(x_in, enc_in, params_in):
            return layer(x_in, enc_in, params_in, buckets)
        value, pull = jax.vjp(forward_one, inputs.astype(jnp.float32), enc.astype(jnp.float32), params)
        input_grad, enc_grad, param_grads = pull(grad.astype(jnp.float32))
        totals = tuple((total + part for total, part in zip(totals, param_grads)))
        return (totals, (value.astype(jnp.bfloat16), input_grad.astype(jnp.bfloat16), enc_grad.astype(jnp.bfloat16)))
    zeros = tuple((jnp.zeros(part.shape, jnp.float32) for part in params))
    totals, (output, hidden_grad, encoded_grad) = lax.scan(step, zeros, (hidden, encoded, out_grad))
    return (output, hidden_grad, encoded_grad, totals[0], totals[1], totals[2], totals[3], totals[4], totals[5], totals[6], totals[7], totals[8], totals[9], totals[10], totals[11], totals[12], totals[13], totals[14])
```

```python
import functools

import jax
import jax.numpy as jnp
from jax import lax
from jax.experimental import pallas as pl
from jax.experimental.pallas import tpu as pltpu
from jax.sharding import PartitionSpec as P

D = 768
H = 12
DH = 64
NB = 32
EPS = 1e-06
F32 = jnp.float32
B16 = jnp.bfloat16
ONES = 16
HIDE = -1e30
MESH = pl.DeviceIdType.MESH
GELU_A = 0.7978845608028654
GELU_B = 0.044715


def dot(a, b):
    return lax.dot_general(a, b, (((1,), (0,)), ((), ())), preferred_element_type=F32)


def dot_t(a, b):
    return lax.dot_general(a, b, (((1,), (1,)), ((), ())), preferred_element_type=F32)


def t_dot(a, b):
    return lax.dot_general(a, b, (((0,), (0,)), ((), ())), preferred_element_type=F32)


def scale_of(v):
    return lax.rsqrt(jnp.mean(v * v, axis=-1, keepdims=True) + EPS)


def norm_back(v, gain, grad):
    r = scale_of(v)
    n = v * r
    c = grad * gain
    dv = r * (c - n * jnp.mean(c * n, axis=-1, keepdims=True))
    return dv, jnp.sum(grad * n, axis=0, keepdims=True)


def whole(shape):
    return pl.BlockSpec(shape, lambda *_: (0,) * len(shape))


def plain_call(kernel, outs, args, name, scratch=(), vmem=60):
    return pl.pallas_call(
        kernel,
        out_shape=[jax.ShapeDtypeStruct(s, t) for s, t in outs],
        in_specs=[pl.BlockSpec(memory_space=pltpu.VMEM)] * len(args),
        out_specs=[pl.BlockSpec(memory_space=pltpu.VMEM)] * len(outs),
        scratch_shapes=list(scratch),
        compiler_params=pltpu.CompilerParams(vmem_limit_bytes=vmem * 2**20),
        name=name,
    )(*args)


class Plan:
    def __init__(self, seqs, toks, rows):
        self.S, self.T, self.R = seqs, toks, rows
        groups = 1
        for g in range(1, H + 1):
            if H % g == 0 and seqs * g <= rows and rows % (2 * seqs * g) == 0:
                groups = g
        self.G = groups
        self.HG = H // groups
        self.F = self.HG * DH
        self.U = seqs * groups
        self.W = rows // self.U
        self.J = rows // self.W
        self.NP = self.J // 2
        self.CK = 2 * self.W * toks
        self.L = rows * toks

    def worker_of(self, r):
        m = r % (2 * self.W)
        late = m // self.W
        return m * (1 - late) + (2 * self.W - 1 - m) * late

    def slot_of(self, r):
        return 2 * (r // (2 * self.W)) + (r % (2 * self.W)) // self.W

    def source(self, j, w):
        if j % 2 == 0:
            return 2 * self.W * (j // 2) + w
        return 2 * self.W * (j // 2) + 2 * self.W - 1 - w


def enter(rows):
    me = lax.axis_index("rep")
    barrier = pltpu.get_barrier_semaphore()
    for k in range(1, rows):
        pl.semaphore_signal(
            barrier, inc=1, device_id={"rep": (me + k) % rows}, device_id_type=MESH
        )
    pl.semaphore_wait(barrier, rows - 1)
    return me


def remote(src, dst, send, recv, to):
    return pltpu.make_async_remote_copy(
        src_ref=src,
        dst_ref=dst,
        send_sem=send,
        recv_sem=recv,
        device_id={"rep": to},
        device_id_type=MESH,
    )


def start_either(me, to, src, dst, send, recv):
    @pl.when(to == me)
    def _():
        pltpu.make_async_copy(src, dst, recv).start()

    @pl.when(to != me)
    def _():
        remote(src, dst, send, recv, to).start()


def end_either(me, to, src, dst, send, recv):
    @pl.when(to != me)
    def _():
        remote(src, dst, send, recv, to).wait_send()


def landed(ref, sem):
    pltpu.make_async_copy(ref, ref, sem).wait()


def scatter_tokens(plan, send, recv, send_sem, relay_sem, recv_sem):
    p = plan
    me = enter(p.R)
    w = me % p.W
    mine = p.worker_of(me)
    for u in range(p.U):
        start_either(me, u * p.W + mine, send.at[u], recv.at[me], send_sem.at[u], recv_sem.at[me])
    for j in range(p.J):
        r = p.source(j, w)
        landed(recv.at[r], recv_sem.at[r])
        for k in range(1, p.W):
            part = recv.at[r, pl.ds(p.F, 2 * p.F)]
            remote(
                part, part, relay_sem.at[k - 1, j], recv_sem.at[r], me - w + (w + k) % p.W
            ).start()
    for k in range(1, p.W):
        for j in range(p.J):
            r = p.source(j, (w + k) % p.W)
            landed(recv.at[r, pl.ds(p.F, 2 * p.F)], recv_sem.at[r])
    for u in range(p.U):
        end_either(me, u * p.W + mine, send.at[u], recv.at[me], send_sem.at[u], recv_sem.at[me])
    for k in range(1, p.W):
        for j in range(p.J):
            r = p.source(j, w)
            part = recv.at[r, pl.ds(p.F, 2 * p.F)]
            remote(
                part, part, relay_sem.at[k - 1, j], recv_sem.at[r], me - w + (w + k) % p.W
            ).wait_send()


def return_tokens(plan, send, recv, send_sem, recv_sem):
    p = plan
    me = enter(p.R)
    w = me % p.W
    unit = me // p.W
    for j in range(p.J):
        r = p.source(j, w)
        start_either(me, r, send.at[j], recv.at[unit], send_sem.at[j], recv_sem.at[unit])
    for u in range(p.U):
        landed(recv.at[u], recv_sem.at[u])
    for j in range(p.J):
        r = p.source(j, w)
        end_either(me, r, send.at[j], recv.at[unit], send_sem.at[j], recv_sem.at[unit])


def scatter_rows(plan, send, recv, send_sem, recv_sem):
    p = plan
    me = enter(p.R)
    mine = p.worker_of(me)
    slot = p.slot_of(me)
    for u in range(p.U):
        start_either(
            me, u * p.W + mine, send.at[u], recv.at[slot], send_sem.at[u], recv_sem.at[slot]
        )
    for j in range(p.J):
        landed(recv.at[j], recv_sem.at[j])
    for u in range(p.U):
        end_either(
            me, u * p.W + mine, send.at[u], recv.at[slot], send_sem.at[u], recv_sem.at[slot]
        )


def return_grads(plan, dq, dkv, recv, buf, out, send_sem, part_sem, got_sem, recv_sem):
    p = plan
    me = enter(p.R)
    w = me % p.W
    unit = me // p.W

    def give(k, j):
        to = (w + k) % p.W
        r = p.source(j, to)
        return remote(
            dkv.at[r],
            buf.at[k - 1, j],
            part_sem.at[k - 1, j],
            got_sem.at[k - 1, j],
            me - w + to,
        )

    for j in range(p.J):
        for k in range(1, p.W):
            give(k, j).start()
    for j in range(p.J):
        r = p.source(j, w)
        total = dkv[r].astype(F32)
        for k in range(1, p.W):
            landed(buf.at[k - 1, j], got_sem.at[k - 1, j])
            total = total + buf[k - 1, j].astype(F32)
        out[j, 0 : p.F, :] = dq[j]
        out[j, p.F : 3 * p.F, :] = total.astype(B16)
        start_either(me, r, out.at[j], recv.at[unit], send_sem.at[j], recv_sem.at[unit])
    for u in range(p.U):
        landed(recv.at[u], recv_sem.at[u])
    for j in range(p.J):
        r = p.source(j, w)
        end_either(me, r, out.at[j], recv.at[unit], send_sem.at[j], recv_sem.at[unit])
        for k in range(1, p.W):
            give(k, j).wait_send()


def comm_call(kernel, out, args, scratch, collective, name, space=pl.ANY):
    return pl.pallas_call(
        kernel,
        out_shape=jax.ShapeDtypeStruct(out, B16),
        in_specs=[pl.BlockSpec(memory_space=space)] * len(args),
        out_specs=pl.BlockSpec(memory_space=space),
        scratch_shapes=list(scratch),
        compiler_params=pltpu.CompilerParams(
            collective_id=collective, has_side_effects=True, vmem_limit_bytes=40 * 2**20
        ),
        name=name,
    )(*args)


def project_kernel(plan, hidden, gain, wq, wk, wv, a1_ref, send):
    p = plan
    x = hidden[...].reshape(p.S * p.T, D).astype(F32)
    a1 = (x * scale_of(x) * gain[...]).astype(B16)
    a1_ref[...] = a1
    for n, weight in enumerate((wq, wk, wv)):
        rows = dot(a1, weight[...])
        for s in range(p.S):
            turned = jnp.transpose(rows[s * p.T : (s + 1) * p.T]).astype(B16)
            for g in range(p.G):
                send[s * p.G + g, n * p.F : (n + 1) * p.F, :] = turned[g * p.F : (g + 1) * p.F]


def bias_tiles(plan, w, line, tiles):
    p = plan
    far = line[0:1, 2 * p.T - 1 : 2 * p.T]
    near = pltpu.roll(
        jnp.broadcast_to(line[0:1, :], (p.T, 2 * p.T)), 0, 1, stride=1, stride_axis=0
    )
    key = lax.broadcasted_iota(jnp.int32, (p.T, p.T), 0)
    query = lax.broadcasted_iota(jnp.int32, (p.T, p.T), 1)
    same = jnp.where(query >= key, near[:, : p.T], HIDE)
    next_ = near[:, p.T :]
    farb = jnp.broadcast_to(far, (p.T, p.T))
    tiles[0] = jnp.broadcast_to(far, (p.CK, 2 * p.T))
    for a in range(2):
        ahead = w if a == 0 else 2 * p.W - 1 - w
        for b in range(2 * p.W):
            diff = ahead - b
            tile = jnp.where(
                diff == 0, same, jnp.where(diff == 1, next_, jnp.where(diff < 0, HIDE, farb))
            )
            tiles[2, b * p.T : (b + 1) * p.T, a * p.T : (a + 1) * p.T] = tile
            back = diff + 2 * p.W
            tiles[1, b * p.T : (b + 1) * p.T, a * p.T : (a + 1) * p.T] = jnp.where(
                back == 1, next_, farb
            )


def block_pair(plan, ref, pair, w, row, count):
    p = plan
    return jnp.concatenate(
        [
            ref[p.source(2 * pair, w), pl.ds(row, count), :],
            ref[p.source(2 * pair + 1, w), pl.ds(row, count), :],
        ],
        axis=1,
    )


def attend_kernel(plan, recv, lines, o_ref, of_ref, rl_ref, kn, vt, tiles):
    p = plan
    me = lax.axis_index("rep")
    w = me % p.W
    group = (me // p.W) % p.G
    h = pl.program_id(0)
    row = pl.multiple_of(h * DH, DH)
    bias_tiles(p, w, lines.at[group * p.HG + h], tiles)
    for r in range(p.R):
        kn[r * p.T : (r + 1) * p.T, :] = jnp.transpose(
            recv[r, pl.ds(p.F + row, DH), :].astype(F32)
        ).astype(B16)
        vt[0:DH, r * p.T : (r + 1) * p.T] = recv[r, pl.ds(2 * p.F + row, DH), :]
    vt[DH : DH + ONES, :] = jnp.ones((ONES, p.L), B16)
    for pair in range(p.NP):
        qt = block_pair(p, recv, pair, w, row, DH)

        def step(i, acc, pair=pair, qt=qt):
            start = pl.multiple_of(i * p.CK, p.CK)
            s = dot(kn[pl.ds(start, p.CK), :], qt)
            e = jnp.exp(s + tiles[jnp.maximum(i - pair + 2, 0)])
            return acc + dot(vt[:, pl.ds(start, p.CK)], e.astype(B16))

        acc = lax.fori_loop(0, pair + 1, step, jnp.zeros((DH + ONES, 2 * p.T), F32))
        rl = 1.0 / acc[DH : DH + 1]
        of = acc[:DH] * rl
        rl_ref[h, pair] = rl
        for a in range(2):
            part = of[:, a * p.T : (a + 1) * p.T]
            of_ref[2 * pair + a, pl.ds(row, DH), :] = part
            o_ref[2 * pair + a, pl.ds(row, DH), :] = part.astype(B16)


def attend_back_kernel(
    plan, recv, lines, dout, of_ref, rl_ref, dq_ref, dkv_ref, line_ref, kn, vn, kt, dk, dv, tiles, near
):
    p = plan
    me = lax.axis_index("rep")
    w = me % p.W
    group = (me // p.W) % p.G
    h = pl.program_id(0)
    row = pl.multiple_of(h * DH, DH)
    bias_tiles(p, w, lines.at[group * p.HG + h], tiles)
    for r in range(p.R):
        kn[r * p.T : (r + 1) * p.T, :] = jnp.transpose(
            recv[r, pl.ds(p.F + row, DH), :].astype(F32)
        ).astype(B16)
        vn[r * p.T : (r + 1) * p.T, :] = jnp.transpose(
            recv[r, pl.ds(2 * p.F + row, DH), :].astype(F32)
        ).astype(B16)
        kt[0:DH, r * p.T : (r + 1) * p.T] = recv[r, pl.ds(p.F + row, DH), :]
    kt[DH : DH + ONES, :] = jnp.ones((ONES, p.L), B16)
    dk[...] = jnp.zeros_like(dk)
    dv[...] = jnp.zeros_like(dv)
    near[...] = jnp.zeros_like(near)
    total = jnp.zeros((1, 2 * p.T), F32)
    for pair in range(p.NP):
        qt = block_pair(p, recv, pair, w, row, DH)
        dot_rows = jnp.concatenate(
            [dout[2 * pair + a, pl.ds(row, DH), :] for a in range(2)], axis=1
        )
        of = jnp.concatenate([of_ref[2 * pair + a, pl.ds(row, DH), :] for a in range(2)], axis=1)
        delta = jnp.sum(dot_rows.astype(F32) * of, axis=0, keepdims=True)
        rl = rl_ref[h, pair]
        qn = jnp.transpose(qt.astype(F32)).astype(B16)
        don = jnp.transpose(dot_rows.astype(F32)).astype(B16)

        def step(i, acc, pair=pair, qt=qt, dot_rows=dot_rows, delta=delta, rl=rl, qn=qn, don=don):
            start = pl.multiple_of(i * p.CK, p.CK)
            kind = jnp.maximum(i - pair + 2, 0)
            keys = pl.ds(start, p.CK)
            prob = jnp.exp(dot(kn[keys, :], qt) + tiles[kind]) * rl
            ds = (prob * (dot(vn[keys, :], dot_rows) - delta)).astype(B16)
            near[kind] += ds.astype(F32)
            dk[keys, :] += dot(ds, qn)
            dv[keys, :] += dot(prob.astype(B16), don)
            return acc + dot(kt[:, keys], ds)

        acc = lax.fori_loop(0, pair + 1, step, jnp.zeros((DH + ONES, 2 * p.T), F32))
        total = total + acc[DH : DH + 1]
        for a in range(2):
            dq_ref[2 * pair + a, pl.ds(row, DH), :] = acc[:DH, a * p.T : (a + 1) * p.T].astype(B16)
    for r in range(p.R):
        dkv_ref[r, pl.ds(row, DH), :] = jnp.transpose(dk[r * p.T : (r + 1) * p.T, :]).astype(B16)
        dkv_ref[r, pl.ds(p.F + row, DH), :] = jnp.transpose(dv[r * p.T : (r + 1) * p.T, :]).astype(
            B16
        )
    same = jnp.zeros((p.T, p.T), F32)
    next_ = jnp.zeros((p.T, p.T), F32)
    for a in range(2):
        ahead = w if a == 0 else 2 * p.W - 1 - w
        for b in range(2 * p.W):
            diff = ahead - b
            spot = (slice(b * p.T, (b + 1) * p.T), slice(a * p.T, (a + 1) * p.T))
            tile = near[(2, *spot)]
            same = same + jnp.where(diff == 0, tile, 0.0)
            next_ = next_ + jnp.where(diff == 1, tile, 0.0)
            next_ = next_ + jnp.where(diff + 2 * p.W == 1, near[(1, *spot)], 0.0)
    both = jnp.concatenate([same, next_], axis=1)
    key = lax.broadcasted_iota(jnp.int32, (p.T, p.T), 0)
    other = lax.broadcasted_iota(jnp.int32, (p.T, p.T), 1)
    swap = (key + other == p.T - 1).astype(F32)
    turned = lax.dot_general(
        swap,
        both,
        (((1,), (0,)), ((), ())),
        precision=lax.Precision.HIGHEST,
        preferred_element_type=F32,
    )
    turned = pltpu.roll(turned, p.T + 1, 1, stride=1, stride_axis=0)
    by_distance = jnp.sum(turned, axis=0, keepdims=True)
    rest = jnp.sum(total) - jnp.sum(both)
    place = lax.broadcasted_iota(jnp.int32, (1, 2 * p.T), 1)
    line_ref[h] = by_distance + jnp.where(place == 2 * p.T - 1, rest, 0.0)


def encode_kernel(enc, wk, wv, kn, kt, vn, vt):
    rows = enc.shape[0]
    for weight, natural, turned in ((wk, kn, kt), (wv, vn, vt)):
        value = dot(enc[...], weight[...])
        for h in range(H):
            natural[h] = value[:, h * DH : (h + 1) * DH].astype(B16)
        flipped = jnp.transpose(value).astype(B16)
        for h in range(H):
            turned[h, 0:DH, :] = flipped[h * DH : (h + 1) * DH]
            turned[h, DH : DH + ONES, :] = jnp.ones((ONES, rows), B16)


def cross_kernel(
    seqs, hidden, ot, wo, gain, wcq, wco, kn, vt, x1_ref, x2_ref, a2_ref, qt_ref, of_ref, rl_ref
):
    toks = hidden.shape[1]
    span = kn.shape[1] // seqs
    x = hidden[...].reshape(seqs * toks, D).astype(F32)
    o = jnp.concatenate(
        [jnp.transpose(ot[s].astype(F32)) for s in range(seqs)], axis=0
    ).astype(B16)
    x1 = x + dot(o, wo[...])
    x1_ref[...] = x1
    a2 = (x1 * scale_of(x1) * gain[...]).astype(B16)
    a2_ref[...] = a2
    q2 = dot(a2, wcq[...])
    for s in range(seqs):
        qt_ref[s] = jnp.transpose(q2[s * toks : (s + 1) * toks]).astype(B16)

    def heads(i, carry):
        for sub in range(2):
            h = 2 * i + sub
            row = pl.multiple_of(h * DH, DH)
            for s in range(seqs):
                keys = slice(s * span, (s + 1) * span)
                e = jnp.exp(dot(kn[h, keys, :], qt_ref[s, pl.ds(row, DH), :]))
                acc = dot(vt[h, :, keys], e.astype(B16))
                rl = 1.0 / acc[DH : DH + 1]
                of_ref[s, pl.ds(row, DH), :] = acc[:DH] * rl
                rl_ref[s, h] = rl
        return carry

    lax.fori_loop(0, H // 2, heads, 0)
    o2 = jnp.concatenate([jnp.transpose(of_ref[s]) for s in range(seqs)], axis=0).astype(B16)
    x2_ref[...] = x1 + dot(o2, wco[...])


def ffn_kernel(
    x2_ref, og_ref, gain, wg, wu, wd, out_ref, dx2_ref, dgain_ref, dwg, dwu, dwd, a3, acc, da3
):
    step = pl.program_id(0)

    @pl.when(step == 0)
    def _():
        x2 = x2_ref[...]
        a3[...] = (x2 * scale_of(x2) * gain[...]).astype(B16)
        acc[...] = x2
        da3[...] = jnp.zeros_like(da3)

    rows = a3[...]
    og = og_ref[...]
    gate = dot(rows, wg[...])
    up = dot(rows, wu[...])
    square = gate * gate
    th = jnp.tanh(GELU_A * gate * (1.0 + GELU_B * square))
    half = 0.5 * (1.0 + th)
    value = gate * half
    slope = half + 0.5 * gate * (1.0 - th * th) * (GELU_A * (1.0 + 3.0 * GELU_B * square))
    inner = (value * up).astype(B16)
    acc[...] += dot(inner, wd[...])
    dwd[...] = t_dot(inner, og).astype(B16)
    dinner = dot_t(og, wd[...]).astype(B16).astype(F32)
    dgate = (dinner * up * slope).astype(B16)
    dup = (dinner * value).astype(B16)
    dwg[...] = t_dot(rows, dgate).astype(B16)
    dwu[...] = t_dot(rows, dup).astype(B16)
    da3[...] += dot_t(dgate, wg[...]) + dot_t(dup, wu[...])

    @pl.when(step == pl.num_programs(0) - 1)
    def _():
        out_ref[...] = acc[...].astype(B16)
        dv, dgain = norm_back(x2_ref[...], gain[...], da3[...])
        dx2_ref[...] = og_ref[...].astype(F32) + dv
        dgain_ref[...] = dgain


def cross_back_kernel(
    seqs,
    groups,
    dx2_ref,
    x1_ref,
    a2_ref,
    gain,
    qt_ref,
    of_ref,
    rl_ref,
    kn,
    kt,
    vn,
    enc,
    wco,
    wcq,
    wck,
    wcv,
    wo,
    ot,
    dx1_ref,
    dgain_ref,
    dot_ref,
    denc_ref,
    dwco,
    dwcq,
    dwck,
    dwcv,
    dwo,
    dt,
    dqt,
    dk,
    dv,
):
    toks = qt_ref.shape[2]
    span = kn.shape[1] // seqs
    dx2 = dx2_ref[...]
    dc = dx2.astype(B16)
    o2t = [of_ref[s].astype(B16) for s in range(seqs)]
    total = dot(o2t[0], dc[0:toks])
    for s in range(1, seqs):
        total = total + dot(o2t[s], dc[s * toks : (s + 1) * toks])
    dwco[...] = total.astype(B16)
    do2 = dot_t(dc, wco[...])
    for s in range(seqs):
        dt[s] = jnp.transpose(do2[s * toks : (s + 1) * toks]).astype(B16)

    def heads(i, carry):
        col = pl.multiple_of(2 * i * DH, 2 * DH)
        for s in range(seqs):
            keys = slice(s * span, (s + 1) * span)
            dks, dvs = [], []
            q_pair = jnp.transpose(qt_ref[s, pl.ds(col, 2 * DH), :].astype(F32)).astype(B16)
            d_pair = jnp.transpose(dt[s, pl.ds(col, 2 * DH), :].astype(F32)).astype(B16)
            for sub in range(2):
                h = 2 * i + sub
                row = pl.multiple_of(h * DH, DH)
                d_rows = dt[s, pl.ds(row, DH), :]
                prob = jnp.exp(dot(kn[h, keys, :], qt_ref[s, pl.ds(row, DH), :])) * rl_ref[s, h]
                delta = jnp.sum(
                    d_rows.astype(F32) * of_ref[s, pl.ds(row, DH), :], axis=0, keepdims=True
                )
                ds = (prob * (dot(vn[h, keys, :], d_rows) - delta)).astype(B16)
                dqt[s, pl.ds(row, DH), :] = dot(kt[h, 0:DH, keys], ds).astype(B16)
                dks.append(dot(ds, q_pair[:, sub * DH : (sub + 1) * DH]))
                dvs.append(dot(prob.astype(B16), d_pair[:, sub * DH : (sub + 1) * DH]))
            dk[keys, pl.ds(col, 2 * DH)] = jnp.concatenate(dks, axis=1).astype(B16)
            dv[keys, pl.ds(col, 2 * DH)] = jnp.concatenate(dvs, axis=1).astype(B16)
        return carry

    lax.fori_loop(0, H // 2, heads, 0)
    dwck[...] = t_dot(enc[...], dk[...]).astype(B16)
    dwcv[...] = t_dot(enc[...], dv[...]).astype(B16)
    denc_ref[...] = (dot_t(dk[...], wck[...]) + dot_t(dv[...], wcv[...])).astype(B16)
    dq2 = jnp.concatenate(
        [jnp.transpose(dqt[s].astype(F32)) for s in range(seqs)], axis=0
    ).astype(B16)
    dwcq[...] = t_dot(a2_ref[...], dq2).astype(B16)
    term, dgain = norm_back(x1_ref[...], gain[...], dot_t(dq2, wcq[...]))
    dgain_ref[...] = dgain
    dx1 = dx2 + term
    dx1_ref[...] = dx1
    db = dx1.astype(B16)
    total = dot(ot[0], db[0:toks])
    for s in range(1, seqs):
        total = total + dot(ot[s], db[s * toks : (s + 1) * toks])
    dwo[...] = total.astype(B16)
    do = dot_t(db, wo[...])
    width = D // groups
    for s in range(seqs):
        turned = jnp.transpose(do[s * toks : (s + 1) * toks]).astype(B16)
        for g in range(groups):
            dot_ref[s * groups + g] = turned[g * width : (g + 1) * width]


def last_kernel(plan, hidden, grads, a1, gain, dx1, wq, wk, wv, dh_ref, dgain_ref, dwq, dwk, dwv):
    p = plan
    x = hidden[...].reshape(p.S * p.T, D).astype(F32)
    da1 = jnp.zeros((p.S * p.T, D), F32)
    for n, (weight, dw) in enumerate(((wq, dwq), (wk, dwk), (wv, dwv))):
        rows = []
        for s in range(p.S):
            turned = jnp.concatenate(
                [grads[s * p.G + g, n * p.F : (n + 1) * p.F, :] for g in range(p.G)], axis=0
            )
            rows.append(jnp.transpose(turned.astype(F32)))
        d = jnp.concatenate(rows, axis=0).astype(B16)
        dw[...] = t_dot(a1[...], d).astype(B16)
        da1 = da1 + dot_t(d, weight[...])
    term, dgain = norm_back(x, gain[...], da1)
    dgain_ref[...] = dgain
    dh_ref[...] = (dx1[...] + term).astype(B16).reshape(dh_ref.shape)


def gather_rows(part):
    count = lax.axis_size("shard")
    rows, cols = part.shape
    half = rows // 2
    mine = lax.axis_index("shard")
    core = lax.axis_index("rep") % 2
    pairs = [(r, r ^ 1) for r in range(lax.axis_size("rep"))]
    own = lax.dynamic_slice(part, (core * half, 0), (half, cols))
    full = jnp.zeros((count, rows, cols), part.dtype)
    full = lax.dynamic_update_slice(full, part[None], (mine, 0, 0))
    for k in range(1, count):
        got = lax.ppermute(own, "shard", [(i, (i + k) % count) for i in range(count)])
        also = lax.ppermute(got, "rep", pairs)
        owner = (mine - k) % count
        full = lax.dynamic_update_slice(full, got[None], (owner, core * half, 0))
        full = lax.dynamic_update_slice(full, also[None], (owner, (1 - core) * half, 0))
    return full.reshape(count * rows, cols)


def reduce_grads(grads):
    owned = [lax.psum_scatter(g, "shard", scatter_dimension=0, tiled=True) for g in grads]
    summed = lax.psum(tuple(owned), "rep")
    return [s.astype(F32) for s in summed]


def local(
    hidden,
    encoded,
    out_grad,
    self_query,
    self_key,
    self_value,
    self_out,
    cross_query,
    cross_key,
    cross_value,
    cross_out,
    ffn_gate,
    ffn_up,
    ffn_down,
    gain_self,
    gain_cross,
    gain_ffn,
    bias_table,
    buckets,
):
    seqs, toks = hidden.shape[0], hidden.shape[1]
    p = Plan(seqs, toks, lax.axis_size("rep"))
    tokens = seqs * toks
    ff = ffn_gate.shape[1]
    enc_rows = seqs * encoded.shape[1] * p.R
    dma = pltpu.SemaphoreType.DMA

    small = jnp.concatenate(
        [
            jnp.stack([gain_self, gain_cross, gain_ffn]).reshape(-1),
            bias_table.reshape(-1),
        ]
    ).astype(B16)
    small = lax.all_gather(small, "shard", axis=0)
    part = gain_self.shape[0]
    gains = [
        small[:, i * part : (i + 1) * part].reshape(1, D).astype(F32) for i in range(3)
    ]
    table = small[:, 3 * part :].reshape(NB, H)
    near = buckets[: 2 * toks]
    onehot = (near[:, None] == jnp.arange(NB, dtype=jnp.int32)[None, :]).astype(B16)
    lines = jnp.einsum("lb,bh->hl", onehot, table, preferred_element_type=F32)[:, None, :]

    wq, wk, wv, wo, wcq, wck, wcv, wco, wg, wu, wd = [
        gather_rows(m.astype(B16))
        for m in (
            self_query,
            self_key,
            self_value,
            self_out,
            cross_query,
            cross_key,
            cross_value,
            cross_out,
            ffn_gate,
            ffn_up,
            ffn_down,
        )
    ]
    enc = lax.all_gather(encoded, "rep", axis=1, tiled=True).reshape(enc_rows, D)

    a1, send = plain_call(
        functools.partial(project_kernel, p),
        [((tokens, D), B16), ((p.U, 3 * p.F, toks), B16)],
        (hidden, gains[0], wq, wk, wv),
        "project",
    )
    recv = comm_call(
        functools.partial(scatter_tokens, p),
        (p.R, 3 * p.F, toks),
        (send,),
        [dma((p.U,)), dma((max(p.W - 1, 1), p.J)), dma((p.R,))],
        0,
        "scatter_tokens",
    )
    ckn, ckt, cvn, cvt = plain_call(
        encode_kernel,
        [
            ((H, enc_rows, DH), B16),
            ((H, DH + ONES, enc_rows), B16),
            ((H, enc_rows, DH), B16),
            ((H, DH + ONES, enc_rows), B16),
        ],
        (enc, wck, wcv),
        "encode",
    )
    o, of, rl = pl.pallas_call(
        functools.partial(attend_kernel, p),
        grid=(p.HG,),
        out_shape=[
            jax.ShapeDtypeStruct((p.J, p.F, toks), B16),
            jax.ShapeDtypeStruct((p.J, p.F, toks), F32),
            jax.ShapeDtypeStruct((p.HG, p.NP, 1, 2 * toks), F32),
        ],
        in_specs=[whole((p.R, 3 * p.F, toks)), whole((H, 1, 2 * toks))],
        out_specs=[
            whole((p.J, p.F, toks)),
            whole((p.J, p.F, toks)),
            whole((p.HG, p.NP, 1, 2 * toks)),
        ],
        scratch_shapes=[
            pltpu.VMEM((p.L, DH), B16),
            pltpu.VMEM((DH + ONES, p.L), B16),
            pltpu.VMEM((3, p.CK, 2 * toks), F32),
        ],
        compiler_params=pltpu.CompilerParams(vmem_limit_bytes=56 * 2**20),
        name="attend",
    )(recv, lines)
    ot = comm_call(
        functools.partial(return_tokens, p),
        (p.U, p.F, toks),
        (o,),
        [dma((p.J,)), dma((p.U,))],
        1,
        "return_tokens",
    ).reshape(seqs, D, toks)

    x1, x2, a2, qt2, of2, rl2 = plain_call(
        functools.partial(cross_kernel, seqs),
        [
            ((tokens, D), F32),
            ((tokens, D), F32),
            ((tokens, D), B16),
            ((seqs, D, toks), B16),
            ((seqs, D, toks), F32),
            ((seqs, H, 1, toks), F32),
        ],
        (hidden, ot, wo, gains[1], wcq, wco, ckn, cvt),
        "cross",
    )

    chunk = min(512, ff)
    const = lambda s: pl.BlockSpec(s, lambda i: (0, 0))
    output, dx2, dg_ffn, dwg, dwu, dwd = pl.pallas_call(
        ffn_kernel,
        grid=(ff // chunk,),
        out_shape=[
            jax.ShapeDtypeStruct((tokens, D), B16),
            jax.ShapeDtypeStruct((tokens, D), F32),
            jax.ShapeDtypeStruct((1, D), F32),
            jax.ShapeDtypeStruct((D, ff), B16),
            jax.ShapeDtypeStruct((D, ff), B16),
            jax.ShapeDtypeStruct((ff, D), B16),
        ],
        in_specs=[
            const((tokens, D)),
            const((tokens, D)),
            const((1, D)),
            pl.BlockSpec((D, chunk), lambda i: (0, i)),
            pl.BlockSpec((D, chunk), lambda i: (0, i)),
            pl.BlockSpec((chunk, D), lambda i: (i, 0)),
        ],
        out_specs=[
            const((tokens, D)),
            const((tokens, D)),
            const((1, D)),
            pl.BlockSpec((D, chunk), lambda i: (0, i)),
            pl.BlockSpec((D, chunk), lambda i: (0, i)),
            pl.BlockSpec((chunk, D), lambda i: (i, 0)),
        ],
        scratch_shapes=[
            pltpu.VMEM((tokens, D), B16),
            pltpu.VMEM((tokens, D), F32),
            pltpu.VMEM((tokens, D), F32),
        ],
        compiler_params=pltpu.CompilerParams(vmem_limit_bytes=56 * 2**20),
        name="ffn",
    )(x2, out_grad.reshape(tokens, D), gains[2], wg, wu, wd)

    dx1, dg_cross, dot_, denc, dwco, dwcq, dwck, dwcv, dwo = plain_call(
        functools.partial(cross_back_kernel, seqs, p.G),
        [
            ((tokens, D), F32),
            ((1, D), F32),
            ((p.U, p.F, toks), B16),
            ((enc_rows, D), B16),
        ]
        + [((D, D), B16)] * 5,
        (dx2, x1, a2, gains[1], qt2, of2, rl2, ckn, ckt, cvn, enc, wco, wcq, wck, wcv, wo, ot),
        "cross_back",
        scratch=[
            pltpu.VMEM((seqs, D, toks), B16),
            pltpu.VMEM((seqs, D, toks), B16),
            pltpu.VMEM((enc_rows, D), B16),
            pltpu.VMEM((enc_rows, D), B16),
        ],
    )
    encoded_grad = lax.psum_scatter(
        denc.reshape(seqs, enc_rows // seqs, D), "rep", scatter_dimension=1, tiled=True
    )
    dout = comm_call(
        functools.partial(scatter_rows, p),
        (p.J, p.F, toks),
        (dot_,),
        [dma((p.U,)), dma((p.J,))],
        2,
        "scatter_rows",
    )
    dq, dkv, line = pl.pallas_call(
        functools.partial(attend_back_kernel, p),
        grid=(p.HG,),
        out_shape=[
            jax.ShapeDtypeStruct((p.J, p.F, toks), B16),
            jax.ShapeDtypeStruct((p.R, 2 * p.F, toks), B16),
            jax.ShapeDtypeStruct((p.HG, 1, 2 * toks), F32),
        ],
        in_specs=[
            whole((p.R, 3 * p.F, toks)),
            whole((H, 1, 2 * toks)),
            whole((p.J, p.F, toks)),
            whole((p.J, p.F, toks)),
            whole((p.HG, p.NP, 1, 2 * toks)),
        ],
        out_specs=[
            whole((p.J, p.F, toks)),
            whole((p.R, 2 * p.F, toks)),
            whole((p.HG, 1, 2 * toks)),
        ],
        scratch_shapes=[
            pltpu.VMEM((p.L, DH), B16),
            pltpu.VMEM((p.L, DH), B16),
            pltpu.VMEM((DH + ONES, p.L), B16),
            pltpu.VMEM((p.L, DH), F32),
            pltpu.VMEM((p.L, DH), F32),
            pltpu.VMEM((3, p.CK, 2 * toks), F32),
            pltpu.VMEM((3, p.CK, 2 * toks), F32),
        ],
        compiler_params=pltpu.CompilerParams(vmem_limit_bytes=56 * 2**20),
        name="attend_back",
    )(recv, lines, dout, of, rl)
    grads = comm_call(
        functools.partial(return_grads, p),
        (p.U, 3 * p.F, toks),
        (dq, dkv),
        [
            pltpu.VMEM((max(p.W - 1, 1), p.J, 2 * p.F, toks), B16),
            pltpu.VMEM((p.J, 3 * p.F, toks), B16),
            dma((p.J,)),
            dma((max(p.W - 1, 1), p.J)),
            dma((max(p.W - 1, 1), p.J)),
            dma((p.U,)),
        ],
        3,
        "return_grads",
        space=pltpu.VMEM,
    )
    hidden_grad, dg_self, dwq, dwk, dwv = plain_call(
        functools.partial(last_kernel, p),
        [(hidden.shape, B16), ((1, D), F32)] + [((D, D), B16)] * 3,
        (hidden, grads, a1, gains[0], dx1, wq, wk, wv),
        "last",
    )

    group = (lax.axis_index("rep") // p.W) % p.G
    by_bucket = jnp.einsum(
        "hl,lb->bh", line[:, 0, :], onehot.astype(F32), precision=lax.Precision.HIGHEST
    )
    dtable = lax.dynamic_update_slice(jnp.zeros((NB, H), F32), by_bucket, (0, group * p.HG))

    mats = reduce_grads([dwq, dwk, dwv, dwo, dwcq, dwck, dwcv, dwco, dwg, dwu, dwd])
    n_shard = lax.axis_size("shard")
    lot = jnp.concatenate(
        [g.reshape(n_shard, part) for g in (dg_self, dg_cross, dg_ffn)]
        + [dtable.reshape(n_shard, -1)],
        axis=1,
    )
    lot = lax.psum(lot, ("shard", "rep"))
    lot = lax.dynamic_slice(lot, (lax.axis_index("shard"), 0), (1, lot.shape[1]))[0]
    dgains = [lot[i * part : (i + 1) * part] for i in range(3)]
    dtab = lot[3 * part :].reshape(bias_table.shape)
    return (
        output.reshape(hidden.shape),
        hidden_grad,
        encoded_grad,
        *mats,
        *dgains,
        dtab,
    )


def solution(mesh):
    tok = P("shard", "rep", None)
    mat = P("shard", None)
    in_specs = (tok,) * 3 + (mat,) * 11 + (P("shard"),) * 3 + (mat, P())
    out_specs = (tok,) * 3 + (mat,) * 11 + (P("shard"),) * 3 + (mat,)
    return jax.shard_map(local, mesh=mesh, in_specs=in_specs, out_specs=out_specs, check_vma=False)
```

```python
import functools

import jax
import jax.numpy as jnp
from jax import lax
from jax.experimental import pallas as pl
from jax.experimental.pallas import tpu as pltpu
from jax.sharding import PartitionSpec as P

D = 768
H = 12
DH = 64
NB = 32
EPS = 1e-06
F32 = jnp.float32
B16 = jnp.bfloat16
ONES = 16
HIDE = -1e30
MESH = pl.DeviceIdType.MESH
GELU_A = 0.7978845608028654
GELU_B = 0.044715


def dot(a, b):
    return lax.dot_general(a, b, (((1,), (0,)), ((), ())), preferred_element_type=F32)


def dot_t(a, b):
    return lax.dot_general(a, b, (((1,), (1,)), ((), ())), preferred_element_type=F32)


def t_dot(a, b):
    return lax.dot_general(a, b, (((0,), (0,)), ((), ())), preferred_element_type=F32)


def scale_of(v):
    return lax.rsqrt(jnp.mean(v * v, axis=-1, keepdims=True) + EPS)


def norm_back(v, gain, grad):
    r = scale_of(v)
    n = v * r
    c = grad * gain
    dv = r * (c - n * jnp.mean(c * n, axis=-1, keepdims=True))
    return dv, jnp.sum(grad * n, axis=0, keepdims=True)


def whole(shape):
    return pl.BlockSpec(shape, lambda *_: (0,) * len(shape))


def plain_call(kernel, outs, args, name, scratch=(), vmem=60):
    return pl.pallas_call(
        kernel,
        out_shape=[jax.ShapeDtypeStruct(s, t) for s, t in outs],
        in_specs=[pl.BlockSpec(memory_space=pltpu.VMEM)] * len(args),
        out_specs=[pl.BlockSpec(memory_space=pltpu.VMEM)] * len(outs),
        scratch_shapes=list(scratch),
        compiler_params=pltpu.CompilerParams(vmem_limit_bytes=vmem * 2**20),
        name=name,
    )(*args)


class Plan:
    def __init__(self, seqs, toks, rows):
        self.S, self.T, self.R = seqs, toks, rows
        groups = 1
        for g in range(1, H + 1):
            if H % g == 0 and seqs * g <= rows and rows % (2 * seqs * g) == 0:
                groups = g
        self.G = groups
        self.HG = H // groups
        self.F = self.HG * DH
        self.U = seqs * groups
        self.W = rows // self.U
        self.J = rows // self.W
        self.NP = self.J // 2
        self.CK = 2 * self.W * toks
        self.L = rows * toks

    def worker_of(self, r):
        m = r % (2 * self.W)
        late = m // self.W
        return m * (1 - late) + (2 * self.W - 1 - m) * late

    def slot_of(self, r):
        return 2 * (r // (2 * self.W)) + (r % (2 * self.W)) // self.W

    def source(self, j, w):
        if j % 2 == 0:
            return 2 * self.W * (j // 2) + w
        return 2 * self.W * (j // 2) + 2 * self.W - 1 - w


def enter(rows):
    me = lax.axis_index("rep")
    barrier = pltpu.get_barrier_semaphore()
    for k in range(1, rows):
        pl.semaphore_signal(
            barrier, inc=1, device_id={"rep": (me + k) % rows}, device_id_type=MESH
        )
    pl.semaphore_wait(barrier, rows - 1)
    return me


def remote(src, dst, send, recv, to):
    return pltpu.make_async_remote_copy(
        src_ref=src,
        dst_ref=dst,
        send_sem=send,
        recv_sem=recv,
        device_id={"rep": to},
        device_id_type=MESH,
    )


def start_either(me, to, src, dst, send, recv):
    @pl.when(to == me)
    def _():
        pltpu.make_async_copy(src, dst, recv).start()

    @pl.when(to != me)
    def _():
        remote(src, dst, send, recv, to).start()


def end_either(me, to, src, dst, send, recv):
    @pl.when(to != me)
    def _():
        remote(src, dst, send, recv, to).wait_send()


def landed(ref, sem):
    pltpu.make_async_copy(ref, ref, sem).wait()


def scatter_tokens(plan, send, recv, send_sem, relay_sem, recv_sem):
    p = plan
    me = enter(p.R)
    w = me % p.W
    mine = p.worker_of(me)
    for u in range(p.U):
        start_either(me, u * p.W + mine, send.at[u], recv.at[me], send_sem.at[u], recv_sem.at[me])
    for j in range(p.J):
        r = p.source(j, w)
        landed(recv.at[r], recv_sem.at[r])
        for k in range(1, p.W):
            part = recv.at[r, pl.ds(p.F, 2 * p.F)]
            remote(
                part, part, relay_sem.at[k - 1, j], recv_sem.at[r], me - w + (w + k) % p.W
            ).start()
    for k in range(1, p.W):
        for j in range(p.J):
            r = p.source(j, (w + k) % p.W)
            landed(recv.at[r, pl.ds(p.F, 2 * p.F)], recv_sem.at[r])
    for u in range(p.U):
        end_either(me, u * p.W + mine, send.at[u], recv.at[me], send_sem.at[u], recv_sem.at[me])
    for k in range(1, p.W):
        for j in range(p.J):
            r = p.source(j, w)
            part = recv.at[r, pl.ds(p.F, 2 * p.F)]
            remote(
                part, part, relay_sem.at[k - 1, j], recv_sem.at[r], me - w + (w + k) % p.W
            ).wait_send()


def return_tokens(plan, send, recv, send_sem, recv_sem):
    p = plan
    me = enter(p.R)
    w = me % p.W
    unit = me // p.W
    for j in range(p.J):
        r = p.source(j, w)
        start_either(me, r, send.at[j], recv.at[unit], send_sem.at[j], recv_sem.at[unit])
    for u in range(p.U):
        landed(recv.at[u], recv_sem.at[u])
    for j in range(p.J):
        r = p.source(j, w)
        end_either(me, r, send.at[j], recv.at[unit], send_sem.at[j], recv_sem.at[unit])


def scatter_rows(plan, send, recv, send_sem, recv_sem):
    p = plan
    me = enter(p.R)
    mine = p.worker_of(me)
    slot = p.slot_of(me)
    for u in range(p.U):
        start_either(
            me, u * p.W + mine, send.at[u], recv.at[slot], send_sem.at[u], recv_sem.at[slot]
        )
    for j in range(p.J):
        landed(recv.at[j], recv_sem.at[j])
    for u in range(p.U):
        end_either(
            me, u * p.W + mine, send.at[u], recv.at[slot], send_sem.at[u], recv_sem.at[slot]
        )


def return_grads(plan, dq, dkv, recv, buf, out, send_sem, part_sem, got_sem, recv_sem):
    p = plan
    me = enter(p.R)
    w = me % p.W
    unit = me // p.W

    def give(k, j):
        to = (w + k) % p.W
        r = p.source(j, to)
        return remote(
            dkv.at[r],
            buf.at[k - 1, j],
            part_sem.at[k - 1, j],
            got_sem.at[k - 1, j],
            me - w + to,
        )

    for j in range(p.J):
        for k in range(1, p.W):
            give(k, j).start()
    for j in range(p.J):
        r = p.source(j, w)
        total = dkv[r].astype(F32)
        for k in range(1, p.W):
            landed(buf.at[k - 1, j], got_sem.at[k - 1, j])
            total = total + buf[k - 1, j].astype(F32)
        out[j, 0 : p.F, :] = dq[j]
        out[j, p.F : 3 * p.F, :] = total.astype(B16)
        start_either(me, r, out.at[j], recv.at[unit], send_sem.at[j], recv_sem.at[unit])
    for u in range(p.U):
        landed(recv.at[u], recv_sem.at[u])
    for j in range(p.J):
        r = p.source(j, w)
        end_either(me, r, out.at[j], recv.at[unit], send_sem.at[j], recv_sem.at[unit])
        for k in range(1, p.W):
            give(k, j).wait_send()


def comm_call(kernel, out, args, scratch, collective, name, space=pl.ANY):
    return pl.pallas_call(
        kernel,
        out_shape=jax.ShapeDtypeStruct(out, B16),
        in_specs=[pl.BlockSpec(memory_space=space)] * len(args),
        out_specs=pl.BlockSpec(memory_space=space),
        scratch_shapes=list(scratch),
        compiler_params=pltpu.CompilerParams(
            collective_id=collective, has_side_effects=True, vmem_limit_bytes=40 * 2**20
        ),
        name=name,
    )(*args)


def project_kernel(plan, hidden, gain, wq, wk, wv, a1_ref, send):
    p = plan
    x = hidden[...].reshape(p.S * p.T, D).astype(F32)
    a1 = (x * scale_of(x) * gain[...]).astype(B16)
    a1_ref[...] = a1
    for n, weight in enumerate((wq, wk, wv)):
        rows = dot(a1, weight[...])
        for s in range(p.S):
            turned = jnp.transpose(rows[s * p.T : (s + 1) * p.T]).astype(B16)
            for g in range(p.G):
                send[s * p.G + g, n * p.F : (n + 1) * p.F, :] = turned[g * p.F : (g + 1) * p.F]


def bias_tiles(plan, w, line, tiles):
    p = plan
    far = line[0:1, 2 * p.T - 1 : 2 * p.T]
    near = pltpu.roll(
        jnp.broadcast_to(line[0:1, :], (p.T, 2 * p.T)), 0, 1, stride=1, stride_axis=0
    )
    key = lax.broadcasted_iota(jnp.int32, (p.T, p.T), 0)
    query = lax.broadcasted_iota(jnp.int32, (p.T, p.T), 1)
    same = jnp.where(query >= key, near[:, : p.T], HIDE)
    next_ = near[:, p.T :]
    farb = jnp.broadcast_to(far, (p.T, p.T))
    tiles[0] = jnp.broadcast_to(far, (p.CK, 2 * p.T))
    for a in range(2):
        ahead = w if a == 0 else 2 * p.W - 1 - w
        for b in range(2 * p.W):
            diff = ahead - b
            tile = jnp.where(
                diff == 0, same, jnp.where(diff == 1, next_, jnp.where(diff < 0, HIDE, farb))
            )
            tiles[2, b * p.T : (b + 1) * p.T, a * p.T : (a + 1) * p.T] = tile
            back = diff + 2 * p.W
            tiles[1, b * p.T : (b + 1) * p.T, a * p.T : (a + 1) * p.T] = jnp.where(
                back == 1, next_, farb
            )


def block_pair(plan, ref, pair, w, row, count):
    p = plan
    return jnp.concatenate(
        [
            ref[p.source(2 * pair, w), pl.ds(row, count), :],
            ref[p.source(2 * pair + 1, w), pl.ds(row, count), :],
        ],
        axis=1,
    )


def attend_kernel(plan, recv, lines, o_ref, of_ref, rl_ref, kn, vt, tiles):
    p = plan
    me = lax.axis_index("rep")
    w = me % p.W
    group = (me // p.W) % p.G
    h = pl.program_id(0)
    row = pl.multiple_of(h * DH, DH)
    bias_tiles(p, w, lines.at[group * p.HG + h], tiles)
    for r in range(p.R):
        kn[r * p.T : (r + 1) * p.T, :] = jnp.transpose(
            recv[r, pl.ds(p.F + row, DH), :].astype(F32)
        ).astype(B16)
        vt[0:DH, r * p.T : (r + 1) * p.T] = recv[r, pl.ds(2 * p.F + row, DH), :]
    vt[DH : DH + ONES, :] = jnp.ones((ONES, p.L), B16)
    for pair in range(p.NP):
        qt = block_pair(p, recv, pair, w, row, DH)

        def step(i, acc, pair=pair, qt=qt):
            start = pl.multiple_of(i * p.CK, p.CK)
            s = dot(kn[pl.ds(start, p.CK), :], qt)
            e = jnp.exp(s + tiles[jnp.maximum(i - pair + 2, 0)])
            return acc + dot(vt[:, pl.ds(start, p.CK)], e.astype(B16))

        acc = lax.fori_loop(0, pair + 1, step, jnp.zeros((DH + ONES, 2 * p.T), F32))
        rl = 1.0 / acc[DH : DH + 1]
        of = acc[:DH] * rl
        rl_ref[h, pair] = rl
        for a in range(2):
            part = of[:, a * p.T : (a + 1) * p.T]
            of_ref[2 * pair + a, pl.ds(row, DH), :] = part
            o_ref[2 * pair + a, pl.ds(row, DH), :] = part.astype(B16)


def attend_back_kernel(
    plan, recv, lines, dout, of_ref, rl_ref, dq_ref, dkv_ref, line_ref, kn, vn, kt, dk, dv, tiles, near
):
    p = plan
    me = lax.axis_index("rep")
    w = me % p.W
    group = (me // p.W) % p.G
    h = pl.program_id(0)
    row = pl.multiple_of(h * DH, DH)
    bias_tiles(p, w, lines.at[group * p.HG + h], tiles)
    for r in range(p.R):
        kn[r * p.T : (r + 1) * p.T, :] = jnp.transpose(
            recv[r, pl.ds(p.F + row, DH), :].astype(F32)
        ).astype(B16)
        vn[r * p.T : (r + 1) * p.T, :] = jnp.transpose(
            recv[r, pl.ds(2 * p.F + row, DH), :].astype(F32)
        ).astype(B16)
        kt[0:DH, r * p.T : (r + 1) * p.T] = recv[r, pl.ds(p.F + row, DH), :]
    kt[DH : DH + ONES, :] = jnp.ones((ONES, p.L), B16)
    dk[...] = jnp.zeros_like(dk)
    dv[...] = jnp.zeros_like(dv)
    near[...] = jnp.zeros_like(near)
    total = jnp.zeros((1, 2 * p.T), F32)
    for pair in range(p.NP):
        qt = block_pair(p, recv, pair, w, row, DH)
        dot_rows = jnp.concatenate(
            [dout[2 * pair + a, pl.ds(row, DH), :] for a in range(2)], axis=1
        )
        of = jnp.concatenate([of_ref[2 * pair + a, pl.ds(row, DH), :] for a in range(2)], axis=1)
        delta = jnp.sum(dot_rows.astype(F32) * of, axis=0, keepdims=True)
        rl = rl_ref[h, pair]
        qn = jnp.transpose(qt.astype(F32)).astype(B16)
        don = jnp.transpose(dot_rows.astype(F32)).astype(B16)

        def step(i, acc, pair=pair, qt=qt, dot_rows=dot_rows, delta=delta, rl=rl, qn=qn, don=don):
            start = pl.multiple_of(i * p.CK, p.CK)
            kind = jnp.maximum(i - pair + 2, 0)
            keys = pl.ds(start, p.CK)
            prob = jnp.exp(dot(kn[keys, :], qt) + tiles[kind]) * rl
            ds = (prob * (dot(vn[keys, :], dot_rows) - delta)).astype(B16)
            near[kind] += ds.astype(F32)
            dk[keys, :] += dot(ds, qn)
            dv[keys, :] += dot(prob.astype(B16), don)
            return acc + dot(kt[:, keys], ds)

        acc = lax.fori_loop(0, pair + 1, step, jnp.zeros((DH + ONES, 2 * p.T), F32))
        total = total + acc[DH : DH + 1]
        for a in range(2):
            dq_ref[2 * pair + a, pl.ds(row, DH), :] = acc[:DH, a * p.T : (a + 1) * p.T].astype(B16)
    for r in range(p.R):
        dkv_ref[r, pl.ds(row, DH), :] = jnp.transpose(dk[r * p.T : (r + 1) * p.T, :]).astype(B16)
        dkv_ref[r, pl.ds(p.F + row, DH), :] = jnp.transpose(dv[r * p.T : (r + 1) * p.T, :]).astype(
            B16
        )
    same = jnp.zeros((p.T, p.T), F32)
    next_ = jnp.zeros((p.T, p.T), F32)
    for a in range(2):
        ahead = w if a == 0 else 2 * p.W - 1 - w
        for b in range(2 * p.W):
            diff = ahead - b
            spot = (slice(b * p.T, (b + 1) * p.T), slice(a * p.T, (a + 1) * p.T))
            tile = near[(2, *spot)]
            same = same + jnp.where(diff == 0, tile, 0.0)
            next_ = next_ + jnp.where(diff == 1, tile, 0.0)
            next_ = next_ + jnp.where(diff + 2 * p.W == 1, near[(1, *spot)], 0.0)
    both = jnp.concatenate([same, next_], axis=1)
    key = lax.broadcasted_iota(jnp.int32, (p.T, p.T), 0)
    other = lax.broadcasted_iota(jnp.int32, (p.T, p.T), 1)
    swap = (key + other == p.T - 1).astype(F32)
    turned = lax.dot_general(
        swap,
        both,
        (((1,), (0,)), ((), ())),
        precision=lax.Precision.HIGHEST,
        preferred_element_type=F32,
    )
    turned = pltpu.roll(turned, p.T + 1, 1, stride=1, stride_axis=0)
    by_distance = jnp.sum(turned, axis=0, keepdims=True)
    rest = jnp.sum(total) - jnp.sum(both)
    place = lax.broadcasted_iota(jnp.int32, (1, 2 * p.T), 1)
    line_ref[h] = by_distance + jnp.where(place == 2 * p.T - 1, rest, 0.0)


def encode_kernel(enc, wk, wv, kn, kt, vn, vt):
    rows = enc.shape[0]
    for weight, natural, turned in ((wk, kn, kt), (wv, vn, vt)):
        value = dot(enc[...], weight[...])
        for h in range(H):
            natural[h] = value[:, h * DH : (h + 1) * DH].astype(B16)
        flipped = jnp.transpose(value).astype(B16)
        for h in range(H):
            turned[h, 0:DH, :] = flipped[h * DH : (h + 1) * DH]
            turned[h, DH : DH + ONES, :] = jnp.ones((ONES, rows), B16)


def cross_kernel(
    seqs, hidden, ot, wo, gain, wcq, wco, kn, vt, x1_ref, x2_ref, a2_ref, qt_ref, of_ref, rl_ref
):
    toks = hidden.shape[1]
    span = kn.shape[1] // seqs
    x = hidden[...].reshape(seqs * toks, D).astype(F32)
    o = jnp.concatenate(
        [jnp.transpose(ot[s].astype(F32)) for s in range(seqs)], axis=0
    ).astype(B16)
    x1 = x + dot(o, wo[...])
    x1_ref[...] = x1
    a2 = (x1 * scale_of(x1) * gain[...]).astype(B16)
    a2_ref[...] = a2
    q2 = dot(a2, wcq[...])
    for s in range(seqs):
        qt_ref[s] = jnp.transpose(q2[s * toks : (s + 1) * toks]).astype(B16)

    def heads(i, carry):
        for sub in range(2):
            h = 2 * i + sub
            row = pl.multiple_of(h * DH, DH)
            for s in range(seqs):
                keys = slice(s * span, (s + 1) * span)
                e = jnp.exp(dot(kn[h, keys, :], qt_ref[s, pl.ds(row, DH), :]))
                acc = dot(vt[h, :, keys], e.astype(B16))
                rl = 1.0 / acc[DH : DH + 1]
                of_ref[s, pl.ds(row, DH), :] = acc[:DH] * rl
                rl_ref[s, h] = rl
        return carry

    lax.fori_loop(0, H // 2, heads, 0)
    o2 = jnp.concatenate([jnp.transpose(of_ref[s]) for s in range(seqs)], axis=0).astype(B16)
    x2_ref[...] = x1 + dot(o2, wco[...])


def ffn_kernel(
    x2_ref, og_ref, gain, wg, wu, wd, out_ref, dx2_ref, dgain_ref, dwg, dwu, dwd, a3, acc, da3
):
    step = pl.program_id(0)

    @pl.when(step == 0)
    def _():
        x2 = x2_ref[...]
        a3[...] = (x2 * scale_of(x2) * gain[...]).astype(B16)
        acc[...] = x2
        da3[...] = jnp.zeros_like(da3)

    rows = a3[...]
    og = og_ref[...]
    gate = dot(rows, wg[...])
    up = dot(rows, wu[...])
    square = gate * gate
    th = jnp.tanh(GELU_A * gate * (1.0 + GELU_B * square))
    half = 0.5 * (1.0 + th)
    value = gate * half
    slope = half + 0.5 * gate * (1.0 - th * th) * (GELU_A * (1.0 + 3.0 * GELU_B * square))
    inner = (value * up).astype(B16)
    acc[...] += dot(inner, wd[...])
    dwd[...] = t_dot(inner, og).astype(B16)
    dinner = dot_t(og, wd[...]).astype(B16).astype(F32)
    dgate = (dinner * up * slope).astype(B16)
    dup = (dinner * value).astype(B16)
    dwg[...] = t_dot(rows, dgate).astype(B16)
    dwu[...] = t_dot(rows, dup).astype(B16)
    da3[...] += dot_t(dgate, wg[...]) + dot_t(dup, wu[...])

    @pl.when(step == pl.num_programs(0) - 1)
    def _():
        out_ref[...] = acc[...].astype(B16)
        dv, dgain = norm_back(x2_ref[...], gain[...], da3[...])
        dx2_ref[...] = og_ref[...].astype(F32) + dv
        dgain_ref[...] = dgain


def cross_back_kernel(
    seqs,
    groups,
    dx2_ref,
    x1_ref,
    a2_ref,
    gain,
    qt_ref,
    of_ref,
    rl_ref,
    kn,
    kt,
    vn,
    enc,
    wco,
    wcq,
    wck,
    wcv,
    wo,
    ot,
    dx1_ref,
    dgain_ref,
    dot_ref,
    denc_ref,
    dwco,
    dwcq,
    dwck,
    dwcv,
    dwo,
    dt,
    dqt,
    dk,
    dv,
):
    toks = qt_ref.shape[2]
    span = kn.shape[1] // seqs
    dx2 = dx2_ref[...]
    dc = dx2.astype(B16)
    o2t = [of_ref[s].astype(B16) for s in range(seqs)]
    total = dot(o2t[0], dc[0:toks])
    for s in range(1, seqs):
        total = total + dot(o2t[s], dc[s * toks : (s + 1) * toks])
    dwco[...] = total.astype(B16)
    do2 = dot_t(dc, wco[...])
    for s in range(seqs):
        dt[s] = jnp.transpose(do2[s * toks : (s + 1) * toks]).astype(B16)

    def heads(i, carry):
        col = pl.multiple_of(2 * i * DH, 2 * DH)
        for s in range(seqs):
            keys = slice(s * span, (s + 1) * span)
            dks, dvs = [], []
            q_pair = jnp.transpose(qt_ref[s, pl.ds(col, 2 * DH), :].astype(F32)).astype(B16)
            d_pair = jnp.transpose(dt[s, pl.ds(col, 2 * DH), :].astype(F32)).astype(B16)
            for sub in range(2):
                h = 2 * i + sub
                row = pl.multiple_of(h * DH, DH)
                d_rows = dt[s, pl.ds(row, DH), :]
                prob = jnp.exp(dot(kn[h, keys, :], qt_ref[s, pl.ds(row, DH), :])) * rl_ref[s, h]
                delta = jnp.sum(
                    d_rows.astype(F32) * of_ref[s, pl.ds(row, DH), :], axis=0, keepdims=True
                )
                ds = (prob * (dot(vn[h, keys, :], d_rows) - delta)).astype(B16)
                dqt[s, pl.ds(row, DH), :] = dot(kt[h, 0:DH, keys], ds).astype(B16)
                dks.append(dot(ds, q_pair[:, sub * DH : (sub + 1) * DH]))
                dvs.append(dot(prob.astype(B16), d_pair[:, sub * DH : (sub + 1) * DH]))
            dk[keys, pl.ds(col, 2 * DH)] = jnp.concatenate(dks, axis=1).astype(B16)
            dv[keys, pl.ds(col, 2 * DH)] = jnp.concatenate(dvs, axis=1).astype(B16)
        return carry

    lax.fori_loop(0, H // 2, heads, 0)
    dwck[...] = t_dot(enc[...], dk[...]).astype(B16)
    dwcv[...] = t_dot(enc[...], dv[...]).astype(B16)
    denc_ref[...] = (dot_t(dk[...], wck[...]) + dot_t(dv[...], wcv[...])).astype(B16)
    dq2 = jnp.concatenate(
        [jnp.transpose(dqt[s].astype(F32)) for s in range(seqs)], axis=0
    ).astype(B16)
    dwcq[...] = t_dot(a2_ref[...], dq2).astype(B16)
    term, dgain = norm_back(x1_ref[...], gain[...], dot_t(dq2, wcq[...]))
    dgain_ref[...] = dgain
    dx1 = dx2 + term
    dx1_ref[...] = dx1
    db = dx1.astype(B16)
    total = dot(ot[0], db[0:toks])
    for s in range(1, seqs):
        total = total + dot(ot[s], db[s * toks : (s + 1) * toks])
    dwo[...] = total.astype(B16)
    do = dot_t(db, wo[...])
    width = D // groups
    for s in range(seqs):
        turned = jnp.transpose(do[s * toks : (s + 1) * toks]).astype(B16)
        for g in range(groups):
            dot_ref[s * groups + g] = turned[g * width : (g + 1) * width]


def last_kernel(plan, hidden, grads, a1, gain, dx1, wq, wk, wv, dh_ref, dgain_ref, dwq, dwk, dwv):
    p = plan
    x = hidden[...].reshape(p.S * p.T, D).astype(F32)
    da1 = jnp.zeros((p.S * p.T, D), F32)
    for n, (weight, dw) in enumerate(((wq, dwq), (wk, dwk), (wv, dwv))):
        rows = []
        for s in range(p.S):
            turned = jnp.concatenate(
                [grads[s * p.G + g, n * p.F : (n + 1) * p.F, :] for g in range(p.G)], axis=0
            )
            rows.append(jnp.transpose(turned.astype(F32)))
        d = jnp.concatenate(rows, axis=0).astype(B16)
        dw[...] = t_dot(a1[...], d).astype(B16)
        da1 = da1 + dot_t(d, weight[...])
    term, dgain = norm_back(x, gain[...], da1)
    dgain_ref[...] = dgain
    dh_ref[...] = (dx1[...] + term).astype(B16).reshape(dh_ref.shape)


def gather_rows(part):
    count = lax.axis_size("shard")
    rows, cols = part.shape
    half = rows // 2
    mine = lax.axis_index("shard")
    core = lax.axis_index("rep") % 2
    pairs = [(r, r ^ 1) for r in range(lax.axis_size("rep"))]
    own = lax.dynamic_slice(part, (core * half, 0), (half, cols))
    full = jnp.zeros((count, rows, cols), part.dtype)
    full = lax.dynamic_update_slice(full, part[None], (mine, 0, 0))
    for k in range(1, count):
        got = lax.ppermute(own, "shard", [(i, (i + k) % count) for i in range(count)])
        also = lax.ppermute(got, "rep", pairs)
        owner = (mine - k) % count
        full = lax.dynamic_update_slice(full, got[None], (owner, core * half, 0))
        full = lax.dynamic_update_slice(full, also[None], (owner, (1 - core) * half, 0))
    return full.reshape(count * rows, cols)


def reduce_grads(grads):
    owned = [lax.psum_scatter(g, "shard", scatter_dimension=0, tiled=True) for g in grads]
    summed = lax.psum(tuple(owned), "rep")
    return [s.astype(F32) for s in summed]


BITS = 4


class Job:
    def __init__(self, source, result, rows, col, cols):
        self.source, self.result = source, result
        self.rows, self.col, self.cols = rows, col, cols


def partner(bit):
    me = lax.axis_index("rep")
    half = 2**bit
    mine = (me // half) % 2
    return mine, me + half * (1 - 2 * mine)


def to_rep(src, dst, send, recv, bit):
    return remote(src, dst, send, recv, partner(bit)[1])


def to_row(src, dst, send, recv):
    x = lax.axis_index("shard")
    return pltpu.make_async_remote_copy(
        src_ref=src,
        dst_ref=dst,
        send_sem=send,
        recv_sem=recv,
        device_id={"shard": 1 - x},
        device_id_type=MESH,
    )


def add_into(acc, term, rows):
    step = 16 if rows % 32 else 32

    def body(i, carry):
        at = pl.ds(pl.multiple_of(i * step, step), step)
        acc[at, :] = (acc[at, :].astype(F32) + term[at, :].astype(F32)).astype(B16)
        return carry

    lax.fori_loop(0, rows // step, body, 0)


class JobRun:
    STAGES = 10

    def __init__(self, job, source, result, bufs, sems, index):
        self.job, self.source, self.result = job, source, result
        self.acc, self.core, self.row, *self.part = bufs
        send, recv, local = sems
        self.send = [send.at[index, i] for i in range(9)]
        self.recv = [recv.at[index, i] for i in range(9)]
        self.local = [local.at[index, i] for i in range(2)]
        self.sent = []
        self.x = lax.axis_index("shard")
        self.bits = [partner(b)[0] for b in range(BITS)]
        half = job.cols // 2
        self.half = half
        self.mine = pl.ds(pl.multiple_of(job.col + self.bits[0] * half, 128), half)
        self.other = pl.ds(pl.multiple_of(job.col + (1 - self.bits[0]) * half, 128), half)
        self.first = [0]
        count = job.rows
        for b in range(1, BITS):
            count //= 2
            self.first.append(self.first[-1] + self.bits[b] * count)

    def count(self, level):
        return self.job.rows // 2**level

    def span(self, first, count):
        return pl.ds(pl.multiple_of(first, 16), count)

    def go(self, copy):
        copy.start()
        self.sent.append(copy)

    def stage(self, n):
        job = self.job
        if n == 0:
            pltpu.make_async_copy(
                self.source.at[:, :, self.mine], self.acc, self.local[0]
            ).start()
            self.go(
                to_rep(self.source.at[:, :, self.other], self.core, self.send[0], self.recv[0], 0)
            )
        elif n == 1:
            landed(self.acc, self.local[0])
            landed(self.core, self.recv[0])
            for i in range(2):
                add_into(self.acc.at[i], self.core.at[i], job.rows)
            self.go(to_row(self.acc.at[1 - self.x], self.row, self.send[1], self.recv[1]))
        elif n == 2:
            landed(self.row, self.recv[1])
            add_into(self.acc.at[self.x], self.row, job.rows)
            self.give(1)
        elif n in (3, 4):
            self.take(n - 2)
            self.give(n - 1)
        elif n == 5:
            self.take(3)
            rows = self.span(self.first[3], self.count(3))
            piece = self.acc.at[self.x, rows]
            place = self.result.at[rows, self.mine]
            pltpu.make_async_copy(piece, place, self.local[1]).start()
            self.go(to_rep(piece, place, self.send[5], self.recv[5], 3))
        elif n in (6, 7, 8):
            level = 9 - n
            if n == 6:
                rows = self.span(self.first[3], self.count(3))
                landed(self.result.at[rows, self.mine], self.local[1])
            self.landed_at(level)
            rows = self.span(self.first[level - 1], self.count(level - 1))
            place = self.result.at[rows, self.mine]
            self.go(to_rep(place, place, self.send[n], self.recv[n], level - 1))
        else:
            landed(self.result.at[:, self.other], self.recv[8])
            for copy in self.sent:
                copy.wait_send()

    def give(self, level):
        count = self.count(level)
        first = self.first[level - 1] + (1 - self.bits[level]) * count
        self.go(
            to_rep(
                self.acc.at[self.x, self.span(first, count)],
                self.part[level - 1],
                self.send[level + 1],
                self.recv[level + 1],
                level,
            )
        )

    def take(self, level):
        landed(self.part[level - 1], self.recv[level + 1])
        count = self.count(level)
        rows = self.span(self.first[level], count)
        add_into(self.acc.at[self.x, rows], self.part[level - 1], count)

    def landed_at(self, level):
        count = self.count(level)
        first = self.first[level - 1] + (1 - self.bits[level]) * count
        landed(self.result.at[self.span(first, count), self.mine], self.recv[8 - level])


def job_buffers(job):
    half = job.cols // 2
    return [
        pltpu.VMEM((2, job.rows, half), B16),
        pltpu.VMEM((2, job.rows, half), B16),
        pltpu.VMEM((job.rows, half), B16),
    ] + [pltpu.VMEM((job.rows // 2**b, half), B16) for b in range(1, BITS)]


JOB_BUFFERS = 6


def greet_partners():
    barrier = pltpu.get_barrier_semaphore()
    x = lax.axis_index("shard")
    pl.semaphore_signal(barrier, inc=1, device_id={"shard": 1 - x}, device_id_type=MESH)
    for b in range(BITS):
        pl.semaphore_signal(
            barrier, inc=1, device_id={"rep": partner(b)[1]}, device_id_type=MESH
        )
    pl.semaphore_wait(barrier, BITS + 1)


def sum_kernel(jobs, arrays, *refs):
    sources, results = refs[:arrays], refs[arrays : 2 * arrays]
    scratch = refs[2 * arrays :]
    sems = scratch[:3]
    greet_partners()
    runs = [
        JobRun(
            job,
            sources[job.source],
            results[job.result],
            scratch[3 + i * JOB_BUFFERS : 3 + (i + 1) * JOB_BUFFERS],
            sems,
            i,
        )
        for i, job in enumerate(jobs)
    ]
    for tick in range(len(runs) + JobRun.STAGES - 1):
        for n in reversed(range(JobRun.STAGES)):
            if 0 <= tick - n < len(runs):
                runs[tick - n].stage(n)


def sum_call(grads, collective):
    jobs = []
    for i, g in enumerate(grads):
        rows, cols = g.shape[1:]
        wide = cols // 2 if cols > 1024 else cols
        for col in range(0, cols, wide):
            jobs.append(Job(i, i, rows, col, wide))
    dma = pltpu.SemaphoreType.DMA
    scratch = [dma((len(jobs), 9)), dma((len(jobs), 9)), dma((len(jobs), 2))]
    for job in jobs:
        scratch += job_buffers(job)
    return pl.pallas_call(
        functools.partial(sum_kernel, jobs, len(grads)),
        out_shape=[jax.ShapeDtypeStruct(g.shape[1:], B16) for g in grads],
        in_specs=[pl.BlockSpec(memory_space=pl.ANY)] * len(grads),
        out_specs=[pl.BlockSpec(memory_space=pl.ANY)] * len(grads),
        scratch_shapes=scratch,
        compiler_params=pltpu.CompilerParams(
            collective_id=collective, has_side_effects=True, vmem_limit_bytes=56 * 2**20
        ),
        name="sum_gradients",
    )(*grads)


def local(
    hidden,
    encoded,
    out_grad,
    self_query,
    self_key,
    self_value,
    self_out,
    cross_query,
    cross_key,
    cross_value,
    cross_out,
    ffn_gate,
    ffn_up,
    ffn_down,
    gain_self,
    gain_cross,
    gain_ffn,
    bias_table,
    buckets,
):
    seqs, toks = hidden.shape[0], hidden.shape[1]
    p = Plan(seqs, toks, lax.axis_size("rep"))
    tokens = seqs * toks
    ff = ffn_gate.shape[1]
    enc_rows = seqs * encoded.shape[1] * p.R
    dma = pltpu.SemaphoreType.DMA

    small = jnp.concatenate(
        [
            jnp.stack([gain_self, gain_cross, gain_ffn]).reshape(-1),
            bias_table.reshape(-1),
        ]
    ).astype(B16)
    small = lax.all_gather(small, "shard", axis=0)
    part = gain_self.shape[0]
    gains = [
        small[:, i * part : (i + 1) * part].reshape(1, D).astype(F32) for i in range(3)
    ]
    table = small[:, 3 * part :].reshape(NB, H)
    near = buckets[: 2 * toks]
    onehot = (near[:, None] == jnp.arange(NB, dtype=jnp.int32)[None, :]).astype(B16)
    lines = jnp.einsum("lb,bh->hl", onehot, table, preferred_element_type=F32)[:, None, :]

    wq, wk, wv, wo, wcq, wck, wcv, wco, wg, wu, wd = [
        gather_rows(m.astype(B16))
        for m in (
            self_query,
            self_key,
            self_value,
            self_out,
            cross_query,
            cross_key,
            cross_value,
            cross_out,
            ffn_gate,
            ffn_up,
            ffn_down,
        )
    ]
    enc = lax.all_gather(encoded, "rep", axis=1, tiled=True).reshape(enc_rows, D)

    a1, send = plain_call(
        functools.partial(project_kernel, p),
        [((tokens, D), B16), ((p.U, 3 * p.F, toks), B16)],
        (hidden, gains[0], wq, wk, wv),
        "project",
    )
    recv = comm_call(
        functools.partial(scatter_tokens, p),
        (p.R, 3 * p.F, toks),
        (send,),
        [dma((p.U,)), dma((max(p.W - 1, 1), p.J)), dma((p.R,))],
        0,
        "scatter_tokens",
    )
    ckn, ckt, cvn, cvt = plain_call(
        encode_kernel,
        [
            ((H, enc_rows, DH), B16),
            ((H, DH + ONES, enc_rows), B16),
            ((H, enc_rows, DH), B16),
            ((H, DH + ONES, enc_rows), B16),
        ],
        (enc, wck, wcv),
        "encode",
    )
    o, of, rl = pl.pallas_call(
        functools.partial(attend_kernel, p),
        grid=(p.HG,),
        out_shape=[
            jax.ShapeDtypeStruct((p.J, p.F, toks), B16),
            jax.ShapeDtypeStruct((p.J, p.F, toks), F32),
            jax.ShapeDtypeStruct((p.HG, p.NP, 1, 2 * toks), F32),
        ],
        in_specs=[whole((p.R, 3 * p.F, toks)), whole((H, 1, 2 * toks))],
        out_specs=[
            whole((p.J, p.F, toks)),
            whole((p.J, p.F, toks)),
            whole((p.HG, p.NP, 1, 2 * toks)),
        ],
        scratch_shapes=[
            pltpu.VMEM((p.L, DH), B16),
            pltpu.VMEM((DH + ONES, p.L), B16),
            pltpu.VMEM((3, p.CK, 2 * toks), F32),
        ],
        compiler_params=pltpu.CompilerParams(vmem_limit_bytes=56 * 2**20),
        name="attend",
    )(recv, lines)
    ot = comm_call(
        functools.partial(return_tokens, p),
        (p.U, p.F, toks),
        (o,),
        [dma((p.J,)), dma((p.U,))],
        1,
        "return_tokens",
    ).reshape(seqs, D, toks)

    x1, x2, a2, qt2, of2, rl2 = plain_call(
        functools.partial(cross_kernel, seqs),
        [
            ((tokens, D), F32),
            ((tokens, D), F32),
            ((tokens, D), B16),
            ((seqs, D, toks), B16),
            ((seqs, D, toks), F32),
            ((seqs, H, 1, toks), F32),
        ],
        (hidden, ot, wo, gains[1], wcq, wco, ckn, cvt),
        "cross",
    )

    chunk = min(512, ff)
    const = lambda s: pl.BlockSpec(s, lambda i: (0, 0))
    output, dx2, dg_ffn, dwg, dwu, dwd = pl.pallas_call(
        ffn_kernel,
        grid=(ff // chunk,),
        out_shape=[
            jax.ShapeDtypeStruct((tokens, D), B16),
            jax.ShapeDtypeStruct((tokens, D), F32),
            jax.ShapeDtypeStruct((1, D), F32),
            jax.ShapeDtypeStruct((D, ff), B16),
            jax.ShapeDtypeStruct((D, ff), B16),
            jax.ShapeDtypeStruct((ff, D), B16),
        ],
        in_specs=[
            const((tokens, D)),
            const((tokens, D)),
            const((1, D)),
            pl.BlockSpec((D, chunk), lambda i: (0, i)),
            pl.BlockSpec((D, chunk), lambda i: (0, i)),
            pl.BlockSpec((chunk, D), lambda i: (i, 0)),
        ],
        out_specs=[
            const((tokens, D)),
            const((tokens, D)),
            const((1, D)),
            pl.BlockSpec((D, chunk), lambda i: (0, i)),
            pl.BlockSpec((D, chunk), lambda i: (0, i)),
            pl.BlockSpec((chunk, D), lambda i: (i, 0)),
        ],
        scratch_shapes=[
            pltpu.VMEM((tokens, D), B16),
            pltpu.VMEM((tokens, D), F32),
            pltpu.VMEM((tokens, D), F32),
        ],
        compiler_params=pltpu.CompilerParams(vmem_limit_bytes=56 * 2**20),
        name="ffn",
    )(x2, out_grad.reshape(tokens, D), gains[2], wg, wu, wd)

    dx1, dg_cross, dot_, denc, dwco, dwcq, dwck, dwcv, dwo = plain_call(
        functools.partial(cross_back_kernel, seqs, p.G),
        [
            ((tokens, D), F32),
            ((1, D), F32),
            ((p.U, p.F, toks), B16),
            ((enc_rows, D), B16),
        ]
        + [((D, D), B16)] * 5,
        (dx2, x1, a2, gains[1], qt2, of2, rl2, ckn, ckt, cvn, enc, wco, wcq, wck, wcv, wo, ot),
        "cross_back",
        scratch=[
            pltpu.VMEM((seqs, D, toks), B16),
            pltpu.VMEM((seqs, D, toks), B16),
            pltpu.VMEM((enc_rows, D), B16),
            pltpu.VMEM((enc_rows, D), B16),
        ],
    )
    encoded_grad = lax.psum_scatter(
        denc.reshape(seqs, enc_rows // seqs, D), "rep", scatter_dimension=1, tiled=True
    )
    dout = comm_call(
        functools.partial(scatter_rows, p),
        (p.J, p.F, toks),
        (dot_,),
        [dma((p.U,)), dma((p.J,))],
        2,
        "scatter_rows",
    )
    dq, dkv, line = pl.pallas_call(
        functools.partial(attend_back_kernel, p),
        grid=(p.HG,),
        out_shape=[
            jax.ShapeDtypeStruct((p.J, p.F, toks), B16),
            jax.ShapeDtypeStruct((p.R, 2 * p.F, toks), B16),
            jax.ShapeDtypeStruct((p.HG, 1, 2 * toks), F32),
        ],
        in_specs=[
            whole((p.R, 3 * p.F, toks)),
            whole((H, 1, 2 * toks)),
            whole((p.J, p.F, toks)),
            whole((p.J, p.F, toks)),
            whole((p.HG, p.NP, 1, 2 * toks)),
        ],
        out_specs=[
            whole((p.J, p.F, toks)),
            whole((p.R, 2 * p.F, toks)),
            whole((p.HG, 1, 2 * toks)),
        ],
        scratch_shapes=[
            pltpu.VMEM((p.L, DH), B16),
            pltpu.VMEM((p.L, DH), B16),
            pltpu.VMEM((DH + ONES, p.L), B16),
            pltpu.VMEM((p.L, DH), F32),
            pltpu.VMEM((p.L, DH), F32),
            pltpu.VMEM((3, p.CK, 2 * toks), F32),
            pltpu.VMEM((3, p.CK, 2 * toks), F32),
        ],
        compiler_params=pltpu.CompilerParams(vmem_limit_bytes=56 * 2**20),
        name="attend_back",
    )(recv, lines, dout, of, rl)
    grads = comm_call(
        functools.partial(return_grads, p),
        (p.U, 3 * p.F, toks),
        (dq, dkv),
        [
            pltpu.VMEM((max(p.W - 1, 1), p.J, 2 * p.F, toks), B16),
            pltpu.VMEM((p.J, 3 * p.F, toks), B16),
            dma((p.J,)),
            dma((max(p.W - 1, 1), p.J)),
            dma((max(p.W - 1, 1), p.J)),
            dma((p.U,)),
        ],
        3,
        "return_grads",
        space=pltpu.VMEM,
    )
    hidden_grad, dg_self, dwq, dwk, dwv = plain_call(
        functools.partial(last_kernel, p),
        [(hidden.shape, B16), ((1, D), F32)] + [((D, D), B16)] * 3,
        (hidden, grads, a1, gains[0], dx1, wq, wk, wv),
        "last",
    )

    group = (lax.axis_index("rep") // p.W) % p.G
    by_bucket = jnp.einsum(
        "hl,lb->bh", line[:, 0, :], onehot.astype(F32), precision=lax.Precision.HIGHEST
    )
    dtable = lax.dynamic_update_slice(jnp.zeros((NB, H), F32), by_bucket, (0, group * p.HG))

    mats = [dwg, dwu, dwd, dwo, dwcq, dwck, dwcv, dwco, dwq, dwk, dwv]
    n_shard = lax.axis_size("shard")
    lot = jnp.concatenate(
        [g.reshape(n_shard, part) for g in (dg_self, dg_cross, dg_ffn)]
        + [dtable.reshape(n_shard, -1)],
        axis=1,
    )
    size = lot.shape[1]
    if n_shard == 2 and p.R == 2**BITS:
        lines_in = 16 * 2 ** (BITS - 1)
        lot = jnp.pad(lot.astype(B16), ((0, 0), (0, lines_in * D - size)))
        *sums, lot = sum_call(
            [g.reshape(2, g.shape[0] // 2, g.shape[1]) for g in mats]
            + [lot.reshape(2, lines_in, D)],
            4,
        )
        lot = lot.reshape(-1)[:size].astype(F32)
        mats = [g.astype(F32) for g in sums]
    else:
        mats = reduce_grads(mats)
        lot = lax.psum(lot, ("shard", "rep"))
        lot = lax.dynamic_slice(lot, (lax.axis_index("shard"), 0), (1, size))[0]
    mats = mats[8:] + mats[3:8] + mats[:3]
    dgains = [lot[i * part : (i + 1) * part] for i in range(3)]
    dtab = lot[3 * part :].reshape(bias_table.shape)
    return (
        output.reshape(hidden.shape),
        hidden_grad,
        encoded_grad,
        *mats,
        *dgains,
        dtab,
    )


def solution(mesh):
    tok = P("shard", "rep", None)
    mat = P("shard", None)
    in_specs = (tok,) * 3 + (mat,) * 11 + (P("shard"),) * 3 + (mat, P())
    out_specs = (tok,) * 3 + (mat,) * 11 + (P("shard"),) * 3 + (mat,)
    return jax.shard_map(local, mesh=mesh, in_specs=in_specs, out_specs=out_specs, check_vma=False)
```

```python
import functools

import jax
import jax.numpy as jnp
from jax import lax
from jax.experimental import pallas as pl
from jax.experimental.pallas import tpu as pltpu
from jax.sharding import PartitionSpec as P

D = 768
H = 12
DH = 64
NB = 32
EPS = 1e-06
F32 = jnp.float32
B16 = jnp.bfloat16
ONES = 16
HIDE = -1e30
MESH = pl.DeviceIdType.MESH
GELU_A = 0.7978845608028654
GELU_B = 0.044715


def dot(a, b):
    return lax.dot_general(a, b, (((1,), (0,)), ((), ())), preferred_element_type=F32)


def dot_t(a, b):
    return lax.dot_general(a, b, (((1,), (1,)), ((), ())), preferred_element_type=F32)


def t_dot(a, b):
    return lax.dot_general(a, b, (((0,), (0,)), ((), ())), preferred_element_type=F32)


def scale_of(v):
    return lax.rsqrt(jnp.mean(v * v, axis=-1, keepdims=True) + EPS)


def norm_back(v, gain, grad):
    r = scale_of(v)
    n = v * r
    c = grad * gain
    dv = r * (c - n * jnp.mean(c * n, axis=-1, keepdims=True))
    return dv, jnp.sum(grad * n, axis=0, keepdims=True)


def whole(shape):
    return pl.BlockSpec(shape, lambda *_: (0,) * len(shape))


def plain_call(kernel, outs, args, name, scratch=(), vmem=60):
    return pl.pallas_call(
        kernel,
        out_shape=[jax.ShapeDtypeStruct(s, t) for s, t in outs],
        in_specs=[pl.BlockSpec(memory_space=pltpu.VMEM)] * len(args),
        out_specs=[pl.BlockSpec(memory_space=pltpu.VMEM)] * len(outs),
        scratch_shapes=list(scratch),
        compiler_params=pltpu.CompilerParams(vmem_limit_bytes=vmem * 2**20),
        name=name,
    )(*args)


class Plan:
    def __init__(self, seqs, toks, rows):
        self.S, self.T, self.R = seqs, toks, rows
        groups = 1
        for g in range(1, H + 1):
            if H % g == 0 and seqs * g <= rows and rows % (2 * seqs * g) == 0:
                groups = g
        self.G = groups
        self.HG = H // groups
        self.F = self.HG * DH
        self.U = seqs * groups
        self.W = rows // self.U
        self.J = rows // self.W
        self.NP = self.J // 2
        self.CK = 2 * self.W * toks
        self.L = rows * toks

    def worker_of(self, r):
        m = r % (2 * self.W)
        late = m // self.W
        return m * (1 - late) + (2 * self.W - 1 - m) * late

    def slot_of(self, r):
        return 2 * (r // (2 * self.W)) + (r % (2 * self.W)) // self.W

    def source(self, j, w):
        return self.source_in(j // 2, j % 2, w)

    def source_in(self, pair, late, w):
        if late:
            return 2 * self.W * pair + 2 * self.W - 1 - w
        return 2 * self.W * pair + w


def enter(rows):
    me = lax.axis_index("rep")
    barrier = pltpu.get_barrier_semaphore()
    for k in range(1, rows):
        pl.semaphore_signal(
            barrier, inc=1, device_id={"rep": (me + k) % rows}, device_id_type=MESH
        )
    pl.semaphore_wait(barrier, rows - 1)
    return me


def remote(src, dst, send, recv, to):
    return pltpu.make_async_remote_copy(
        src_ref=src,
        dst_ref=dst,
        send_sem=send,
        recv_sem=recv,
        device_id={"rep": to},
        device_id_type=MESH,
    )


def start_either(me, to, src, dst, send, recv):
    @pl.when(to == me)
    def _():
        pltpu.make_async_copy(src, dst, recv).start()

    @pl.when(to != me)
    def _():
        remote(src, dst, send, recv, to).start()


def end_either(me, to, src, dst, send, recv):
    @pl.when(to != me)
    def _():
        remote(src, dst, send, recv, to).wait_send()


def landed(ref, sem):
    pltpu.make_async_copy(ref, ref, sem).wait()


def scatter_tokens(plan, send, recv, send_sem, relay_sem, recv_sem):
    p = plan
    me = enter(p.R)
    w = me % p.W
    mine = p.worker_of(me)
    for u in range(p.U):
        start_either(me, u * p.W + mine, send.at[u], recv.at[me], send_sem.at[u], recv_sem.at[me])
    for j in range(p.J):
        r = p.source(j, w)
        landed(recv.at[r], recv_sem.at[r])
        for k in range(1, p.W):
            part = recv.at[r, pl.ds(p.F, 2 * p.F)]
            remote(
                part, part, relay_sem.at[k - 1, j], recv_sem.at[r], me - w + (w + k) % p.W
            ).start()
    for k in range(1, p.W):
        for j in range(p.J):
            r = p.source(j, (w + k) % p.W)
            landed(recv.at[r, pl.ds(p.F, 2 * p.F)], recv_sem.at[r])
    for u in range(p.U):
        end_either(me, u * p.W + mine, send.at[u], recv.at[me], send_sem.at[u], recv_sem.at[me])
    for k in range(1, p.W):
        for j in range(p.J):
            r = p.source(j, w)
            part = recv.at[r, pl.ds(p.F, 2 * p.F)]
            remote(
                part, part, relay_sem.at[k - 1, j], recv_sem.at[r], me - w + (w + k) % p.W
            ).wait_send()


def return_tokens(plan, send, recv, send_sem, recv_sem):
    p = plan
    me = enter(p.R)
    w = me % p.W
    unit = me // p.W
    for j in range(p.J):
        r = p.source(j, w)
        start_either(me, r, send.at[j], recv.at[unit], send_sem.at[j], recv_sem.at[unit])
    for u in range(p.U):
        landed(recv.at[u], recv_sem.at[u])
    for j in range(p.J):
        r = p.source(j, w)
        end_either(me, r, send.at[j], recv.at[unit], send_sem.at[j], recv_sem.at[unit])


def scatter_rows(plan, send, recv, send_sem, recv_sem):
    p = plan
    me = enter(p.R)
    mine = p.worker_of(me)
    slot = p.slot_of(me)
    for u in range(p.U):
        start_either(
            me, u * p.W + mine, send.at[u], recv.at[slot], send_sem.at[u], recv_sem.at[slot]
        )
    for j in range(p.J):
        landed(recv.at[j], recv_sem.at[j])
    for u in range(p.U):
        end_either(
            me, u * p.W + mine, send.at[u], recv.at[slot], send_sem.at[u], recv_sem.at[slot]
        )


def return_grads(plan, dq, dkv, recv, buf, out, send_sem, part_sem, got_sem, recv_sem):
    p = plan
    me = enter(p.R)
    w = me % p.W
    unit = me // p.W

    def give(k, j):
        to = (w + k) % p.W
        r = p.source(j, to)
        return remote(
            dkv.at[r],
            buf.at[k - 1, j],
            part_sem.at[k - 1, j],
            got_sem.at[k - 1, j],
            me - w + to,
        )

    for j in range(p.J):
        for k in range(1, p.W):
            give(k, j).start()
    for j in range(p.J):
        r = p.source(j, w)
        total = dkv[r].astype(F32)
        for k in range(1, p.W):
            landed(buf.at[k - 1, j], got_sem.at[k - 1, j])
            total = total + buf[k - 1, j].astype(F32)
        out[j, 0 : p.F, :] = dq[j]
        out[j, p.F : 3 * p.F, :] = total.astype(B16)
        start_either(me, r, out.at[j], recv.at[unit], send_sem.at[j], recv_sem.at[unit])
    for u in range(p.U):
        landed(recv.at[u], recv_sem.at[u])
    for j in range(p.J):
        r = p.source(j, w)
        end_either(me, r, out.at[j], recv.at[unit], send_sem.at[j], recv_sem.at[unit])
        for k in range(1, p.W):
            give(k, j).wait_send()


def comm_call(kernel, out, args, scratch, collective, name, space=pl.ANY):
    return pl.pallas_call(
        kernel,
        out_shape=jax.ShapeDtypeStruct(out, B16),
        in_specs=[pl.BlockSpec(memory_space=space)] * len(args),
        out_specs=pl.BlockSpec(memory_space=space),
        scratch_shapes=list(scratch),
        compiler_params=pltpu.CompilerParams(
            collective_id=collective, has_side_effects=True, vmem_limit_bytes=40 * 2**20
        ),
        name=name,
    )(*args)


def project_kernel(plan, hidden, gain, wq, wk, wv, a1_ref, send):
    p = plan
    x = hidden[...].reshape(p.S * p.T, D).astype(F32)
    a1 = (x * scale_of(x) * gain[...]).astype(B16)
    a1_ref[...] = a1
    for n, weight in enumerate((wq, wk, wv)):
        rows = dot(a1, weight[...])
        for s in range(p.S):
            turned = jnp.transpose(rows[s * p.T : (s + 1) * p.T]).astype(B16)
            for g in range(p.G):
                send[s * p.G + g, n * p.F : (n + 1) * p.F, :] = turned[g * p.F : (g + 1) * p.F]


def bias_tiles(plan, w, line, tiles):
    p = plan
    far = line[0:1, 2 * p.T - 1 : 2 * p.T]
    near = pltpu.roll(
        jnp.broadcast_to(line[0:1, :], (p.T, 2 * p.T)), 0, 1, stride=1, stride_axis=0
    )
    key = lax.broadcasted_iota(jnp.int32, (p.T, p.T), 0)
    query = lax.broadcasted_iota(jnp.int32, (p.T, p.T), 1)
    same = jnp.where(query >= key, near[:, : p.T], HIDE)
    next_ = near[:, p.T :]
    farb = jnp.broadcast_to(far, (p.T, p.T))
    tiles[0] = jnp.broadcast_to(far, (p.CK, 2 * p.T))
    for a in range(2):
        ahead = w if a == 0 else 2 * p.W - 1 - w
        for b in range(2 * p.W):
            diff = ahead - b
            tile = jnp.where(
                diff == 0, same, jnp.where(diff == 1, next_, jnp.where(diff < 0, HIDE, farb))
            )
            tiles[2, b * p.T : (b + 1) * p.T, a * p.T : (a + 1) * p.T] = tile
            back = diff + 2 * p.W
            tiles[1, b * p.T : (b + 1) * p.T, a * p.T : (a + 1) * p.T] = jnp.where(
                back == 1, next_, farb
            )


def block_pair(plan, ref, pair, w, row, count):
    p = plan
    return jnp.concatenate(
        [
            ref[p.source_in(pair, 0, w), pl.ds(row, count), :],
            ref[p.source_in(pair, 1, w), pl.ds(row, count), :],
        ],
        axis=1,
    )


def attend_kernel(plan, recv, lines, o_ref, of_ref, rl_ref, kn, vt, tiles):
    p = plan
    me = lax.axis_index("rep")
    w = me % p.W
    group = (me // p.W) % p.G
    h = pl.program_id(0)
    row = pl.multiple_of(h * DH, DH)
    bias_tiles(p, w, lines.at[group * p.HG + h], tiles)
    for r in range(p.R):
        kn[r * p.T : (r + 1) * p.T, :] = jnp.transpose(
            recv[r, pl.ds(p.F + row, DH), :].astype(F32)
        ).astype(B16)
        vt[0:DH, r * p.T : (r + 1) * p.T] = recv[r, pl.ds(2 * p.F + row, DH), :]
    vt[DH : DH + ONES, :] = jnp.ones((ONES, p.L), B16)
    for pair in range(p.NP):
        qt = block_pair(p, recv, pair, w, row, DH)

        def step(i, acc, pair=pair, qt=qt):
            start = pl.multiple_of(i * p.CK, p.CK)
            s = dot(kn[pl.ds(start, p.CK), :], qt)
            e = jnp.exp(s + tiles[jnp.maximum(i - pair + 2, 0)])
            return acc + dot(vt[:, pl.ds(start, p.CK)], e.astype(B16))

        acc = lax.fori_loop(0, pair + 1, step, jnp.zeros((DH + ONES, 2 * p.T), F32))
        rl = 1.0 / acc[DH : DH + 1]
        of = acc[:DH] * rl
        rl_ref[h, pair] = rl
        for a in range(2):
            part = of[:, a * p.T : (a + 1) * p.T]
            of_ref[2 * pair + a, pl.ds(row, DH), :] = part
            o_ref[2 * pair + a, pl.ds(row, DH), :] = part.astype(B16)


def back_head(
    p, w, row, line, recv, dout, of_ref, rl, dq_ref, dkv_ref, kn, vn, kt, dk, dv, tiles, near
):
    bias_tiles(p, w, line, tiles)
    for r in range(p.R):
        kn[r * p.T : (r + 1) * p.T, :] = jnp.transpose(
            recv[r, pl.ds(p.F + row, DH), :].astype(F32)
        ).astype(B16)
        vn[r * p.T : (r + 1) * p.T, :] = jnp.transpose(
            recv[r, pl.ds(2 * p.F + row, DH), :].astype(F32)
        ).astype(B16)
        kt[0:DH, r * p.T : (r + 1) * p.T] = recv[r, pl.ds(p.F + row, DH), :]
    kt[DH : DH + ONES, :] = jnp.ones((ONES, p.L), B16)
    dk[...] = jnp.zeros_like(dk)
    dv[...] = jnp.zeros_like(dv)
    near[...] = jnp.zeros_like(near)

    def one_pair(pair, total):
        qt = block_pair(p, recv, pair, w, row, DH)
        dot_rows = jnp.concatenate(
            [dout[2 * pair + a, pl.ds(row, DH), :] for a in range(2)], axis=1
        )
        of = jnp.concatenate([of_ref[2 * pair + a, pl.ds(row, DH), :] for a in range(2)], axis=1)
        delta = jnp.sum(dot_rows.astype(F32) * of, axis=0, keepdims=True)
        scale = rl[pair]
        qn = jnp.transpose(qt.astype(F32)).astype(B16)
        don = jnp.transpose(dot_rows.astype(F32)).astype(B16)

        def step(i, acc):
            start = pl.multiple_of(i * p.CK, p.CK)
            kind = jnp.maximum(i - pair + 2, 0)
            keys = pl.ds(start, p.CK)
            prob = jnp.exp(dot(kn[keys, :], qt) + tiles[kind]) * scale
            ds = (prob * (dot(vn[keys, :], dot_rows) - delta)).astype(B16)
            near[kind] += ds.astype(F32)
            dk[keys, :] += dot(ds, qn)
            dv[keys, :] += dot(prob.astype(B16), don)
            return acc + dot(kt[:, keys], ds)

        acc = lax.fori_loop(0, pair + 1, step, jnp.zeros((DH + ONES, 2 * p.T), F32))
        for a in range(2):
            dq_ref[2 * pair + a, pl.ds(row, DH), :] = acc[:DH, a * p.T : (a + 1) * p.T].astype(B16)
        return total + acc[DH : DH + 1]

    total = lax.fori_loop(0, p.NP, one_pair, jnp.zeros((1, 2 * p.T), F32))
    for r in range(p.R):
        dkv_ref[r, pl.ds(row, DH), :] = jnp.transpose(dk[r * p.T : (r + 1) * p.T, :]).astype(B16)
        dkv_ref[r, pl.ds(p.F + row, DH), :] = jnp.transpose(dv[r * p.T : (r + 1) * p.T, :]).astype(
            B16
        )
    same = jnp.zeros((p.T, p.T), F32)
    next_ = jnp.zeros((p.T, p.T), F32)
    for a in range(2):
        ahead = w if a == 0 else 2 * p.W - 1 - w
        for b in range(2 * p.W):
            diff = ahead - b
            spot = (slice(b * p.T, (b + 1) * p.T), slice(a * p.T, (a + 1) * p.T))
            tile = near[(2, *spot)]
            same = same + jnp.where(diff == 0, tile, 0.0)
            next_ = next_ + jnp.where(diff == 1, tile, 0.0)
            next_ = next_ + jnp.where(diff + 2 * p.W == 1, near[(1, *spot)], 0.0)
    both = jnp.concatenate([same, next_], axis=1)
    key = lax.broadcasted_iota(jnp.int32, (p.T, p.T), 0)
    other = lax.broadcasted_iota(jnp.int32, (p.T, p.T), 1)
    swap = (key + other == p.T - 1).astype(F32)
    turned = lax.dot_general(
        swap,
        both,
        (((1,), (0,)), ((), ())),
        precision=lax.Precision.HIGHEST,
        preferred_element_type=F32,
    )
    turned = pltpu.roll(turned, p.T + 1, 1, stride=1, stride_axis=0)
    by_distance = jnp.sum(turned, axis=0, keepdims=True)
    rest = jnp.sum(total) - jnp.sum(both)
    place = lax.broadcasted_iota(jnp.int32, (1, 2 * p.T), 1)
    return by_distance + jnp.where(place == 2 * p.T - 1, rest, 0.0)


def back_scratch(p):
    return [
        pltpu.VMEM((p.L, DH), B16),
        pltpu.VMEM((p.L, DH), B16),
        pltpu.VMEM((DH + ONES, p.L), B16),
        pltpu.VMEM((p.L, DH), F32),
        pltpu.VMEM((p.L, DH), F32),
        pltpu.VMEM((3, p.CK, 2 * p.T), F32),
        pltpu.VMEM((3, p.CK, 2 * p.T), F32),
    ]


def attend_back_kernel(plan, recv, lines, dout, of_ref, rl_ref, dq_ref, dkv_ref, line_ref, *scratch):
    p = plan
    me = lax.axis_index("rep")
    w = me % p.W
    group = (me // p.W) % p.G
    h = pl.program_id(0)
    row = pl.multiple_of(h * DH, DH)
    line_ref[h] = back_head(
        p,
        w,
        row,
        lines.at[group * p.HG + h],
        recv,
        dout,
        of_ref,
        rl_ref.at[h],
        dq_ref,
        dkv_ref,
        *scratch,
    )


def encode_kernel(enc, wk, wv, kn, kt, vn, vt):
    rows = enc.shape[0]
    for weight, natural, turned in ((wk, kn, kt), (wv, vn, vt)):
        value = dot(enc[...], weight[...])
        for h in range(H):
            natural[h] = value[:, h * DH : (h + 1) * DH].astype(B16)
        flipped = jnp.transpose(value).astype(B16)
        for h in range(H):
            turned[h, 0:DH, :] = flipped[h * DH : (h + 1) * DH]
            turned[h, DH : DH + ONES, :] = jnp.ones((ONES, rows), B16)


def cross_kernel(
    seqs, hidden, ot, wo, gain, wcq, wco, kn, vt, x1_ref, x2_ref, a2_ref, qt_ref, of_ref, rl_ref
):
    toks = hidden.shape[1]
    span = kn.shape[1] // seqs
    x = hidden[...].reshape(seqs * toks, D).astype(F32)
    o = jnp.concatenate(
        [jnp.transpose(ot[s].astype(F32)) for s in range(seqs)], axis=0
    ).astype(B16)
    x1 = x + dot(o, wo[...])
    x1_ref[...] = x1
    a2 = (x1 * scale_of(x1) * gain[...]).astype(B16)
    a2_ref[...] = a2
    q2 = dot(a2, wcq[...])
    for s in range(seqs):
        qt_ref[s] = jnp.transpose(q2[s * toks : (s + 1) * toks]).astype(B16)

    def heads(i, carry):
        for sub in range(2):
            h = 2 * i + sub
            row = pl.multiple_of(h * DH, DH)
            for s in range(seqs):
                keys = slice(s * span, (s + 1) * span)
                e = jnp.exp(dot(kn[h, keys, :], qt_ref[s, pl.ds(row, DH), :]))
                acc = dot(vt[h, :, keys], e.astype(B16))
                rl = 1.0 / acc[DH : DH + 1]
                of_ref[s, pl.ds(row, DH), :] = acc[:DH] * rl
                rl_ref[s, h] = rl
        return carry

    lax.fori_loop(0, H // 2, heads, 0)
    o2 = jnp.concatenate([jnp.transpose(of_ref[s]) for s in range(seqs)], axis=0).astype(B16)
    x2_ref[...] = x1 + dot(o2, wco[...])


def ffn_kernel(
    x2_ref, og_ref, gain, wg, wu, wd, out_ref, dx2_ref, dgain_ref, dwg, dwu, dwd, a3, acc, da3
):
    step = pl.program_id(0)

    @pl.when(step == 0)
    def _():
        x2 = x2_ref[...]
        a3[...] = (x2 * scale_of(x2) * gain[...]).astype(B16)
        acc[...] = x2
        da3[...] = jnp.zeros_like(da3)

    rows = a3[...]
    og = og_ref[...]
    gate = dot(rows, wg[...])
    up = dot(rows, wu[...])
    square = gate * gate
    th = jnp.tanh(GELU_A * gate * (1.0 + GELU_B * square))
    half = 0.5 * (1.0 + th)
    value = gate * half
    slope = half + 0.5 * gate * (1.0 - th * th) * (GELU_A * (1.0 + 3.0 * GELU_B * square))
    inner = (value * up).astype(B16)
    acc[...] += dot(inner, wd[...])
    dwd[...] = t_dot(inner, og).astype(B16)
    dinner = dot_t(og, wd[...]).astype(B16).astype(F32)
    dgate = (dinner * up * slope).astype(B16)
    dup = (dinner * value).astype(B16)
    dwg[...] = t_dot(rows, dgate).astype(B16)
    dwu[...] = t_dot(rows, dup).astype(B16)
    da3[...] += dot_t(dgate, wg[...]) + dot_t(dup, wu[...])

    @pl.when(step == pl.num_programs(0) - 1)
    def _():
        out_ref[...] = acc[...].astype(B16)
        dv, dgain = norm_back(x2_ref[...], gain[...], da3[...])
        dx2_ref[...] = og_ref[...].astype(F32) + dv
        dgain_ref[...] = dgain


def cross_back_kernel(
    seqs,
    groups,
    dx2_ref,
    x1_ref,
    a2_ref,
    gain,
    qt_ref,
    of_ref,
    rl_ref,
    kn,
    kt,
    vn,
    enc,
    wco,
    wcq,
    wck,
    wcv,
    wo,
    ot,
    dx1_ref,
    dgain_ref,
    dot_ref,
    denc_ref,
    dwco,
    dwcq,
    dwck,
    dwcv,
    dwo,
    dt,
    dqt,
    dk,
    dv,
):
    toks = qt_ref.shape[2]
    span = kn.shape[1] // seqs
    dx2 = dx2_ref[...]
    dc = dx2.astype(B16)
    o2t = [of_ref[s].astype(B16) for s in range(seqs)]
    total = dot(o2t[0], dc[0:toks])
    for s in range(1, seqs):
        total = total + dot(o2t[s], dc[s * toks : (s + 1) * toks])
    dwco[...] = total.astype(B16)
    do2 = dot_t(dc, wco[...])
    for s in range(seqs):
        dt[s] = jnp.transpose(do2[s * toks : (s + 1) * toks]).astype(B16)

    def heads(i, carry):
        col = pl.multiple_of(2 * i * DH, 2 * DH)
        for s in range(seqs):
            keys = slice(s * span, (s + 1) * span)
            dks, dvs = [], []
            q_pair = jnp.transpose(qt_ref[s, pl.ds(col, 2 * DH), :].astype(F32)).astype(B16)
            d_pair = jnp.transpose(dt[s, pl.ds(col, 2 * DH), :].astype(F32)).astype(B16)
            for sub in range(2):
                h = 2 * i + sub
                row = pl.multiple_of(h * DH, DH)
                d_rows = dt[s, pl.ds(row, DH), :]
                prob = jnp.exp(dot(kn[h, keys, :], qt_ref[s, pl.ds(row, DH), :])) * rl_ref[s, h]
                delta = jnp.sum(
                    d_rows.astype(F32) * of_ref[s, pl.ds(row, DH), :], axis=0, keepdims=True
                )
                ds = (prob * (dot(vn[h, keys, :], d_rows) - delta)).astype(B16)
                dqt[s, pl.ds(row, DH), :] = dot(kt[h, 0:DH, keys], ds).astype(B16)
                dks.append(dot(ds, q_pair[:, sub * DH : (sub + 1) * DH]))
                dvs.append(dot(prob.astype(B16), d_pair[:, sub * DH : (sub + 1) * DH]))
            dk[keys, pl.ds(col, 2 * DH)] = jnp.concatenate(dks, axis=1).astype(B16)
            dv[keys, pl.ds(col, 2 * DH)] = jnp.concatenate(dvs, axis=1).astype(B16)
        return carry

    lax.fori_loop(0, H // 2, heads, 0)
    dwck[...] = t_dot(enc[...], dk[...]).astype(B16)
    dwcv[...] = t_dot(enc[...], dv[...]).astype(B16)
    denc_ref[...] = (dot_t(dk[...], wck[...]) + dot_t(dv[...], wcv[...])).astype(B16)
    dq2 = jnp.concatenate(
        [jnp.transpose(dqt[s].astype(F32)) for s in range(seqs)], axis=0
    ).astype(B16)
    dwcq[...] = t_dot(a2_ref[...], dq2).astype(B16)
    term, dgain = norm_back(x1_ref[...], gain[...], dot_t(dq2, wcq[...]))
    dgain_ref[...] = dgain
    dx1 = dx2 + term
    dx1_ref[...] = dx1
    db = dx1.astype(B16)
    total = dot(ot[0], db[0:toks])
    for s in range(1, seqs):
        total = total + dot(ot[s], db[s * toks : (s + 1) * toks])
    dwo[...] = total.astype(B16)
    do = dot_t(db, wo[...])
    width = D // groups
    for s in range(seqs):
        turned = jnp.transpose(do[s * toks : (s + 1) * toks]).astype(B16)
        for g in range(groups):
            dot_ref[s * groups + g] = turned[g * width : (g + 1) * width]


def last_kernel(plan, hidden, grads, a1, gain, dx1, wq, wk, wv, dh_ref, dgain_ref, dwq, dwk, dwv):
    dgain_ref[...] = last_products(
        plan, hidden, grads, a1, gain, dx1, wq, wk, wv, dh_ref, dwq, dwk, dwv
    )


def last_products(p, hidden, grads, a1, gain, dx1, wq, wk, wv, dh_ref, dwq, dwk, dwv):
    x = hidden[...].reshape(p.S * p.T, D).astype(F32)
    da1 = jnp.zeros((p.S * p.T, D), F32)
    for n, (weight, dw) in enumerate(((wq, dwq), (wk, dwk), (wv, dwv))):
        rows = []
        for s in range(p.S):
            turned = jnp.concatenate(
                [grads[s * p.G + g, n * p.F : (n + 1) * p.F, :] for g in range(p.G)], axis=0
            )
            rows.append(jnp.transpose(turned.astype(F32)))
        d = jnp.concatenate(rows, axis=0).astype(B16)
        dw[...] = t_dot(a1[...], d).astype(B16).reshape(dw.shape)
        da1 = da1 + dot_t(d, weight[...])
    term, dgain = norm_back(x, gain[...], da1)
    dh_ref[...] = (dx1[...] + term).astype(B16).reshape(dh_ref.shape)
    return dgain


def gather_rows(part):
    count = lax.axis_size("shard")
    rows, cols = part.shape
    half = rows // 2
    mine = lax.axis_index("shard")
    core = lax.axis_index("rep") % 2
    pairs = [(r, r ^ 1) for r in range(lax.axis_size("rep"))]
    own = lax.dynamic_slice(part, (core * half, 0), (half, cols))
    full = jnp.zeros((count, rows, cols), part.dtype)
    full = lax.dynamic_update_slice(full, part[None], (mine, 0, 0))
    for k in range(1, count):
        got = lax.ppermute(own, "shard", [(i, (i + k) % count) for i in range(count)])
        also = lax.ppermute(got, "rep", pairs)
        owner = (mine - k) % count
        full = lax.dynamic_update_slice(full, got[None], (owner, core * half, 0))
        full = lax.dynamic_update_slice(full, also[None], (owner, (1 - core) * half, 0))
    return full.reshape(count * rows, cols)


def reduce_grads(grads):
    owned = [lax.psum_scatter(g, "shard", scatter_dimension=0, tiled=True) for g in grads]
    summed = lax.psum(tuple(owned), "rep")
    return [s.astype(F32) for s in summed]


BITS = 4


class Job:
    def __init__(self, source, result, row, rows, col, cols):
        self.source, self.result = source, result
        self.row, self.rows, self.col, self.cols = row, rows, col, cols


def partner(bit):
    me = lax.axis_index("rep")
    half = 2**bit
    mine = (me // half) % 2
    return mine, me + half * (1 - 2 * mine)


def to_rep(src, dst, send, recv, bit):
    return remote(src, dst, send, recv, partner(bit)[1])


def to_row(src, dst, send, recv):
    x = lax.axis_index("shard")
    return pltpu.make_async_remote_copy(
        src_ref=src,
        dst_ref=dst,
        send_sem=send,
        recv_sem=recv,
        device_id={"shard": 1 - x},
        device_id_type=MESH,
    )


def add_into(acc, term, rows):
    step = 16 if rows % 32 else 32

    def body(i, carry):
        at = pl.ds(pl.multiple_of(i * step, step), step)
        acc[at, :] = (acc[at, :].astype(F32) + term[at, :].astype(F32)).astype(B16)
        return carry

    lax.fori_loop(0, rows // step, body, 0)


class JobRun:
    STAGES = 10

    def __init__(self, job, source, result, bufs, sems, index):
        self.job, self.source, self.result = job, source, result
        self.acc, self.core, self.row, *self.part = bufs
        send, recv, local = sems
        self.send = [send.at[index, i] for i in range(9)]
        self.recv = [recv.at[index, i] for i in range(9)]
        self.local = [local.at[index, i] for i in range(2)]
        self.sent = []
        self.x = lax.axis_index("shard")
        self.bits = [partner(b)[0] for b in range(BITS)]
        half = job.cols // 2
        self.half = half
        self.mine = pl.ds(pl.multiple_of(job.col + self.bits[0] * half, 128), half)
        self.other = pl.ds(pl.multiple_of(job.col + (1 - self.bits[0]) * half, 128), half)
        self.all = pl.ds(job.row, job.rows)
        self.first = [0]
        count = job.rows
        for b in range(1, BITS):
            count //= 2
            self.first.append(self.first[-1] + self.bits[b] * count)

    def count(self, level):
        return self.job.rows // 2**level

    def span(self, first, count):
        return pl.ds(pl.multiple_of(first, 16), count)

    def out(self, first, count):
        return self.result.at[self.span(self.job.row + first, count), self.mine]

    def go(self, copy):
        copy.start()
        self.sent.append(copy)

    def stage(self, n):
        job = self.job
        if n == 0:
            pltpu.make_async_copy(
                self.source.at[:, self.all, self.mine], self.acc, self.local[0]
            ).start()
            self.go(
                to_rep(
                    self.source.at[:, self.all, self.other],
                    self.core,
                    self.send[0],
                    self.recv[0],
                    0,
                )
            )
        elif n == 1:
            landed(self.acc, self.local[0])
            landed(self.core, self.recv[0])
            for i in range(2):
                add_into(self.acc.at[i], self.core.at[i], job.rows)
            self.go(to_row(self.acc.at[1 - self.x], self.row, self.send[1], self.recv[1]))
        elif n == 2:
            landed(self.row, self.recv[1])
            add_into(self.acc.at[self.x], self.row, job.rows)
            self.give(1)
        elif n in (3, 4):
            self.take(n - 2)
            self.give(n - 1)
        elif n == 5:
            self.take(3)
            piece = self.acc.at[self.x, self.span(self.first[3], self.count(3))]
            place = self.out(self.first[3], self.count(3))
            pltpu.make_async_copy(piece, place, self.local[1]).start()
            self.go(to_rep(piece, place, self.send[5], self.recv[5], 3))
        elif n in (6, 7, 8):
            level = 9 - n
            if n == 6:
                landed(self.out(self.first[3], self.count(3)), self.local[1])
            self.landed_at(level)
            place = self.out(self.first[level - 1], self.count(level - 1))
            self.go(to_rep(place, place, self.send[n], self.recv[n], level - 1))
        else:
            landed(self.result.at[self.all, self.other], self.recv[8])
            for copy in self.sent:
                copy.wait_send()

    def give(self, level):
        count = self.count(level)
        first = self.first[level - 1] + (1 - self.bits[level]) * count
        self.go(
            to_rep(
                self.acc.at[self.x, self.span(first, count)],
                self.part[level - 1],
                self.send[level + 1],
                self.recv[level + 1],
                level,
            )
        )

    def take(self, level):
        landed(self.part[level - 1], self.recv[level + 1])
        count = self.count(level)
        rows = self.span(self.first[level], count)
        add_into(self.acc.at[self.x, rows], self.part[level - 1], count)

    def landed_at(self, level):
        count = self.count(level)
        first = self.first[level - 1] + (1 - self.bits[level]) * count
        landed(self.out(first, count), self.recv[8 - level])


def job_buffers(job):
    half = job.cols // 2
    return [
        pltpu.VMEM((2, job.rows, half), B16),
        pltpu.VMEM((2, job.rows, half), B16),
        pltpu.VMEM((job.rows, half), B16),
    ] + [pltpu.VMEM((job.rows // 2**b, half), B16) for b in range(1, BITS)]


JOB_BUFFERS = 6


class SmallRun:
    STAGES = BITS + 2

    def __init__(self, sums, terms, send, recv):
        self.sums, self.terms, self.send, self.recv = sums, terms, send, recv

    def copy(self, n):
        args = (self.sums.at[n], self.terms.at[n], self.send.at[n], self.recv.at[n])
        return to_row(*args) if n == BITS else to_rep(*args, n)

    def stage(self, n):
        if n > 0:
            landed(self.terms.at[n - 1], self.recv.at[n - 1])
            self.sums[n] = self.sums[n - 1] + self.terms[n - 1]
        if n <= BITS:
            self.copy(n).start()
        else:
            for i in range(BITS + 1):
                self.copy(i).wait_send()


def in_ticks(runs):
    last = max(i + run.STAGES for i, run in enumerate(runs))
    for tick in range(last):
        for n in range(max(run.STAGES for run in runs)):
            if 0 <= tick - n < len(runs) and n < runs[tick - n].STAGES:
                runs[tick - n].stage(n)
        yield


def jobs_of(shapes):
    jobs = []
    for i, (rows, cols) in enumerate(shapes):
        wide = cols // 2 if cols > 1024 else cols
        tall = rows // 2 if rows > 512 else rows
        for row in range(0, rows, tall):
            for col in range(0, cols, wide):
                jobs.append(Job(i, i, row, tall, col, wide))
    return jobs


SMALL_ROWS = 16


def tail_kernel(p, jobs, early, arrays, *refs):
    refs = list(refs)
    take = lambda n: [refs.pop(0) for _ in range(n)]
    sources = take(early)
    (dot_,) = take(1)
    recv, lines, of_ref, rl_ref, hidden, a1, gain, dx1, dgc, dgf, wq, wk, wv = take(13)
    results = take(arrays)
    small, dh_ref = take(2)
    dout, dq, dkv, part, out, grads = take(6)
    late = take(arrays - early)
    small_sums, small_terms = take(2)
    back = take(7)
    rows_send, rows_recv, part_sem, got_sem, ret_send, ret_recv = take(6)
    small_send, small_recv = take(2)
    sems = take(3)
    sources = sources + late
    runs = [
        JobRun(job, sources[job.source], results[job.result], take(JOB_BUFFERS), sems, i)
        for i, job in enumerate(jobs)
    ]
    ready = sum(1 for job in jobs if job.source < early)
    runs.insert(ready, SmallRun(small_sums, small_terms, small_send, small_recv))

    me = lax.axis_index("rep")
    w = me % p.W
    unit = me // p.W
    group = unit % p.G
    mine = p.worker_of(me)
    slot = p.slot_of(me)
    barrier = pltpu.get_barrier_semaphore()
    for k in range(1, p.R):
        pl.semaphore_signal(
            barrier, inc=1, device_id={"rep": (me + k) % p.R}, device_id_type=MESH
        )
    x = lax.axis_index("shard")
    pl.semaphore_signal(barrier, inc=1, device_id={"shard": 1 - x}, device_id_type=MESH)
    pl.semaphore_wait(barrier, p.R)

    pipeline = in_ticks(runs)
    passed = 0

    def tick(count=1):
        nonlocal passed
        for _ in range(count):
            next(pipeline)
        passed += count

    for u in range(p.U):
        start_either(
            me, u * p.W + mine, dot_.at[u], dout.at[slot], rows_send.at[u], rows_recv.at[slot]
        )
    tick(2)
    for j in range(p.J):
        landed(dout.at[j], rows_recv.at[j])
    lines_at = lax.broadcasted_iota(jnp.int32, (SMALL_ROWS, D), 0)
    block = jnp.zeros((SMALL_ROWS, D), F32)
    for h in range(p.HG):
        sums = back_head(
            p,
            w,
            h * DH,
            lines.at[group * p.HG + h],
            recv,
            dout,
            of_ref,
            rl_ref.at[h],
            dq,
            dkv,
            *back,
        )
        sums = jnp.concatenate([sums, jnp.zeros((1, D - 2 * p.T), F32)], axis=1)
        block = jnp.where(lines_at == 3 + group * p.HG + h, sums, block)
        tick()

    def give(k, j):
        to = (w + k) % p.W
        return remote(
            dkv.at[p.source(j, to)],
            part.at[k - 1, j],
            part_sem.at[k - 1, j],
            got_sem.at[k - 1, j],
            me - w + to,
        )

    for j in range(p.J):
        for k in range(1, p.W):
            give(k, j).start()
    tick()
    for j in range(p.J):
        r = p.source(j, w)
        total = dkv[r].astype(F32)
        for k in range(1, p.W):
            landed(part.at[k - 1, j], got_sem.at[k - 1, j])
            total = total + part[k - 1, j].astype(F32)
        out[j, 0 : p.F, :] = dq[j]
        out[j, p.F : 3 * p.F, :] = total.astype(B16)
        start_either(me, r, out.at[j], grads.at[unit], ret_send.at[j], ret_recv.at[unit])
    tick(2)
    for u in range(p.U):
        landed(grads.at[u], ret_recv.at[u])
    dgain = last_products(p, hidden, grads, a1, gain, dx1, wq, wk, wv, dh_ref, *late)
    for i, row in enumerate((dgain, dgc[...], dgf[...])):
        block = jnp.where(lines_at == i, row, block)
    small_sums[0] = block
    assert passed <= ready
    for _ in pipeline:
        pass
    small[...] = small_sums[BITS + 1]
    for u in range(p.U):
        end_either(
            me, u * p.W + mine, dot_.at[u], dout.at[slot], rows_send.at[u], rows_recv.at[slot]
        )
    for j in range(p.J):
        r = p.source(j, w)
        end_either(me, r, out.at[j], grads.at[unit], ret_send.at[j], ret_recv.at[unit])
        for k in range(1, p.W):
            give(k, j).wait_send()


def tail_call(p, mats, dot_, held, hidden, collective):
    half = D // 2
    shapes = [m.shape[1:] for m in mats] + [(half, D)] * 3
    jobs = jobs_of(shapes)
    dma = pltpu.SemaphoreType.DMA
    others = max(p.W - 1, 1)
    scratch = [
        pltpu.VMEM((p.J, p.F, p.T), B16),
        pltpu.VMEM((p.J, p.F, p.T), B16),
        pltpu.VMEM((p.R, 2 * p.F, p.T), B16),
        pltpu.VMEM((others, p.J, 2 * p.F, p.T), B16),
        pltpu.VMEM((p.J, 3 * p.F, p.T), B16),
        pltpu.VMEM((p.U, 3 * p.F, p.T), B16),
    ]
    scratch += [pltpu.VMEM((2, half, D), B16)] * 3
    scratch += [
        pltpu.VMEM((BITS + 2, SMALL_ROWS, D), F32),
        pltpu.VMEM((BITS + 1, SMALL_ROWS, D), F32),
    ]
    scratch += back_scratch(p)
    scratch += [
        dma((p.U,)),
        dma((p.J,)),
        dma((others, p.J)),
        dma((others, p.J)),
        dma((p.J,)),
        dma((p.U,)),
        dma((BITS + 1,)),
        dma((BITS + 1,)),
        dma((len(jobs), 9)),
        dma((len(jobs), 9)),
        dma((len(jobs), 2)),
    ]
    for job in jobs:
        scratch += job_buffers(job)
    anywhere = pl.BlockSpec(memory_space=pl.ANY)
    near = pl.BlockSpec(memory_space=pltpu.VMEM)
    *sums, small, dh = pl.pallas_call(
        functools.partial(tail_kernel, p, jobs, len(mats), len(shapes)),
        out_shape=[jax.ShapeDtypeStruct(s, B16) for s in shapes]
        + [
            jax.ShapeDtypeStruct((SMALL_ROWS, D), F32),
            jax.ShapeDtypeStruct(hidden.shape, B16),
        ],
        in_specs=[anywhere] * (len(mats) + 1) + [near] * len(held),
        out_specs=[anywhere] * len(shapes) + [near] * 2,
        scratch_shapes=scratch,
        compiler_params=pltpu.CompilerParams(
            collective_id=collective, has_side_effects=True, vmem_limit_bytes=60 * 2**20
        ),
        name="tail",
    )(*mats, dot_, *held)
    return sums, small, dh


def widen_kernel(count, *refs):
    for i in range(count):
        refs[count + i][...] = refs[i][...].astype(F32)


def widen(mats):
    parts = 8
    blocks = [
        pl.BlockSpec((m.shape[0] // parts, m.shape[1]), lambda i: (i, 0)) for m in mats
    ]
    return pl.pallas_call(
        functools.partial(widen_kernel, len(mats)),
        grid=(parts,),
        out_shape=[jax.ShapeDtypeStruct(m.shape, F32) for m in mats],
        in_specs=blocks,
        out_specs=blocks,
        compiler_params=pltpu.CompilerParams(vmem_limit_bytes=40 * 2**20),
        name="widen",
    )(*mats)


def local(
    hidden,
    encoded,
    out_grad,
    self_query,
    self_key,
    self_value,
    self_out,
    cross_query,
    cross_key,
    cross_value,
    cross_out,
    ffn_gate,
    ffn_up,
    ffn_down,
    gain_self,
    gain_cross,
    gain_ffn,
    bias_table,
    buckets,
):
    seqs, toks = hidden.shape[0], hidden.shape[1]
    p = Plan(seqs, toks, lax.axis_size("rep"))
    tokens = seqs * toks
    ff = ffn_gate.shape[1]
    enc_rows = seqs * encoded.shape[1] * p.R
    dma = pltpu.SemaphoreType.DMA

    small = jnp.concatenate(
        [
            jnp.stack([gain_self, gain_cross, gain_ffn]).reshape(-1),
            bias_table.reshape(-1),
        ]
    ).astype(B16)
    small = lax.all_gather(small, "shard", axis=0)
    part = gain_self.shape[0]
    gains = [
        small[:, i * part : (i + 1) * part].reshape(1, D).astype(F32) for i in range(3)
    ]
    table = small[:, 3 * part :].reshape(NB, H)
    near = buckets[: 2 * toks]
    onehot = (near[:, None] == jnp.arange(NB, dtype=jnp.int32)[None, :]).astype(B16)
    lines = jnp.einsum("lb,bh->hl", onehot, table, preferred_element_type=F32)[:, None, :]

    wq, wk, wv, wo, wcq, wck, wcv, wco, wg, wu, wd = [
        gather_rows(m.astype(B16))
        for m in (
            self_query,
            self_key,
            self_value,
            self_out,
            cross_query,
            cross_key,
            cross_value,
            cross_out,
            ffn_gate,
            ffn_up,
            ffn_down,
        )
    ]
    enc = lax.all_gather(encoded, "rep", axis=1, tiled=True).reshape(enc_rows, D)

    a1, send = plain_call(
        functools.partial(project_kernel, p),
        [((tokens, D), B16), ((p.U, 3 * p.F, toks), B16)],
        (hidden, gains[0], wq, wk, wv),
        "project",
    )
    recv = comm_call(
        functools.partial(scatter_tokens, p),
        (p.R, 3 * p.F, toks),
        (send,),
        [dma((p.U,)), dma((max(p.W - 1, 1), p.J)), dma((p.R,))],
        0,
        "scatter_tokens",
    )
    ckn, ckt, cvn, cvt = plain_call(
        encode_kernel,
        [
            ((H, enc_rows, DH), B16),
            ((H, DH + ONES, enc_rows), B16),
            ((H, enc_rows, DH), B16),
            ((H, DH + ONES, enc_rows), B16),
        ],
        (enc, wck, wcv),
        "encode",
    )
    o, of, rl = pl.pallas_call(
        functools.partial(attend_kernel, p),
        grid=(p.HG,),
        out_shape=[
            jax.ShapeDtypeStruct((p.J, p.F, toks), B16),
            jax.ShapeDtypeStruct((p.J, p.F, toks), F32),
            jax.ShapeDtypeStruct((p.HG, p.NP, 1, 2 * toks), F32),
        ],
        in_specs=[whole((p.R, 3 * p.F, toks)), whole((H, 1, 2 * toks))],
        out_specs=[
            whole((p.J, p.F, toks)),
            whole((p.J, p.F, toks)),
            whole((p.HG, p.NP, 1, 2 * toks)),
        ],
        scratch_shapes=[
            pltpu.VMEM((p.L, DH), B16),
            pltpu.VMEM((DH + ONES, p.L), B16),
            pltpu.VMEM((3, p.CK, 2 * toks), F32),
        ],
        compiler_params=pltpu.CompilerParams(vmem_limit_bytes=56 * 2**20),
        name="attend",
    )(recv, lines)
    ot = comm_call(
        functools.partial(return_tokens, p),
        (p.U, p.F, toks),
        (o,),
        [dma((p.J,)), dma((p.U,))],
        1,
        "return_tokens",
    ).reshape(seqs, D, toks)

    x1, x2, a2, qt2, of2, rl2 = plain_call(
        functools.partial(cross_kernel, seqs),
        [
            ((tokens, D), F32),
            ((tokens, D), F32),
            ((tokens, D), B16),
            ((seqs, D, toks), B16),
            ((seqs, D, toks), F32),
            ((seqs, H, 1, toks), F32),
        ],
        (hidden, ot, wo, gains[1], wcq, wco, ckn, cvt),
        "cross",
    )

    chunk = min(512, ff)
    const = lambda s: pl.BlockSpec(s, lambda i: (0, 0))
    output, dx2, dg_ffn, dwg, dwu, dwd = pl.pallas_call(
        ffn_kernel,
        grid=(ff // chunk,),
        out_shape=[
            jax.ShapeDtypeStruct((tokens, D), B16),
            jax.ShapeDtypeStruct((tokens, D), F32),
            jax.ShapeDtypeStruct((1, D), F32),
            jax.ShapeDtypeStruct((D, ff), B16),
            jax.ShapeDtypeStruct((D, ff), B16),
            jax.ShapeDtypeStruct((ff, D), B16),
        ],
        in_specs=[
            const((tokens, D)),
            const((tokens, D)),
            const((1, D)),
            pl.BlockSpec((D, chunk), lambda i: (0, i)),
            pl.BlockSpec((D, chunk), lambda i: (0, i)),
            pl.BlockSpec((chunk, D), lambda i: (i, 0)),
        ],
        out_specs=[
            const((tokens, D)),
            const((tokens, D)),
            const((1, D)),
            pl.BlockSpec((D, chunk), lambda i: (0, i)),
            pl.BlockSpec((D, chunk), lambda i: (0, i)),
            pl.BlockSpec((chunk, D), lambda i: (i, 0)),
        ],
        scratch_shapes=[
            pltpu.VMEM((tokens, D), B16),
            pltpu.VMEM((tokens, D), F32),
            pltpu.VMEM((tokens, D), F32),
        ],
        compiler_params=pltpu.CompilerParams(vmem_limit_bytes=56 * 2**20),
        name="ffn",
    )(x2, out_grad.reshape(tokens, D), gains[2], wg, wu, wd)

    dx1, dg_cross, dot_, denc, dwco, dwcq, dwck, dwcv, dwo = plain_call(
        functools.partial(cross_back_kernel, seqs, p.G),
        [
            ((tokens, D), F32),
            ((1, D), F32),
            ((p.U, p.F, toks), B16),
            ((enc_rows, D), B16),
        ]
        + [((D, D), B16)] * 5,
        (dx2, x1, a2, gains[1], qt2, of2, rl2, ckn, ckt, cvn, enc, wco, wcq, wck, wcv, wo, ot),
        "cross_back",
        scratch=[
            pltpu.VMEM((seqs, D, toks), B16),
            pltpu.VMEM((seqs, D, toks), B16),
            pltpu.VMEM((enc_rows, D), B16),
            pltpu.VMEM((enc_rows, D), B16),
        ],
    )
    encoded_grad = lax.psum_scatter(
        denc.reshape(seqs, enc_rows // seqs, D), "rep", scatter_dimension=1, tiled=True
    )
    n_shard = lax.axis_size("shard")
    mine = lax.axis_index("shard")
    if n_shard == 2 and p.R == 2**BITS and 3 + H <= SMALL_ROWS:
        early = [
            g.reshape(2, g.shape[0] // 2, g.shape[1])
            for g in (dwd, dwg, dwu, dwo, dwcq, dwck, dwcv, dwco)
        ]
        held = (recv, lines, of, rl, hidden, a1, gains[0], dx1, dg_cross, dg_ffn, wq, wk, wv)
        sums, block, hidden_grad = tail_call(p, early, dot_, held, hidden, 2)
        dwd, dwg, dwu, dwo, dwcq, dwck, dwcv, dwco, dwq, dwk, dwv = widen(sums)
        mats = [dwq, dwk, dwv, dwo, dwcq, dwck, dwcv, dwco, dwg, dwu, dwd]
        dgains = lax.dynamic_slice(block, (0, mine * part), (3, part))
        by_bucket = jnp.einsum(
            "hl,lb->bh",
            block[3 : 3 + H, : 2 * toks],
            onehot.astype(F32),
            precision=lax.Precision.HIGHEST,
        )
        dtab = lax.dynamic_slice(
            by_bucket, (mine * bias_table.shape[0], 0), bias_table.shape
        )
    else:
        dout = comm_call(
            functools.partial(scatter_rows, p),
            (p.J, p.F, toks),
            (dot_,),
            [dma((p.U,)), dma((p.J,))],
            2,
            "scatter_rows",
        )
        dq, dkv, line = pl.pallas_call(
            functools.partial(attend_back_kernel, p),
            grid=(p.HG,),
            out_shape=[
                jax.ShapeDtypeStruct((p.J, p.F, toks), B16),
                jax.ShapeDtypeStruct((p.R, 2 * p.F, toks), B16),
                jax.ShapeDtypeStruct((p.HG, 1, 2 * toks), F32),
            ],
            in_specs=[
                whole((p.R, 3 * p.F, toks)),
                whole((H, 1, 2 * toks)),
                whole((p.J, p.F, toks)),
                whole((p.J, p.F, toks)),
                whole((p.HG, p.NP, 1, 2 * toks)),
            ],
            out_specs=[
                whole((p.J, p.F, toks)),
                whole((p.R, 2 * p.F, toks)),
                whole((p.HG, 1, 2 * toks)),
            ],
            scratch_shapes=back_scratch(p),
            compiler_params=pltpu.CompilerParams(vmem_limit_bytes=56 * 2**20),
            name="attend_back",
        )(recv, lines, dout, of, rl)
        grads = comm_call(
            functools.partial(return_grads, p),
            (p.U, 3 * p.F, toks),
            (dq, dkv),
            [
                pltpu.VMEM((max(p.W - 1, 1), p.J, 2 * p.F, toks), B16),
                pltpu.VMEM((p.J, 3 * p.F, toks), B16),
                dma((p.J,)),
                dma((max(p.W - 1, 1), p.J)),
                dma((max(p.W - 1, 1), p.J)),
                dma((p.U,)),
            ],
            3,
            "return_grads",
            space=pltpu.VMEM,
        )
        hidden_grad, dg_self, dwq, dwk, dwv = plain_call(
            functools.partial(last_kernel, p),
            [(hidden.shape, B16), ((1, D), F32)] + [((D, D), B16)] * 3,
            (hidden, grads, a1, gains[0], dx1, wq, wk, wv),
            "last",
        )

        group = (lax.axis_index("rep") // p.W) % p.G
        by_bucket = jnp.einsum(
            "hl,lb->bh", line[:, 0, :], onehot.astype(F32), precision=lax.Precision.HIGHEST
        )
        dtable = lax.dynamic_update_slice(jnp.zeros((NB, H), F32), by_bucket, (0, group * p.HG))

        mats = reduce_grads([dwq, dwk, dwv, dwo, dwcq, dwck, dwcv, dwco, dwg, dwu, dwd])
        lot = jnp.concatenate(
            [g.reshape(n_shard, part) for g in (dg_self, dg_cross, dg_ffn)]
            + [dtable.reshape(n_shard, -1)],
            axis=1,
        )
        size = lot.shape[1]
        lot = lax.psum(lot, ("shard", "rep"))
        lot = lax.dynamic_slice(lot, (mine, 0), (1, size))[0]
        dgains = [lot[i * part : (i + 1) * part] for i in range(3)]
        dtab = lot[3 * part :].reshape(bias_table.shape)
    return (
        output.reshape(hidden.shape),
        hidden_grad,
        encoded_grad,
        *mats,
        *dgains,
        dtab,
    )


def solution(mesh):
    tok = P("shard", "rep", None)
    mat = P("shard", None)
    in_specs = (tok,) * 3 + (mat,) * 11 + (P("shard"),) * 3 + (mat, P())
    out_specs = (tok,) * 3 + (mat,) * 11 + (P("shard"),) * 3 + (mat,)
    return jax.shard_map(local, mesh=mesh, in_specs=in_specs, out_specs=out_specs, check_vma=False)
```

```python
import functools

import jax
import jax.numpy as jnp
from jax import lax
from jax.experimental import pallas as pl
from jax.experimental.pallas import tpu as pltpu
from jax.sharding import PartitionSpec as P

D = 768
H = 12
DH = 64
NB = 32
EPS = 1e-06
F32 = jnp.float32
B16 = jnp.bfloat16
ONES = 16
HIDE = -1e30
MESH = pl.DeviceIdType.MESH
GELU_A = 0.7978845608028654
GELU_B = 0.044715


def dot(a, b):
    return lax.dot_general(a, b, (((1,), (0,)), ((), ())), preferred_element_type=F32)


def dot_t(a, b):
    return lax.dot_general(a, b, (((1,), (1,)), ((), ())), preferred_element_type=F32)


def t_dot(a, b):
    return lax.dot_general(a, b, (((0,), (0,)), ((), ())), preferred_element_type=F32)


def mat(ref):
    return ref[...].reshape(-1, ref.shape[-1])


def scale_of(v):
    return lax.rsqrt(jnp.mean(v * v, axis=-1, keepdims=True) + EPS)


def norm_back(v, gain, grad):
    r = scale_of(v)
    n = v * r
    c = grad * gain
    dv = r * (c - n * jnp.mean(c * n, axis=-1, keepdims=True))
    return dv, jnp.sum(grad * n, axis=0, keepdims=True)


def whole(shape):
    return pl.BlockSpec(shape, lambda *_: (0,) * len(shape))


def plain_call(kernel, outs, args, name, scratch=(), vmem=60):
    return pl.pallas_call(
        kernel,
        out_shape=[jax.ShapeDtypeStruct(s, t) for s, t in outs],
        in_specs=[pl.BlockSpec(memory_space=pltpu.VMEM)] * len(args),
        out_specs=[pl.BlockSpec(memory_space=pltpu.VMEM)] * len(outs),
        scratch_shapes=list(scratch),
        compiler_params=pltpu.CompilerParams(vmem_limit_bytes=vmem * 2**20),
        name=name,
    )(*args)


class Plan:
    def __init__(self, seqs, toks, rows):
        self.S, self.T, self.R = seqs, toks, rows
        groups = 1
        for g in range(1, H + 1):
            if H % g == 0 and seqs * g <= rows and rows % (2 * seqs * g) == 0:
                groups = g
        self.G = groups
        self.HG = H // groups
        self.F = self.HG * DH
        self.U = seqs * groups
        self.W = rows // self.U
        self.J = rows // self.W
        self.NP = self.J // 2
        self.CK = 2 * self.W * toks
        self.L = rows * toks

    def worker_of(self, r):
        m = r % (2 * self.W)
        late = m // self.W
        return m * (1 - late) + (2 * self.W - 1 - m) * late

    def slot_of(self, r):
        return 2 * (r // (2 * self.W)) + (r % (2 * self.W)) // self.W

    def source(self, j, w):
        return self.source_in(j // 2, j % 2, w)

    def source_in(self, pair, late, w):
        if late:
            return 2 * self.W * pair + 2 * self.W - 1 - w
        return 2 * self.W * pair + w


def enter(rows):
    me = lax.axis_index("rep")
    barrier = pltpu.get_barrier_semaphore()
    for k in range(1, rows):
        pl.semaphore_signal(
            barrier, inc=1, device_id={"rep": (me + k) % rows}, device_id_type=MESH
        )
    pl.semaphore_wait(barrier, rows - 1)
    return me


def remote(src, dst, send, recv, to):
    return pltpu.make_async_remote_copy(
        src_ref=src,
        dst_ref=dst,
        send_sem=send,
        recv_sem=recv,
        device_id={"rep": to},
        device_id_type=MESH,
    )


def start_either(me, to, src, dst, send, recv):
    @pl.when(to == me)
    def _():
        pltpu.make_async_copy(src, dst, recv).start()

    @pl.when(to != me)
    def _():
        remote(src, dst, send, recv, to).start()


def end_either(me, to, src, dst, send, recv):
    @pl.when(to != me)
    def _():
        remote(src, dst, send, recv, to).wait_send()


def landed(ref, sem):
    pltpu.make_async_copy(ref, ref, sem).wait()


def scatter_tokens(plan, send, recv, send_sem, relay_sem, recv_sem):
    p = plan
    me = enter(p.R)
    w = me % p.W
    mine = p.worker_of(me)
    for u in range(p.U):
        start_either(me, u * p.W + mine, send.at[u], recv.at[me], send_sem.at[u], recv_sem.at[me])
    for j in range(p.J):
        r = p.source(j, w)
        landed(recv.at[r], recv_sem.at[r])
        for k in range(1, p.W):
            part = recv.at[r, pl.ds(p.F, 2 * p.F)]
            remote(
                part, part, relay_sem.at[k - 1, j], recv_sem.at[r], me - w + (w + k) % p.W
            ).start()
    for k in range(1, p.W):
        for j in range(p.J):
            r = p.source(j, (w + k) % p.W)
            landed(recv.at[r, pl.ds(p.F, 2 * p.F)], recv_sem.at[r])
    for u in range(p.U):
        end_either(me, u * p.W + mine, send.at[u], recv.at[me], send_sem.at[u], recv_sem.at[me])
    for k in range(1, p.W):
        for j in range(p.J):
            r = p.source(j, w)
            part = recv.at[r, pl.ds(p.F, 2 * p.F)]
            remote(
                part, part, relay_sem.at[k - 1, j], recv_sem.at[r], me - w + (w + k) % p.W
            ).wait_send()


def return_tokens(plan, send, recv, send_sem, recv_sem):
    p = plan
    me = enter(p.R)
    w = me % p.W
    unit = me // p.W
    for j in range(p.J):
        r = p.source(j, w)
        start_either(me, r, send.at[j], recv.at[unit], send_sem.at[j], recv_sem.at[unit])
    for u in range(p.U):
        landed(recv.at[u], recv_sem.at[u])
    for j in range(p.J):
        r = p.source(j, w)
        end_either(me, r, send.at[j], recv.at[unit], send_sem.at[j], recv_sem.at[unit])


def scatter_rows(plan, send, recv, send_sem, recv_sem):
    p = plan
    me = enter(p.R)
    mine = p.worker_of(me)
    slot = p.slot_of(me)
    for u in range(p.U):
        start_either(
            me, u * p.W + mine, send.at[u], recv.at[slot], send_sem.at[u], recv_sem.at[slot]
        )
    for j in range(p.J):
        landed(recv.at[j], recv_sem.at[j])
    for u in range(p.U):
        end_either(
            me, u * p.W + mine, send.at[u], recv.at[slot], send_sem.at[u], recv_sem.at[slot]
        )


def return_grads(plan, dq, dkv, recv, buf, out, send_sem, part_sem, got_sem, recv_sem):
    p = plan
    me = enter(p.R)
    w = me % p.W
    unit = me // p.W

    def give(k, j):
        to = (w + k) % p.W
        r = p.source(j, to)
        return remote(
            dkv.at[r],
            buf.at[k - 1, j],
            part_sem.at[k - 1, j],
            got_sem.at[k - 1, j],
            me - w + to,
        )

    for j in range(p.J):
        for k in range(1, p.W):
            give(k, j).start()
    for j in range(p.J):
        r = p.source(j, w)
        total = dkv[r].astype(F32)
        for k in range(1, p.W):
            landed(buf.at[k - 1, j], got_sem.at[k - 1, j])
            total = total + buf[k - 1, j].astype(F32)
        out[j, 0 : p.F, :] = dq[j]
        out[j, p.F : 3 * p.F, :] = total.astype(B16)
        start_either(me, r, out.at[j], recv.at[unit], send_sem.at[j], recv_sem.at[unit])
    for u in range(p.U):
        landed(recv.at[u], recv_sem.at[u])
    for j in range(p.J):
        r = p.source(j, w)
        end_either(me, r, out.at[j], recv.at[unit], send_sem.at[j], recv_sem.at[unit])
        for k in range(1, p.W):
            give(k, j).wait_send()


def comm_call(kernel, out, args, scratch, collective, name, space=pl.ANY):
    return pl.pallas_call(
        kernel,
        out_shape=jax.ShapeDtypeStruct(out, B16),
        in_specs=[pl.BlockSpec(memory_space=space)] * len(args),
        out_specs=pl.BlockSpec(memory_space=space),
        scratch_shapes=list(scratch),
        compiler_params=pltpu.CompilerParams(
            collective_id=collective, has_side_effects=True, vmem_limit_bytes=40 * 2**20
        ),
        name=name,
    )(*args)


def project_kernel(plan, hidden, gain, wq, wk, wv, a1_ref, send):
    p = plan
    x = hidden[...].reshape(p.S * p.T, D).astype(F32)
    a1 = (x * scale_of(x) * gain[0:1, :]).astype(B16)
    a1_ref[...] = a1
    for n, weight in enumerate((wq, wk, wv)):
        rows = dot(a1, mat(weight))
        for s in range(p.S):
            turned = jnp.transpose(rows[s * p.T : (s + 1) * p.T]).astype(B16)
            for g in range(p.G):
                send[s * p.G + g, n * p.F : (n + 1) * p.F, :] = turned[g * p.F : (g + 1) * p.F]


def bias_tiles(plan, w, line, tiles):
    p = plan
    far = line[:, 2 * p.T - 1 : 2 * p.T]
    near = pltpu.roll(jnp.broadcast_to(line, (p.T, 2 * p.T)), 0, 1, stride=1, stride_axis=0)
    key = lax.broadcasted_iota(jnp.int32, (p.T, p.T), 0)
    query = lax.broadcasted_iota(jnp.int32, (p.T, p.T), 1)
    same = jnp.where(query >= key, near[:, : p.T], HIDE)
    next_ = near[:, p.T :]
    farb = jnp.broadcast_to(far, (p.T, p.T))
    tiles[0] = jnp.broadcast_to(far, (p.CK, 2 * p.T))
    for a in range(2):
        ahead = w if a == 0 else 2 * p.W - 1 - w
        for b in range(2 * p.W):
            diff = ahead - b
            tile = jnp.where(
                diff == 0, same, jnp.where(diff == 1, next_, jnp.where(diff < 0, HIDE, farb))
            )
            tiles[2, b * p.T : (b + 1) * p.T, a * p.T : (a + 1) * p.T] = tile
            back = diff + 2 * p.W
            tiles[1, b * p.T : (b + 1) * p.T, a * p.T : (a + 1) * p.T] = jnp.where(
                back == 1, next_, farb
            )


def block_pair(plan, ref, pair, w, row, count):
    p = plan
    return jnp.concatenate(
        [
            ref[p.source_in(pair, 0, w), pl.ds(row, count), :],
            ref[p.source_in(pair, 1, w), pl.ds(row, count), :],
        ],
        axis=1,
    )


def line_of(p, block, head):
    return block[pl.ds(3 + head, 1), 0 : 2 * p.T]


def attend_head(p, w, row, line, recv, o_ref, of_ref, rl, kn, vt, tiles):
    bias_tiles(p, w, line, tiles)
    for r in range(p.R):
        kn[r * p.T : (r + 1) * p.T, :] = jnp.transpose(
            recv[r, pl.ds(p.F + row, DH), :].astype(F32)
        ).astype(B16)
        vt[0:DH, r * p.T : (r + 1) * p.T] = recv[r, pl.ds(2 * p.F + row, DH), :]
    vt[DH : DH + ONES, :] = jnp.ones((ONES, p.L), B16)

    def one_pair(pair, carry):
        qt = block_pair(p, recv, pair, w, row, DH)

        def step(i, acc):
            start = pl.multiple_of(i * p.CK, p.CK)
            e = jnp.exp(dot(kn[pl.ds(start, p.CK), :], qt) + tiles[jnp.maximum(i - pair + 2, 0)])
            return acc + dot(vt[:, pl.ds(start, p.CK)], e.astype(B16))

        acc = lax.fori_loop(0, pair + 1, step, jnp.zeros((DH + ONES, 2 * p.T), F32))
        scale = 1.0 / acc[DH : DH + 1]
        of = acc[:DH] * scale
        rl[pair] = scale
        for a in range(2):
            part = of[:, a * p.T : (a + 1) * p.T]
            of_ref[2 * pair + a, pl.ds(row, DH), :] = part
            o_ref[2 * pair + a, pl.ds(row, DH), :] = part.astype(B16)
        return carry

    lax.fori_loop(0, p.NP, one_pair, 0)


def attend_scratch(p):
    return [
        pltpu.VMEM((p.L, DH), B16),
        pltpu.VMEM((DH + ONES, p.L), B16),
        pltpu.VMEM((3, p.CK, 2 * p.T), F32),
    ]


def attend_kernel(plan, recv, block, o_ref, of_ref, rl_ref, *scratch):
    p = plan
    me = lax.axis_index("rep")
    w = me % p.W
    group = (me // p.W) % p.G
    h = pl.program_id(0)
    row = pl.multiple_of(h * DH, DH)
    line = line_of(p, block, group * p.HG + h)
    attend_head(p, w, row, line, recv, o_ref, of_ref, rl_ref.at[h], *scratch)


def back_head(
    p, w, row, line, recv, dout, of_ref, rl, dq_ref, dkv_ref, kn, vn, kt, dk, dv, tiles, near
):
    bias_tiles(p, w, line, tiles)
    for r in range(p.R):
        kn[r * p.T : (r + 1) * p.T, :] = jnp.transpose(
            recv[r, pl.ds(p.F + row, DH), :].astype(F32)
        ).astype(B16)
        vn[r * p.T : (r + 1) * p.T, :] = jnp.transpose(
            recv[r, pl.ds(2 * p.F + row, DH), :].astype(F32)
        ).astype(B16)
        kt[0:DH, r * p.T : (r + 1) * p.T] = recv[r, pl.ds(p.F + row, DH), :]
    kt[DH : DH + ONES, :] = jnp.ones((ONES, p.L), B16)
    dk[...] = jnp.zeros_like(dk)
    dv[...] = jnp.zeros_like(dv)
    near[...] = jnp.zeros_like(near)

    def one_pair(pair, total):
        qt = block_pair(p, recv, pair, w, row, DH)
        dot_rows = jnp.concatenate(
            [dout[2 * pair + a, pl.ds(row, DH), :] for a in range(2)], axis=1
        )
        of = jnp.concatenate([of_ref[2 * pair + a, pl.ds(row, DH), :] for a in range(2)], axis=1)
        delta = jnp.sum(dot_rows.astype(F32) * of, axis=0, keepdims=True)
        scale = rl[pair]
        qn = jnp.transpose(qt.astype(F32)).astype(B16)
        don = jnp.transpose(dot_rows.astype(F32)).astype(B16)

        def step(i, acc):
            start = pl.multiple_of(i * p.CK, p.CK)
            kind = jnp.maximum(i - pair + 2, 0)
            keys = pl.ds(start, p.CK)
            prob = jnp.exp(dot(kn[keys, :], qt) + tiles[kind]) * scale
            ds = (prob * (dot(vn[keys, :], dot_rows) - delta)).astype(B16)
            near[kind] += ds.astype(F32)
            dk[keys, :] += dot(ds, qn)
            dv[keys, :] += dot(prob.astype(B16), don)
            return acc + dot(kt[:, keys], ds)

        acc = lax.fori_loop(0, pair + 1, step, jnp.zeros((DH + ONES, 2 * p.T), F32))
        for a in range(2):
            dq_ref[2 * pair + a, pl.ds(row, DH), :] = acc[:DH, a * p.T : (a + 1) * p.T].astype(B16)
        return total + acc[DH : DH + 1]

    total = lax.fori_loop(0, p.NP, one_pair, jnp.zeros((1, 2 * p.T), F32))
    for r in range(p.R):
        dkv_ref[r, pl.ds(row, DH), :] = jnp.transpose(dk[r * p.T : (r + 1) * p.T, :]).astype(B16)
        dkv_ref[r, pl.ds(p.F + row, DH), :] = jnp.transpose(dv[r * p.T : (r + 1) * p.T, :]).astype(
            B16
        )
    same = jnp.zeros((p.T, p.T), F32)
    next_ = jnp.zeros((p.T, p.T), F32)
    for a in range(2):
        ahead = w if a == 0 else 2 * p.W - 1 - w
        for b in range(2 * p.W):
            diff = ahead - b
            spot = (slice(b * p.T, (b + 1) * p.T), slice(a * p.T, (a + 1) * p.T))
            tile = near[(2, *spot)]
            same = same + jnp.where(diff == 0, tile, 0.0)
            next_ = next_ + jnp.where(diff == 1, tile, 0.0)
            next_ = next_ + jnp.where(diff + 2 * p.W == 1, near[(1, *spot)], 0.0)
    both = jnp.concatenate([same, next_], axis=1)
    key = lax.broadcasted_iota(jnp.int32, (p.T, p.T), 0)
    other = lax.broadcasted_iota(jnp.int32, (p.T, p.T), 1)
    swap = (key + other == p.T - 1).astype(F32)
    turned = lax.dot_general(
        swap,
        both,
        (((1,), (0,)), ((), ())),
        precision=lax.Precision.HIGHEST,
        preferred_element_type=F32,
    )
    turned = pltpu.roll(turned, p.T + 1, 1, stride=1, stride_axis=0)
    by_distance = jnp.sum(turned, axis=0, keepdims=True)
    rest = jnp.sum(total) - jnp.sum(both)
    place = lax.broadcasted_iota(jnp.int32, (1, 2 * p.T), 1)
    return by_distance + jnp.where(place == 2 * p.T - 1, rest, 0.0)


def back_scratch(p):
    return [
        pltpu.VMEM((p.L, DH), B16),
        pltpu.VMEM((p.L, DH), B16),
        pltpu.VMEM((DH + ONES, p.L), B16),
        pltpu.VMEM((p.L, DH), F32),
        pltpu.VMEM((p.L, DH), F32),
        pltpu.VMEM((3, p.CK, 2 * p.T), F32),
        pltpu.VMEM((3, p.CK, 2 * p.T), F32),
    ]


def attend_back_kernel(plan, recv, block, dout, of_ref, rl_ref, dq_ref, dkv_ref, line_ref, *scratch):
    p = plan
    me = lax.axis_index("rep")
    w = me % p.W
    group = (me // p.W) % p.G
    h = pl.program_id(0)
    row = pl.multiple_of(h * DH, DH)
    line_ref[h] = back_head(
        p,
        w,
        row,
        line_of(p, block, group * p.HG + h),
        recv,
        dout,
        of_ref,
        rl_ref.at[h],
        dq_ref,
        dkv_ref,
        *scratch,
    )


def encode_kernel(enc, wk, wv, kn, kt, vn, vt):
    encode_one(enc, wk, kn, kt)
    encode_one(enc, wv, vn, vt)


def encode_one(enc, weight, natural, turned):
    rows = turned.shape[2]
    value = dot(mat(enc), mat(weight))
    for h in range(H):
        natural[h] = value[:, h * DH : (h + 1) * DH].astype(B16)
    flipped = jnp.transpose(value).astype(B16)
    for h in range(H):
        turned[h, 0:DH, :] = flipped[h * DH : (h + 1) * DH]
        turned[h, DH : DH + ONES, :] = jnp.ones((ONES, rows), B16)


def rows_of(units, s, seqs):
    groups = units.shape[0] // seqs
    return units[s * groups : (s + 1) * groups].reshape(-1, units.shape[-1])


def cross_kernel(
    seqs,
    hidden,
    ot,
    wo,
    gain,
    wcq,
    wco,
    kn,
    vt,
    x1_ref,
    x2_ref,
    a2_ref,
    qt_ref,
    of_ref,
    rl_ref,
    pause=lambda: None,
):
    toks = hidden.shape[1]
    span = kn.shape[1] // seqs
    x = hidden[...].reshape(seqs * toks, D).astype(F32)
    o = jnp.concatenate(
        [jnp.transpose(rows_of(ot, s, seqs).astype(F32)) for s in range(seqs)], axis=0
    ).astype(B16)
    x1 = x + dot(o, mat(wo))
    x1_ref[...] = x1
    a2 = (x1 * scale_of(x1) * gain[1:2, :]).astype(B16)
    a2_ref[...] = a2
    q2 = dot(a2, mat(wcq))
    for s in range(seqs):
        qt_ref[s] = jnp.transpose(q2[s * toks : (s + 1) * toks]).astype(B16)
    pause()

    def heads(i, carry):
        for sub in range(2):
            h = 2 * i + sub
            row = pl.multiple_of(h * DH, DH)
            for s in range(seqs):
                keys = slice(s * span, (s + 1) * span)
                e = jnp.exp(dot(kn[h, keys, :], qt_ref[s, pl.ds(row, DH), :]))
                acc = dot(vt[h, :, keys], e.astype(B16))
                rl = 1.0 / acc[DH : DH + 1]
                of_ref[s, pl.ds(row, DH), :] = acc[:DH] * rl
                rl_ref[s, h] = rl
        return carry

    lax.fori_loop(0, H // 2, heads, 0)
    pause()
    o2 = jnp.concatenate([jnp.transpose(of_ref[s]) for s in range(seqs)], axis=0).astype(B16)
    x2_ref[...] = x1_ref[...] + dot(o2, mat(wco))


def ffn_kernel(
    x2_ref, og_ref, gain, wg, wu, wd, out_ref, dx2_ref, dgain_ref, dwg, dwu, dwd, a3, acc, da3
):
    step = pl.program_id(0)

    @pl.when(step == 0)
    def _():
        x2 = x2_ref[...]
        a3[...] = (x2 * scale_of(x2) * gain[2:3, :]).astype(B16)
        acc[...] = x2
        da3[...] = jnp.zeros_like(da3)

    rows = a3[...]
    og = og_ref[...]
    gate = dot(rows, wg[...])
    up = dot(rows, wu[...])
    square = gate * gate
    th = jnp.tanh(GELU_A * gate * (1.0 + GELU_B * square))
    half = 0.5 * (1.0 + th)
    value = gate * half
    slope = half + 0.5 * gate * (1.0 - th * th) * (GELU_A * (1.0 + 3.0 * GELU_B * square))
    inner = (value * up).astype(B16)
    acc[...] += dot(inner, wd[...])
    dwd[...] = t_dot(inner, og).astype(B16)
    dinner = dot_t(og, wd[...]).astype(B16).astype(F32)
    dgate = (dinner * up * slope).astype(B16)
    dup = (dinner * value).astype(B16)
    dwg[...] = t_dot(rows, dgate).astype(B16)
    dwu[...] = t_dot(rows, dup).astype(B16)
    da3[...] += dot_t(dgate, wg[...]) + dot_t(dup, wu[...])

    @pl.when(step == pl.num_programs(0) - 1)
    def _():
        out_ref[...] = acc[...].astype(B16)
        dv, dgain = norm_back(x2_ref[...], gain[2:3, :], da3[...])
        dx2_ref[...] = og_ref[...].astype(F32) + dv
        dgain_ref[...] = dgain


def cross_back_kernel(
    seqs,
    groups,
    dx2_ref,
    x1_ref,
    a2_ref,
    gain,
    qt_ref,
    of_ref,
    rl_ref,
    kn,
    kt,
    vn,
    enc,
    wco,
    wcq,
    wck,
    wcv,
    wo,
    ot,
    dx1_ref,
    dgain_ref,
    dot_ref,
    denc_ref,
    dwco,
    dwcq,
    dwck,
    dwcv,
    dwo,
    dt,
    dqt,
    dk,
    dv,
):
    toks = qt_ref.shape[2]
    span = kn.shape[1] // seqs
    dx2 = dx2_ref[...]
    dc = dx2.astype(B16)
    o2t = [of_ref[s].astype(B16) for s in range(seqs)]
    total = dot(o2t[0], dc[0:toks])
    for s in range(1, seqs):
        total = total + dot(o2t[s], dc[s * toks : (s + 1) * toks])
    dwco[...] = total.astype(B16)
    do2 = dot_t(dc, mat(wco))
    for s in range(seqs):
        dt[s] = jnp.transpose(do2[s * toks : (s + 1) * toks]).astype(B16)

    def heads(i, carry):
        col = pl.multiple_of(2 * i * DH, 2 * DH)
        for s in range(seqs):
            keys = slice(s * span, (s + 1) * span)
            dks, dvs = [], []
            q_pair = jnp.transpose(qt_ref[s, pl.ds(col, 2 * DH), :].astype(F32)).astype(B16)
            d_pair = jnp.transpose(dt[s, pl.ds(col, 2 * DH), :].astype(F32)).astype(B16)
            for sub in range(2):
                h = 2 * i + sub
                row = pl.multiple_of(h * DH, DH)
                d_rows = dt[s, pl.ds(row, DH), :]
                prob = jnp.exp(dot(kn[h, keys, :], qt_ref[s, pl.ds(row, DH), :])) * rl_ref[s, h]
                delta = jnp.sum(
                    d_rows.astype(F32) * of_ref[s, pl.ds(row, DH), :], axis=0, keepdims=True
                )
                ds = (prob * (dot(vn[h, keys, :], d_rows) - delta)).astype(B16)
                dqt[s, pl.ds(row, DH), :] = dot(kt[h, 0:DH, keys], ds).astype(B16)
                dks.append(dot(ds, q_pair[:, sub * DH : (sub + 1) * DH]))
                dvs.append(dot(prob.astype(B16), d_pair[:, sub * DH : (sub + 1) * DH]))
            dk[keys, pl.ds(col, 2 * DH)] = jnp.concatenate(dks, axis=1).astype(B16)
            dv[keys, pl.ds(col, 2 * DH)] = jnp.concatenate(dvs, axis=1).astype(B16)
        return carry

    lax.fori_loop(0, H // 2, heads, 0)
    dwck[...] = t_dot(mat(enc), dk[...]).astype(B16)
    dwcv[...] = t_dot(mat(enc), dv[...]).astype(B16)
    denc_ref[...] = (dot_t(dk[...], mat(wck)) + dot_t(dv[...], mat(wcv))).astype(B16)
    dq2 = jnp.concatenate(
        [jnp.transpose(dqt[s].astype(F32)) for s in range(seqs)], axis=0
    ).astype(B16)
    dwcq[...] = t_dot(a2_ref[...], dq2).astype(B16)
    term, dgain = norm_back(x1_ref[...], gain[1:2, :], dot_t(dq2, mat(wcq)))
    dgain_ref[...] = dgain
    dx1 = dx2 + term
    dx1_ref[...] = dx1
    db = dx1.astype(B16)
    total = dot(rows_of(ot, 0, seqs), db[0:toks])
    for s in range(1, seqs):
        total = total + dot(rows_of(ot, s, seqs), db[s * toks : (s + 1) * toks])
    dwo[...] = total.astype(B16)
    do = dot_t(db, mat(wo))
    width = D // groups
    for s in range(seqs):
        turned = jnp.transpose(do[s * toks : (s + 1) * toks]).astype(B16)
        for g in range(groups):
            dot_ref[s * groups + g] = turned[g * width : (g + 1) * width]


def last_kernel(plan, hidden, grads, a1, gain, dx1, wq, wk, wv, dh_ref, dgain_ref, dwq, dwk, dwv):
    dgain_ref[...] = last_products(
        plan, hidden, grads, a1, gain, dx1, wq, wk, wv, dh_ref, dwq, dwk, dwv
    )


def last_products(p, hidden, grads, a1, gain, dx1, wq, wk, wv, dh_ref, dwq, dwk, dwv):
    x = hidden[...].reshape(p.S * p.T, D).astype(F32)
    da1 = jnp.zeros((p.S * p.T, D), F32)
    for n, (weight, dw) in enumerate(((wq, dwq), (wk, dwk), (wv, dwv))):
        rows = []
        for s in range(p.S):
            turned = jnp.concatenate(
                [grads[s * p.G + g, n * p.F : (n + 1) * p.F, :] for g in range(p.G)], axis=0
            )
            rows.append(jnp.transpose(turned.astype(F32)))
        d = jnp.concatenate(rows, axis=0).astype(B16)
        dw[...] = t_dot(a1[...], d).astype(B16).reshape(dw.shape)
        da1 = da1 + dot_t(d, mat(weight))
    term, dgain = norm_back(x, gain[0:1, :], da1)
    dh_ref[...] = (dx1[...] + term).astype(B16).reshape(dh_ref.shape)
    return dgain


def gather_rows(part):
    count = lax.axis_size("shard")
    rows, cols = part.shape
    half = rows // 2
    mine = lax.axis_index("shard")
    core = lax.axis_index("rep") % 2
    pairs = [(r, r ^ 1) for r in range(lax.axis_size("rep"))]
    own = lax.dynamic_slice(part, (core * half, 0), (half, cols))
    full = jnp.zeros((count, rows, cols), part.dtype)
    full = lax.dynamic_update_slice(full, part[None], (mine, 0, 0))
    for k in range(1, count):
        got = lax.ppermute(own, "shard", [(i, (i + k) % count) for i in range(count)])
        also = lax.ppermute(got, "rep", pairs)
        owner = (mine - k) % count
        full = lax.dynamic_update_slice(full, got[None], (owner, core * half, 0))
        full = lax.dynamic_update_slice(full, also[None], (owner, (1 - core) * half, 0))
    return full.reshape(count * rows, cols)


def reduce_grads(grads):
    owned = [lax.psum_scatter(g, "shard", scatter_dimension=0, tiled=True) for g in grads]
    summed = lax.psum(tuple(owned), "rep")
    return [s.astype(F32) for s in summed]


BITS = 4


class Job:
    def __init__(self, source, result, row, rows, col, cols):
        self.source, self.result = source, result
        self.row, self.rows, self.col, self.cols = row, rows, col, cols


def partner(bit):
    me = lax.axis_index("rep")
    half = 2**bit
    mine = (me // half) % 2
    return mine, me + half * (1 - 2 * mine)


def to_rep(src, dst, send, recv, bit):
    return remote(src, dst, send, recv, partner(bit)[1])


def to_row(src, dst, send, recv):
    x = lax.axis_index("shard")
    return pltpu.make_async_remote_copy(
        src_ref=src,
        dst_ref=dst,
        send_sem=send,
        recv_sem=recv,
        device_id={"shard": 1 - x},
        device_id_type=MESH,
    )


def add_into(acc, term, rows):
    step = 16 if rows % 32 else 32

    def body(i, carry):
        at = pl.ds(pl.multiple_of(i * step, step), step)
        acc[at, :] = (acc[at, :].astype(F32) + term[at, :].astype(F32)).astype(B16)
        return carry

    lax.fori_loop(0, rows // step, body, 0)


class JobRun:
    STAGES = 10

    def __init__(self, job, source, result, bufs, sems, index):
        self.job, self.source, self.result = job, source, result
        self.acc, self.core, self.row, *self.part = bufs
        send, recv, local = sems
        self.send = [send.at[index, i] for i in range(9)]
        self.recv = [recv.at[index, i] for i in range(9)]
        self.local = [local.at[index, i] for i in range(2)]
        self.sent = []
        self.x = lax.axis_index("shard")
        self.bits = [partner(b)[0] for b in range(BITS)]
        half = job.cols // 2
        self.half = half
        self.mine = pl.ds(pl.multiple_of(job.col + self.bits[0] * half, 128), half)
        self.other = pl.ds(pl.multiple_of(job.col + (1 - self.bits[0]) * half, 128), half)
        self.all = pl.ds(job.row, job.rows)
        self.first = [0]
        count = job.rows
        for b in range(1, BITS):
            count //= 2
            self.first.append(self.first[-1] + self.bits[b] * count)

    def count(self, level):
        return self.job.rows // 2**level

    def span(self, first, count):
        return pl.ds(pl.multiple_of(first, 16), count)

    def out(self, first, count):
        return self.result.at[self.span(self.job.row + first, count), self.mine]

    def go(self, copy):
        copy.start()
        self.sent.append(copy)

    def stage(self, n):
        job = self.job
        if n == 0:
            pltpu.make_async_copy(
                self.source.at[:, self.all, self.mine], self.acc, self.local[0]
            ).start()
            self.go(
                to_rep(
                    self.source.at[:, self.all, self.other],
                    self.core,
                    self.send[0],
                    self.recv[0],
                    0,
                )
            )
        elif n == 1:
            landed(self.acc, self.local[0])
            landed(self.core, self.recv[0])
            for i in range(2):
                add_into(self.acc.at[i], self.core.at[i], job.rows)
            self.go(to_row(self.acc.at[1 - self.x], self.row, self.send[1], self.recv[1]))
        elif n == 2:
            landed(self.row, self.recv[1])
            add_into(self.acc.at[self.x], self.row, job.rows)
            self.give(1)
        elif n in (3, 4):
            self.take(n - 2)
            self.give(n - 1)
        elif n == 5:
            self.take(3)
            piece = self.acc.at[self.x, self.span(self.first[3], self.count(3))]
            place = self.out(self.first[3], self.count(3))
            pltpu.make_async_copy(piece, place, self.local[1]).start()
            self.go(to_rep(piece, place, self.send[5], self.recv[5], 3))
        elif n in (6, 7, 8):
            level = 9 - n
            if n == 6:
                landed(self.out(self.first[3], self.count(3)), self.local[1])
            self.landed_at(level)
            place = self.out(self.first[level - 1], self.count(level - 1))
            self.go(to_rep(place, place, self.send[n], self.recv[n], level - 1))
        else:
            landed(self.result.at[self.all, self.other], self.recv[8])
            for copy in self.sent:
                copy.wait_send()

    def give(self, level):
        count = self.count(level)
        first = self.first[level - 1] + (1 - self.bits[level]) * count
        self.go(
            to_rep(
                self.acc.at[self.x, self.span(first, count)],
                self.part[level - 1],
                self.send[level + 1],
                self.recv[level + 1],
                level,
            )
        )

    def take(self, level):
        landed(self.part[level - 1], self.recv[level + 1])
        count = self.count(level)
        rows = self.span(self.first[level], count)
        add_into(self.acc.at[self.x, rows], self.part[level - 1], count)

    def landed_at(self, level):
        count = self.count(level)
        first = self.first[level - 1] + (1 - self.bits[level]) * count
        landed(self.out(first, count), self.recv[8 - level])


def job_buffers(job):
    half = job.cols // 2
    return [
        pltpu.VMEM((2, job.rows, half), B16),
        pltpu.VMEM((2, job.rows, half), B16),
        pltpu.VMEM((job.rows, half), B16),
    ] + [pltpu.VMEM((job.rows // 2**b, half), B16) for b in range(1, BITS)]


JOB_BUFFERS = 6


class SmallRun:
    STAGES = BITS + 2

    def __init__(self, sums, terms, send, recv):
        self.sums, self.terms, self.send, self.recv = sums, terms, send, recv

    def copy(self, n):
        args = (self.sums.at[n], self.terms.at[n], self.send.at[n], self.recv.at[n])
        return to_row(*args) if n == BITS else to_rep(*args, n)

    def stage(self, n):
        if n > 0:
            landed(self.terms.at[n - 1], self.recv.at[n - 1])
            self.sums[n] = self.sums[n - 1] + self.terms[n - 1]
        if n <= BITS:
            self.copy(n).start()
        else:
            for i in range(BITS + 1):
                self.copy(i).wait_send()


def in_ticks(runs):
    last = max(i + run.STAGES for i, run in enumerate(runs))
    for tick in range(last):
        for n in range(max(run.STAGES for run in runs)):
            if 0 <= tick - n < len(runs) and n < runs[tick - n].STAGES:
                runs[tick - n].stage(n)
        yield


def jobs_of(shapes):
    jobs = []
    for i, (rows, cols) in enumerate(shapes):
        wide = cols // 2 if cols > 1024 else cols
        tall = rows // 2 if rows > 512 else rows
        for row in range(0, rows, tall):
            for col in range(0, cols, wide):
                jobs.append(Job(i, i, row, tall, col, wide))
    return jobs


SMALL_ROWS = 16


def tail_kernel(p, jobs, early, arrays, *refs):
    refs = list(refs)
    take = lambda n: [refs.pop(0) for _ in range(n)]
    sources = take(early)
    (dot_,) = take(1)
    recv, lines, of_ref, rl_ref, hidden, a1, dx1, dgc, dgf, wq, wk, wv = take(12)
    results = take(arrays)
    small, dh_ref = take(2)
    dout, dq, dkv, part, out, grads = take(6)
    late = take(arrays - early)
    small_sums, small_terms = take(2)
    back = take(7)
    rows_send, rows_recv, part_sem, got_sem, ret_send, ret_recv = take(6)
    small_send, small_recv = take(2)
    sems = take(3)
    sources = sources + late
    runs = [
        JobRun(job, sources[job.source], results[job.result], take(JOB_BUFFERS), sems, i)
        for i, job in enumerate(jobs)
    ]
    ready = sum(1 for job in jobs if job.source < early)
    runs.insert(ready, SmallRun(small_sums, small_terms, small_send, small_recv))

    me = lax.axis_index("rep")
    w = me % p.W
    unit = me // p.W
    group = unit % p.G
    mine = p.worker_of(me)
    slot = p.slot_of(me)
    barrier = pltpu.get_barrier_semaphore()
    for k in range(1, p.R):
        pl.semaphore_signal(
            barrier, inc=1, device_id={"rep": (me + k) % p.R}, device_id_type=MESH
        )
    x = lax.axis_index("shard")
    pl.semaphore_signal(barrier, inc=1, device_id={"shard": 1 - x}, device_id_type=MESH)
    pl.semaphore_wait(barrier, p.R)

    pipeline = in_ticks(runs)
    passed = 0

    def tick(count=1):
        nonlocal passed
        for _ in range(count):
            next(pipeline)
        passed += count

    for u in range(p.U):
        start_either(
            me, u * p.W + mine, dot_.at[u], dout.at[slot], rows_send.at[u], rows_recv.at[slot]
        )
    tick(2)
    for j in range(p.J):
        landed(dout.at[j], rows_recv.at[j])
    lines_at = lax.broadcasted_iota(jnp.int32, (SMALL_ROWS, D), 0)
    block = jnp.zeros((SMALL_ROWS, D), F32)
    for h in range(p.HG):
        sums = back_head(
            p,
            w,
            h * DH,
            line_of(p, lines, group * p.HG + h),
            recv,
            dout,
            of_ref,
            rl_ref.at[h],
            dq,
            dkv,
            *back,
        )
        sums = jnp.concatenate([sums, jnp.zeros((1, D - 2 * p.T), F32)], axis=1)
        block = jnp.where(lines_at == 3 + group * p.HG + h, sums, block)
        tick()

    def give(k, j):
        to = (w + k) % p.W
        return remote(
            dkv.at[p.source(j, to)],
            part.at[k - 1, j],
            part_sem.at[k - 1, j],
            got_sem.at[k - 1, j],
            me - w + to,
        )

    for j in range(p.J):
        for k in range(1, p.W):
            give(k, j).start()
    tick()
    for j in range(p.J):
        r = p.source(j, w)
        total = dkv[r].astype(F32)
        for k in range(1, p.W):
            landed(part.at[k - 1, j], got_sem.at[k - 1, j])
            total = total + part[k - 1, j].astype(F32)
        out[j, 0 : p.F, :] = dq[j]
        out[j, p.F : 3 * p.F, :] = total.astype(B16)
        start_either(me, r, out.at[j], grads.at[unit], ret_send.at[j], ret_recv.at[unit])
    tick(2)
    for u in range(p.U):
        landed(grads.at[u], ret_recv.at[u])
    dgain = last_products(p, hidden, grads, a1, lines, dx1, wq, wk, wv, dh_ref, *late)
    for i, row in enumerate((dgain, dgc[...], dgf[...])):
        block = jnp.where(lines_at == i, row, block)
    small_sums[0] = block
    assert passed <= ready
    for _ in pipeline:
        pass
    small[...] = small_sums[BITS + 1]
    for u in range(p.U):
        end_either(
            me, u * p.W + mine, dot_.at[u], dout.at[slot], rows_send.at[u], rows_recv.at[slot]
        )
    for j in range(p.J):
        r = p.source(j, w)
        end_either(me, r, out.at[j], grads.at[unit], ret_send.at[j], ret_recv.at[unit])
        for k in range(1, p.W):
            give(k, j).wait_send()


def tail_call(p, mats, dot_, held, hidden, collective):
    half = D // 2
    shapes = [m.shape[1:] for m in mats] + [(half, D)] * 3
    jobs = jobs_of(shapes)
    dma = pltpu.SemaphoreType.DMA
    others = max(p.W - 1, 1)
    scratch = [
        pltpu.VMEM((p.J, p.F, p.T), B16),
        pltpu.VMEM((p.J, p.F, p.T), B16),
        pltpu.VMEM((p.R, 2 * p.F, p.T), B16),
        pltpu.VMEM((others, p.J, 2 * p.F, p.T), B16),
        pltpu.VMEM((p.J, 3 * p.F, p.T), B16),
        pltpu.VMEM((p.U, 3 * p.F, p.T), B16),
    ]
    scratch += [pltpu.VMEM((2, half, D), B16)] * 3
    scratch += [
        pltpu.VMEM((BITS + 2, SMALL_ROWS, D), F32),
        pltpu.VMEM((BITS + 1, SMALL_ROWS, D), F32),
    ]
    scratch += back_scratch(p)
    scratch += [
        dma((p.U,)),
        dma((p.J,)),
        dma((others, p.J)),
        dma((others, p.J)),
        dma((p.J,)),
        dma((p.U,)),
        dma((BITS + 1,)),
        dma((BITS + 1,)),
        dma((len(jobs), 9)),
        dma((len(jobs), 9)),
        dma((len(jobs), 2)),
    ]
    for job in jobs:
        scratch += job_buffers(job)
    anywhere = pl.BlockSpec(memory_space=pl.ANY)
    near = pl.BlockSpec(memory_space=pltpu.VMEM)
    *sums, small, dh = pl.pallas_call(
        functools.partial(tail_kernel, p, jobs, len(mats), len(shapes)),
        out_shape=[jax.ShapeDtypeStruct(s, B16) for s in shapes]
        + [
            jax.ShapeDtypeStruct((SMALL_ROWS, D), F32),
            jax.ShapeDtypeStruct(hidden.shape, B16),
        ],
        in_specs=[anywhere] * (len(mats) + 1) + [near] * len(held),
        out_specs=[anywhere] * len(shapes) + [near] * 2,
        scratch_shapes=scratch,
        compiler_params=pltpu.CompilerParams(
            collective_id=collective, has_side_effects=True, vmem_limit_bytes=60 * 2**20
        ),
        name="tail",
    )(*mats, dot_, *held)
    return sums, small, dh


def widen_kernel(count, *refs):
    for i in range(count):
        refs[count + i][...] = refs[i][...].astype(F32)


def widen(mats):
    parts = 8
    blocks = [
        pl.BlockSpec((m.shape[0] // parts, m.shape[1]), lambda i: (i, 0)) for m in mats
    ]
    return pl.pallas_call(
        functools.partial(widen_kernel, len(mats)),
        grid=(parts,),
        out_shape=[jax.ShapeDtypeStruct(m.shape, F32) for m in mats],
        in_specs=blocks,
        out_specs=blocks,
        compiler_params=pltpu.CompilerParams(vmem_limit_bytes=40 * 2**20),
        name="widen",
    )(*mats)


class Fetch:
    def __init__(self, master, held, staged, out, first, rows, col, cols, stage, own, sems, index):
        self.x = lax.axis_index("shard")
        self.core = lax.axis_index("rep") % 2
        self.rows, self.staged = rows, staged
        self.master = master.at[pl.ds(first, rows), pl.ds(col, cols)]
        self.stage_ref = stage.at[pl.ds(0, rows), pl.ds(0, cols)]
        self.own = own
        self.out, self.first, self.col, self.cols = out, first, col, cols
        load, send, recv, relay_send, relay_recv, keep = sems
        self.load, self.keep = load.at[index], keep.at[index]
        self.send, self.recv = send.at[index], recv.at[index]
        self.relay_send, self.relay_recv = relay_send.at[index], relay_recv.at[index]

    def place(self, owner, core):
        half = self.rows // 2
        first = pl.multiple_of(self.first + core * half, 16)
        return self.out.at[owner, pl.ds(first, half), pl.ds(self.col, self.cols)]

    def read(self):
        pltpu.make_async_copy(self.master, self.stage_ref, self.load).start()

    def kept(self):
        return self.out.at[self.x, pl.ds(self.first, self.rows), pl.ds(self.col, self.cols)]

    def across(self):
        half = self.rows // 2
        first = pl.multiple_of(self.core * half, 16)
        return to_row(self.own.at[pl.ds(first, half)], self.place(self.x, self.core), self.send, self.recv)

    def start(self):
        landed(self.stage_ref, self.load)
        step = 32

        def body(i, carry):
            at = pl.ds(pl.multiple_of(i * step, step), step)
            self.own[at, :] = self.stage_ref[at, :].astype(B16)
            return carry

        lax.fori_loop(0, self.rows // step, body, 0)
        self.across().start()
        if self.staged:
            pltpu.make_async_copy(self.own, self.kept(), self.keep).start()

    def over(self):
        place = self.place(1 - self.x, self.core)
        return to_rep(place, place, self.relay_send, self.relay_recv, 0)

    def relay(self):
        landed(self.place(1 - self.x, self.core), self.recv)
        self.over().start()

    def finish(self):
        landed(self.place(1 - self.x, 1 - self.core), self.relay_recv)

    def end(self):
        self.across().wait_send()
        self.over().wait_send()
        if self.staged:
            landed(self.kept(), self.keep)


def small_block(p, gains, table, buckets, x):
    at = lax.broadcasted_iota(jnp.int32, (SMALL_ROWS, D), 0)
    block = jnp.zeros((SMALL_ROWS, D), F32)
    for i, gain in enumerate(gains):
        part = gain[...].astype(B16).astype(F32)
        none = jnp.zeros_like(part)
        row = jnp.where(
            x == 0,
            jnp.concatenate([part, none], axis=1),
            jnp.concatenate([none, part], axis=1),
        )
        block = jnp.where(at == i, row, block)
    held = table.shape[0]
    bucket = lax.broadcasted_iota(jnp.int32, (held, 2 * p.T), 0) + x * held
    onehot = (buckets[...] == bucket).astype(F32).astype(B16)
    lines = t_dot(table[...].astype(B16), onehot)
    lines = jnp.concatenate([lines, jnp.zeros((H, D - 2 * p.T), F32)], axis=1)
    lines = jnp.concatenate(
        [jnp.zeros((3, D), F32), lines, jnp.zeros((SMALL_ROWS - 3 - H, D), F32)], axis=0
    )
    return block + lines


def head_kernel(p, *refs):
    refs = list(refs)
    take = lambda n: [refs.pop(0) for _ in range(n)]
    masters = take(11)
    hidden, encoded, g1, g2, g3, table, buckets = take(7)
    mats = take(8)
    wide = take(3)
    small, a1, recv, of_ref, rl_ref, enc, kn, kt, vn, vt, ot = take(11)
    x1, x2, a2, qt2, of2, rl2 = take(6)
    send, o_ref, mine_small, their_small = take(4)
    stages = take(4)
    owns = take(6)
    att = take(3)
    fetch_sems = take(6)
    small_send, small_recv, enc_send, enc_recv = take(4)
    tok_send, relay_sem, tok_recv, back_send, back_recv = take(5)

    me = lax.axis_index("rep")
    x = lax.axis_index("shard")
    w = me % p.W
    unit = me // p.W
    group = unit % p.G
    mine = p.worker_of(me)
    bits = [(me // 2**b) % 2 for b in range(BITS)]

    half = D // 2
    jobs = []
    for i in range(8):
        jobs.append((masters[i], mats[i], 0, half, 0, D))
    for i, ref in enumerate(wide):
        rows, cols = ref.shape[1:]
        tall = rows // 2 if rows > 512 else rows
        part = cols // 2 if cols > 1024 else cols
        for row in range(0, rows, tall):
            for col in range(0, cols, part):
                jobs.append((masters[8 + i], ref, row, tall, col, part))
    fetches = []
    for i, (master, out, row, rows, col, cols) in enumerate(jobs):
        staged = i >= 8
        own = owns[i - 8] if staged else out.at[x]
        fetches.append(
            Fetch(
                master, out, staged, out, row, rows, col, cols, stages[i % 4], own, fetch_sems, i
            )
        )

    barrier = pltpu.get_barrier_semaphore()
    for k in range(1, p.R):
        pl.semaphore_signal(
            barrier, inc=1, device_id={"rep": (me + k) % p.R}, device_id_type=MESH
        )
    pl.semaphore_signal(barrier, inc=1, device_id={"shard": 1 - x}, device_id_type=MESH)
    for fetch in fetches[:4]:
        fetch.read()
    mine_small[...] = small_block(p, (g1, g2, g3), table, buckets, x)
    enc[:, bits[3], bits[2], bits[1], bits[0]] = encoded[...]
    pl.semaphore_wait(barrier, p.R)

    share = to_row(mine_small, their_small, small_send, small_recv)
    share.start()

    def enc_copy(n):
        at = (slice(None),) * (1 + n) + tuple(bits[b] for b in range(BITS - 1 - n, -1, -1))
        part = enc.at[at]
        return to_rep(part, part, enc_send.at[n], enc_recv.at[n], BITS - 1 - n)

    def enc_landed(n):
        b = [bits[i] for i in range(BITS - 1 - n, -1, -1)]
        b[0] = 1 - b[0]
        landed(enc.at[(slice(None),) * (1 + n) + tuple(b)], enc_recv.at[n])

    started = 0
    relayed = 0

    def begin(count=1):
        nonlocal started
        for _ in range(count):
            if started < len(fetches):
                fetches[started].start()
                if started + 4 < len(fetches):
                    fetches[started + 4].read()
                started += 1

    def pass_on(count=1):
        nonlocal relayed
        for _ in range(count):
            if relayed < started:
                fetches[relayed].relay()
                relayed += 1

    begin(3)
    enc_copy(0).start()
    landed(their_small, small_recv)
    small[...] = mine_small[...] + their_small[...]
    enc_landed(0)
    enc_copy(1).start()
    pass_on()
    begin()
    enc_landed(1)
    enc_copy(2).start()
    pass_on()
    begin()
    pass_on()
    for fetch in fetches[:3]:
        fetch.finish()
    project_kernel(p, hidden, small, *mats[:3], a1, send)
    for u in range(p.U):
        start_either(
            me, u * p.W + mine, send.at[u], recv.at[me], tok_send.at[u], tok_recv.at[me]
        )
    enc_landed(2)
    enc_copy(3).start()
    begin()
    pass_on(2)
    enc_landed(3)
    for fetch, natural, turned in ((fetches[3], kn, kt), (fetches[4], vn, vt)):
        fetch.finish()
        encode_one(enc, fetch.out, natural, turned)
        begin()
        pass_on()

    def relay(k, j):
        part = recv.at[p.source(j, w), pl.ds(p.F, 2 * p.F)]
        to = me - w + (w + k) % p.W
        return remote(part, part, relay_sem.at[k - 1, j], tok_recv.at[p.source(j, w)], to)

    for j in range(p.J):
        landed(recv.at[p.source(j, w)], tok_recv.at[p.source(j, w)])
        for k in range(1, p.W):
            relay(k, j).start()
    begin()
    pass_on()
    for k in range(1, p.W):
        for j in range(p.J):
            r = p.source(j, (w + k) % p.W)
            landed(recv.at[r, pl.ds(p.F, 2 * p.F)], tok_recv.at[r])
    for h in range(p.HG):
        line = line_of(p, small, group * p.HG + h)
        attend_head(p, w, h * DH, line, recv, o_ref, of_ref, rl_ref.at[h], *att)
        begin()
        pass_on()
    for j in range(p.J):
        r = p.source(j, w)
        start_either(me, r, o_ref.at[j], ot.at[unit], back_send.at[j], back_recv.at[unit])
    begin()
    pass_on(2)
    for u in range(p.U):
        landed(ot.at[u], back_recv.at[u])
    for fetch in fetches[5:8]:
        fetch.finish()

    def pause():
        begin()
        pass_on()

    cross_kernel(
        p.S, hidden, ot, mats[5], small, mats[6], mats[7], kn, vt, x1, x2, a2, qt2, of2, rl2, pause
    )
    begin(len(fetches))
    pass_on(len(fetches))
    for fetch in fetches[8:]:
        fetch.finish()
    for fetch in fetches:
        fetch.end()
    share.wait_send()
    for n in range(BITS):
        enc_copy(n).wait_send()
    for u in range(p.U):
        end_either(
            me, u * p.W + mine, send.at[u], recv.at[me], tok_send.at[u], tok_recv.at[me]
        )
    for j in range(p.J):
        r = p.source(j, w)
        end_either(me, r, o_ref.at[j], ot.at[unit], back_send.at[j], back_recv.at[unit])
        for k in range(1, p.W):
            relay(k, j).wait_send()


def head_call(p, masters, hidden, encoded, gains, table, buckets, collective):
    half, tokens = D // 2, p.S * p.T
    piece = encoded.shape[1]
    enc_rows = p.S * piece * p.R
    wides = [m.shape for m in masters[8:]]
    near = pl.BlockSpec(memory_space=pltpu.VMEM)
    anywhere = pl.BlockSpec(memory_space=pl.ANY)
    outs = [((2, half, D), B16)] * 8 + [((2, *s), B16) for s in wides]
    outs += [
        ((SMALL_ROWS, D), F32),
        ((tokens, D), B16),
        ((p.R, 3 * p.F, p.T), B16),
        ((p.J, p.F, p.T), F32),
        ((p.HG, p.NP, 1, 2 * p.T), F32),
        ((p.S,) + (2,) * BITS + (piece, D), B16),
        ((H, enc_rows, DH), B16),
        ((H, DH + ONES, enc_rows), B16),
        ((H, enc_rows, DH), B16),
        ((H, DH + ONES, enc_rows), B16),
        ((p.U, p.F, p.T), B16),
        ((tokens, D), F32),
        ((tokens, D), F32),
        ((tokens, D), B16),
        ((p.S, D, p.T), B16),
        ((p.S, D, p.T), F32),
        ((p.S, H, 1, p.T), F32),
    ]
    parts = [(half, D)] * 8
    for rows, cols in wides:
        tall = rows // 2 if rows > 512 else rows
        part = cols // 2 if cols > 1024 else cols
        parts += [(tall, part)] * ((rows // tall) * (cols // part))
    count = len(parts)
    dma = pltpu.SemaphoreType.DMA
    scratch = [
        pltpu.VMEM((p.U, 3 * p.F, p.T), B16),
        pltpu.VMEM((p.J, p.F, p.T), B16),
        pltpu.VMEM((SMALL_ROWS, D), F32),
        pltpu.VMEM((SMALL_ROWS, D), F32),
    ]
    tallest = max(r for r, _ in parts)
    widest = max(c for _, c in parts)
    scratch += [pltpu.VMEM((tallest, widest), F32)] * 4
    scratch += [pltpu.VMEM(s, B16) for s in parts[8:]]
    scratch += attend_scratch(p)
    scratch += [dma((count,))] * 6
    scratch += [dma, dma, dma((BITS,)), dma((BITS,))]
    scratch += [
        dma((p.U,)),
        dma((max(p.W - 1, 1), p.J)),
        dma((p.R,)),
        dma((p.J,)),
        dma((p.U,)),
    ]
    return pl.pallas_call(
        functools.partial(head_kernel, p),
        out_shape=[jax.ShapeDtypeStruct(s, t) for s, t in outs],
        in_specs=[anywhere] * 11 + [near] * 7,
        out_specs=[near] * 8 + [anywhere] * 3 + [near] * 17,
        scratch_shapes=scratch,
        compiler_params=pltpu.CompilerParams(
            collective_id=collective, has_side_effects=True, vmem_limit_bytes=62 * 2**20
        ),
        name="head",
    )(*masters, hidden, encoded, *gains, table, buckets)


def local(
    hidden,
    encoded,
    out_grad,
    self_query,
    self_key,
    self_value,
    self_out,
    cross_query,
    cross_key,
    cross_value,
    cross_out,
    ffn_gate,
    ffn_up,
    ffn_down,
    gain_self,
    gain_cross,
    gain_ffn,
    bias_table,
    buckets,
):
    seqs, toks = hidden.shape[0], hidden.shape[1]
    p = Plan(seqs, toks, lax.axis_size("rep"))
    tokens = seqs * toks
    ff = ffn_gate.shape[1]
    enc_rows = seqs * encoded.shape[1] * p.R
    dma = pltpu.SemaphoreType.DMA

    n_shard = lax.axis_size("shard")
    mine = lax.axis_index("shard")
    part = gain_self.shape[0]
    near = buckets[: 2 * toks]
    onehot = (near[:, None] == jnp.arange(NB, dtype=jnp.int32)[None, :]).astype(B16)
    paired = n_shard == 2 and p.R == 2**BITS and 3 + H <= SMALL_ROWS
    if paired:
        masters = (
            self_query,
            self_key,
            self_value,
            cross_key,
            cross_value,
            self_out,
            cross_query,
            cross_out,
            ffn_gate,
            ffn_up,
            ffn_down,
        )
        gains = [g.reshape(1, part) for g in (gain_self, gain_cross, gain_ffn)]
        got = head_call(
            p, masters, hidden, encoded, gains, bias_table, near.reshape(1, -1), 0
        )
        wq, wk, wv, wck, wcv, wo, wcq, wco = got[:8]
        wg, wu, wd = [g.reshape(-1, g.shape[-1]) for g in got[8:11]]
        small, a1, recv, of, rl, enc, ckn, ckt, cvn, cvt, ot = got[11:22]
        x1, x2, a2, qt2, of2, rl2 = got[22:]
    else:
        lot = jnp.concatenate(
            [
                jnp.stack([gain_self, gain_cross, gain_ffn]).reshape(-1),
                bias_table.reshape(-1),
            ]
        ).astype(B16)
        lot = lax.all_gather(lot, "shard", axis=0)
        gains = [
            lot[:, i * part : (i + 1) * part].reshape(1, D).astype(F32) for i in range(3)
        ]
        table = lot[:, 3 * part :].reshape(NB, H)
        lines = jnp.einsum("lb,bh->hl", onehot, table, preferred_element_type=F32)
        lines = jnp.pad(lines, ((0, SMALL_ROWS - 3 - H), (0, D - 2 * toks)))
        small = jnp.concatenate([*gains, lines], axis=0)

        wq, wk, wv, wo, wcq, wck, wcv, wco, wg, wu, wd = [
            gather_rows(m.astype(B16))
            for m in (
                self_query,
                self_key,
                self_value,
                self_out,
                cross_query,
                cross_key,
                cross_value,
                cross_out,
                ffn_gate,
                ffn_up,
                ffn_down,
            )
        ]
        enc = lax.all_gather(encoded, "rep", axis=1, tiled=True).reshape(enc_rows, D)

        a1, send = plain_call(
            functools.partial(project_kernel, p),
            [((tokens, D), B16), ((p.U, 3 * p.F, toks), B16)],
            (hidden, small, wq, wk, wv),
            "project",
        )
        recv = comm_call(
            functools.partial(scatter_tokens, p),
            (p.R, 3 * p.F, toks),
            (send,),
            [dma((p.U,)), dma((max(p.W - 1, 1), p.J)), dma((p.R,))],
            0,
            "scatter_tokens",
        )
        ckn, ckt, cvn, cvt = plain_call(
            encode_kernel,
            [
                ((H, enc_rows, DH), B16),
                ((H, DH + ONES, enc_rows), B16),
                ((H, enc_rows, DH), B16),
                ((H, DH + ONES, enc_rows), B16),
            ],
            (enc, wck, wcv),
            "encode",
        )
        o, of, rl = pl.pallas_call(
            functools.partial(attend_kernel, p),
            grid=(p.HG,),
            out_shape=[
                jax.ShapeDtypeStruct((p.J, p.F, toks), B16),
                jax.ShapeDtypeStruct((p.J, p.F, toks), F32),
                jax.ShapeDtypeStruct((p.HG, p.NP, 1, 2 * toks), F32),
            ],
            in_specs=[whole((p.R, 3 * p.F, toks)), whole((SMALL_ROWS, D))],
            out_specs=[
                whole((p.J, p.F, toks)),
                whole((p.J, p.F, toks)),
                whole((p.HG, p.NP, 1, 2 * toks)),
            ],
            scratch_shapes=attend_scratch(p),
            compiler_params=pltpu.CompilerParams(vmem_limit_bytes=56 * 2**20),
            name="attend",
        )(recv, small)
        ot = comm_call(
            functools.partial(return_tokens, p),
            (p.U, p.F, toks),
            (o,),
            [dma((p.J,)), dma((p.U,))],
            1,
            "return_tokens",
        )

        x1, x2, a2, qt2, of2, rl2 = plain_call(
            functools.partial(cross_kernel, seqs),
            [
                ((tokens, D), F32),
                ((tokens, D), F32),
                ((tokens, D), B16),
                ((seqs, D, toks), B16),
                ((seqs, D, toks), F32),
                ((seqs, H, 1, toks), F32),
            ],
            (hidden, ot, wo, small, wcq, wco, ckn, cvt),
            "cross",
        )

    chunk = min(512, ff)
    const = lambda s: pl.BlockSpec(s, lambda i: (0, 0))
    output, dx2, dg_ffn, dwg, dwu, dwd = pl.pallas_call(
        ffn_kernel,
        grid=(ff // chunk,),
        out_shape=[
            jax.ShapeDtypeStruct((tokens, D), B16),
            jax.ShapeDtypeStruct((tokens, D), F32),
            jax.ShapeDtypeStruct((1, D), F32),
            jax.ShapeDtypeStruct((D, ff), B16),
            jax.ShapeDtypeStruct((D, ff), B16),
            jax.ShapeDtypeStruct((ff, D), B16),
        ],
        in_specs=[
            const((tokens, D)),
            const((tokens, D)),
            const((SMALL_ROWS, D)),
            pl.BlockSpec((D, chunk), lambda i: (0, i)),
            pl.BlockSpec((D, chunk), lambda i: (0, i)),
            pl.BlockSpec((chunk, D), lambda i: (i, 0)),
        ],
        out_specs=[
            const((tokens, D)),
            const((tokens, D)),
            const((1, D)),
            pl.BlockSpec((D, chunk), lambda i: (0, i)),
            pl.BlockSpec((D, chunk), lambda i: (0, i)),
            pl.BlockSpec((chunk, D), lambda i: (i, 0)),
        ],
        scratch_shapes=[
            pltpu.VMEM((tokens, D), B16),
            pltpu.VMEM((tokens, D), F32),
            pltpu.VMEM((tokens, D), F32),
        ],
        compiler_params=pltpu.CompilerParams(vmem_limit_bytes=56 * 2**20),
        name="ffn",
    )(x2, out_grad.reshape(tokens, D), small, wg, wu, wd)

    dx1, dg_cross, dot_, denc, dwco, dwcq, dwck, dwcv, dwo = plain_call(
        functools.partial(cross_back_kernel, seqs, p.G),
        [
            ((tokens, D), F32),
            ((1, D), F32),
            ((p.U, p.F, toks), B16),
            ((enc_rows, D), B16),
        ]
        + [((D, D), B16)] * 5,
        (dx2, x1, a2, small, qt2, of2, rl2, ckn, ckt, cvn, enc, wco, wcq, wck, wcv, wo, ot),
        "cross_back",
        scratch=[
            pltpu.VMEM((seqs, D, toks), B16),
            pltpu.VMEM((seqs, D, toks), B16),
            pltpu.VMEM((enc_rows, D), B16),
            pltpu.VMEM((enc_rows, D), B16),
        ],
    )
    encoded_grad = lax.psum_scatter(
        denc.reshape(seqs, enc_rows // seqs, D), "rep", scatter_dimension=1, tiled=True
    )
    if paired:
        early = [
            g.reshape(2, g.shape[0] // 2, g.shape[1])
            for g in (dwd, dwg, dwu, dwo, dwcq, dwck, dwcv, dwco)
        ]
        held = (recv, small, of, rl, hidden, a1, dx1, dg_cross, dg_ffn, wq, wk, wv)
        sums, block, hidden_grad = tail_call(p, early, dot_, held, hidden, 2)
        dwd, dwg, dwu, dwo, dwcq, dwck, dwcv, dwco, dwq, dwk, dwv = widen(sums)
        mats = [dwq, dwk, dwv, dwo, dwcq, dwck, dwcv, dwco, dwg, dwu, dwd]
        dgains = lax.dynamic_slice(block, (0, mine * part), (3, part))
        by_bucket = jnp.einsum(
            "hl,lb->bh",
            block[3 : 3 + H, : 2 * toks],
            onehot.astype(F32),
            precision=lax.Precision.HIGHEST,
        )
        dtab = lax.dynamic_slice(
            by_bucket, (mine * bias_table.shape[0], 0), bias_table.shape
        )
    else:
        dout = comm_call(
            functools.partial(scatter_rows, p),
            (p.J, p.F, toks),
            (dot_,),
            [dma((p.U,)), dma((p.J,))],
            2,
            "scatter_rows",
        )
        dq, dkv, line = pl.pallas_call(
            functools.partial(attend_back_kernel, p),
            grid=(p.HG,),
            out_shape=[
                jax.ShapeDtypeStruct((p.J, p.F, toks), B16),
                jax.ShapeDtypeStruct((p.R, 2 * p.F, toks), B16),
                jax.ShapeDtypeStruct((p.HG, 1, 2 * toks), F32),
            ],
            in_specs=[
                whole((p.R, 3 * p.F, toks)),
                whole((SMALL_ROWS, D)),
                whole((p.J, p.F, toks)),
                whole((p.J, p.F, toks)),
                whole((p.HG, p.NP, 1, 2 * toks)),
            ],
            out_specs=[
                whole((p.J, p.F, toks)),
                whole((p.R, 2 * p.F, toks)),
                whole((p.HG, 1, 2 * toks)),
            ],
            scratch_shapes=back_scratch(p),
            compiler_params=pltpu.CompilerParams(vmem_limit_bytes=56 * 2**20),
            name="attend_back",
        )(recv, small, dout, of, rl)
        grads = comm_call(
            functools.partial(return_grads, p),
            (p.U, 3 * p.F, toks),
            (dq, dkv),
            [
                pltpu.VMEM((max(p.W - 1, 1), p.J, 2 * p.F, toks), B16),
                pltpu.VMEM((p.J, 3 * p.F, toks), B16),
                dma((p.J,)),
                dma((max(p.W - 1, 1), p.J)),
                dma((max(p.W - 1, 1), p.J)),
                dma((p.U,)),
            ],
            3,
            "return_grads",
            space=pltpu.VMEM,
        )
        hidden_grad, dg_self, dwq, dwk, dwv = plain_call(
            functools.partial(last_kernel, p),
            [(hidden.shape, B16), ((1, D), F32)] + [((D, D), B16)] * 3,
            (hidden, grads, a1, small, dx1, wq, wk, wv),
            "last",
        )

        group = (lax.axis_index("rep") // p.W) % p.G
        by_bucket = jnp.einsum(
            "hl,lb->bh", line[:, 0, :], onehot.astype(F32), precision=lax.Precision.HIGHEST
        )
        dtable = lax.dynamic_update_slice(jnp.zeros((NB, H), F32), by_bucket, (0, group * p.HG))

        mats = reduce_grads([dwq, dwk, dwv, dwo, dwcq, dwck, dwcv, dwco, dwg, dwu, dwd])
        lot = jnp.concatenate(
            [g.reshape(n_shard, part) for g in (dg_self, dg_cross, dg_ffn)]
            + [dtable.reshape(n_shard, -1)],
            axis=1,
        )
        size = lot.shape[1]
        lot = lax.psum(lot, ("shard", "rep"))
        lot = lax.dynamic_slice(lot, (mine, 0), (1, size))[0]
        dgains = [lot[i * part : (i + 1) * part] for i in range(3)]
        dtab = lot[3 * part :].reshape(bias_table.shape)
    return (
        output.reshape(hidden.shape),
        hidden_grad,
        encoded_grad,
        *mats,
        *dgains,
        dtab,
    )


def solution(mesh):
    tok = P("shard", "rep", None)
    mat = P("shard", None)
    in_specs = (tok,) * 3 + (mat,) * 11 + (P("shard"),) * 3 + (mat, P())
    out_specs = (tok,) * 3 + (mat,) * 11 + (P("shard"),) * 3 + (mat,)
    return jax.shard_map(local, mesh=mesh, in_specs=in_specs, out_specs=out_specs, check_vma=False)
```

```python
import functools

import jax
import jax.numpy as jnp
from jax import lax
from jax.experimental import pallas as pl
from jax.experimental.pallas import tpu as pltpu
from jax.sharding import PartitionSpec as P

D = 768
H = 12
DH = 64
NB = 32
EPS = 1e-06
F32 = jnp.float32
B16 = jnp.bfloat16
ONES = 16
HIDE = -1e30
MESH = pl.DeviceIdType.MESH
GELU_A = 0.7978845608028654
GELU_B = 0.044715


def dot(a, b):
    return lax.dot_general(a, b, (((1,), (0,)), ((), ())), preferred_element_type=F32)


def dot_t(a, b):
    return lax.dot_general(a, b, (((1,), (1,)), ((), ())), preferred_element_type=F32)


def t_dot(a, b):
    return lax.dot_general(a, b, (((0,), (0,)), ((), ())), preferred_element_type=F32)


def mat(ref):
    return ref[...].reshape(-1, ref.shape[-1])


def scale_of(v):
    return lax.rsqrt(jnp.mean(v * v, axis=-1, keepdims=True) + EPS)


def norm_back(v, gain, grad):
    r = scale_of(v)
    n = v * r
    c = grad * gain
    dv = r * (c - n * jnp.mean(c * n, axis=-1, keepdims=True))
    return dv, jnp.sum(grad * n, axis=0, keepdims=True)


def whole(shape):
    return pl.BlockSpec(shape, lambda *_: (0,) * len(shape))


def plain_call(kernel, outs, args, name, scratch=(), vmem=60):
    return pl.pallas_call(
        kernel,
        out_shape=[jax.ShapeDtypeStruct(s, t) for s, t in outs],
        in_specs=[pl.BlockSpec(memory_space=pltpu.VMEM)] * len(args),
        out_specs=[pl.BlockSpec(memory_space=pltpu.VMEM)] * len(outs),
        scratch_shapes=list(scratch),
        compiler_params=pltpu.CompilerParams(vmem_limit_bytes=vmem * 2**20),
        name=name,
    )(*args)


class Plan:
    def __init__(self, seqs, toks, rows):
        self.S, self.T, self.R = seqs, toks, rows
        groups = 1
        for g in range(1, H + 1):
            if H % g == 0 and seqs * g <= rows and rows % (2 * seqs * g) == 0:
                groups = g
        self.G = groups
        self.HG = H // groups
        self.F = self.HG * DH
        self.U = seqs * groups
        self.W = rows // self.U
        self.J = rows // self.W
        self.NP = self.J // 2
        self.CK = 2 * self.W * toks
        self.L = rows * toks

    def worker_of(self, r):
        m = r % (2 * self.W)
        late = m // self.W
        return m * (1 - late) + (2 * self.W - 1 - m) * late

    def slot_of(self, r):
        return 2 * (r // (2 * self.W)) + (r % (2 * self.W)) // self.W

    def source(self, j, w):
        return self.source_in(j // 2, j % 2, w)

    def source_in(self, pair, late, w):
        if late:
            return 2 * self.W * pair + 2 * self.W - 1 - w
        return 2 * self.W * pair + w


def enter(rows):
    me = lax.axis_index("rep")
    barrier = pltpu.get_barrier_semaphore()
    for k in range(1, rows):
        pl.semaphore_signal(
            barrier, inc=1, device_id={"rep": (me + k) % rows}, device_id_type=MESH
        )
    pl.semaphore_wait(barrier, rows - 1)
    return me


def remote(src, dst, send, recv, to):
    return pltpu.make_async_remote_copy(
        src_ref=src,
        dst_ref=dst,
        send_sem=send,
        recv_sem=recv,
        device_id={"rep": to},
        device_id_type=MESH,
    )


def start_either(me, to, src, dst, send, recv):
    @pl.when(to == me)
    def _():
        pltpu.make_async_copy(src, dst, recv).start()

    @pl.when(to != me)
    def _():
        remote(src, dst, send, recv, to).start()


def end_either(me, to, src, dst, send, recv):
    @pl.when(to != me)
    def _():
        remote(src, dst, send, recv, to).wait_send()


def landed(ref, sem):
    pltpu.make_async_copy(ref, ref, sem).wait()


def scatter_tokens(plan, send, recv, send_sem, relay_sem, recv_sem):
    p = plan
    me = enter(p.R)
    w = me % p.W
    mine = p.worker_of(me)
    for u in range(p.U):
        start_either(me, u * p.W + mine, send.at[u], recv.at[me], send_sem.at[u], recv_sem.at[me])
    for j in range(p.J):
        r = p.source(j, w)
        landed(recv.at[r], recv_sem.at[r])
        for k in range(1, p.W):
            part = recv.at[r, pl.ds(p.F, 2 * p.F)]
            remote(
                part, part, relay_sem.at[k - 1, j], recv_sem.at[r], me - w + (w + k) % p.W
            ).start()
    for k in range(1, p.W):
        for j in range(p.J):
            r = p.source(j, (w + k) % p.W)
            landed(recv.at[r, pl.ds(p.F, 2 * p.F)], recv_sem.at[r])
    for u in range(p.U):
        end_either(me, u * p.W + mine, send.at[u], recv.at[me], send_sem.at[u], recv_sem.at[me])
    for k in range(1, p.W):
        for j in range(p.J):
            r = p.source(j, w)
            part = recv.at[r, pl.ds(p.F, 2 * p.F)]
            remote(
                part, part, relay_sem.at[k - 1, j], recv_sem.at[r], me - w + (w + k) % p.W
            ).wait_send()


def return_tokens(plan, send, recv, send_sem, recv_sem):
    p = plan
    me = enter(p.R)
    w = me % p.W
    unit = me // p.W
    for j in range(p.J):
        r = p.source(j, w)
        start_either(me, r, send.at[j], recv.at[unit], send_sem.at[j], recv_sem.at[unit])
    for u in range(p.U):
        landed(recv.at[u], recv_sem.at[u])
    for j in range(p.J):
        r = p.source(j, w)
        end_either(me, r, send.at[j], recv.at[unit], send_sem.at[j], recv_sem.at[unit])


def scatter_rows(plan, send, recv, send_sem, recv_sem):
    p = plan
    me = enter(p.R)
    mine = p.worker_of(me)
    slot = p.slot_of(me)
    for u in range(p.U):
        start_either(
            me, u * p.W + mine, send.at[u], recv.at[slot], send_sem.at[u], recv_sem.at[slot]
        )
    for j in range(p.J):
        landed(recv.at[j], recv_sem.at[j])
    for u in range(p.U):
        end_either(
            me, u * p.W + mine, send.at[u], recv.at[slot], send_sem.at[u], recv_sem.at[slot]
        )


def return_grads(plan, dq, dkv, recv, buf, out, send_sem, part_sem, got_sem, recv_sem):
    p = plan
    me = enter(p.R)
    w = me % p.W
    unit = me // p.W

    def give(k, j):
        to = (w + k) % p.W
        r = p.source(j, to)
        return remote(
            dkv.at[r],
            buf.at[k - 1, j],
            part_sem.at[k - 1, j],
            got_sem.at[k - 1, j],
            me - w + to,
        )

    for j in range(p.J):
        for k in range(1, p.W):
            give(k, j).start()
    for j in range(p.J):
        r = p.source(j, w)
        total = dkv[r].astype(F32)
        for k in range(1, p.W):
            landed(buf.at[k - 1, j], got_sem.at[k - 1, j])
            total = total + buf[k - 1, j].astype(F32)
        out[j, 0 : p.F, :] = dq[j]
        out[j, p.F : 3 * p.F, :] = total.astype(B16)
        start_either(me, r, out.at[j], recv.at[unit], send_sem.at[j], recv_sem.at[unit])
    for u in range(p.U):
        landed(recv.at[u], recv_sem.at[u])
    for j in range(p.J):
        r = p.source(j, w)
        end_either(me, r, out.at[j], recv.at[unit], send_sem.at[j], recv_sem.at[unit])
        for k in range(1, p.W):
            give(k, j).wait_send()


def comm_call(kernel, out, args, scratch, collective, name, space=pl.ANY):
    return pl.pallas_call(
        kernel,
        out_shape=jax.ShapeDtypeStruct(out, B16),
        in_specs=[pl.BlockSpec(memory_space=space)] * len(args),
        out_specs=pl.BlockSpec(memory_space=space),
        scratch_shapes=list(scratch),
        compiler_params=pltpu.CompilerParams(
            collective_id=collective, has_side_effects=True, vmem_limit_bytes=40 * 2**20
        ),
        name=name,
    )(*args)


def project_kernel(plan, hidden, gain, wq, wk, wv, a1_ref, send):
    p = plan
    x = hidden[...].reshape(p.S * p.T, D).astype(F32)
    a1 = (x * scale_of(x) * gain[0:1, :]).astype(B16)
    a1_ref[...] = a1
    for n, weight in enumerate((wq, wk, wv)):
        rows = dot(a1, mat(weight))
        for s in range(p.S):
            turned = jnp.transpose(rows[s * p.T : (s + 1) * p.T]).astype(B16)
            for g in range(p.G):
                send[s * p.G + g, n * p.F : (n + 1) * p.F, :] = turned[g * p.F : (g + 1) * p.F]


def bias_tiles(plan, w, line, tiles):
    p = plan
    far = line[:, 2 * p.T - 1 : 2 * p.T]
    near = pltpu.roll(jnp.broadcast_to(line, (p.T, 2 * p.T)), 0, 1, stride=1, stride_axis=0)
    key = lax.broadcasted_iota(jnp.int32, (p.T, p.T), 0)
    query = lax.broadcasted_iota(jnp.int32, (p.T, p.T), 1)
    same = jnp.where(query >= key, near[:, : p.T], HIDE)
    next_ = near[:, p.T :]
    farb = jnp.broadcast_to(far, (p.T, p.T))
    tiles[0] = jnp.broadcast_to(far, (p.CK, 2 * p.T))
    for a in range(2):
        ahead = w if a == 0 else 2 * p.W - 1 - w
        for b in range(2 * p.W):
            diff = ahead - b
            tile = jnp.where(
                diff == 0, same, jnp.where(diff == 1, next_, jnp.where(diff < 0, HIDE, farb))
            )
            tiles[2, b * p.T : (b + 1) * p.T, a * p.T : (a + 1) * p.T] = tile
            back = diff + 2 * p.W
            tiles[1, b * p.T : (b + 1) * p.T, a * p.T : (a + 1) * p.T] = jnp.where(
                back == 1, next_, farb
            )


def block_pair(plan, ref, pair, w, row, count):
    p = plan
    return jnp.concatenate(
        [
            ref[p.source_in(pair, 0, w), pl.ds(row, count), :],
            ref[p.source_in(pair, 1, w), pl.ds(row, count), :],
        ],
        axis=1,
    )


def line_of(p, block, head):
    return block[pl.ds(3 + head, 1), 0 : 2 * p.T]


def attend_head(p, w, row, line, recv, o_ref, of_ref, rl, kn, vt, tiles):
    bias_tiles(p, w, line, tiles)
    for r in range(p.R):
        kn[r * p.T : (r + 1) * p.T, :] = jnp.transpose(
            recv[r, pl.ds(p.F + row, DH), :].astype(F32)
        ).astype(B16)
        vt[0:DH, r * p.T : (r + 1) * p.T] = recv[r, pl.ds(2 * p.F + row, DH), :]
    vt[DH : DH + ONES, :] = jnp.ones((ONES, p.L), B16)

    def one_pair(pair, carry):
        qt = block_pair(p, recv, pair, w, row, DH)

        def step(i, acc):
            start = pl.multiple_of(i * p.CK, p.CK)
            e = jnp.exp(dot(kn[pl.ds(start, p.CK), :], qt) + tiles[jnp.maximum(i - pair + 2, 0)])
            return acc + dot(vt[:, pl.ds(start, p.CK)], e.astype(B16))

        acc = lax.fori_loop(0, pair + 1, step, jnp.zeros((DH + ONES, 2 * p.T), F32))
        scale = 1.0 / acc[DH : DH + 1]
        of = acc[:DH] * scale
        rl[pair] = scale
        for a in range(2):
            part = of[:, a * p.T : (a + 1) * p.T]
            of_ref[2 * pair + a, pl.ds(row, DH), :] = part
            o_ref[2 * pair + a, pl.ds(row, DH), :] = part.astype(B16)
        return carry

    lax.fori_loop(0, p.NP, one_pair, 0)


def attend_scratch(p):
    return [
        pltpu.VMEM((p.L, DH), B16),
        pltpu.VMEM((DH + ONES, p.L), B16),
        pltpu.VMEM((3, p.CK, 2 * p.T), F32),
    ]


def attend_kernel(plan, recv, block, o_ref, of_ref, rl_ref, *scratch):
    p = plan
    me = lax.axis_index("rep")
    w = me % p.W
    group = (me // p.W) % p.G
    h = pl.program_id(0)
    row = pl.multiple_of(h * DH, DH)
    line = line_of(p, block, group * p.HG + h)
    attend_head(p, w, row, line, recv, o_ref, of_ref, rl_ref.at[h], *scratch)


def back_head(
    p, w, row, line, recv, dout, of_ref, rl, dq_ref, dkv_ref, kn, vn, kt, dk, dv, tiles, near
):
    bias_tiles(p, w, line, tiles)
    for r in range(p.R):
        kn[r * p.T : (r + 1) * p.T, :] = jnp.transpose(
            recv[r, pl.ds(p.F + row, DH), :].astype(F32)
        ).astype(B16)
        vn[r * p.T : (r + 1) * p.T, :] = jnp.transpose(
            recv[r, pl.ds(2 * p.F + row, DH), :].astype(F32)
        ).astype(B16)
        kt[0:DH, r * p.T : (r + 1) * p.T] = recv[r, pl.ds(p.F + row, DH), :]
    kt[DH : DH + ONES, :] = jnp.ones((ONES, p.L), B16)
    dk[...] = jnp.zeros_like(dk)
    dv[...] = jnp.zeros_like(dv)
    near[...] = jnp.zeros_like(near)

    def one_pair(pair, total):
        qt = block_pair(p, recv, pair, w, row, DH)
        dot_rows = jnp.concatenate(
            [dout[2 * pair + a, pl.ds(row, DH), :] for a in range(2)], axis=1
        )
        of = jnp.concatenate([of_ref[2 * pair + a, pl.ds(row, DH), :] for a in range(2)], axis=1)
        delta = jnp.sum(dot_rows.astype(F32) * of, axis=0, keepdims=True)
        scale = rl[pair]
        qn = jnp.transpose(qt.astype(F32)).astype(B16)
        don = jnp.transpose(dot_rows.astype(F32)).astype(B16)

        def step(i, acc):
            start = pl.multiple_of(i * p.CK, p.CK)
            kind = jnp.maximum(i - pair + 2, 0)
            keys = pl.ds(start, p.CK)
            prob = jnp.exp(dot(kn[keys, :], qt) + tiles[kind]) * scale
            ds = (prob * (dot(vn[keys, :], dot_rows) - delta)).astype(B16)
            near[kind] += ds.astype(F32)
            dk[keys, :] += dot(ds, qn)
            dv[keys, :] += dot(prob.astype(B16), don)
            return acc + dot(kt[:, keys], ds)

        acc = lax.fori_loop(0, pair + 1, step, jnp.zeros((DH + ONES, 2 * p.T), F32))
        for a in range(2):
            dq_ref[2 * pair + a, pl.ds(row, DH), :] = acc[:DH, a * p.T : (a + 1) * p.T].astype(B16)
        return total + acc[DH : DH + 1]

    total = lax.fori_loop(0, p.NP, one_pair, jnp.zeros((1, 2 * p.T), F32))
    for r in range(p.R):
        dkv_ref[r, pl.ds(row, DH), :] = jnp.transpose(dk[r * p.T : (r + 1) * p.T, :]).astype(B16)
        dkv_ref[r, pl.ds(p.F + row, DH), :] = jnp.transpose(dv[r * p.T : (r + 1) * p.T, :]).astype(
            B16
        )
    same = jnp.zeros((p.T, p.T), F32)
    next_ = jnp.zeros((p.T, p.T), F32)
    for a in range(2):
        ahead = w if a == 0 else 2 * p.W - 1 - w
        for b in range(2 * p.W):
            diff = ahead - b
            spot = (slice(b * p.T, (b + 1) * p.T), slice(a * p.T, (a + 1) * p.T))
            tile = near[(2, *spot)]
            same = same + jnp.where(diff == 0, tile, 0.0)
            next_ = next_ + jnp.where(diff == 1, tile, 0.0)
            next_ = next_ + jnp.where(diff + 2 * p.W == 1, near[(1, *spot)], 0.0)
    both = jnp.concatenate([same, next_], axis=1)
    key = lax.broadcasted_iota(jnp.int32, (p.T, p.T), 0)
    other = lax.broadcasted_iota(jnp.int32, (p.T, p.T), 1)
    swap = (key + other == p.T - 1).astype(F32)
    turned = lax.dot_general(
        swap,
        both,
        (((1,), (0,)), ((), ())),
        precision=lax.Precision.HIGHEST,
        preferred_element_type=F32,
    )
    turned = pltpu.roll(turned, p.T + 1, 1, stride=1, stride_axis=0)
    by_distance = jnp.sum(turned, axis=0, keepdims=True)
    rest = jnp.sum(total) - jnp.sum(both)
    place = lax.broadcasted_iota(jnp.int32, (1, 2 * p.T), 1)
    return by_distance + jnp.where(place == 2 * p.T - 1, rest, 0.0)


def back_scratch(p):
    return [
        pltpu.VMEM((p.L, DH), B16),
        pltpu.VMEM((p.L, DH), B16),
        pltpu.VMEM((DH + ONES, p.L), B16),
        pltpu.VMEM((p.L, DH), F32),
        pltpu.VMEM((p.L, DH), F32),
        pltpu.VMEM((3, p.CK, 2 * p.T), F32),
        pltpu.VMEM((3, p.CK, 2 * p.T), F32),
    ]


def attend_back_kernel(plan, recv, block, dout, of_ref, rl_ref, dq_ref, dkv_ref, line_ref, *scratch):
    p = plan
    me = lax.axis_index("rep")
    w = me % p.W
    group = (me // p.W) % p.G
    h = pl.program_id(0)
    row = pl.multiple_of(h * DH, DH)
    line_ref[h] = back_head(
        p,
        w,
        row,
        line_of(p, block, group * p.HG + h),
        recv,
        dout,
        of_ref,
        rl_ref.at[h],
        dq_ref,
        dkv_ref,
        *scratch,
    )


def encode_kernel(enc, wk, wv, kn, kt, vn, vt):
    encode_one(enc, wk, kn, kt)
    encode_one(enc, wv, vn, vt)


def encode_one(enc, weight, natural, turned):
    rows = turned.shape[2]
    value = dot(mat(enc), mat(weight))
    for h in range(H):
        natural[h] = value[:, h * DH : (h + 1) * DH].astype(B16)
    flipped = jnp.transpose(value).astype(B16)
    for h in range(H):
        turned[h, 0:DH, :] = flipped[h * DH : (h + 1) * DH]
        turned[h, DH : DH + ONES, :] = jnp.ones((ONES, rows), B16)


def rows_of(units, s, seqs):
    groups = units.shape[0] // seqs
    return units[s * groups : (s + 1) * groups].reshape(-1, units.shape[-1])


def cross_kernel(
    seqs,
    hidden,
    ot,
    wo,
    gain,
    wcq,
    wco,
    kn,
    vt,
    x1_ref,
    x2_ref,
    a2_ref,
    qt_ref,
    of_ref,
    rl_ref,
    pause=lambda: None,
):
    toks = hidden.shape[1]
    span = kn.shape[1] // seqs
    x = hidden[...].reshape(seqs * toks, D).astype(F32)
    o = jnp.concatenate(
        [jnp.transpose(rows_of(ot, s, seqs).astype(F32)) for s in range(seqs)], axis=0
    ).astype(B16)
    x1 = x + dot(o, mat(wo))
    x1_ref[...] = x1
    a2 = (x1 * scale_of(x1) * gain[1:2, :]).astype(B16)
    a2_ref[...] = a2
    q2 = dot(a2, mat(wcq))
    for s in range(seqs):
        qt_ref[s] = jnp.transpose(q2[s * toks : (s + 1) * toks]).astype(B16)
    pause()

    def heads(i, carry):
        for sub in range(2):
            h = 2 * i + sub
            row = pl.multiple_of(h * DH, DH)
            for s in range(seqs):
                keys = slice(s * span, (s + 1) * span)
                e = jnp.exp(dot(kn[h, keys, :], qt_ref[s, pl.ds(row, DH), :]))
                acc = dot(vt[h, :, keys], e.astype(B16))
                rl = 1.0 / acc[DH : DH + 1]
                of_ref[s, pl.ds(row, DH), :] = acc[:DH] * rl
                rl_ref[s, h] = rl
        return carry

    lax.fori_loop(0, H // 2, heads, 0)
    pause()
    o2 = jnp.concatenate([jnp.transpose(of_ref[s]) for s in range(seqs)], axis=0).astype(B16)
    x2_ref[...] = x1_ref[...] + dot(o2, mat(wco))


def ffn_products(rows, og, wg, wu, wd, acc, da3):
    gate = dot(rows, wg[...])
    up = dot(rows, wu[...])
    square = gate * gate
    th = jnp.tanh(GELU_A * gate * (1.0 + GELU_B * square))
    half = 0.5 * (1.0 + th)
    value = gate * half
    slope = half + 0.5 * gate * (1.0 - th * th) * (GELU_A * (1.0 + 3.0 * GELU_B * square))
    inner = (value * up).astype(B16)
    acc[...] += dot(inner, wd[...])
    dwd = t_dot(inner, og).astype(B16)
    dinner = dot_t(og, wd[...]).astype(B16).astype(F32)
    dgate = (dinner * up * slope).astype(B16)
    dup = (dinner * value).astype(B16)
    da3[...] += dot_t(dgate, wg[...]) + dot_t(dup, wu[...])
    return t_dot(rows, dgate).astype(B16), t_dot(rows, dup).astype(B16), dwd


def ffn_pair_kernel(x2_ref, og_ref, gain, wg, wu, wd, out_ref, dx2_ref, dgain_ref, *refs):
    kept, theirs = refs[0:6], refs[6:12]
    a3, acc, da3, own, give, got, own_d, give_d, got_d, send, recv = refs[12:]
    step = pl.program_id(0)
    x = lax.axis_index("shard")
    core = lax.axis_index("rep") % 2
    slot = step // 2
    half = D // 2

    @pl.when(step == 0)
    def _():
        barrier = pltpu.get_barrier_semaphore()
        pl.semaphore_signal(
            barrier, inc=1, device_id={"rep": partner(0)[1]}, device_id_type=MESH
        )
        x2 = x2_ref[...]
        a3[...] = (x2 * scale_of(x2) * gain[2:3, :]).astype(B16)
        acc[...] = x2
        da3[...] = jnp.zeros_like(da3)
        pl.semaphore_wait(barrier, 1)

    def pass_wide(i, at):
        return to_rep(give.at[i, at], got.at[i, at], send.at[i, at], recv.at[i, at], 0)

    def pass_down(at):
        return to_rep(give_d.at[at], got_d.at[at], send.at[2, at], recv.at[2, at], 0)

    *wide, down = ffn_products(a3[...], og_ref[...], wg, wu, wd, acc, da3)
    for i, dw in enumerate(wide):
        dw = dw.reshape(2, half, dw.shape[1])

        @pl.when(step % 2 == core)
        def _(i=i, dw=dw):
            own[i, slot] = dw

        @pl.when(step % 2 != core)
        def _(i=i, dw=dw):
            give[i, slot] = dw
            pass_wide(i, slot).start()

    @pl.when(core == 0)
    def _():
        own_d[step] = down[:, :half]
        give_d[step] = down[:, half:]

    @pl.when(core != 0)
    def _():
        own_d[step] = down[:, half:]
        give_d[step] = down[:, :half]

    pass_down(step).start()

    def both(a, b):
        return (a.astype(F32) + b.astype(F32)).astype(B16)

    def finish_wide(at):
        for i in range(2):
            landed(got.at[i, at], recv.at[i, at])
            kept[2 * i + at][...] = both(own[i, at, x], got[i, at, x])
            theirs[2 * i + at][...] = both(own[i, at, 1 - x], got[i, at, 1 - x])

    @pl.when(step == 2)
    def _():
        finish_wide(0)

    @pl.when(step == 3)
    def _():
        out_ref[...] = acc[...].astype(B16)
        dv, dgain = norm_back(x2_ref[...], gain[2:3, :], da3[...])
        dx2_ref[...] = og_ref[...].astype(F32) + dv
        dgain_ref[...] = dgain
        finish_wide(1)
        for at in range(4):
            landed(got_d.at[at], recv.at[2, at])
        for at in range(2):
            kept[4 + at][...] = both(own_d[2 * x + at], got_d[2 * x + at])
            theirs[4 + at][...] = both(own_d[2 - 2 * x + at], got_d[2 - 2 * x + at])
        for at in range(4):
            pass_down(at).wait_send()
        for at in range(2):
            for i in range(2):
                pass_wide(i, at).wait_send()


def ffn_pair_call(x2, og, small, wg, wu, wd, collective):
    tokens, ff = x2.shape[0], wg.shape[1]
    half, chunk = D // 2, ff // 4
    const = lambda s: pl.BlockSpec(s, lambda i: (0, 0))
    parts = [(half, chunk)] * 4 + [(chunk, half)] * 2
    outs = [((tokens, D), B16), ((tokens, D), F32), ((1, D), F32)]
    outs += [(s, B16) for s in parts + parts]
    dma = pltpu.SemaphoreType.DMA
    return pl.pallas_call(
        ffn_pair_kernel,
        grid=(4,),
        out_shape=[jax.ShapeDtypeStruct(s, t) for s, t in outs],
        in_specs=[
            const((tokens, D)),
            const((tokens, D)),
            const((SMALL_ROWS, D)),
            pl.BlockSpec((D, chunk), lambda i: (0, i)),
            pl.BlockSpec((D, chunk), lambda i: (0, i)),
            pl.BlockSpec((chunk, D), lambda i: (i, 0)),
        ],
        out_specs=[const(s) for s, _ in outs],
        scratch_shapes=[
            pltpu.VMEM((tokens, D), B16),
            pltpu.VMEM((tokens, D), F32),
            pltpu.VMEM((tokens, D), F32),
        ]
        + [pltpu.VMEM((2, 2, 2, half, chunk), B16)] * 3
        + [pltpu.VMEM((4, chunk, half), B16)] * 3
        + [dma((3, 4)), dma((3, 4))],
        compiler_params=pltpu.CompilerParams(
            collective_id=collective, has_side_effects=True, vmem_limit_bytes=60 * 2**20
        ),
        name="ffn",
    )(x2, og, small, wg, wu, wd)


def ffn_kernel(
    x2_ref, og_ref, gain, wg, wu, wd, out_ref, dx2_ref, dgain_ref, dwg, dwu, dwd, a3, acc, da3
):
    step = pl.program_id(0)

    @pl.when(step == 0)
    def _():
        x2 = x2_ref[...]
        a3[...] = (x2 * scale_of(x2) * gain[2:3, :]).astype(B16)
        acc[...] = x2
        da3[...] = jnp.zeros_like(da3)

    dwg[...], dwu[...], dwd[...] = ffn_products(a3[...], og_ref[...], wg, wu, wd, acc, da3)

    @pl.when(step == pl.num_programs(0) - 1)
    def _():
        out_ref[...] = acc[...].astype(B16)
        dv, dgain = norm_back(x2_ref[...], gain[2:3, :], da3[...])
        dx2_ref[...] = og_ref[...].astype(F32) + dv
        dgain_ref[...] = dgain


def cross_back_kernel(
    seqs,
    groups,
    dx2_ref,
    x1_ref,
    a2_ref,
    gain,
    qt_ref,
    of_ref,
    rl_ref,
    kn,
    kt,
    vn,
    enc,
    wco,
    wcq,
    wck,
    wcv,
    wo,
    ot,
    dx1_ref,
    dgain_ref,
    dot_ref,
    denc_ref,
    dwco,
    dwcq,
    dwck,
    dwcv,
    dwo,
    dt,
    dqt,
    dk,
    dv,
    need=lambda *refs: None,
    done=lambda ref: None,
):
    toks = qt_ref.shape[2]
    span = kn.shape[1] // seqs
    dx2 = dx2_ref[...]
    dc = dx2.astype(B16)
    o2t = [of_ref[s].astype(B16) for s in range(seqs)]
    total = dot(o2t[0], dc[0:toks])
    for s in range(1, seqs):
        total = total + dot(o2t[s], dc[s * toks : (s + 1) * toks])
    dwco[...] = total.astype(B16)
    done(dwco)
    need(wco)
    do2 = dot_t(dc, mat(wco))
    for s in range(seqs):
        dt[s] = jnp.transpose(do2[s * toks : (s + 1) * toks]).astype(B16)

    need(kn, kt, vn)

    def heads(i, carry):
        col = pl.multiple_of(2 * i * DH, 2 * DH)
        for s in range(seqs):
            keys = slice(s * span, (s + 1) * span)
            dks, dvs = [], []
            q_pair = jnp.transpose(qt_ref[s, pl.ds(col, 2 * DH), :].astype(F32)).astype(B16)
            d_pair = jnp.transpose(dt[s, pl.ds(col, 2 * DH), :].astype(F32)).astype(B16)
            for sub in range(2):
                h = 2 * i + sub
                row = pl.multiple_of(h * DH, DH)
                d_rows = dt[s, pl.ds(row, DH), :]
                prob = jnp.exp(dot(kn[h, keys, :], qt_ref[s, pl.ds(row, DH), :])) * rl_ref[s, h]
                delta = jnp.sum(
                    d_rows.astype(F32) * of_ref[s, pl.ds(row, DH), :], axis=0, keepdims=True
                )
                ds = (prob * (dot(vn[h, keys, :], d_rows) - delta)).astype(B16)
                dqt[s, pl.ds(row, DH), :] = dot(kt[h, 0:DH, keys], ds).astype(B16)
                dks.append(dot(ds, q_pair[:, sub * DH : (sub + 1) * DH]))
                dvs.append(dot(prob.astype(B16), d_pair[:, sub * DH : (sub + 1) * DH]))
            dk[keys, pl.ds(col, 2 * DH)] = jnp.concatenate(dks, axis=1).astype(B16)
            dv[keys, pl.ds(col, 2 * DH)] = jnp.concatenate(dvs, axis=1).astype(B16)
        return carry

    lax.fori_loop(0, H // 2, heads, 0)
    need(enc, wck, wcv, wcq, wo)
    dwck[...] = t_dot(mat(enc), dk[...]).astype(B16)
    done(dwck)
    dwcv[...] = t_dot(mat(enc), dv[...]).astype(B16)
    done(dwcv)
    denc_ref[...] = (dot_t(dk[...], mat(wck)) + dot_t(dv[...], mat(wcv))).astype(B16)
    done(denc_ref)
    dq2 = jnp.concatenate(
        [jnp.transpose(dqt[s].astype(F32)) for s in range(seqs)], axis=0
    ).astype(B16)
    dwcq[...] = t_dot(a2_ref[...], dq2).astype(B16)
    done(dwcq)
    term, dgain = norm_back(x1_ref[...], gain[1:2, :], dot_t(dq2, mat(wcq)))
    dgain_ref[...] = dgain
    dx1 = dx2 + term
    dx1_ref[...] = dx1
    db = dx1.astype(B16)
    total = dot(rows_of(ot, 0, seqs), db[0:toks])
    for s in range(1, seqs):
        total = total + dot(rows_of(ot, s, seqs), db[s * toks : (s + 1) * toks])
    dwo[...] = total.astype(B16)
    done(dwo)
    do = dot_t(db, mat(wo))
    width = D // groups
    for s in range(seqs):
        turned = jnp.transpose(do[s * toks : (s + 1) * toks]).astype(B16)
        for g in range(groups):
            dot_ref[s * groups + g] = turned[g * width : (g + 1) * width]


def cross_back_pair_kernel(kernel, ins, outs, far_ins, far_outs, count, *refs):
    refs = list(refs)
    take = lambda n: [refs.pop(0) for _ in range(n)]
    args, sources, results_, crossed = take(ins), take(count), take(outs), take(count)
    scratch = take(4)
    near_in, near_out = take(len(far_ins)), take(len(far_outs))
    sems, *cross_sems = refs
    moves = Moves(sems)
    moves.bring([(args[i], near) for i, near in zip(far_ins, near_in)])
    if count:
        send, recv = cross_sems
        barrier = pltpu.get_barrier_semaphore()
        x = lax.axis_index("shard")
        pl.semaphore_signal(barrier, inc=1, device_id={"shard": 1 - x}, device_id_type=MESH)
        pl.semaphore_wait(barrier, 1)
    copies = [
        to_row(sources[i], crossed[i], send.at[i], recv.at[i]) for i in range(count)
    ]
    for copy in copies:
        copy.start()
    for i, near in zip(far_ins, near_in):
        args[i] = near
    made = {}
    for i, near in zip(far_outs, near_out):
        made[id(near)] = (near, results_[i])
        results_[i] = near

    def done(ref):
        moves.take(*made[id(ref)])

    kernel(*args, *results_, *scratch, need=moves.need, done=done)
    moves.end()
    for copy in copies:
        copy.wait()


def cross_back_pair_call(kernel, outs, args, scratch, sources, collective):
    near = pl.BlockSpec(memory_space=pltpu.VMEM)
    anywhere = pl.BlockSpec(memory_space=pl.ANY)
    count = len(sources)
    far_ins = [11, 7, 8, 9, 10, 13, 14, 12, 15]
    far_outs = [3, 4, 5, 6, 7, 8]
    dma = pltpu.SemaphoreType.DMA
    scratch = [*scratch]
    scratch += [pltpu.VMEM(args[i].shape, args[i].dtype) for i in far_ins]
    scratch += [pltpu.VMEM(*outs[i]) for i in far_outs]
    scratch += [dma((len(far_ins) + len(far_outs),))]
    if count:
        scratch += [dma((count,)), dma((count,))]
        params = dict(collective_id=collective, has_side_effects=True)
    else:
        params = {}
    return pl.pallas_call(
        functools.partial(
            cross_back_pair_kernel, kernel, len(args), len(outs), far_ins, far_outs, count
        ),
        out_shape=[jax.ShapeDtypeStruct(s, t) for s, t in outs]
        + [jax.ShapeDtypeStruct(s.shape, s.dtype) for s in sources],
        in_specs=[anywhere if i in far_ins else near for i in range(len(args))]
        + [anywhere] * count,
        out_specs=[anywhere if i in far_outs else near for i in range(len(outs))]
        + [anywhere] * count,
        scratch_shapes=scratch,
        compiler_params=pltpu.CompilerParams(vmem_limit_bytes=60 * 2**20, **params),
        name="cross_back",
    )(*args, *sources)


def last_kernel(plan, hidden, grads, a1, gain, dx1, wq, wk, wv, dh_ref, dgain_ref, dwq, dwk, dwv):
    dgain_ref[...] = last_products(
        plan, hidden, grads, a1, gain, dx1, wq, wk, wv, dh_ref, dwq, dwk, dwv
    )


def last_products(p, hidden, grads, a1, gain, dx1, wq, wk, wv, dh_ref, dwq, dwk, dwv):
    x = hidden[...].reshape(p.S * p.T, D).astype(F32)
    da1 = jnp.zeros((p.S * p.T, D), F32)
    for n, (weight, dw) in enumerate(((wq, dwq), (wk, dwk), (wv, dwv))):
        rows = []
        for s in range(p.S):
            turned = jnp.concatenate(
                [grads[s * p.G + g, n * p.F : (n + 1) * p.F, :] for g in range(p.G)], axis=0
            )
            rows.append(jnp.transpose(turned.astype(F32)))
        d = jnp.concatenate(rows, axis=0).astype(B16)
        dw[...] = t_dot(a1[...], d).astype(B16).reshape(dw.shape)
        da1 = da1 + dot_t(d, mat(weight))
    term, dgain = norm_back(x, gain[0:1, :], da1)
    dh_ref[...] = (dx1[...] + term).astype(B16).reshape(dh_ref.shape)
    return dgain


def gather_rows(part):
    count = lax.axis_size("shard")
    rows, cols = part.shape
    half = rows // 2
    mine = lax.axis_index("shard")
    core = lax.axis_index("rep") % 2
    pairs = [(r, r ^ 1) for r in range(lax.axis_size("rep"))]
    own = lax.dynamic_slice(part, (core * half, 0), (half, cols))
    full = jnp.zeros((count, rows, cols), part.dtype)
    full = lax.dynamic_update_slice(full, part[None], (mine, 0, 0))
    for k in range(1, count):
        got = lax.ppermute(own, "shard", [(i, (i + k) % count) for i in range(count)])
        also = lax.ppermute(got, "rep", pairs)
        owner = (mine - k) % count
        full = lax.dynamic_update_slice(full, got[None], (owner, core * half, 0))
        full = lax.dynamic_update_slice(full, also[None], (owner, (1 - core) * half, 0))
    return full.reshape(count * rows, cols)


def reduce_grads(grads):
    owned = [lax.psum_scatter(g, "shard", scatter_dimension=0, tiled=True) for g in grads]
    summed = lax.psum(tuple(owned), "rep")
    return [s.astype(F32) for s in summed]


class Moves:
    def __init__(self, sems):
        self.sems, self.used, self.coming, self.going = sems, 0, {}, []

    def sem(self):
        self.used += 1
        return self.sems.at[self.used - 1]

    def bring(self, pairs):
        for far, near in pairs:
            sem = self.sem()
            pltpu.make_async_copy(far, near, sem).start()
            self.coming[id(near)] = (near, sem)

    def need(self, *refs):
        for ref in refs:
            if id(ref) in self.coming:
                near, sem = self.coming.pop(id(ref))
                landed(near, sem)

    def take(self, near, far):
        sem = self.sem()
        pltpu.make_async_copy(near, far, sem).start()
        self.going.append((near, sem))

    def end(self):
        for near, sem in self.going:
            landed(near, sem)


BITS = 4


class Job:
    def __init__(self, result, row, rows, col, cols, taken=None):
        self.result, self.taken = result, taken
        self.row, self.rows, self.col, self.cols = row, rows, col, cols


def partner(bit):
    me = lax.axis_index("rep")
    half = 2**bit
    mine = (me // half) % 2
    return mine, me + half * (1 - 2 * mine)


def to_rep(src, dst, send, recv, bit):
    return remote(src, dst, send, recv, partner(bit)[1])


def to_row(src, dst, send, recv):
    x = lax.axis_index("shard")
    return pltpu.make_async_remote_copy(
        src_ref=src,
        dst_ref=dst,
        send_sem=send,
        recv_sem=recv,
        device_id={"shard": 1 - x},
        device_id_type=MESH,
    )


def add_into(acc, term, rows):
    step = 16 if rows % 32 else 32

    def body(i, carry):
        at = pl.ds(pl.multiple_of(i * step, step), step)
        acc[at, :] = (acc[at, :].astype(F32) + term[at, :].astype(F32)).astype(B16)
        return carry

    lax.fori_loop(0, rows // step, body, 0)


class JobRun:
    def __init__(self, job, sources, result, bufs, sems, index, order, depth):
        self.order = (0, *order)
        self.job, self.sources, self.result = job, sources, result
        bufs = list(bufs)
        self.x = lax.axis_index("shard")
        if job.taken is None:
            self.acc, self.core = bufs.pop(0), bufs.pop(0)
            self.kept = self.acc.at[self.x]
            self.steps = [(0, 1), (1, depth)]
        else:
            self.kept = bufs.pop(0)
            self.steps = [(0, depth if job.taken == "sent" else 1)]
        self.steps += [(n, LAG) for n in range(2, 10)]
        self.row, *self.part = bufs
        send, recv, local = sems
        self.send = [send.at[index, i] for i in range(9)]
        self.recv = [recv.at[index, i] for i in range(9)]
        self.local = [local.at[index, i] for i in range(2)]
        self.sent = []
        self.bits = [partner(b)[0] for b in self.order]
        half = job.cols // 2
        self.mine = pl.ds(pl.multiple_of(job.col + self.bits[0] * half, 128), half)
        self.other = pl.ds(pl.multiple_of(job.col + (1 - self.bits[0]) * half, 128), half)
        self.all = pl.ds(job.row, job.rows)
        self.first = [0]
        count = job.rows
        for b in range(1, BITS):
            count //= 2
            self.first.append(self.first[-1] + self.bits[b] * count)

    def count(self, level):
        return self.job.rows // 2**level

    def span(self, first, count):
        return pl.ds(pl.multiple_of(first, 16), count)

    def out(self, first, count):
        return self.result.at[self.span(self.job.row + first, count), self.mine]

    def go(self, copy):
        copy.start()
        self.sent.append(copy)

    def begin(self):
        if self.job.taken is None:
            (source,) = self.sources
            pltpu.make_async_copy(
                source.at[:, self.all, self.mine], self.acc, self.local[0]
            ).start()
            theirs = source.at[:, self.all, self.other]
            self.go(to_rep(theirs, self.core, self.send[0], self.recv[0], 0))
            return
        mine, theirs = self.sources
        pltpu.make_async_copy(mine, self.kept, self.local[0]).start()
        if self.job.taken == "sent":
            self.go(to_row(theirs, self.row, self.send[1], self.recv[1]))
        else:
            pltpu.make_async_copy(theirs, self.row, self.recv[1]).start()

    def stage(self, n):
        job = self.job
        if n == 0:
            self.begin()
        elif n == 1:
            landed(self.acc, self.local[0])
            landed(self.core, self.recv[0])
            for i in range(2):
                add_into(self.acc.at[i], self.core.at[i], job.rows)
            self.go(to_row(self.acc.at[1 - self.x], self.row, self.send[1], self.recv[1]))
        elif n == 2:
            if job.taken is not None:
                landed(self.kept, self.local[0])
            landed(self.row, self.recv[1])
            add_into(self.kept, self.row, job.rows)
            self.give(1)
        elif n in (3, 4):
            self.take(n - 2)
            self.give(n - 1)
        elif n == 5:
            self.take(3)
            piece = self.kept.at[self.span(self.first[3], self.count(3))]
            place = self.out(self.first[3], self.count(3))
            pltpu.make_async_copy(piece, place, self.local[1]).start()
            self.go(to_rep(piece, place, self.send[5], self.recv[5], self.order[3]))
        elif n in (6, 7, 8):
            level = 9 - n
            if n == 6:
                landed(self.out(self.first[3], self.count(3)), self.local[1])
            self.landed_at(level)
            place = self.out(self.first[level - 1], self.count(level - 1))
            self.go(
                to_rep(place, place, self.send[n], self.recv[n], self.order[level - 1])
            )
        else:
            landed(self.result.at[self.all, self.other], self.recv[8])
            for copy in self.sent:
                copy.wait_send()

    def give(self, level):
        count = self.count(level)
        first = self.first[level - 1] + (1 - self.bits[level]) * count
        self.go(
            to_rep(
                self.kept.at[self.span(first, count)],
                self.part[level - 1],
                self.send[level + 1],
                self.recv[level + 1],
                self.order[level],
            )
        )

    def take(self, level):
        landed(self.part[level - 1], self.recv[level + 1])
        count = self.count(level)
        rows = self.span(self.first[level], count)
        add_into(self.kept.at[rows], self.part[level - 1], count)

    def landed_at(self, level):
        count = self.count(level)
        first = self.first[level - 1] + (1 - self.bits[level]) * count
        landed(self.out(first, count), self.recv[8 - level])


def job_buffers(job):
    half = job.cols // 2
    if job.taken is None:
        shapes = [(2, job.rows, half)] * 2
    else:
        shapes = [(job.rows, half)]
    shapes += [(job.rows // 2**b, half) for b in range(BITS)]
    return [pltpu.VMEM(s, B16) for s in shapes]


class SmallRun:
    steps = [(n, 1) for n in range(BITS + 2)]

    def __init__(self, sums, terms, send, recv):
        self.sums, self.terms, self.send, self.recv = sums, terms, send, recv

    def copy(self, n):
        args = (self.sums.at[n], self.terms.at[n], self.send.at[n], self.recv.at[n])
        return to_row(*args) if n == BITS else to_rep(*args, n)

    def stage(self, n):
        if n > 0:
            landed(self.terms.at[n - 1], self.recv.at[n - 1])
            self.sums[n] = self.sums[n - 1] + self.terms[n - 1]
        if n <= BITS:
            self.copy(n).start()
        else:
            for i in range(BITS + 1):
                self.copy(i).wait_send()


class EncodedRun:
    def __init__(self, source, result, bufs, send, recv, load, lag):
        self.source, self.result, self.send, self.recv, self.load = source, result, send, recv, load
        self.acc, self.terms = bufs[0], bufs[1:]
        self.bits = [partner(b)[0] for b in range(BITS)]
        self.steps = [(0, 1)] + [(n + 1, lag) for n in range(1, BITS + 1)]
        self.sent = []

    def part(self, ref, n, bit):
        at = (slice(None),) * (BITS - n) + (bit,)
        return ref.at[at]

    def go(self, n, source):
        copy = to_rep(source, self.terms[n], self.send.at[n], self.recv.at[n], n)
        copy.start()
        self.sent.append(copy)

    def fixed(self, n):
        return self.acc.at[
            (slice(None),) * (BITS + 1 - n) + tuple(self.bits[b] for b in range(n - 1, 0, -1))
        ]

    def add(self, n):
        left = self.fixed(n + 1)
        terms = self.terms[n]
        lead = left.shape[:-2]
        count = 1
        for d in lead:
            count *= d

        def body(i, carry):
            at, rest = [], i
            for d in reversed(lead):
                at.insert(0, rest % d)
                rest = rest // d
            at = tuple(at)
            left[at] = (left[at].astype(F32) + terms[at].astype(F32)).astype(B16)
            return carry

        lax.fori_loop(0, count, body, 0)

    def stage(self, step):
        if step == 0:
            pltpu.make_async_copy(
                self.part(self.source, 0, self.bits[0]), self.acc, self.load
            ).start()
            self.go(0, self.part(self.source, 0, 1 - self.bits[0]))
            return
        n = step - 1
        if n == 1:
            landed(self.acc, self.load)
        landed(self.terms[n - 1], self.recv.at[n - 1])
        self.add(n - 1)
        if n < BITS:
            self.go(n, self.part(self.fixed(n), n, 1 - self.bits[n]))
        else:
            self.result[...] = self.fixed(BITS)[...]
            for copy in self.sent:
                copy.wait_send()


class Pipeline:
    def __init__(self):
        self.waiting, self.active, self.now = [], [], 0

    def add(self, runs):
        self.waiting += runs

    def tick(self, count=1):
        for _ in range(count):
            if self.waiting:
                self.active.insert(0, [self.waiting.pop(0), 0, self.now])
            early = [e for e in self.active if e[0].steps[e[1]][0] < 2]
            late = [e for e in self.active if e[0].steps[e[1]][0] >= 2]
            for entry in early + late:
                run, at, due = entry
                if due <= self.now:
                    stage, wait = run.steps[at]
                    run.stage(stage)
                    entry[1:] = [at + 1, self.now + wait]
            self.active = [e for e in self.active if e[1] < len(e[0].steps)]
            self.now += 1

    def finish(self):
        while self.waiting or self.active:
            self.tick()


def jobs_of(result, rows, cols):
    wide = cols // 2 if cols > 1024 else cols
    tall = rows // 2 if rows > 512 else rows
    return [
        Job(result, row, tall, col, wide)
        for row in range(0, rows, tall)
        for col in range(0, cols, wide)
    ]


SMALL_ROWS = 16
HOSTED = None
X_DEPTH = 3
LAG = 2
TICKS = (4, 1, 1, 2)


def tail_kernel(p, jobs, counts, arrays, *refs):
    refs = list(refs)
    take = lambda n: [refs.pop(0) for _ in range(n)]
    given = [take(n) for n in counts]
    dot_, denc, *far = take(7)
    lines, rl_ref, hidden, a1, dx1, dgc, dgf = take(7)
    results = take(arrays)
    small, dh_ref, denc_out = take(3)
    dout, dq, dkv, part, out, grads = take(6)
    late = take(3)
    recv, of_ref, wq, wk, wv = held = take(5)
    enc_bufs = take(BITS + 1)
    enc_send, enc_recv, enc_load, move_sems = take(4)
    small_sums, small_terms = take(2)
    back = take(7)
    rows_send, rows_recv, part_sem, got_sem, ret_send, ret_recv = take(6)
    small_send, small_recv = take(2)
    sems = take(3)
    moves = Moves(move_sems)
    moves.bring(zip(far, held))
    ready = len(given)
    given += [[ref] for ref in late]
    runs = []
    for i, (job, pair) in enumerate(zip(jobs, given)):
        bufs = take(len(job_buffers(job)))
        order = (2, 1, 3) if i % 4 == 1 else (1, 2, 3)
        runs.append(JobRun(job, pair, results[job.result], bufs, sems, i, order, X_DEPTH))
    enc_run = EncodedRun(denc, denc_out, enc_bufs, enc_send, enc_recv, enc_load.at[0], LAG)

    me = lax.axis_index("rep")
    w = me % p.W
    unit = me // p.W
    group = unit % p.G
    mine = p.worker_of(me)
    slot = p.slot_of(me)
    barrier = pltpu.get_barrier_semaphore()
    for k in range(1, p.R):
        pl.semaphore_signal(
            barrier, inc=1, device_id={"rep": (me + k) % p.R}, device_id_type=MESH
        )
    x = lax.axis_index("shard")
    pl.semaphore_signal(barrier, inc=1, device_id={"shard": 1 - x}, device_id_type=MESH)
    pl.semaphore_wait(barrier, p.R)

    pipeline = Pipeline()
    pipeline.add([*runs[:2], enc_run, *runs[2:ready]])
    tick = pipeline.tick
    for u in range(p.U):
        start_either(
            me, u * p.W + mine, dot_.at[u], dout.at[slot], rows_send.at[u], rows_recv.at[slot]
        )
    tick(TICKS[0])
    for j in range(p.J):
        landed(dout.at[j], rows_recv.at[j])
    lines_at = lax.broadcasted_iota(jnp.int32, (SMALL_ROWS, D), 0)
    block = jnp.zeros((SMALL_ROWS, D), F32)
    moves.need(recv, of_ref)
    for h in range(p.HG):
        sums = back_head(
            p,
            w,
            h * DH,
            line_of(p, lines, group * p.HG + h),
            recv,
            dout,
            of_ref,
            rl_ref.at[h],
            dq,
            dkv,
            *back,
        )
        sums = jnp.concatenate([sums, jnp.zeros((1, D - 2 * p.T), F32)], axis=1)
        block = jnp.where(lines_at == 3 + group * p.HG + h, sums, block)
        tick(TICKS[1])

    def give(k, j):
        to = (w + k) % p.W
        return remote(
            dkv.at[p.source(j, to)],
            part.at[k - 1, j],
            part_sem.at[k - 1, j],
            got_sem.at[k - 1, j],
            me - w + to,
        )

    for j in range(p.J):
        for k in range(1, p.W):
            give(k, j).start()
    tick(TICKS[2])
    for j in range(p.J):
        r = p.source(j, w)
        total = dkv[r].astype(F32)
        for k in range(1, p.W):
            landed(part.at[k - 1, j], got_sem.at[k - 1, j])
            total = total + part[k - 1, j].astype(F32)
        out[j, 0 : p.F, :] = dq[j]
        out[j, p.F : 3 * p.F, :] = total.astype(B16)
        start_either(me, r, out.at[j], grads.at[unit], ret_send.at[j], ret_recv.at[unit])
    tick(TICKS[3])
    for u in range(p.U):
        landed(grads.at[u], ret_recv.at[u])
    moves.need(wq, wk, wv)
    dgain = last_products(p, hidden, grads, a1, lines, dx1, wq, wk, wv, dh_ref, *late)
    for i, row in enumerate((dgain, dgc[...], dgf[...])):
        block = jnp.where(lines_at == i, row, block)
    small_sums[0] = block
    pipeline.add([*runs[ready:], SmallRun(small_sums, small_terms, small_send, small_recv)])
    pipeline.finish()
    small[...] = small_sums[BITS + 1]
    for u in range(p.U):
        end_either(
            me, u * p.W + mine, dot_.at[u], dout.at[slot], rows_send.at[u], rows_recv.at[slot]
        )
    for j in range(p.J):
        r = p.source(j, w)
        end_either(me, r, out.at[j], grads.at[unit], ret_send.at[j], ret_recv.at[unit])
        for k in range(1, p.W):
            give(k, j).wait_send()


def tail_call(p, work, dot_, denc, far, held, collective):
    half = D // 2
    jobs = [job for job, _ in work]
    shapes = []
    for result in range(1 + max(job.result for job in jobs)):
        parts = [job for job in jobs if job.result == result]
        shapes.append((max(j.row + j.rows for j in parts), max(j.col + j.cols for j in parts)))
    for _ in range(3):
        jobs.append(Job(len(shapes), 0, half, 0, D))
        shapes.append((half, D))
    sources = [s for _, pair in work for s in pair]
    piece = denc.shape[0] // (p.S * p.R)
    denc = denc.reshape((p.S,) + (2,) * BITS + (piece, D))
    dma = pltpu.SemaphoreType.DMA
    others = max(p.W - 1, 1)
    scratch = [
        pltpu.VMEM((p.J, p.F, p.T), B16),
        pltpu.VMEM((p.J, p.F, p.T), B16),
        pltpu.VMEM((p.R, 2 * p.F, p.T), B16),
        pltpu.VMEM((others, p.J, 2 * p.F, p.T), B16),
        pltpu.VMEM((p.J, 3 * p.F, p.T), B16),
        pltpu.VMEM((p.U, 3 * p.F, p.T), B16),
    ]
    scratch += [pltpu.VMEM((2, half, D), B16)] * 3
    scratch += [pltpu.VMEM(a.shape, a.dtype) for a in far]
    scratch += [pltpu.VMEM((p.S,) + (2,) * (BITS - 1) + (piece, D), B16)]
    scratch += [
        pltpu.VMEM((p.S,) + (2,) * (BITS - 1 - n) + (piece, D), B16) for n in range(BITS)
    ]
    scratch += [dma((BITS,)), dma((BITS,)), dma((1,)), dma((len(far),))]
    scratch += [
        pltpu.VMEM((BITS + 2, SMALL_ROWS, D), F32),
        pltpu.VMEM((BITS + 1, SMALL_ROWS, D), F32),
    ]
    scratch += back_scratch(p)
    scratch += [
        dma((p.U,)),
        dma((p.J,)),
        dma((others, p.J)),
        dma((others, p.J)),
        dma((p.J,)),
        dma((p.U,)),
        dma((BITS + 1,)),
        dma((BITS + 1,)),
        dma((len(jobs), 9)),
        dma((len(jobs), 9)),
        dma((len(jobs), 2)),
    ]
    for job in jobs:
        scratch += job_buffers(job)
    anywhere = pl.BlockSpec(memory_space=pl.ANY)
    near = pl.BlockSpec(memory_space=pltpu.VMEM)
    *sums, small, dh, denc = pl.pallas_call(
        functools.partial(tail_kernel, p, jobs, [len(pair) for _, pair in work], len(shapes)),
        out_shape=[jax.ShapeDtypeStruct(s, B16) for s in shapes]
        + [
            jax.ShapeDtypeStruct((SMALL_ROWS, D), F32),
            jax.ShapeDtypeStruct((p.S, p.T, D), B16),
            jax.ShapeDtypeStruct((p.S, piece, D), B16),
        ],
        in_specs=[anywhere] * (len(sources) + 2 + len(far)) + [near] * len(held),
        out_specs=[anywhere] * len(shapes) + [near] * 3,
        scratch_shapes=scratch,
        compiler_params=pltpu.CompilerParams(
            collective_id=collective, has_side_effects=True, vmem_limit_bytes=60 * 2**20
        ),
        name="tail",
    )(*sources, dot_, denc, *far, *held)
    return sums, small, dh, denc


def widen_kernel(count, *refs):
    for i in range(count):
        refs[count + i][...] = refs[i][...].astype(F32)


def widen(mats):
    parts = 8
    blocks = [
        pl.BlockSpec((m.shape[0] // parts, m.shape[1]), lambda i: (i, 0)) for m in mats
    ]
    return pl.pallas_call(
        functools.partial(widen_kernel, len(mats)),
        grid=(parts,),
        out_shape=[jax.ShapeDtypeStruct(m.shape, F32) for m in mats],
        in_specs=blocks,
        out_specs=blocks,
        compiler_params=pltpu.CompilerParams(vmem_limit_bytes=63 * 2**20),
        name="widen",
    )(*mats)


class Fetch:
    def __init__(self, master, staged, out, first, rows, col, cols, stage, own, sems, index, wide):
        self.x = lax.axis_index("shard")
        self.core, self.y = [partner(b)[0] for b in range(2)]
        self.rows, self.staged, self.wide = rows, staged, wide
        self.master = master.at[pl.ds(first, rows), pl.ds(col, cols)]
        self.stage_ref = stage.at[pl.ds(0, rows), pl.ds(0, cols)]
        self.own = own
        self.out, self.first, self.col, self.cols = out, first, col, cols
        load, keep, self.send, self.recv = sems
        self.load, self.keep = load.at[index], keep.at[index]
        self.send = [self.send.at[index, i] for i in range(3)]
        self.recv = [self.recv.at[index, i] for i in range(3)]

    def span(self, core, y=None):
        half = self.rows // 2
        if y is None:
            return core * half, half
        return core * half + y * (half // 2), half // 2

    def place(self, owner, *share):
        first, count = self.span(*share)
        first = pl.multiple_of(self.first + first, 16)
        return self.out.at[owner, pl.ds(first, count), pl.ds(self.col, self.cols)]

    def share(self):
        return (self.core, self.y) if self.wide else (self.core,)

    def read(self):
        pltpu.make_async_copy(self.master, self.stage_ref, self.load).start()

    def kept(self):
        return self.out.at[self.x, pl.ds(self.first, self.rows), pl.ds(self.col, self.cols)]

    def across(self):
        first, count = self.span(*self.share())
        part = self.own.at[pl.ds(pl.multiple_of(first, 16), count)]
        return to_row(part, self.place(self.x, *self.share()), self.send[0], self.recv[0])

    def start(self):
        landed(self.stage_ref, self.load)
        step = 32

        def body(i, carry):
            at = pl.ds(pl.multiple_of(i * step, step), step)
            self.own[at, :] = self.stage_ref[at, :].astype(B16)
            return carry

        lax.fori_loop(0, self.rows // step, body, 0)
        self.across().start()
        if self.staged:
            pltpu.make_async_copy(self.own, self.kept(), self.keep).start()

    def beside(self):
        place = self.place(1 - self.x, self.core, self.y)
        return to_rep(place, place, self.send[2], self.recv[2], 1)

    def over(self):
        place = self.place(1 - self.x, self.core)
        return to_rep(place, place, self.send[1], self.recv[1], 0)

    def relay(self):
        landed(self.place(1 - self.x, *self.share()), self.recv[0])
        if self.wide:
            self.beside().start()
        else:
            self.over().start()

    def relay_more(self):
        if self.wide:
            landed(self.place(1 - self.x, self.core, 1 - self.y), self.recv[2])
            self.over().start()

    def finish(self):
        landed(self.place(1 - self.x, 1 - self.core), self.recv[1])

    def end(self):
        self.across().wait_send()
        self.over().wait_send()
        if self.wide:
            self.beside().wait_send()
        if self.staged:
            landed(self.kept(), self.keep)


def small_block(p, gains, table, buckets, x):
    at = lax.broadcasted_iota(jnp.int32, (SMALL_ROWS, D), 0)
    block = jnp.zeros((SMALL_ROWS, D), F32)
    for i, gain in enumerate(gains):
        part = gain[...].astype(B16).astype(F32).reshape(1, -1)
        none = jnp.zeros_like(part)
        row = jnp.where(
            x == 0,
            jnp.concatenate([part, none], axis=1),
            jnp.concatenate([none, part], axis=1),
        )
        block = jnp.where(at == i, row, block)
    held = table.shape[0]
    bucket = lax.broadcasted_iota(jnp.int32, (held, 2 * p.T), 0) + x * held
    near = buckets[...].reshape(1, -1)[:, : 2 * p.T]
    onehot = (near == bucket).astype(F32).astype(B16)
    lines = t_dot(table[...].astype(B16), onehot)
    lines = jnp.concatenate([lines, jnp.zeros((H, D - 2 * p.T), F32)], axis=1)
    lines = jnp.concatenate(
        [jnp.zeros((3, D), F32), lines, jnp.zeros((SMALL_ROWS - 3 - H, D), F32)], axis=0
    )
    return block + lines


def head_kernel(p, *refs):
    refs = list(refs)
    take = lambda n: [refs.pop(0) for _ in range(n)]
    masters = take(11)
    hidden, encoded, g1, g2, g3, table, buckets = take(7)
    far_mats = take(8)
    wide = take(3)
    far_recv, far_enc, far_kn, far_kt, far_vn = take(5)
    small, a1, of_ref, rl_ref, ot = take(5)
    x1, x2, a2, qt2, of2, rl2 = take(6)
    mats = take(8)
    recv, enc, kn, kt, vn, vt = take(6)
    moves = Moves(take(1)[0])
    send, o_ref, mine_small, their_small = take(4)
    stages = take(4)
    owns = take(6)
    att = take(3)
    fetch_sems = take(4)
    small_send, small_recv, enc_send, enc_recv = take(4)
    tok_send, relay_sem, tok_recv, back_send, back_recv = take(5)

    me = lax.axis_index("rep")
    x = lax.axis_index("shard")
    w = me % p.W
    unit = me // p.W
    group = unit % p.G
    mine = p.worker_of(me)
    bits = [(me // 2**b) % 2 for b in range(BITS)]

    half = D // 2
    jobs = []
    for i in range(8):
        jobs.append((masters[i], mats[i], 0, half, 0, D))
    for i, ref in enumerate(wide):
        rows, cols = ref.shape[1:]
        tall = rows // 2 if rows > 512 else rows
        part = cols // 2 if cols > 1024 else cols
        for row in range(0, rows, tall):
            for col in range(0, cols, part):
                jobs.append((masters[8 + i], ref, row, tall, col, part))
    fetches = []
    for i, (master, out, row, rows, col, cols) in enumerate(jobs):
        staged = i >= 8
        own = owns[i - 8] if staged else out.at[x]
        fetches.append(
            Fetch(
                master,
                staged,
                out,
                row,
                rows,
                col,
                cols,
                stages[i % 4],
                own,
                fetch_sems,
                i,
                i < 5 or i % 2 == 0,
            )
        )

    barrier = pltpu.get_barrier_semaphore()
    for k in range(1, p.R):
        pl.semaphore_signal(
            barrier, inc=1, device_id={"rep": (me + k) % p.R}, device_id_type=MESH
        )
    pl.semaphore_signal(barrier, inc=1, device_id={"shard": 1 - x}, device_id_type=MESH)
    for fetch in fetches[:4]:
        fetch.read()
    mine_small[...] = small_block(p, (g1, g2, g3), table, buckets, x)
    enc[:, bits[3], bits[2], bits[1], bits[0]] = encoded[...]
    pl.semaphore_wait(barrier, p.R)

    share = to_row(mine_small, their_small, small_send, small_recv)
    share.start()

    def enc_copy(n):
        at = (slice(None),) * (1 + n) + tuple(bits[b] for b in range(BITS - 1 - n, -1, -1))
        part = enc.at[at]
        return to_rep(part, part, enc_send.at[n], enc_recv.at[n], BITS - 1 - n)

    def enc_landed(n):
        b = [bits[i] for i in range(BITS - 1 - n, -1, -1)]
        b[0] = 1 - b[0]
        landed(enc.at[(slice(None),) * (1 + n) + tuple(b)], enc_recv.at[n])

    started, relayed, more = 0, 0, 0

    def begin(count=1):
        nonlocal started
        for _ in range(count):
            if started < len(fetches):
                fetches[started].start()
                if started + 4 < len(fetches):
                    fetches[started + 4].read()
                started += 1

    def pass_on(count=1):
        nonlocal relayed, more
        for _ in range(count):
            if more < relayed:
                fetches[more].relay_more()
                more += 1
            if relayed < started:
                fetches[relayed].relay()
                relayed += 1

    begin(3)
    enc_copy(0).start()
    landed(their_small, small_recv)
    small[...] = mine_small[...] + their_small[...]
    enc_landed(0)
    enc_copy(1).start()
    pass_on()
    begin()
    enc_landed(1)
    pass_on()
    begin()
    enc_copy(2).start()
    pass_on()
    begin()
    fetches[2].relay_more()
    more = 3
    for fetch, far in zip(fetches[:3], far_mats):
        fetch.finish()
        moves.take(fetch.out, far)
    project_kernel(p, hidden, small, *mats[:3], a1, send)
    for u in range(p.U):
        start_either(
            me, u * p.W + mine, send.at[u], recv.at[me], tok_send.at[u], tok_recv.at[me]
        )
    enc_landed(2)
    enc_copy(3).start()
    begin()
    pass_on(2)
    begin()
    enc_landed(3)
    moves.take(enc, far_enc)
    fetches[4].relay_more()
    more = 5
    for i, natural, turned in ((3, kn, kt), (4, vn, vt)):
        fetches[i].finish()
        moves.take(mats[i], far_mats[i])
        encode_one(enc, mats[i], natural, turned)
        pass_on()
        begin()

    def relay(k, j):
        part = recv.at[p.source(j, w), pl.ds(p.F, 2 * p.F)]
        to = me - w + (w + k) % p.W
        return remote(part, part, relay_sem.at[k - 1, j], tok_recv.at[p.source(j, w)], to)

    for j in range(p.J):
        landed(recv.at[p.source(j, w)], tok_recv.at[p.source(j, w)])
        for k in range(1, p.W):
            relay(k, j).start()
    pass_on()
    begin()
    for k in range(1, p.W):
        for j in range(p.J):
            r = p.source(j, (w + k) % p.W)
            landed(recv.at[r, pl.ds(p.F, 2 * p.F)], tok_recv.at[r])
    for made, far in ((recv, far_recv), (kn, far_kn), (kt, far_kt), (vn, far_vn)):
        moves.take(made, far)
    for h in range(p.HG):
        line = line_of(p, small, group * p.HG + h)
        attend_head(p, w, h * DH, line, recv, o_ref, of_ref, rl_ref.at[h], *att)
        pass_on()
        begin()
    for j in range(p.J):
        r = p.source(j, w)
        start_either(me, r, o_ref.at[j], ot.at[unit], back_send.at[j], back_recv.at[unit])
    pass_on()
    begin()
    for fetch, far in zip(fetches[5:8], far_mats[5:]):
        fetch.finish()
        moves.take(fetch.out, far)
    for u in range(p.U):
        landed(ot.at[u], back_recv.at[u])

    def pause():
        pass_on()
        begin()

    cross_kernel(
        p.S, hidden, ot, mats[5], small, mats[6], mats[7], kn, vt, x1, x2, a2, qt2, of2, rl2, pause
    )
    begin(len(fetches))
    while more < len(fetches):
        pass_on()
    for fetch in fetches[8:]:
        fetch.finish()
    for fetch in fetches:
        fetch.end()
    moves.end()
    share.wait_send()
    for n in range(BITS):
        enc_copy(n).wait_send()
    for u in range(p.U):
        end_either(
            me, u * p.W + mine, send.at[u], recv.at[me], tok_send.at[u], tok_recv.at[me]
        )
    for j in range(p.J):
        r = p.source(j, w)
        end_either(me, r, o_ref.at[j], ot.at[unit], back_send.at[j], back_recv.at[unit])
        for k in range(1, p.W):
            relay(k, j).wait_send()


def head_call(p, masters, hidden, encoded, gains, table, buckets, collective):
    half, tokens = D // 2, p.S * p.T
    piece = encoded.shape[1]
    enc_rows = p.S * piece * p.R
    wides = [m.shape for m in masters[8:]]
    near = pl.BlockSpec(memory_space=pltpu.VMEM)
    anywhere = pl.BlockSpec(memory_space=pl.ANY)
    outs = [((2, half, D), B16)] * 8 + [((2, *s), B16) for s in wides]
    inner = [
        ((p.R, 3 * p.F, p.T), B16),
        ((p.S,) + (2,) * BITS + (piece, D), B16),
        ((H, enc_rows, DH), B16),
        ((H, DH + ONES, enc_rows), B16),
        ((H, enc_rows, DH), B16),
    ]
    outs += inner
    inner = [((2, half, D), B16)] * 8 + inner + [inner[3]]
    outs += [
        ((SMALL_ROWS, D), F32),
        ((tokens, D), B16),
        ((p.J, p.F, p.T), F32),
        ((p.HG, p.NP, 1, 2 * p.T), F32),
        ((p.U, p.F, p.T), B16),
        ((tokens, D), F32),
        ((tokens, D), F32),
        ((tokens, D), B16),
        ((p.S, D, p.T), B16),
        ((p.S, D, p.T), F32),
        ((p.S, H, 1, p.T), F32),
    ]
    parts = [(half, D)] * 8
    for rows, cols in wides:
        tall = rows // 2 if rows > 512 else rows
        part = cols // 2 if cols > 1024 else cols
        parts += [(tall, part)] * ((rows // tall) * (cols // part))
    count = len(parts)
    dma = pltpu.SemaphoreType.DMA
    scratch = [pltpu.VMEM(s, t) for s, t in inner] + [dma((13,))]
    scratch += [
        pltpu.VMEM((p.U, 3 * p.F, p.T), B16),
        pltpu.VMEM((p.J, p.F, p.T), B16),
        pltpu.VMEM((SMALL_ROWS, D), F32),
        pltpu.VMEM((SMALL_ROWS, D), F32),
    ]
    tallest = max(r for r, _ in parts)
    widest = max(c for _, c in parts)
    scratch += [pltpu.VMEM((tallest, widest), F32)] * 4
    scratch += [pltpu.VMEM(s, B16) for s in parts[8:]]
    scratch += attend_scratch(p)
    scratch += [dma((count,)), dma((count,)), dma((count, 3)), dma((count, 3))]
    scratch += [dma, dma, dma((BITS,)), dma((BITS,))]
    scratch += [
        dma((p.U,)),
        dma((max(p.W - 1, 1), p.J)),
        dma((p.R,)),
        dma((p.J,)),
        dma((p.U,)),
    ]
    return pl.pallas_call(
        functools.partial(head_kernel, p),
        out_shape=[jax.ShapeDtypeStruct(s, t) for s, t in outs],
        in_specs=[anywhere] * 11 + [near] * 7,
        out_specs=[anywhere] * 16 + [near] * 11,
        scratch_shapes=scratch,
        compiler_params=pltpu.CompilerParams(
            collective_id=collective, has_side_effects=True, vmem_limit_bytes=62 * 2**20
        ),
        name="head",
    )(*masters, hidden, encoded, *gains, table, buckets)


def local(
    hidden,
    encoded,
    out_grad,
    self_query,
    self_key,
    self_value,
    self_out,
    cross_query,
    cross_key,
    cross_value,
    cross_out,
    ffn_gate,
    ffn_up,
    ffn_down,
    gain_self,
    gain_cross,
    gain_ffn,
    bias_table,
    buckets,
):
    seqs, toks = hidden.shape[0], hidden.shape[1]
    p = Plan(seqs, toks, lax.axis_size("rep"))
    tokens = seqs * toks
    ff = ffn_gate.shape[1]
    enc_rows = seqs * encoded.shape[1] * p.R
    dma = pltpu.SemaphoreType.DMA

    n_shard = lax.axis_size("shard")
    mine = lax.axis_index("shard")
    part = gain_self.shape[0]
    near = buckets[: 2 * toks]
    onehot = (near[:, None] == jnp.arange(NB, dtype=jnp.int32)[None, :]).astype(B16)
    paired = n_shard == 2 and p.R == 2**BITS and 3 + H <= SMALL_ROWS
    if paired:
        masters = (
            self_query,
            self_key,
            self_value,
            cross_key,
            cross_value,
            self_out,
            cross_query,
            cross_out,
            ffn_gate,
            ffn_up,
            ffn_down,
        )
        gains = [gain_self, gain_cross, gain_ffn]
        got = head_call(
            p, masters, hidden, encoded, gains, bias_table, buckets, 0
        )
        wq, wk, wv, wck, wcv, wo, wcq, wco = got[:8]
        wg, wu, wd = [g.reshape(-1, g.shape[-1]) for g in got[8:11]]
        recv, enc, ckn, ckt, cvn, small, a1, of, rl, ot = got[11:21]
        x1, x2, a2, qt2, of2, rl2 = got[21:]
    else:
        lot = jnp.concatenate(
            [
                jnp.stack([gain_self, gain_cross, gain_ffn]).reshape(-1),
                bias_table.reshape(-1),
            ]
        ).astype(B16)
        lot = lax.all_gather(lot, "shard", axis=0)
        gains = [
            lot[:, i * part : (i + 1) * part].reshape(1, D).astype(F32) for i in range(3)
        ]
        table = lot[:, 3 * part :].reshape(NB, H)
        lines = jnp.einsum("lb,bh->hl", onehot, table, preferred_element_type=F32)
        lines = jnp.pad(lines, ((0, SMALL_ROWS - 3 - H), (0, D - 2 * toks)))
        small = jnp.concatenate([*gains, lines], axis=0)

        wq, wk, wv, wo, wcq, wck, wcv, wco, wg, wu, wd = [
            gather_rows(m.astype(B16))
            for m in (
                self_query,
                self_key,
                self_value,
                self_out,
                cross_query,
                cross_key,
                cross_value,
                cross_out,
                ffn_gate,
                ffn_up,
                ffn_down,
            )
        ]
        enc = lax.all_gather(encoded, "rep", axis=1, tiled=True).reshape(enc_rows, D)

        a1, send = plain_call(
            functools.partial(project_kernel, p),
            [((tokens, D), B16), ((p.U, 3 * p.F, toks), B16)],
            (hidden, small, wq, wk, wv),
            "project",
        )
        recv = comm_call(
            functools.partial(scatter_tokens, p),
            (p.R, 3 * p.F, toks),
            (send,),
            [dma((p.U,)), dma((max(p.W - 1, 1), p.J)), dma((p.R,))],
            0,
            "scatter_tokens",
        )
        ckn, ckt, cvn, cvt = plain_call(
            encode_kernel,
            [
                ((H, enc_rows, DH), B16),
                ((H, DH + ONES, enc_rows), B16),
                ((H, enc_rows, DH), B16),
                ((H, DH + ONES, enc_rows), B16),
            ],
            (enc, wck, wcv),
            "encode",
        )
        o, of, rl = pl.pallas_call(
            functools.partial(attend_kernel, p),
            grid=(p.HG,),
            out_shape=[
                jax.ShapeDtypeStruct((p.J, p.F, toks), B16),
                jax.ShapeDtypeStruct((p.J, p.F, toks), F32),
                jax.ShapeDtypeStruct((p.HG, p.NP, 1, 2 * toks), F32),
            ],
            in_specs=[whole((p.R, 3 * p.F, toks)), whole((SMALL_ROWS, D))],
            out_specs=[
                whole((p.J, p.F, toks)),
                whole((p.J, p.F, toks)),
                whole((p.HG, p.NP, 1, 2 * toks)),
            ],
            scratch_shapes=attend_scratch(p),
            compiler_params=pltpu.CompilerParams(vmem_limit_bytes=56 * 2**20),
            name="attend",
        )(recv, small)
        ot = comm_call(
            functools.partial(return_tokens, p),
            (p.U, p.F, toks),
            (o,),
            [dma((p.J,)), dma((p.U,))],
            1,
            "return_tokens",
        )

        x1, x2, a2, qt2, of2, rl2 = plain_call(
            functools.partial(cross_kernel, seqs),
            [
                ((tokens, D), F32),
                ((tokens, D), F32),
                ((tokens, D), B16),
                ((seqs, D, toks), B16),
                ((seqs, D, toks), F32),
                ((seqs, H, 1, toks), F32),
            ],
            (hidden, ot, wo, small, wcq, wco, ckn, cvt),
            "cross",
        )

    if paired and HOSTED is not None:
        output, dx2, dg_ffn, *parts = ffn_pair_call(
            x2, out_grad.reshape(tokens, D), small, wg, wu, wd, 1
        )
        kept, theirs = parts[:6], parts[6:]
        half, wide = D // 2, ff // 2
        jobs = [Job(i // 2, 0, half, (i % 2) * wide, wide) for i in range(4)]
        jobs += [Job(2, i * (ff // 4), ff // 4, 0, D) for i in range(2)]
        for i, job in enumerate(jobs):
            job.taken = "here" if i < HOSTED else "sent"
    else:
        chunk = min(512, ff)
        const = lambda s: pl.BlockSpec(s, lambda i: (0, 0))
        output, dx2, dg_ffn, dwg, dwu, dwd = pl.pallas_call(
            ffn_kernel,
            grid=(ff // chunk,),
            out_shape=[
                jax.ShapeDtypeStruct((tokens, D), B16),
                jax.ShapeDtypeStruct((tokens, D), F32),
                jax.ShapeDtypeStruct((1, D), F32),
                jax.ShapeDtypeStruct((D, ff), B16),
                jax.ShapeDtypeStruct((D, ff), B16),
                jax.ShapeDtypeStruct((ff, D), B16),
            ],
            in_specs=[
                const((tokens, D)),
                const((tokens, D)),
                const((SMALL_ROWS, D)),
                pl.BlockSpec((D, chunk), lambda i: (0, i)),
                pl.BlockSpec((D, chunk), lambda i: (0, i)),
                pl.BlockSpec((chunk, D), lambda i: (i, 0)),
            ],
            out_specs=[
                const((tokens, D)),
                const((tokens, D)),
                const((1, D)),
                pl.BlockSpec((D, chunk), lambda i: (0, i)),
                pl.BlockSpec((D, chunk), lambda i: (0, i)),
                pl.BlockSpec((chunk, D), lambda i: (i, 0)),
            ],
            scratch_shapes=[
                pltpu.VMEM((tokens, D), B16),
                pltpu.VMEM((tokens, D), F32),
                pltpu.VMEM((tokens, D), F32),
            ],
            compiler_params=pltpu.CompilerParams(vmem_limit_bytes=56 * 2**20),
            name="ffn",
        )(x2, out_grad.reshape(tokens, D), small, wg, wu, wd)

    back_outs = [
        ((tokens, D), F32),
        ((1, D), F32),
        ((p.U, p.F, toks), B16),
        ((enc_rows, D), B16),
    ] + [((D, D), B16)] * 5
    back_args = (dx2, x1, a2, small, qt2, of2, rl2, ckn, ckt, cvn, enc, wco, wcq, wck, wcv, wo, ot)
    back_scratch_ = [
        pltpu.VMEM((seqs, D, toks), B16),
        pltpu.VMEM((seqs, D, toks), B16),
        pltpu.VMEM((enc_rows, D), B16),
        pltpu.VMEM((enc_rows, D), B16),
    ]
    back_kernel = functools.partial(cross_back_kernel, seqs, p.G)
    if paired:
        hosted = [] if HOSTED is None else theirs[:HOSTED]
        got = cross_back_pair_call(back_kernel, back_outs, back_args, back_scratch_, hosted, 2)
        crossed = got[9:]
        got = got[:9]
    else:
        got = plain_call(back_kernel, back_outs, back_args, "cross_back", scratch=back_scratch_)
    dx1, dg_cross, dot_, denc, dwco, dwcq, dwck, dwcv, dwo = got
    if paired:
        half = D // 2
        if HOSTED is None:
            work = []
            for i, g in enumerate((dwg, dwu, dwd)):
                g = g.reshape(2, g.shape[0] // 2, g.shape[1])
                work += [(job, [g]) for job in jobs_of(i, *g.shape[1:])]
        else:
            work = list(zip(jobs, zip(kept, [*crossed, *theirs[HOSTED:]])))
            if HOSTED == 3:
                work = [work[i] for i in (3, 0, 4, 1, 5, 2)]
        work += [
            (Job(3 + i, 0, half, 0, D), [g.reshape(2, half, D)])
            for i, g in enumerate((dwo, dwcq, dwck, dwcv, dwco))
        ]
        sums, block, hidden_grad, encoded_grad = tail_call(
            p,
            work,
            dot_,
            denc,
            (recv, of, wq, wk, wv),
            (small, rl, hidden, a1, dx1, dg_cross, dg_ffn),
            3,
        )
        dwg, dwu, dwd, dwo, dwcq, dwck, dwcv, dwco, dwq, dwk, dwv = widen(sums)
        mats = [dwq, dwk, dwv, dwo, dwcq, dwck, dwcv, dwco, dwg, dwu, dwd]
        dgains = lax.dynamic_slice(block, (0, mine * part), (3, part))
        by_bucket = jnp.einsum(
            "hl,lb->bh",
            block[3 : 3 + H, : 2 * toks],
            onehot.astype(F32),
            precision=lax.Precision.HIGHEST,
        )
        dtab = lax.dynamic_slice(
            by_bucket, (mine * bias_table.shape[0], 0), bias_table.shape
        )
    else:
        encoded_grad = lax.psum_scatter(
            denc.reshape(seqs, enc_rows // seqs, D), "rep", scatter_dimension=1, tiled=True
        )
        dout = comm_call(
            functools.partial(scatter_rows, p),
            (p.J, p.F, toks),
            (dot_,),
            [dma((p.U,)), dma((p.J,))],
            2,
            "scatter_rows",
        )
        dq, dkv, line = pl.pallas_call(
            functools.partial(attend_back_kernel, p),
            grid=(p.HG,),
            out_shape=[
                jax.ShapeDtypeStruct((p.J, p.F, toks), B16),
                jax.ShapeDtypeStruct((p.R, 2 * p.F, toks), B16),
                jax.ShapeDtypeStruct((p.HG, 1, 2 * toks), F32),
            ],
            in_specs=[
                whole((p.R, 3 * p.F, toks)),
                whole((SMALL_ROWS, D)),
                whole((p.J, p.F, toks)),
                whole((p.J, p.F, toks)),
                whole((p.HG, p.NP, 1, 2 * toks)),
            ],
            out_specs=[
                whole((p.J, p.F, toks)),
                whole((p.R, 2 * p.F, toks)),
                whole((p.HG, 1, 2 * toks)),
            ],
            scratch_shapes=back_scratch(p),
            compiler_params=pltpu.CompilerParams(vmem_limit_bytes=56 * 2**20),
            name="attend_back",
        )(recv, small, dout, of, rl)
        grads = comm_call(
            functools.partial(return_grads, p),
            (p.U, 3 * p.F, toks),
            (dq, dkv),
            [
                pltpu.VMEM((max(p.W - 1, 1), p.J, 2 * p.F, toks), B16),
                pltpu.VMEM((p.J, 3 * p.F, toks), B16),
                dma((p.J,)),
                dma((max(p.W - 1, 1), p.J)),
                dma((max(p.W - 1, 1), p.J)),
                dma((p.U,)),
            ],
            3,
            "return_grads",
            space=pltpu.VMEM,
        )
        hidden_grad, dg_self, dwq, dwk, dwv = plain_call(
            functools.partial(last_kernel, p),
            [(hidden.shape, B16), ((1, D), F32)] + [((D, D), B16)] * 3,
            (hidden, grads, a1, small, dx1, wq, wk, wv),
            "last",
        )

        group = (lax.axis_index("rep") // p.W) % p.G
        by_bucket = jnp.einsum(
            "hl,lb->bh", line[:, 0, :], onehot.astype(F32), precision=lax.Precision.HIGHEST
        )
        dtable = lax.dynamic_update_slice(jnp.zeros((NB, H), F32), by_bucket, (0, group * p.HG))

        mats = reduce_grads([dwq, dwk, dwv, dwo, dwcq, dwck, dwcv, dwco, dwg, dwu, dwd])
        lot = jnp.concatenate(
            [g.reshape(n_shard, part) for g in (dg_self, dg_cross, dg_ffn)]
            + [dtable.reshape(n_shard, -1)],
            axis=1,
        )
        size = lot.shape[1]
        lot = lax.psum(lot, ("shard", "rep"))
        lot = lax.dynamic_slice(lot, (mine, 0), (1, size))[0]
        dgains = [lot[i * part : (i + 1) * part] for i in range(3)]
        dtab = lot[3 * part :].reshape(bias_table.shape)
    return (
        output.reshape(hidden.shape),
        hidden_grad,
        encoded_grad,
        *mats,
        *dgains,
        dtab,
    )


def solution(mesh):
    tok = P("shard", "rep", None)
    mat = P("shard", None)
    in_specs = (tok,) * 3 + (mat,) * 11 + (P("shard"),) * 3 + (mat, P())
    out_specs = (tok,) * 3 + (mat,) * 11 + (P("shard"),) * 3 + (mat,)
    return jax.shard_map(local, mesh=mesh, in_specs=in_specs, out_specs=out_specs, check_vma=False)
```

```python
import functools
import itertools

import jax
import jax.numpy as jnp
from jax import lax
from jax.experimental import pallas as pl
from jax.experimental.pallas import tpu as pltpu
from jax.sharding import PartitionSpec as P

D = 768
H = 12
DH = 64
NB = 32
EPS = 1e-06
F32 = jnp.float32
B16 = jnp.bfloat16
ONES = 16
HIDE = -1e30
MESH = pl.DeviceIdType.MESH
GELU_A = 0.7978845608028654
GELU_B = 0.044715


def dot(a, b):
    return lax.dot_general(a, b, (((1,), (0,)), ((), ())), preferred_element_type=F32)


def dot_t(a, b):
    return lax.dot_general(a, b, (((1,), (1,)), ((), ())), preferred_element_type=F32)


def t_dot(a, b):
    return lax.dot_general(a, b, (((0,), (0,)), ((), ())), preferred_element_type=F32)


def mat(ref):
    return ref[...].reshape(-1, ref.shape[-1])


def scale_of(v):
    return lax.rsqrt(jnp.mean(v * v, axis=-1, keepdims=True) + EPS)


def norm_back(v, gain, grad):
    r = scale_of(v)
    n = v * r
    c = grad * gain
    dv = r * (c - n * jnp.mean(c * n, axis=-1, keepdims=True))
    return dv, jnp.sum(grad * n, axis=0, keepdims=True)


def whole(shape):
    return pl.BlockSpec(shape, lambda *_: (0,) * len(shape))


def plain_call(kernel, outs, args, name, scratch=(), vmem=60):
    return pl.pallas_call(
        kernel,
        out_shape=[jax.ShapeDtypeStruct(s, t) for s, t in outs],
        in_specs=[pl.BlockSpec(memory_space=pltpu.VMEM)] * len(args),
        out_specs=[pl.BlockSpec(memory_space=pltpu.VMEM)] * len(outs),
        scratch_shapes=list(scratch),
        compiler_params=pltpu.CompilerParams(vmem_limit_bytes=vmem * 2**20),
        name=name,
    )(*args)


class Plan:
    def __init__(self, seqs, toks, rows):
        self.S, self.T, self.R = seqs, toks, rows
        groups = 1
        for g in range(1, H + 1):
            if H % g == 0 and seqs * g <= rows and rows % (2 * seqs * g) == 0:
                groups = g
        self.G = groups
        self.HG = H // groups
        self.F = self.HG * DH
        self.U = seqs * groups
        self.W = rows // self.U
        self.J = rows // self.W
        self.NP = self.J // 2
        self.CK = 2 * self.W * toks
        self.L = rows * toks

    def worker_of(self, r):
        m = r % (2 * self.W)
        late = m // self.W
        return m * (1 - late) + (2 * self.W - 1 - m) * late

    def slot_of(self, r):
        return 2 * (r // (2 * self.W)) + (r % (2 * self.W)) // self.W

    def source(self, j, w):
        return self.source_in(j // 2, j % 2, w)

    def source_in(self, pair, late, w):
        if late:
            return 2 * self.W * pair + 2 * self.W - 1 - w
        return 2 * self.W * pair + w


def enter(rows):
    me = lax.axis_index("rep")
    barrier = pltpu.get_barrier_semaphore()
    for k in range(1, rows):
        pl.semaphore_signal(
            barrier, inc=1, device_id={"rep": (me + k) % rows}, device_id_type=MESH
        )
    pl.semaphore_wait(barrier, rows - 1)
    return me


def remote(src, dst, send, recv, to):
    return pltpu.make_async_remote_copy(
        src_ref=src,
        dst_ref=dst,
        send_sem=send,
        recv_sem=recv,
        device_id={"rep": to},
        device_id_type=MESH,
    )


def start_either(me, to, src, dst, send, recv):
    @pl.when(to == me)
    def _():
        pltpu.make_async_copy(src, dst, recv).start()

    @pl.when(to != me)
    def _():
        remote(src, dst, send, recv, to).start()


def end_either(me, to, src, dst, send, recv):
    @pl.when(to != me)
    def _():
        remote(src, dst, send, recv, to).wait_send()


def landed(ref, sem):
    pltpu.make_async_copy(ref, ref, sem).wait()


def scatter_tokens(plan, send, recv, send_sem, relay_sem, recv_sem):
    p = plan
    me = enter(p.R)
    w = me % p.W
    mine = p.worker_of(me)
    for u in range(p.U):
        start_either(me, u * p.W + mine, send.at[u], recv.at[me], send_sem.at[u], recv_sem.at[me])
    for j in range(p.J):
        r = p.source(j, w)
        landed(recv.at[r], recv_sem.at[r])
        for k in range(1, p.W):
            part = recv.at[r, :, pl.ds(DH, 2 * DH)]
            remote(
                part, part, relay_sem.at[k - 1, j], recv_sem.at[r], me - w + (w + k) % p.W
            ).start()
    for k in range(1, p.W):
        for j in range(p.J):
            r = p.source(j, (w + k) % p.W)
            landed(recv.at[r, :, pl.ds(DH, 2 * DH)], recv_sem.at[r])
    for u in range(p.U):
        end_either(me, u * p.W + mine, send.at[u], recv.at[me], send_sem.at[u], recv_sem.at[me])
    for k in range(1, p.W):
        for j in range(p.J):
            r = p.source(j, w)
            part = recv.at[r, :, pl.ds(DH, 2 * DH)]
            remote(
                part, part, relay_sem.at[k - 1, j], recv_sem.at[r], me - w + (w + k) % p.W
            ).wait_send()


def return_tokens(plan, send, recv, send_sem, recv_sem):
    p = plan
    me = enter(p.R)
    w = me % p.W
    unit = me // p.W
    for j in range(p.J):
        r = p.source(j, w)
        start_either(me, r, send.at[j], recv.at[unit], send_sem.at[j], recv_sem.at[unit])
    for u in range(p.U):
        landed(recv.at[u], recv_sem.at[u])
    for j in range(p.J):
        r = p.source(j, w)
        end_either(me, r, send.at[j], recv.at[unit], send_sem.at[j], recv_sem.at[unit])


def scatter_rows(plan, send, recv, send_sem, recv_sem):
    p = plan
    me = enter(p.R)
    mine = p.worker_of(me)
    slot = p.slot_of(me)
    for u in range(p.U):
        start_either(
            me, u * p.W + mine, send.at[u], recv.at[slot], send_sem.at[u], recv_sem.at[slot]
        )
    for j in range(p.J):
        landed(recv.at[j], recv_sem.at[j])
    for u in range(p.U):
        end_either(
            me, u * p.W + mine, send.at[u], recv.at[slot], send_sem.at[u], recv_sem.at[slot]
        )


def return_grads(plan, dq, dkv, recv, buf, out, send_sem, part_sem, got_sem, recv_sem):
    p = plan
    me = enter(p.R)
    w = me % p.W
    unit = me // p.W

    def give(k, j):
        to = (w + k) % p.W
        r = p.source(j, to)
        return remote(
            dkv.at[r],
            buf.at[k - 1, j],
            part_sem.at[k - 1, j],
            got_sem.at[k - 1, j],
            me - w + to,
        )

    for j in range(p.J):
        for k in range(1, p.W):
            give(k, j).start()
    for j in range(p.J):
        r = p.source(j, w)
        total = dkv[r].astype(F32)
        for k in range(1, p.W):
            landed(buf.at[k - 1, j], got_sem.at[k - 1, j])
            total = total + buf[k - 1, j].astype(F32)
        out[j, :, 0:DH, :] = dq[j]
        out[j, :, DH : 3 * DH, :] = total.astype(B16)
        start_either(me, r, out.at[j], recv.at[unit], send_sem.at[j], recv_sem.at[unit])
    for u in range(p.U):
        landed(recv.at[u], recv_sem.at[u])
    for j in range(p.J):
        r = p.source(j, w)
        end_either(me, r, out.at[j], recv.at[unit], send_sem.at[j], recv_sem.at[unit])
        for k in range(1, p.W):
            give(k, j).wait_send()


def comm_call(kernel, out, args, scratch, collective, name, space=pl.ANY):
    return pl.pallas_call(
        kernel,
        out_shape=jax.ShapeDtypeStruct(out, B16),
        in_specs=[pl.BlockSpec(memory_space=space)] * len(args),
        out_specs=pl.BlockSpec(memory_space=space),
        scratch_shapes=list(scratch),
        compiler_params=pltpu.CompilerParams(
            collective_id=collective, has_side_effects=True, vmem_limit_bytes=40 * 2**20
        ),
        name=name,
    )(*args)


def project_kernel(plan, hidden, gain, wq, wk, wv, a1_ref, send):
    p = plan
    x = hidden[...].reshape(p.S * p.T, D).astype(F32)
    a1 = (x * scale_of(x) * gain[0:1, :]).astype(B16)
    a1_ref[...] = a1
    for n, weight in enumerate((wq, wk, wv)):
        rows = dot(a1, mat(weight))
        for s in range(p.S):
            turned = jnp.transpose(rows[s * p.T : (s + 1) * p.T]).astype(B16)
            for i in range(H):
                send[s * p.G + i // p.HG, i % p.HG, n * DH : (n + 1) * DH, :] = turned[
                    i * DH : (i + 1) * DH
                ]


def bias_tiles(plan, w, line, tiles):
    p = plan
    far = line[:, 2 * p.T - 1 : 2 * p.T]
    near = pltpu.roll(jnp.broadcast_to(line, (p.T, 2 * p.T)), 0, 1, stride=1, stride_axis=0)
    key = lax.broadcasted_iota(jnp.int32, (p.T, p.T), 0)
    query = lax.broadcasted_iota(jnp.int32, (p.T, p.T), 1)
    same = jnp.where(query >= key, near[:, : p.T], HIDE)
    next_ = near[:, p.T :]
    farb = jnp.broadcast_to(far, (p.T, p.T))
    tiles[0] = jnp.broadcast_to(far, (p.CK, 2 * p.T))
    for a in range(2):
        ahead = w if a == 0 else 2 * p.W - 1 - w
        for b in range(2 * p.W):
            diff = ahead - b
            tile = jnp.where(
                diff == 0, same, jnp.where(diff == 1, next_, jnp.where(diff < 0, HIDE, farb))
            )
            tiles[2, b * p.T : (b + 1) * p.T, a * p.T : (a + 1) * p.T] = tile
            back = diff + 2 * p.W
            tiles[1, b * p.T : (b + 1) * p.T, a * p.T : (a + 1) * p.T] = jnp.where(
                back == 1, next_, farb
            )


def block_pair(plan, ref, pair, w, h):
    p = plan
    return jnp.concatenate(
        [ref[p.source_in(pair, late, w), h, 0:DH, :] for late in range(2)], axis=1
    )


def in_two(count, body, carry, between):
    if between is None:
        return lax.fori_loop(0, count, body, carry)
    carry = lax.fori_loop(0, count - 1, body, carry)
    between()
    return lax.fori_loop(count - 1, count, body, carry)


def line_of(p, block, head):
    return block[pl.ds(3 + head, 1), 0 : 2 * p.T]


def attend_head(p, w, h, line, recv, o_ref, of_ref, rl, kn, vt, tiles, between=None):
    bias_tiles(p, w, line, tiles)
    for r in range(p.R):
        kn[r * p.T : (r + 1) * p.T, :] = jnp.transpose(
            recv[r, h, DH : 2 * DH, :].astype(F32)
        ).astype(B16)
        vt[0:DH, r * p.T : (r + 1) * p.T] = recv[r, h, 2 * DH : 3 * DH, :]
    vt[DH : DH + ONES, :] = jnp.ones((ONES, p.L), B16)

    def one_pair(pair, carry):
        qt = block_pair(p, recv, pair, w, h)

        def step(i, acc):
            start = pl.multiple_of(i * p.CK, p.CK)
            e = jnp.exp(dot(kn[pl.ds(start, p.CK), :], qt) + tiles[jnp.maximum(i - pair + 2, 0)])
            return acc + dot(vt[:, pl.ds(start, p.CK)], e.astype(B16))

        acc = lax.fori_loop(0, pair + 1, step, jnp.zeros((DH + ONES, 2 * p.T), F32))
        scale = 1.0 / acc[DH : DH + 1]
        of = acc[:DH] * scale
        rl[pair] = scale
        for a in range(2):
            part = of[:, a * p.T : (a + 1) * p.T]
            of_ref[2 * pair + a, h] = part
            o_ref[2 * pair + a, h] = part.astype(B16)
        return carry

    in_two(p.NP, one_pair, 0, between)


def attend_scratch(p):
    return [
        pltpu.VMEM((p.L, DH), B16),
        pltpu.VMEM((DH + ONES, p.L), B16),
        pltpu.VMEM((3, p.CK, 2 * p.T), F32),
    ]


def attend_kernel(plan, recv, block, o_ref, of_ref, rl_ref, *scratch):
    p = plan
    me = lax.axis_index("rep")
    w = me % p.W
    group = (me // p.W) % p.G
    h = pl.program_id(0)
    line = line_of(p, block, group * p.HG + h)
    attend_head(p, w, h, line, recv, o_ref, of_ref, rl_ref.at[h], *scratch)


def back_head(
    p,
    w,
    h,
    line,
    recv,
    dout,
    of_ref,
    rl,
    dq_ref,
    dkv_ref,
    kn,
    vn,
    kt,
    dk,
    dv,
    tiles,
    near,
    between=None,
):
    bias_tiles(p, w, line, tiles)
    for r in range(p.R):
        kn[r * p.T : (r + 1) * p.T, :] = jnp.transpose(
            recv[r, h, DH : 2 * DH, :].astype(F32)
        ).astype(B16)
        vn[r * p.T : (r + 1) * p.T, :] = jnp.transpose(
            recv[r, h, 2 * DH : 3 * DH, :].astype(F32)
        ).astype(B16)
        kt[0:DH, r * p.T : (r + 1) * p.T] = recv[r, h, DH : 2 * DH, :]
    kt[DH : DH + ONES, :] = jnp.ones((ONES, p.L), B16)
    dk[...] = jnp.zeros_like(dk)
    dv[...] = jnp.zeros_like(dv)
    near[...] = jnp.zeros_like(near)

    def one_pair(pair, total):
        qt = block_pair(p, recv, pair, w, h)
        dot_rows = jnp.concatenate([dout[2 * pair + a, h] for a in range(2)], axis=1)
        of = jnp.concatenate([of_ref[2 * pair + a, h] for a in range(2)], axis=1)
        delta = jnp.sum(dot_rows.astype(F32) * of, axis=0, keepdims=True)
        scale = rl[pair]
        qn = jnp.transpose(qt.astype(F32)).astype(B16)
        don = jnp.transpose(dot_rows.astype(F32)).astype(B16)

        def step(i, acc):
            start = pl.multiple_of(i * p.CK, p.CK)
            kind = jnp.maximum(i - pair + 2, 0)
            keys = pl.ds(start, p.CK)
            prob = jnp.exp(dot(kn[keys, :], qt) + tiles[kind]) * scale
            ds = (prob * (dot(vn[keys, :], dot_rows) - delta)).astype(B16)
            near[kind] += ds.astype(F32)
            dk[keys, :] += dot(ds, qn)
            dv[keys, :] += dot(prob.astype(B16), don)
            return acc + dot(kt[:, keys], ds)

        acc = lax.fori_loop(0, pair + 1, step, jnp.zeros((DH + ONES, 2 * p.T), F32))
        for a in range(2):
            dq_ref[2 * pair + a, h] = acc[:DH, a * p.T : (a + 1) * p.T].astype(B16)
        return total + acc[DH : DH + 1]

    total = in_two(p.NP, one_pair, jnp.zeros((1, 2 * p.T), F32), between)
    for r in range(p.R):
        dkv_ref[r, h, 0:DH, :] = jnp.transpose(dk[r * p.T : (r + 1) * p.T, :]).astype(B16)
        dkv_ref[r, h, DH : 2 * DH, :] = jnp.transpose(dv[r * p.T : (r + 1) * p.T, :]).astype(B16)
    same = jnp.zeros((p.T, p.T), F32)
    next_ = jnp.zeros((p.T, p.T), F32)
    for a in range(2):
        ahead = w if a == 0 else 2 * p.W - 1 - w
        for b in range(2 * p.W):
            diff = ahead - b
            spot = (slice(b * p.T, (b + 1) * p.T), slice(a * p.T, (a + 1) * p.T))
            tile = near[(2, *spot)]
            same = same + jnp.where(diff == 0, tile, 0.0)
            next_ = next_ + jnp.where(diff == 1, tile, 0.0)
            next_ = next_ + jnp.where(diff + 2 * p.W == 1, near[(1, *spot)], 0.0)
    both = jnp.concatenate([same, next_], axis=1)
    key = lax.broadcasted_iota(jnp.int32, (p.T, p.T), 0)
    other = lax.broadcasted_iota(jnp.int32, (p.T, p.T), 1)
    swap = (key + other == p.T - 1).astype(F32)
    turned = lax.dot_general(
        swap,
        both,
        (((1,), (0,)), ((), ())),
        precision=lax.Precision.HIGHEST,
        preferred_element_type=F32,
    )
    turned = pltpu.roll(turned, p.T + 1, 1, stride=1, stride_axis=0)
    by_distance = jnp.sum(turned, axis=0, keepdims=True)
    rest = jnp.sum(total) - jnp.sum(both)
    place = lax.broadcasted_iota(jnp.int32, (1, 2 * p.T), 1)
    return by_distance + jnp.where(place == 2 * p.T - 1, rest, 0.0)


def back_scratch(p):
    return [
        pltpu.VMEM((p.L, DH), B16),
        pltpu.VMEM((p.L, DH), B16),
        pltpu.VMEM((DH + ONES, p.L), B16),
        pltpu.VMEM((p.L, DH), F32),
        pltpu.VMEM((p.L, DH), F32),
        pltpu.VMEM((3, p.CK, 2 * p.T), F32),
        pltpu.VMEM((3, p.CK, 2 * p.T), F32),
    ]


def attend_back_kernel(plan, recv, block, dout, of_ref, rl_ref, dq_ref, dkv_ref, line_ref, *scratch):
    p = plan
    me = lax.axis_index("rep")
    w = me % p.W
    group = (me // p.W) % p.G
    h = pl.program_id(0)
    line_ref[h] = back_head(
        p,
        w,
        h,
        line_of(p, block, group * p.HG + h),
        recv,
        dout,
        of_ref,
        rl_ref.at[h],
        dq_ref,
        dkv_ref,
        *scratch,
    )


def encode_kernel(enc, wk, wv, kn, kt, vn, vt):
    encode_one(enc, wk, kn, kt)
    encode_one(enc, wv, vn, vt)


def encode_one(enc, weight, natural, turned):
    value = dot(mat(enc), mat(weight))
    natural[...] = value.astype(B16)
    flipped = jnp.transpose(value).astype(B16)
    if len(turned.shape) == 2:
        turned[...] = flipped
        return
    for i in range(H // 2):
        turned[i, 0 : 2 * DH, :] = flipped[2 * i * DH : 2 * (i + 1) * DH]
        turned[i, 2 * DH : 2 * DH + ONES, :] = jnp.ones((ONES, turned.shape[2]), B16)


def apart(pair, axis, other):
    twice = jnp.concatenate([pair, pair], axis=axis)
    half = (pair.shape[axis], pair.shape[other] // 2)
    one = lax.broadcasted_iota(jnp.int32, twice.shape, axis) < half[0]
    two = lax.broadcasted_iota(jnp.int32, twice.shape, other) < half[1]
    return jnp.where(one == two, twice, jnp.zeros_like(twice))


def rows_of(units, s, seqs):
    groups = units.shape[0] // seqs
    return units[s * groups : (s + 1) * groups].reshape(-1, units.shape[-1])


def cross_kernel(
    seqs,
    hidden,
    ot,
    wo,
    gain,
    wcq,
    wco,
    kn,
    vt,
    x1_ref,
    x2_ref,
    a2_ref,
    qt_ref,
    of_ref,
    rl_ref,
    pause=lambda: None,
):
    toks = hidden.shape[1]
    span = kn.shape[0] // seqs
    x = hidden[...].reshape(seqs * toks, D).astype(F32)
    o = jnp.concatenate(
        [jnp.transpose(rows_of(ot, s, seqs).astype(F32)) for s in range(seqs)], axis=0
    ).astype(B16)
    x1 = x + dot(o, mat(wo))
    x1_ref[...] = x1
    a2 = (x1 * scale_of(x1) * gain[1:2, :]).astype(B16)
    a2_ref[...] = a2
    q2 = dot(a2, mat(wcq))
    for s in range(seqs):
        qt_ref[s] = jnp.transpose(q2[s * toks : (s + 1) * toks]).astype(B16)
    pause()

    def heads(i, carry):
        col = pl.multiple_of(2 * i * DH, 2 * DH)
        for s in range(seqs):
            keys = slice(s * span, (s + 1) * span)
            q_pair = apart(qt_ref[s, pl.ds(col, 2 * DH), :], 1, 0)
            e = jnp.exp(dot(kn[keys, pl.ds(col, 2 * DH)], q_pair))
            acc = dot(vt[i, :, keys], e.astype(B16))
            rl = 1.0 / acc[2 * DH : 2 * DH + 1]
            both = acc * rl
            of_ref[s, pl.ds(col, DH), :] = both[:DH, :toks]
            of_ref[s, pl.ds(col + DH, DH), :] = both[DH : 2 * DH, toks:]
            rl_ref[s, i] = rl
        return carry

    lax.fori_loop(0, H // 2, heads, 0)
    pause()
    o2 = jnp.concatenate([jnp.transpose(of_ref[s]) for s in range(seqs)], axis=0).astype(B16)
    x2_ref[...] = x1_ref[...] + dot(o2, mat(wco))


def ffn_products(rows, og, wg, wu, wd, acc, da3):
    gate = dot(rows, wg[...])
    up = dot(rows, wu[...])
    square = gate * gate
    th = jnp.tanh(GELU_A * gate * (1.0 + GELU_B * square))
    half = 0.5 * (1.0 + th)
    value = gate * half
    slope = half + 0.5 * gate * (1.0 - th * th) * (GELU_A * (1.0 + 3.0 * GELU_B * square))
    inner = (value * up).astype(B16)
    acc[...] += dot(inner, wd[...])
    dwd = t_dot(inner, og).astype(B16)
    dinner = dot_t(og, wd[...]).astype(B16).astype(F32)
    dgate = (dinner * up * slope).astype(B16)
    dup = (dinner * value).astype(B16)
    da3[...] += dot_t(dgate, wg[...]) + dot_t(dup, wu[...])
    return t_dot(rows, dgate).astype(B16), t_dot(rows, dup).astype(B16), dwd


def ffn_kernel(
    x2_ref, og_ref, gain, wg, wu, wd, out_ref, dx2_ref, dgain_ref, dwg, dwu, dwd, a3, acc, da3
):
    step = pl.program_id(0)

    @pl.when(step == 0)
    def _():
        x2 = x2_ref[...]
        a3[...] = (x2 * scale_of(x2) * gain[2:3, :]).astype(B16)
        acc[...] = x2
        da3[...] = jnp.zeros_like(da3)

    dwg[...], dwu[...], dwd[...] = ffn_products(a3[...], og_ref[...], wg, wu, wd, acc, da3)

    @pl.when(step == pl.num_programs(0) - 1)
    def _():
        out_ref[...] = acc[...].astype(B16)
        dv, dgain = norm_back(x2_ref[...], gain[2:3, :], da3[...])
        dx2_ref[...] = og_ref[...].astype(F32) + dv
        dgain_ref[...] = dgain


def cross_back_kernel(
    seqs,
    groups,
    dx2_ref,
    x1_ref,
    a2_ref,
    gain,
    qt_ref,
    of_ref,
    rl_ref,
    kn,
    kt,
    vn,
    enc,
    wco,
    wcq,
    wck,
    wcv,
    wo,
    ot,
    dx1_ref,
    dgain_ref,
    dot_ref,
    denc_ref,
    dwco,
    dwcq,
    dwck,
    dwcv,
    dwo,
    dt,
    dqt,
    dk,
    dv,
    need=lambda *refs: None,
    done=lambda ref: None,
):
    toks = qt_ref.shape[2]
    span = kn.shape[0] // seqs
    dx2 = dx2_ref[...]
    dc = dx2.astype(B16)
    o2t = [of_ref[s].astype(B16) for s in range(seqs)]
    total = dot(o2t[0], dc[0:toks])
    for s in range(1, seqs):
        total = total + dot(o2t[s], dc[s * toks : (s + 1) * toks])
    dwco[...] = total.astype(B16)
    done(dwco)
    need(wco)
    do2 = dot_t(dc, mat(wco))
    for s in range(seqs):
        dt[s] = jnp.transpose(do2[s * toks : (s + 1) * toks]).astype(B16)

    need(kn, kt, vn)

    def heads(i, carry):
        col = pl.multiple_of(2 * i * DH, 2 * DH)
        pair = pl.ds(col, 2 * DH)
        for s in range(seqs):
            keys = slice(s * span, (s + 1) * span)
            q_rows, d_rows = qt_ref[s, pair, :], dt[s, pair, :]
            q_pair = apart(jnp.transpose(q_rows.astype(F32)), 0, 1).astype(B16)
            d_pair = apart(jnp.transpose(d_rows.astype(F32)), 0, 1).astype(B16)
            prob = jnp.exp(dot(kn[keys, pair], apart(q_rows, 1, 0))) * rl_ref[s, i]
            terms = d_rows.astype(F32) * of_ref[s, pair, :]
            delta = jnp.concatenate(
                [jnp.sum(terms[n * DH : (n + 1) * DH], axis=0, keepdims=True) for n in range(2)],
                axis=1,
            )
            ds = (prob * (dot(vn[keys, pair], apart(d_rows, 1, 0)) - delta)).astype(B16)
            dq = dot(kt[pair, keys], ds).astype(B16)
            dqt[s, pl.ds(col, DH), :] = dq[:DH, :toks]
            dqt[s, pl.ds(col + DH, DH), :] = dq[DH:, toks:]
            dk[keys, pair] = dot(ds, q_pair).astype(B16)
            dv[keys, pair] = dot(prob.astype(B16), d_pair).astype(B16)
        return carry

    lax.fori_loop(0, H // 2, heads, 0)
    need(enc, wck, wcv, wcq, wo)
    dwck[...] = t_dot(mat(enc), dk[...]).astype(B16)
    done(dwck)
    dwcv[...] = t_dot(mat(enc), dv[...]).astype(B16)
    done(dwcv)
    denc_ref[...] = (dot_t(dk[...], mat(wck)) + dot_t(dv[...], mat(wcv))).astype(B16)
    done(denc_ref)
    dq2 = jnp.concatenate(
        [jnp.transpose(dqt[s].astype(F32)) for s in range(seqs)], axis=0
    ).astype(B16)
    dwcq[...] = t_dot(a2_ref[...], dq2).astype(B16)
    done(dwcq)
    term, dgain = norm_back(x1_ref[...], gain[1:2, :], dot_t(dq2, mat(wcq)))
    dgain_ref[...] = dgain
    dx1 = dx2 + term
    dx1_ref[...] = dx1
    db = dx1.astype(B16)
    total = dot(rows_of(ot, 0, seqs), db[0:toks])
    for s in range(1, seqs):
        total = total + dot(rows_of(ot, s, seqs), db[s * toks : (s + 1) * toks])
    dwo[...] = total.astype(B16)
    done(dwo)
    do = dot_t(db, mat(wo))
    width = D // groups
    for s in range(seqs):
        turned = jnp.transpose(do[s * toks : (s + 1) * toks]).astype(B16)
        for g in range(groups):
            dot_ref[s * groups + g] = turned[g * width : (g + 1) * width].reshape(
                dot_ref.shape[1:]
            )


def cross_back_moves_kernel(kernel, ins, outs, far_ins, far_outs, *refs):
    refs = list(refs)
    take = lambda n: [refs.pop(0) for _ in range(n)]
    args, results, scratch = take(ins), take(outs), take(4)
    near_in, near_out = take(len(far_ins)), take(len(far_outs))
    moves = Moves(refs[0])
    moves.bring([(args[i], near) for i, near in zip(far_ins, near_in)])
    for i, near in zip(far_ins, near_in):
        args[i] = near
    made = {}
    for i, near in zip(far_outs, near_out):
        made[id(near)] = (near, results[i])
        results[i] = near

    def done(ref):
        moves.take(*made[id(ref)])

    kernel(*args, *results, *scratch, need=moves.need, done=done)
    moves.end()


def cross_back_moves_call(kernel, outs, args, scratch):
    near = pl.BlockSpec(memory_space=pltpu.VMEM)
    anywhere = pl.BlockSpec(memory_space=pl.ANY)
    far_ins = [11, 7, 8, 9, 10, 13, 14, 12, 15]
    far_outs = [3, 4, 5, 6, 7, 8]
    scratch = [*scratch]
    scratch += [pltpu.VMEM(args[i].shape, args[i].dtype) for i in far_ins]
    scratch += [pltpu.VMEM(*outs[i]) for i in far_outs]
    scratch += [pltpu.SemaphoreType.DMA((len(far_ins) + len(far_outs),))]
    return pl.pallas_call(
        functools.partial(
            cross_back_moves_kernel, kernel, len(args), len(outs), far_ins, far_outs
        ),
        out_shape=[jax.ShapeDtypeStruct(s, t) for s, t in outs],
        in_specs=[anywhere if i in far_ins else near for i in range(len(args))],
        out_specs=[anywhere if i in far_outs else near for i in range(len(outs))],
        scratch_shapes=scratch,
        compiler_params=pltpu.CompilerParams(vmem_limit_bytes=60 * 2**20),
        name="cross_back",
    )(*args)


def last_kernel(plan, hidden, grads, a1, gain, dx1, wq, wk, wv, dh_ref, dgain_ref, dwq, dwk, dwv):
    dgain_ref[...] = last_products(
        plan, hidden, grads, a1, gain, dx1, wq, wk, wv, dh_ref, dwq, dwk, dwv
    )


def last_products(p, hidden, grads, a1, gain, dx1, wq, wk, wv, dh_ref, dwq, dwk, dwv):
    x = hidden[...].reshape(p.S * p.T, D).astype(F32)
    da1 = jnp.zeros((p.S * p.T, D), F32)
    for n, (weight, dw) in enumerate(((wq, dwq), (wk, dwk), (wv, dwv))):
        rows = []
        for s in range(p.S):
            turned = jnp.concatenate(
                [
                    grads[s * p.G + i // p.HG, i % p.HG, n * DH : (n + 1) * DH, :]
                    for i in range(H)
                ],
                axis=0,
            )
            rows.append(jnp.transpose(turned.astype(F32)))
        d = jnp.concatenate(rows, axis=0).astype(B16)
        dw[...] = t_dot(a1[...], d).astype(B16).reshape(dw.shape)
        da1 = da1 + dot_t(d, mat(weight))
    term, dgain = norm_back(x, gain[0:1, :], da1)
    dh_ref[...] = (dx1[...] + term).astype(B16).reshape(dh_ref.shape)
    return dgain


def gather_rows(part):
    count = lax.axis_size("shard")
    rows, cols = part.shape
    half = rows // 2
    mine = lax.axis_index("shard")
    core = lax.axis_index("rep") % 2
    pairs = [(r, r ^ 1) for r in range(lax.axis_size("rep"))]
    own = lax.dynamic_slice(part, (core * half, 0), (half, cols))
    full = jnp.zeros((count, rows, cols), part.dtype)
    full = lax.dynamic_update_slice(full, part[None], (mine, 0, 0))
    for k in range(1, count):
        got = lax.ppermute(own, "shard", [(i, (i + k) % count) for i in range(count)])
        also = lax.ppermute(got, "rep", pairs)
        owner = (mine - k) % count
        full = lax.dynamic_update_slice(full, got[None], (owner, core * half, 0))
        full = lax.dynamic_update_slice(full, also[None], (owner, (1 - core) * half, 0))
    return full.reshape(count * rows, cols)


def reduce_grads(grads):
    owned = [lax.psum_scatter(g, "shard", scatter_dimension=0, tiled=True) for g in grads]
    summed = lax.psum(tuple(owned), "rep")
    return [s.astype(F32) for s in summed]


class Moves:
    def __init__(self, sems):
        self.sems, self.used, self.coming, self.going = sems, 0, {}, []

    def sem(self):
        self.used += 1
        return self.sems.at[self.used - 1]

    def bring(self, pairs):
        for far, near in pairs:
            sem = self.sem()
            pltpu.make_async_copy(far, near, sem).start()
            self.coming[id(near)] = (near, sem)

    def need(self, *refs):
        for ref in refs:
            if id(ref) in self.coming:
                near, sem = self.coming.pop(id(ref))
                landed(near, sem)

    def take(self, near, far):
        sem = self.sem()
        pltpu.make_async_copy(near, far, sem).start()
        self.going.append((near, sem))

    def end(self):
        for near, sem in self.going:
            landed(near, sem)


BITS = 4
ROW = -1


class Job:
    def __init__(self, result, row, rows, col, cols, order):
        self.result, self.order = result, order
        self.row, self.rows, self.col, self.cols = row, rows, col, cols

    def buffers(self):
        half, rows, lead = self.cols // 2, self.rows, (2,)
        shapes = [(2, rows, half)] * 2
        for axis in self.order:
            if axis == ROW:
                lead = ()
            else:
                rows //= 2
            shapes.append((*lead, rows, half))
        return shapes


def partner(bit):
    me = lax.axis_index("rep")
    half = 2**bit
    mine = (me // half) % 2
    return mine, me + half * (1 - 2 * mine)


def to_rep(src, dst, send, recv, bit):
    return remote(src, dst, send, recv, partner(bit)[1])


def to_row(src, dst, send, recv):
    x = lax.axis_index("shard")
    return pltpu.make_async_remote_copy(
        src_ref=src,
        dst_ref=dst,
        send_sem=send,
        recv_sem=recv,
        device_id={"shard": 1 - x},
        device_id_type=MESH,
    )


def add_into(acc, term, rows):
    step = 16 if rows % 32 else 32

    def body(i, carry):
        at = pl.ds(pl.multiple_of(i * step, step), step)
        acc[at, :] = (acc[at, :].astype(F32) + term[at, :].astype(F32)).astype(B16)
        return carry

    lax.fori_loop(0, rows // step, body, 0)


class JobRun:
    def __init__(self, job, source, result, bufs, sems, index):
        self.job, self.source, self.result = job, source, result
        self.acc, self.core, *self.part = bufs
        self.steps = [(0, 1), (1, FIRST_LAG)] + [(n, LAG) for n in range(2, 10)]
        send, recv, local = sems
        self.send = [send.at[index, i] for i in range(9)]
        self.recv = [recv.at[index, i] for i in range(9)]
        self.local = [local.at[index, i] for i in range(2)]
        self.sent = []
        self.x = lax.axis_index("shard")
        half = job.cols // 2
        core = partner(0)[0]
        self.mine = pl.ds(pl.multiple_of(job.col + core * half, 128), half)
        self.other = pl.ds(pl.multiple_of(job.col + (1 - core) * half, 128), half)
        self.all = pl.ds(job.row, job.rows)
        self.plan, self.back = [], []
        owners, first, count = (0, 1), 0, job.rows
        for axis in job.order:
            if axis == ROW:
                keep = give = (first, count)
                owners, others = (self.x,), (1 - self.x,)
            else:
                count //= 2
                bit = partner(axis)[0]
                keep, give = (first + bit * count, count), (first + (1 - bit) * count, count)
                self.back.insert(0, (axis, (first, 2 * count), give))
                first, others = keep[0], owners
            self.plan.append((axis, owners, keep, others, give))
        self.last = (first, count)

    def span(self, first, count):
        return pl.ds(pl.multiple_of(first, 16), count)

    def out(self, first, count):
        return self.result.at[self.span(self.job.row + first, count), self.mine]

    def held(self, owners, rows):
        at = slice(None) if len(owners) == 2 else owners[0]
        return self.acc.at[at, self.span(*rows)]

    def go(self, n, source, target, axis):
        copy = (to_row if axis == ROW else to_rep)(
            source, target, self.send[n], self.recv[n], *(() if axis == ROW else (axis,))
        )
        copy.start()
        self.sent.append(copy)

    def stage(self, n):
        job = self.job
        if n == 0:
            pltpu.make_async_copy(
                self.source.at[:, self.all, self.mine], self.acc, self.local[0]
            ).start()
            self.go(0, self.source.at[:, self.all, self.other], self.core, 0)
        elif n <= 5:
            if n == 1:
                landed(self.acc, self.local[0])
                landed(self.core, self.recv[0])
                for i in range(2):
                    add_into(self.acc.at[i], self.core.at[i], job.rows)
            else:
                _, owners, keep, _, _ = self.plan[n - 2]
                terms = self.part[n - 2]
                landed(terms, self.recv[n - 1])
                for i, owner in enumerate(owners):
                    add_into(
                        self.held((owner,), keep),
                        terms.at[i] if len(owners) == 2 else terms,
                        keep[1],
                    )
            if n < 5:
                axis, _, _, others, give = self.plan[n - 1]
                self.go(n, self.held(others, give), self.part[n - 1], axis)
            else:
                piece, place = self.held((self.x,), self.last), self.out(*self.last)
                pltpu.make_async_copy(piece, place, self.local[1]).start()
                self.go(5, piece, place, self.back[0][0])
        elif n <= 8:
            if n == 6:
                landed(self.out(*self.last), self.local[1])
            _, rows, came = self.back[n - 6]
            landed(self.out(*came), self.recv[n - 1])
            place = self.out(*rows)
            self.go(n, place, place, self.back[n - 5][0] if n < 8 else 0)
        else:
            landed(self.result.at[self.all, self.other], self.recv[8])
            for copy in self.sent:
                copy.wait_send()


def job_buffers(job):
    return [pltpu.VMEM(shape, B16) for shape in job.buffers()]


class SmallRun:
    steps = [(n, 1) for n in range(BITS + 2)]

    def __init__(self, sums, terms, send, recv):
        self.sums, self.terms, self.send, self.recv = sums, terms, send, recv

    def copy(self, n):
        args = (self.sums.at[n], self.terms.at[n], self.send.at[n], self.recv.at[n])
        return to_row(*args) if n == BITS else to_rep(*args, n)

    def stage(self, n):
        if n > 0:
            landed(self.terms.at[n - 1], self.recv.at[n - 1])
            self.sums[n] = self.sums[n - 1] + self.terms[n - 1]
        if n <= BITS:
            self.copy(n).start()
        else:
            for i in range(BITS + 1):
                self.copy(i).wait_send()


class EncodedRun:
    def __init__(self, source, result, bufs, send, recv, load, lag):
        self.source, self.result, self.send, self.recv, self.load = source, result, send, recv, load
        self.acc, self.terms = bufs[0], bufs[1:]
        self.bits = [partner(b)[0] for b in range(BITS)]
        self.steps = [(0, 1)] + [(n + 1, lag) for n in range(1, BITS + 1)]
        self.sent = []

    def part(self, ref, n, bit):
        at = (slice(None),) * (BITS - n) + (bit,)
        return ref.at[at]

    def go(self, n, source):
        copy = to_rep(source, self.terms[n], self.send.at[n], self.recv.at[n], n)
        copy.start()
        self.sent.append(copy)

    def fixed(self, n):
        return self.acc.at[
            (slice(None),) * (BITS + 1 - n) + tuple(self.bits[b] for b in range(n - 1, 0, -1))
        ]

    def add(self, n):
        left = self.fixed(n + 1)
        terms = self.terms[n]
        lead = left.shape[:-2]
        count = 1
        for d in lead:
            count *= d

        def body(i, carry):
            at, rest = [], i
            for d in reversed(lead):
                at.insert(0, rest % d)
                rest = rest // d
            at = tuple(at)
            left[at] = (left[at].astype(F32) + terms[at].astype(F32)).astype(B16)
            return carry

        lax.fori_loop(0, count, body, 0)

    def stage(self, step):
        if step == 0:
            pltpu.make_async_copy(
                self.part(self.source, 0, self.bits[0]), self.acc, self.load
            ).start()
            self.go(0, self.part(self.source, 0, 1 - self.bits[0]))
            return
        n = step - 1
        if n == 1:
            landed(self.acc, self.load)
        landed(self.terms[n - 1], self.recv.at[n - 1])
        self.add(n - 1)
        if n < BITS:
            self.go(n, self.part(self.fixed(n), n, 1 - self.bits[n]))
        else:
            self.result[...] = self.fixed(BITS)[...]
            for copy in self.sent:
                copy.wait_send()


class Pipeline:
    def __init__(self):
        self.waiting, self.active, self.now = [], [], 0

    def add(self, runs):
        self.waiting += runs

    def tick(self, count=1):
        for _ in range(count):
            if self.waiting:
                self.active.insert(0, [self.waiting.pop(0), 0, self.now])
            early = [e for e in self.active if e[0].steps[e[1]][0] < 2]
            late = [e for e in self.active if e[0].steps[e[1]][0] >= 2]
            for entry in early + late:
                run, at, due = entry
                if due <= self.now:
                    stage, wait = run.steps[at]
                    run.stage(stage)
                    entry[1:] = [at + 1, self.now + wait]
            self.active = [e for e in self.active if e[1] < len(e[0].steps)]
            self.now += 1

    def finish(self):
        while self.waiting or self.active:
            self.tick()


def jobs_of(result, rows, cols, orders):
    wide = cols // 2 if cols > 1024 else cols
    tall = rows // 2 if rows > 512 else rows
    return [
        Job(result, row, tall, col, wide, next(orders))
        for row in range(0, rows, tall)
        for col in range(0, cols, wide)
    ]


EARLY = [(ROW, 1, 2, 3), (ROW, 2, 1, 3), (ROW, 1, 2, 3), (ROW, 1, 2, 3)]
LATE = [(ROW, 1, 2, 3)] * 3
SMALL_ROWS = 16
FETCH_LAG = 3
FIRST_LAG = 3
LAG = 2
TICKS = (4, 1, 1, 2)


def tail_kernel(p, jobs, early, arrays, *refs):
    refs = list(refs)
    take = lambda n: [refs.pop(0) for _ in range(n)]
    sources = take(early)
    dot_, denc, *far = take(7)
    lines, rl_ref, hidden, a1, dx1, dgc, dgf = take(7)
    results = take(arrays)
    small, dh_ref, denc_out = take(3)
    dout, dq, dkv, part, out, grads = take(6)
    late = take(3)
    recv, of_ref, wq, wk, wv = held = take(5)
    enc_bufs = take(BITS + 1)
    enc_send, enc_recv, enc_load, move_sems = take(4)
    small_sums, small_terms = take(2)
    back = take(7)
    rows_send, rows_recv, part_sem, got_sem, ret_send, ret_recv = take(6)
    small_send, small_recv = take(2)
    sems = take(3)
    moves = Moves(move_sems)
    moves.bring(zip(far, held))
    sources = sources + late
    runs = []
    for i, job in enumerate(jobs):
        bufs = take(len(job.buffers()))
        runs.append(JobRun(job, sources[job.result], results[job.result], bufs, sems, i))
    ready = len(jobs) - 3
    enc_run = EncodedRun(denc, denc_out, enc_bufs, enc_send, enc_recv, enc_load.at[0], LAG)

    me = lax.axis_index("rep")
    w = me % p.W
    unit = me // p.W
    group = unit % p.G
    mine = p.worker_of(me)
    slot = p.slot_of(me)
    barrier = pltpu.get_barrier_semaphore()
    for k in range(1, p.R):
        pl.semaphore_signal(
            barrier, inc=1, device_id={"rep": (me + k) % p.R}, device_id_type=MESH
        )
    x = lax.axis_index("shard")
    pl.semaphore_signal(barrier, inc=1, device_id={"shard": 1 - x}, device_id_type=MESH)
    pl.semaphore_wait(barrier, p.R)

    pipeline = Pipeline()
    pipeline.add([*runs[:2], enc_run, *runs[2:ready]])
    tick = pipeline.tick
    def outward(u, h):
        to, sem = u * p.W + mine, rows_recv.at[slot, h]
        return me, to, dot_.at[u, h], dout.at[slot, h], rows_send.at[u, h], sem

    def give(k, j, h):
        to = (w + k) % p.W
        return remote(
            dkv.at[p.source(j, to), h],
            part.at[k - 1, j, h],
            part_sem.at[k - 1, j, h],
            got_sem.at[k - 1, j, h],
            me - w + to,
        )

    def returned(j, h):
        r, sem = p.source(j, w), ret_recv.at[unit, h]
        return me, r, out.at[j, h], grads.at[unit, h], ret_send.at[j, h], sem

    def return_all(h):
        for j in range(p.J):
            total = dkv[p.source(j, w), h].astype(F32)
            for k in range(1, p.W):
                landed(part.at[k - 1, j, h], got_sem.at[k - 1, j, h])
                total = total + part[k - 1, j, h].astype(F32)
            out[j, h, 0:DH, :] = dq[j, h]
            out[j, h, DH : 3 * DH, :] = total.astype(B16)
            start_either(*returned(j, h))

    for h in range(p.HG):
        for u in range(p.U):
            start_either(*outward(u, h))
    tick(TICKS[0])
    lines_at = lax.broadcasted_iota(jnp.int32, (SMALL_ROWS, D), 0)
    block = jnp.zeros((SMALL_ROWS, D), F32)
    moves.need(recv, of_ref)
    for h in range(p.HG):
        for j in range(p.J):
            landed(dout.at[j, h], rows_recv.at[j, h])
        between = functools.partial(return_all, h - 1) if h > 0 else None
        sums = back_head(
            p,
            w,
            h,
            line_of(p, lines, group * p.HG + h),
            recv,
            dout,
            of_ref,
            rl_ref.at[h],
            dq,
            dkv,
            *back,
            between=between,
        )
        for j in range(p.J):
            for k in range(1, p.W):
                give(k, j, h).start()
        sums = jnp.concatenate([sums, jnp.zeros((1, D - 2 * p.T), F32)], axis=1)
        block = jnp.where(lines_at == 3 + group * p.HG + h, sums, block)
        tick(TICKS[1])
    tick(TICKS[2])
    return_all(p.HG - 1)
    tick(TICKS[3])
    for u in range(p.U):
        for h in range(p.HG):
            landed(grads.at[u, h], ret_recv.at[u, h])
    moves.need(wq, wk, wv)
    dgain = last_products(p, hidden, grads, a1, lines, dx1, wq, wk, wv, dh_ref, *late)
    for i, row in enumerate((dgain, dgc[...], dgf[...])):
        block = jnp.where(lines_at == i, row, block)
    small_sums[0] = block
    pipeline.add([*runs[ready:], SmallRun(small_sums, small_terms, small_send, small_recv)])
    pipeline.finish()
    small[...] = small_sums[BITS + 1]
    moves.end()
    for h in range(p.HG):
        for u in range(p.U):
            end_either(*outward(u, h))
        for j in range(p.J):
            end_either(*returned(j, h))
            for k in range(1, p.W):
                give(k, j, h).wait_send()


def tail_call(p, early, dot_, denc, far, held, collective):
    half = D // 2
    shapes = [g.shape[1:] for g in early] + [(half, D)] * 3
    turn = itertools.cycle(EARLY)
    jobs = [job for i in range(len(early)) for job in jobs_of(i, *shapes[i], turn)]
    jobs += [Job(len(early) + i, 0, half, 0, D, order) for i, order in enumerate(LATE)]
    sources = early
    piece = denc.shape[0] // (p.S * p.R)
    denc = denc.reshape((p.S,) + (2,) * BITS + (piece, D))
    dma = pltpu.SemaphoreType.DMA
    others = max(p.W - 1, 1)
    scratch = [
        pltpu.VMEM((p.J, p.HG, DH, p.T), B16),
        pltpu.VMEM((p.J, p.HG, DH, p.T), B16),
        pltpu.VMEM((p.R, p.HG, 2 * DH, p.T), B16),
        pltpu.VMEM((others, p.J, p.HG, 2 * DH, p.T), B16),
        pltpu.VMEM((p.J, p.HG, 3 * DH, p.T), B16),
        pltpu.VMEM((p.U, p.HG, 3 * DH, p.T), B16),
    ]
    scratch += [pltpu.VMEM((2, half, D), B16)] * 3
    scratch += [pltpu.VMEM(a.shape, a.dtype) for a in far]
    scratch += [pltpu.VMEM((p.S,) + (2,) * (BITS - 1) + (piece, D), B16)]
    scratch += [
        pltpu.VMEM((p.S,) + (2,) * (BITS - 1 - n) + (piece, D), B16) for n in range(BITS)
    ]
    scratch += [dma((BITS,)), dma((BITS,)), dma((1,)), dma((len(far),))]
    scratch += [
        pltpu.VMEM((BITS + 2, SMALL_ROWS, D), F32),
        pltpu.VMEM((BITS + 1, SMALL_ROWS, D), F32),
    ]
    scratch += back_scratch(p)
    scratch += [
        dma((p.U, p.HG)),
        dma((p.J, p.HG)),
        dma((others, p.J, p.HG)),
        dma((others, p.J, p.HG)),
        dma((p.J, p.HG)),
        dma((p.U, p.HG)),
        dma((BITS + 1,)),
        dma((BITS + 1,)),
        dma((len(jobs), 9)),
        dma((len(jobs), 9)),
        dma((len(jobs), 2)),
    ]
    for job in jobs:
        scratch += job_buffers(job)
    anywhere = pl.BlockSpec(memory_space=pl.ANY)
    near = pl.BlockSpec(memory_space=pltpu.VMEM)
    *sums, small, dh, denc = pl.pallas_call(
        functools.partial(tail_kernel, p, jobs, len(early), len(shapes)),
        out_shape=[jax.ShapeDtypeStruct(s, B16) for s in shapes]
        + [
            jax.ShapeDtypeStruct((SMALL_ROWS, D), F32),
            jax.ShapeDtypeStruct((p.S, p.T, D), B16),
            jax.ShapeDtypeStruct((p.S, piece, D), B16),
        ],
        in_specs=[anywhere] * (len(sources) + 2 + len(far)) + [near] * len(held),
        out_specs=[anywhere] * len(shapes) + [near] * 3,
        scratch_shapes=scratch,
        compiler_params=pltpu.CompilerParams(
            collective_id=collective, has_side_effects=True, vmem_limit_bytes=60 * 2**20
        ),
        name="tail",
    )(*sources, dot_, denc, *far, *held)
    return sums, small, dh, denc


def widen_kernel(count, *refs):
    for i in range(count):
        refs[count + i][...] = refs[i][...].astype(F32)


def widen(mats):
    parts = 8
    blocks = [
        pl.BlockSpec((m.shape[0] // parts, m.shape[1]), lambda i: (i, 0)) for m in mats
    ]
    return pl.pallas_call(
        functools.partial(widen_kernel, len(mats)),
        grid=(parts,),
        out_shape=[jax.ShapeDtypeStruct(m.shape, F32) for m in mats],
        in_specs=blocks,
        out_specs=blocks,
        compiler_params=pltpu.CompilerParams(vmem_limit_bytes=63 * 2**20),
        name="widen",
    )(*mats)


class Fetch:
    def __init__(self, master, staged, out, first, rows, col, cols, stage, own, sems, index, wide):
        self.x = lax.axis_index("shard")
        self.core, self.y = [partner(b)[0] for b in range(2)]
        self.rows, self.staged, self.wide = rows, staged, wide
        self.master = master.at[pl.ds(first, rows), pl.ds(col, cols)]
        self.stage_ref = stage.at[pl.ds(0, rows), pl.ds(0, cols)]
        self.own = own
        self.out, self.first, self.col, self.cols = out, first, col, cols
        load, keep, self.send, self.recv = sems
        self.load, self.keep = load.at[index], keep.at[index]
        self.send = [self.send.at[index, i] for i in range(3)]
        self.recv = [self.recv.at[index, i] for i in range(3)]

    def span(self, core, y=None):
        half = self.rows // 2
        if y is None:
            return core * half, half
        return core * half + y * (half // 2), half // 2

    def place(self, owner, *share):
        first, count = self.span(*share)
        first = pl.multiple_of(self.first + first, 16)
        return self.out.at[owner, pl.ds(first, count), pl.ds(self.col, self.cols)]

    def share(self):
        return (self.core, self.y) if self.wide else (self.core,)

    def read(self):
        pltpu.make_async_copy(self.master, self.stage_ref, self.load).start()

    def kept(self):
        return self.out.at[self.x, pl.ds(self.first, self.rows), pl.ds(self.col, self.cols)]

    def across(self):
        first, count = self.span(*self.share())
        part = self.own.at[pl.ds(pl.multiple_of(first, 16), count)]
        return to_row(part, self.place(self.x, *self.share()), self.send[0], self.recv[0])

    def start(self):
        landed(self.stage_ref, self.load)
        step = 32

        def body(i, carry):
            at = pl.ds(pl.multiple_of(i * step, step), step)
            self.own[at, :] = self.stage_ref[at, :].astype(B16)
            return carry

        lax.fori_loop(0, self.rows // step, body, 0)
        self.across().start()
        if self.staged:
            pltpu.make_async_copy(self.own, self.kept(), self.keep).start()

    def beside(self):
        place = self.place(1 - self.x, self.core, self.y)
        return to_rep(place, place, self.send[2], self.recv[2], 1)

    def over(self):
        place = self.place(1 - self.x, self.core)
        return to_rep(place, place, self.send[1], self.recv[1], 0)

    def relay(self):
        landed(self.place(1 - self.x, *self.share()), self.recv[0])
        if self.wide:
            self.beside().start()
        else:
            self.over().start()

    def relay_more(self):
        if self.wide:
            landed(self.place(1 - self.x, self.core, 1 - self.y), self.recv[2])
            self.over().start()

    def finish(self):
        landed(self.place(1 - self.x, 1 - self.core), self.recv[1])

    def end(self):
        self.across().wait_send()
        self.over().wait_send()
        if self.wide:
            self.beside().wait_send()
        if self.staged:
            landed(self.kept(), self.keep)


def small_block(p, gains, table, buckets, x):
    at = lax.broadcasted_iota(jnp.int32, (SMALL_ROWS, D), 0)
    block = jnp.zeros((SMALL_ROWS, D), F32)
    for i, gain in enumerate(gains):
        part = gain[...].astype(B16).astype(F32).reshape(1, -1)
        none = jnp.zeros_like(part)
        row = jnp.where(
            x == 0,
            jnp.concatenate([part, none], axis=1),
            jnp.concatenate([none, part], axis=1),
        )
        block = jnp.where(at == i, row, block)
    held = table.shape[0]
    bucket = lax.broadcasted_iota(jnp.int32, (held, 2 * p.T), 0) + x * held
    near = buckets[...].reshape(1, -1)[:, : 2 * p.T]
    onehot = (near == bucket).astype(F32).astype(B16)
    lines = t_dot(table[...].astype(B16), onehot)
    lines = jnp.concatenate([lines, jnp.zeros((H, D - 2 * p.T), F32)], axis=1)
    lines = jnp.concatenate(
        [jnp.zeros((3, D), F32), lines, jnp.zeros((SMALL_ROWS - 3 - H, D), F32)], axis=0
    )
    return block + lines


def head_kernel(p, *refs):
    refs = list(refs)
    take = lambda n: [refs.pop(0) for _ in range(n)]
    masters = take(11)
    hidden, encoded, g1, g2, g3, table, buckets = take(7)
    far_mats = take(8)
    wide = take(3)
    far_recv, far_enc, far_kn, far_kt, far_vn = take(5)
    small, a1, of_ref, rl_ref, ot = take(5)
    x1, x2, a2, qt2, of2, rl2 = take(6)
    mats = take(8)
    recv, enc, kn, kt, vn, vt = take(6)
    moves = Moves(take(1)[0])
    send, o_ref, mine_small, their_small = take(4)
    stages = take(4)
    owns = take(6)
    att = take(3)
    fetch_sems = take(4)
    small_send, small_recv, enc_send, enc_recv = take(4)
    tok_send, relay_sem, tok_recv, back_send, back_recv = take(5)

    me = lax.axis_index("rep")
    x = lax.axis_index("shard")
    w = me % p.W
    unit = me // p.W
    group = unit % p.G
    mine = p.worker_of(me)
    bits = [(me // 2**b) % 2 for b in range(BITS)]

    half = D // 2
    jobs = []
    for i in range(8):
        jobs.append((masters[i], mats[i], 0, half, 0, D))
    for i, ref in enumerate(wide):
        rows, cols = ref.shape[1:]
        tall = rows // 2 if rows > 512 else rows
        part = cols // 2 if cols > 1024 else cols
        for row in range(0, rows, tall):
            for col in range(0, cols, part):
                jobs.append((masters[8 + i], ref, row, tall, col, part))
    fetches = []
    for i, (master, out, row, rows, col, cols) in enumerate(jobs):
        staged = i >= 8
        own = owns[i - 8] if staged else out.at[x]
        fetches.append(
            Fetch(
                master,
                staged,
                out,
                row,
                rows,
                col,
                cols,
                stages[i % 4],
                own,
                fetch_sems,
                i,
                i < 5 or i % 2 == 0,
            )
        )

    barrier = pltpu.get_barrier_semaphore()
    for k in range(1, p.R):
        pl.semaphore_signal(
            barrier, inc=1, device_id={"rep": (me + k) % p.R}, device_id_type=MESH
        )
    pl.semaphore_signal(barrier, inc=1, device_id={"shard": 1 - x}, device_id_type=MESH)
    for fetch in fetches[:4]:
        fetch.read()
    mine_small[...] = small_block(p, (g1, g2, g3), table, buckets, x)
    enc[:, bits[3], bits[2], bits[1], bits[0]] = encoded[...]
    pl.semaphore_wait(barrier, p.R)

    share = to_row(mine_small, their_small, small_send, small_recv)
    share.start()

    def enc_copy(n):
        at = (slice(None),) * (1 + n) + tuple(bits[b] for b in range(BITS - 1 - n, -1, -1))
        part = enc.at[at]
        return to_rep(part, part, enc_send.at[n], enc_recv.at[n], BITS - 1 - n)

    def enc_landed(n):
        b = [bits[i] for i in range(BITS - 1 - n, -1, -1)]
        b[0] = 1 - b[0]
        landed(enc.at[(slice(None),) * (1 + n) + tuple(b)], enc_recv.at[n])

    started, relayed, more = 0, 0, 0

    def begin(count=1):
        nonlocal started
        for _ in range(count):
            if started < len(fetches):
                fetches[started].start()
                if started + 4 < len(fetches):
                    fetches[started + 4].read()
                started += 1

    def pass_on(count=1):
        nonlocal relayed, more
        for _ in range(count):
            if more < relayed:
                fetches[more].relay_more()
                more += 1
            if relayed < started:
                fetches[relayed].relay()
                relayed += 1

    def slot():
        begin()
        if started - relayed > FETCH_LAG or started == len(fetches):
            pass_on()

    begin(3)
    enc_copy(0).start()
    landed(their_small, small_recv)
    small[...] = mine_small[...] + their_small[...]
    enc_landed(0)
    enc_copy(1).start()
    pass_on(2)
    enc_landed(1)
    enc_copy(2).start()
    pass_on()
    begin(2)
    fetches[2].relay_more()
    more = 3
    for fetch, far in zip(fetches[:3], far_mats):
        fetch.finish()
        moves.take(fetch.out, far)
    project_kernel(p, hidden, small, *mats[:3], a1, send)

    def token(u, h):
        to, sem = u * p.W + mine, tok_recv.at[me, h]
        return me, to, send.at[u, h], recv.at[me, h], tok_send.at[u, h], sem

    def relay(k, j, h):
        r = p.source(j, w)
        part = recv.at[r, h, pl.ds(DH, 2 * DH)]
        to = me - w + (w + k) % p.W
        return remote(part, part, relay_sem.at[k - 1, j, h], tok_recv.at[r, h], to)

    def returned(j, h):
        r, sem = p.source(j, w), back_recv.at[unit, h]
        return me, r, o_ref.at[j, h], ot.at[unit, h], back_send.at[j, h], sem

    def relay_all(h):
        for j in range(p.J):
            r = p.source(j, w)
            landed(recv.at[r, h], tok_recv.at[r, h])
            for k in range(1, p.W):
                relay(k, j, h).start()

    def relayed_all(h):
        for k in range(1, p.W):
            for j in range(p.J):
                r = p.source(j, (w + k) % p.W)
                landed(recv.at[r, h, pl.ds(DH, 2 * DH)], tok_recv.at[r, h])

    def send_all(h):
        for u in range(p.U):
            start_either(*token(u, h))

    send_all(0)
    enc_landed(2)
    enc_copy(3).start()
    begin()
    pass_on(2)
    enc_landed(3)
    moves.take(enc, far_enc)
    fetches[4].relay_more()
    more = 5

    def encode(i, natural, turned):
        fetches[i].finish()
        moves.take(mats[i], far_mats[i])
        encode_one(enc, mats[i], natural, turned)
        slot()

    encode(3, kn, kt)
    if p.HG > 1:
        send_all(1)
    relay_all(0)
    encode(4, vn, vt)
    for h in range(2, p.HG):
        send_all(h)
    for made, far in ((kn, far_kn), (kt, far_kt), (vn, far_vn)):
        moves.take(made, far)
    slot()
    relayed_all(0)
    for h in range(p.HG):
        line = line_of(p, small, group * p.HG + h)
        between = functools.partial(relay_all, h + 1) if h + 1 < p.HG else None
        attend_head(p, w, h, line, recv, o_ref, of_ref, rl_ref.at[h], *att, between=between)
        for j in range(p.J):
            start_either(*returned(j, h))
        slot()
        if h + 1 < p.HG:
            relayed_all(h + 1)
    moves.take(recv, far_recv)
    slot()
    while more < 8:
        pass_on()
    for fetch, far in zip(fetches[5:8], far_mats[5:]):
        fetch.finish()
        moves.take(fetch.out, far)
    for u in range(p.U):
        for h in range(p.HG):
            landed(ot.at[u, h], back_recv.at[u, h])

    pause = slot
    cross_kernel(
        p.S, hidden, ot, mats[5], small, mats[6], mats[7], kn, vt, x1, x2, a2, qt2, of2, rl2, pause
    )
    begin(len(fetches))
    while more < len(fetches):
        pass_on()
    for fetch in fetches[8:]:
        fetch.finish()
    for fetch in fetches:
        fetch.end()
    moves.end()
    share.wait_send()
    for n in range(BITS):
        enc_copy(n).wait_send()
    for h in range(p.HG):
        for u in range(p.U):
            end_either(*token(u, h))
        for j in range(p.J):
            end_either(*returned(j, h))
            for k in range(1, p.W):
                relay(k, j, h).wait_send()


def head_call(p, masters, hidden, encoded, gains, table, buckets, collective):
    half, tokens = D // 2, p.S * p.T
    piece = encoded.shape[1]
    enc_rows = p.S * piece * p.R
    wides = [m.shape for m in masters[8:]]
    near = pl.BlockSpec(memory_space=pltpu.VMEM)
    anywhere = pl.BlockSpec(memory_space=pl.ANY)
    outs = [((2, half, D), B16)] * 8 + [((2, *s), B16) for s in wides]
    inner = [
        ((p.R, p.HG, 3 * DH, p.T), B16),
        ((p.S,) + (2,) * BITS + (piece, D), B16),
        ((enc_rows, D), B16),
        ((D, enc_rows), B16),
        ((enc_rows, D), B16),
    ]
    outs += inner
    inner = [((2, half, D), B16)] * 8 + inner + [((H // 2, 2 * DH + ONES, enc_rows), B16)]
    outs += [
        ((SMALL_ROWS, D), F32),
        ((tokens, D), B16),
        ((p.J, p.HG, DH, p.T), F32),
        ((p.HG, p.NP, 1, 2 * p.T), F32),
        ((p.U, p.HG, DH, p.T), B16),
        ((tokens, D), F32),
        ((tokens, D), F32),
        ((tokens, D), B16),
        ((p.S, D, p.T), B16),
        ((p.S, D, p.T), F32),
        ((p.S, H // 2, 1, 2 * p.T), F32),
    ]
    parts = [(half, D)] * 8
    for rows, cols in wides:
        tall = rows // 2 if rows > 512 else rows
        part = cols // 2 if cols > 1024 else cols
        parts += [(tall, part)] * ((rows // tall) * (cols // part))
    count = len(parts)
    dma = pltpu.SemaphoreType.DMA
    scratch = [pltpu.VMEM(s, t) for s, t in inner] + [dma((13,))]
    scratch += [
        pltpu.VMEM((p.U, p.HG, 3 * DH, p.T), B16),
        pltpu.VMEM((p.J, p.HG, DH, p.T), B16),
        pltpu.VMEM((SMALL_ROWS, D), F32),
        pltpu.VMEM((SMALL_ROWS, D), F32),
    ]
    tallest = max(r for r, _ in parts)
    widest = max(c for _, c in parts)
    scratch += [pltpu.VMEM((tallest, widest), F32)] * 4
    scratch += [pltpu.VMEM(s, B16) for s in parts[8:]]
    scratch += attend_scratch(p)
    scratch += [dma((count,)), dma((count,)), dma((count, 3)), dma((count, 3))]
    scratch += [dma, dma, dma((BITS,)), dma((BITS,))]
    scratch += [
        dma((p.U, p.HG)),
        dma((max(p.W - 1, 1), p.J, p.HG)),
        dma((p.R, p.HG)),
        dma((p.J, p.HG)),
        dma((p.U, p.HG)),
    ]
    return pl.pallas_call(
        functools.partial(head_kernel, p),
        out_shape=[jax.ShapeDtypeStruct(s, t) for s, t in outs],
        in_specs=[anywhere] * 11 + [near] * 7,
        out_specs=[anywhere] * 16 + [near] * 11,
        scratch_shapes=scratch,
        compiler_params=pltpu.CompilerParams(
            collective_id=collective, has_side_effects=True, vmem_limit_bytes=62 * 2**20
        ),
        name="head",
    )(*masters, hidden, encoded, *gains, table, buckets)


def local(
    hidden,
    encoded,
    out_grad,
    self_query,
    self_key,
    self_value,
    self_out,
    cross_query,
    cross_key,
    cross_value,
    cross_out,
    ffn_gate,
    ffn_up,
    ffn_down,
    gain_self,
    gain_cross,
    gain_ffn,
    bias_table,
    buckets,
):
    seqs, toks = hidden.shape[0], hidden.shape[1]
    p = Plan(seqs, toks, lax.axis_size("rep"))
    tokens = seqs * toks
    ff = ffn_gate.shape[1]
    enc_rows = seqs * encoded.shape[1] * p.R
    dma = pltpu.SemaphoreType.DMA

    n_shard = lax.axis_size("shard")
    mine = lax.axis_index("shard")
    part = gain_self.shape[0]
    near = buckets[: 2 * toks]
    onehot = (near[:, None] == jnp.arange(NB, dtype=jnp.int32)[None, :]).astype(B16)
    paired = n_shard == 2 and p.R == 2**BITS and 3 + H <= SMALL_ROWS
    if paired:
        masters = (
            self_query,
            self_key,
            self_value,
            cross_key,
            cross_value,
            self_out,
            cross_query,
            cross_out,
            ffn_gate,
            ffn_up,
            ffn_down,
        )
        gains = [gain_self, gain_cross, gain_ffn]
        got = head_call(
            p, masters, hidden, encoded, gains, bias_table, buckets, 0
        )
        wq, wk, wv, wck, wcv, wo, wcq, wco = got[:8]
        wg, wu, wd = [g.reshape(-1, g.shape[-1]) for g in got[8:11]]
        recv, enc, ckn, ckt, cvn, small, a1, of, rl, ot = got[11:21]
        x1, x2, a2, qt2, of2, rl2 = got[21:]
    else:
        lot = jnp.concatenate(
            [
                jnp.stack([gain_self, gain_cross, gain_ffn]).reshape(-1),
                bias_table.reshape(-1),
            ]
        ).astype(B16)
        lot = lax.all_gather(lot, "shard", axis=0)
        gains = [
            lot[:, i * part : (i + 1) * part].reshape(1, D).astype(F32) for i in range(3)
        ]
        table = lot[:, 3 * part :].reshape(NB, H)
        lines = jnp.einsum("lb,bh->hl", onehot, table, preferred_element_type=F32)
        lines = jnp.pad(lines, ((0, SMALL_ROWS - 3 - H), (0, D - 2 * toks)))
        small = jnp.concatenate([*gains, lines], axis=0)

        wq, wk, wv, wo, wcq, wck, wcv, wco, wg, wu, wd = [
            gather_rows(m.astype(B16))
            for m in (
                self_query,
                self_key,
                self_value,
                self_out,
                cross_query,
                cross_key,
                cross_value,
                cross_out,
                ffn_gate,
                ffn_up,
                ffn_down,
            )
        ]
        enc = lax.all_gather(encoded, "rep", axis=1, tiled=True).reshape(enc_rows, D)

        a1, send = plain_call(
            functools.partial(project_kernel, p),
            [((tokens, D), B16), ((p.U, p.HG, 3 * DH, toks), B16)],
            (hidden, small, wq, wk, wv),
            "project",
        )
        recv = comm_call(
            functools.partial(scatter_tokens, p),
            (p.R, p.HG, 3 * DH, toks),
            (send,),
            [dma((p.U,)), dma((max(p.W - 1, 1), p.J)), dma((p.R,))],
            0,
            "scatter_tokens",
        )
        ckn, ckt, cvn, cvt = plain_call(
            encode_kernel,
            [
                ((enc_rows, D), B16),
                ((D, enc_rows), B16),
                ((enc_rows, D), B16),
                ((H // 2, 2 * DH + ONES, enc_rows), B16),
            ],
            (enc, wck, wcv),
            "encode",
        )
        o, of, rl = pl.pallas_call(
            functools.partial(attend_kernel, p),
            grid=(p.HG,),
            out_shape=[
                jax.ShapeDtypeStruct((p.J, p.HG, DH, toks), B16),
                jax.ShapeDtypeStruct((p.J, p.HG, DH, toks), F32),
                jax.ShapeDtypeStruct((p.HG, p.NP, 1, 2 * toks), F32),
            ],
            in_specs=[whole((p.R, p.HG, 3 * DH, toks)), whole((SMALL_ROWS, D))],
            out_specs=[
                whole((p.J, p.HG, DH, toks)),
                whole((p.J, p.HG, DH, toks)),
                whole((p.HG, p.NP, 1, 2 * toks)),
            ],
            scratch_shapes=attend_scratch(p),
            compiler_params=pltpu.CompilerParams(vmem_limit_bytes=56 * 2**20),
            name="attend",
        )(recv, small)
        ot = comm_call(
            functools.partial(return_tokens, p),
            (p.U, p.HG, DH, toks),
            (o,),
            [dma((p.J,)), dma((p.U,))],
            1,
            "return_tokens",
        )

        x1, x2, a2, qt2, of2, rl2 = plain_call(
            functools.partial(cross_kernel, seqs),
            [
                ((tokens, D), F32),
                ((tokens, D), F32),
                ((tokens, D), B16),
                ((seqs, D, toks), B16),
                ((seqs, D, toks), F32),
                ((seqs, H // 2, 1, 2 * toks), F32),
            ],
            (hidden, ot, wo, small, wcq, wco, ckn, cvt),
            "cross",
        )

    chunk = min(512, ff)
    const = lambda s: pl.BlockSpec(s, lambda i: (0, 0))
    output, dx2, dg_ffn, dwg, dwu, dwd = pl.pallas_call(
        ffn_kernel,
        grid=(ff // chunk,),
        out_shape=[
            jax.ShapeDtypeStruct((tokens, D), B16),
            jax.ShapeDtypeStruct((tokens, D), F32),
            jax.ShapeDtypeStruct((1, D), F32),
            jax.ShapeDtypeStruct((D, ff), B16),
            jax.ShapeDtypeStruct((D, ff), B16),
            jax.ShapeDtypeStruct((ff, D), B16),
        ],
        in_specs=[
            const((tokens, D)),
            const((tokens, D)),
            const((SMALL_ROWS, D)),
            pl.BlockSpec((D, chunk), lambda i: (0, i)),
            pl.BlockSpec((D, chunk), lambda i: (0, i)),
            pl.BlockSpec((chunk, D), lambda i: (i, 0)),
        ],
        out_specs=[
            const((tokens, D)),
            const((tokens, D)),
            const((1, D)),
            pl.BlockSpec((D, chunk), lambda i: (0, i)),
            pl.BlockSpec((D, chunk), lambda i: (0, i)),
            pl.BlockSpec((chunk, D), lambda i: (i, 0)),
        ],
        scratch_shapes=[
            pltpu.VMEM((tokens, D), B16),
            pltpu.VMEM((tokens, D), F32),
            pltpu.VMEM((tokens, D), F32),
        ],
        compiler_params=pltpu.CompilerParams(vmem_limit_bytes=56 * 2**20),
        name="ffn",
    )(x2, out_grad.reshape(tokens, D), small, wg, wu, wd)

    back_outs = [
        ((tokens, D), F32),
        ((1, D), F32),
        ((p.U, p.HG, DH, toks), B16),
        ((enc_rows, D), B16),
    ] + [((D, D), B16)] * 5
    back_args = (dx2, x1, a2, small, qt2, of2, rl2, ckn, ckt, cvn, enc, wco, wcq, wck, wcv, wo, ot)
    back_scratch_ = [
        pltpu.VMEM((seqs, D, toks), B16),
        pltpu.VMEM((seqs, D, toks), B16),
        pltpu.VMEM((enc_rows, D), B16),
        pltpu.VMEM((enc_rows, D), B16),
    ]
    back_kernel = functools.partial(cross_back_kernel, seqs, p.G)
    if paired:
        got = cross_back_moves_call(back_kernel, back_outs, back_args, back_scratch_)
    else:
        got = plain_call(back_kernel, back_outs, back_args, "cross_back", scratch=back_scratch_)
    dx1, dg_cross, dot_, denc, dwco, dwcq, dwck, dwcv, dwo = got
    if paired:
        early = [
            g.reshape(2, g.shape[0] // 2, g.shape[1])
            for g in (dwg, dwu, dwd, dwo, dwcq, dwck, dwcv, dwco)
        ]
        sums, block, hidden_grad, encoded_grad = tail_call(
            p,
            early,
            dot_,
            denc,
            (recv, of, wq, wk, wv),
            (small, rl, hidden, a1, dx1, dg_cross, dg_ffn),
            3,
        )
        dwg, dwu, dwd, dwo, dwcq, dwck, dwcv, dwco, dwq, dwk, dwv = widen(sums)
        mats = [dwq, dwk, dwv, dwo, dwcq, dwck, dwcv, dwco, dwg, dwu, dwd]
        dgains = lax.dynamic_slice(block, (0, mine * part), (3, part))
        by_bucket = jnp.einsum(
            "hl,lb->bh",
            block[3 : 3 + H, : 2 * toks],
            onehot.astype(F32),
            precision=lax.Precision.HIGHEST,
        )
        dtab = lax.dynamic_slice(
            by_bucket, (mine * bias_table.shape[0], 0), bias_table.shape
        )
    else:
        encoded_grad = lax.psum_scatter(
            denc.reshape(seqs, enc_rows // seqs, D), "rep", scatter_dimension=1, tiled=True
        )
        dout = comm_call(
            functools.partial(scatter_rows, p),
            (p.J, p.HG, DH, toks),
            (dot_,),
            [dma((p.U,)), dma((p.J,))],
            2,
            "scatter_rows",
        )
        dq, dkv, line = pl.pallas_call(
            functools.partial(attend_back_kernel, p),
            grid=(p.HG,),
            out_shape=[
                jax.ShapeDtypeStruct((p.J, p.HG, DH, toks), B16),
                jax.ShapeDtypeStruct((p.R, p.HG, 2 * DH, toks), B16),
                jax.ShapeDtypeStruct((p.HG, 1, 2 * toks), F32),
            ],
            in_specs=[
                whole((p.R, p.HG, 3 * DH, toks)),
                whole((SMALL_ROWS, D)),
                whole((p.J, p.HG, DH, toks)),
                whole((p.J, p.HG, DH, toks)),
                whole((p.HG, p.NP, 1, 2 * toks)),
            ],
            out_specs=[
                whole((p.J, p.HG, DH, toks)),
                whole((p.R, p.HG, 2 * DH, toks)),
                whole((p.HG, 1, 2 * toks)),
            ],
            scratch_shapes=back_scratch(p),
            compiler_params=pltpu.CompilerParams(vmem_limit_bytes=56 * 2**20),
            name="attend_back",
        )(recv, small, dout, of, rl)
        grads = comm_call(
            functools.partial(return_grads, p),
            (p.U, p.HG, 3 * DH, toks),
            (dq, dkv),
            [
                pltpu.VMEM((max(p.W - 1, 1), p.J, p.HG, 2 * DH, toks), B16),
                pltpu.VMEM((p.J, p.HG, 3 * DH, toks), B16),
                dma((p.J,)),
                dma((max(p.W - 1, 1), p.J)),
                dma((max(p.W - 1, 1), p.J)),
                dma((p.U,)),
            ],
            3,
            "return_grads",
            space=pltpu.VMEM,
        )
        hidden_grad, dg_self, dwq, dwk, dwv = plain_call(
            functools.partial(last_kernel, p),
            [(hidden.shape, B16), ((1, D), F32)] + [((D, D), B16)] * 3,
            (hidden, grads, a1, small, dx1, wq, wk, wv),
            "last",
        )

        group = (lax.axis_index("rep") // p.W) % p.G
        by_bucket = jnp.einsum(
            "hl,lb->bh", line[:, 0, :], onehot.astype(F32), precision=lax.Precision.HIGHEST
        )
        dtable = lax.dynamic_update_slice(jnp.zeros((NB, H), F32), by_bucket, (0, group * p.HG))

        mats = reduce_grads([dwq, dwk, dwv, dwo, dwcq, dwck, dwcv, dwco, dwg, dwu, dwd])
        lot = jnp.concatenate(
            [g.reshape(n_shard, part) for g in (dg_self, dg_cross, dg_ffn)]
            + [dtable.reshape(n_shard, -1)],
            axis=1,
        )
        size = lot.shape[1]
        lot = lax.psum(lot, ("shard", "rep"))
        lot = lax.dynamic_slice(lot, (mine, 0), (1, size))[0]
        dgains = [lot[i * part : (i + 1) * part] for i in range(3)]
        dtab = lot[3 * part :].reshape(bias_table.shape)
    return (
        output.reshape(hidden.shape),
        hidden_grad,
        encoded_grad,
        *mats,
        *dgains,
        dtab,
    )


def solution(mesh):
    tok = P("shard", "rep", None)
    mat = P("shard", None)
    in_specs = (tok,) * 3 + (mat,) * 11 + (P("shard"),) * 3 + (mat, P())
    out_specs = (tok,) * 3 + (mat,) * 11 + (P("shard"),) * 3 + (mat,)
    return jax.shard_map(local, mesh=mesh, in_specs=in_specs, out_specs=out_specs, check_vma=False)
```

```python
import functools
import itertools

import jax
import jax.numpy as jnp
from jax import lax
from jax.experimental import pallas as pl
from jax.experimental.pallas import tpu as pltpu
from jax.sharding import PartitionSpec as P

D = 768
H = 12
DH = 64
NB = 32
EPS = 1e-06
F32 = jnp.float32
B16 = jnp.bfloat16
ONES = 16
HIDE = -1e30
MESH = pl.DeviceIdType.MESH
GELU_A = 0.7978845608028654
GELU_B = 0.044715


def dot(a, b):
    return lax.dot_general(a, b, (((1,), (0,)), ((), ())), preferred_element_type=F32)


def dot_t(a, b):
    return lax.dot_general(a, b, (((1,), (1,)), ((), ())), preferred_element_type=F32)


def t_dot(a, b):
    return lax.dot_general(a, b, (((0,), (0,)), ((), ())), preferred_element_type=F32)


def mat(ref):
    return ref[...].reshape(-1, ref.shape[-1])


def scale_of(v):
    return lax.rsqrt(jnp.mean(v * v, axis=-1, keepdims=True) + EPS)


def norm_back(v, gain, grad):
    r = scale_of(v)
    n = v * r
    c = grad * gain
    dv = r * (c - n * jnp.mean(c * n, axis=-1, keepdims=True))
    return dv, jnp.sum(grad * n, axis=0, keepdims=True)


def whole(shape):
    return pl.BlockSpec(shape, lambda *_: (0,) * len(shape))


def plain_call(kernel, outs, args, name, scratch=(), vmem=60):
    return pl.pallas_call(
        kernel,
        out_shape=[jax.ShapeDtypeStruct(s, t) for s, t in outs],
        in_specs=[pl.BlockSpec(memory_space=pltpu.VMEM)] * len(args),
        out_specs=[pl.BlockSpec(memory_space=pltpu.VMEM)] * len(outs),
        scratch_shapes=list(scratch),
        compiler_params=pltpu.CompilerParams(vmem_limit_bytes=vmem * 2**20),
        name=name,
    )(*args)


class Plan:
    def __init__(self, seqs, toks, rows):
        self.S, self.T, self.R = seqs, toks, rows
        groups = 1
        for g in range(1, H + 1):
            if H % g == 0 and seqs * g <= rows and rows % (2 * seqs * g) == 0:
                groups = g
        self.G = groups
        self.HG = H // groups
        self.F = self.HG * DH
        self.U = seqs * groups
        self.W = rows // self.U
        self.J = rows // self.W
        self.NP = self.J // 2
        self.CK = 2 * self.W * toks
        self.L = rows * toks

    def worker_of(self, r):
        m = r % (2 * self.W)
        late = m // self.W
        return m * (1 - late) + (2 * self.W - 1 - m) * late

    def slot_of(self, r):
        return 2 * (r // (2 * self.W)) + (r % (2 * self.W)) // self.W

    def source(self, j, w):
        return self.source_in(j // 2, j % 2, w)

    def source_in(self, pair, late, w):
        if late:
            return 2 * self.W * pair + 2 * self.W - 1 - w
        return 2 * self.W * pair + w


def enter(rows):
    me = lax.axis_index("rep")
    barrier = pltpu.get_barrier_semaphore()
    for k in range(1, rows):
        pl.semaphore_signal(
            barrier, inc=1, device_id={"rep": (me + k) % rows}, device_id_type=MESH
        )
    pl.semaphore_wait(barrier, rows - 1)
    return me


def remote(src, dst, send, recv, to):
    return pltpu.make_async_remote_copy(
        src_ref=src,
        dst_ref=dst,
        send_sem=send,
        recv_sem=recv,
        device_id={"rep": to},
        device_id_type=MESH,
    )


def start_either(me, to, src, dst, send, recv):
    @pl.when(to == me)
    def _():
        pltpu.make_async_copy(src, dst, recv).start()

    @pl.when(to != me)
    def _():
        remote(src, dst, send, recv, to).start()


def end_either(me, to, src, dst, send, recv):
    @pl.when(to != me)
    def _():
        remote(src, dst, send, recv, to).wait_send()


def landed(ref, sem):
    pltpu.make_async_copy(ref, ref, sem).wait()


def scatter_tokens(plan, send, recv, send_sem, relay_sem, recv_sem):
    p = plan
    me = enter(p.R)
    w = me % p.W
    mine = p.worker_of(me)
    for u in range(p.U):
        start_either(me, u * p.W + mine, send.at[u], recv.at[me], send_sem.at[u], recv_sem.at[me])
    for j in range(p.J):
        r = p.source(j, w)
        landed(recv.at[r], recv_sem.at[r])
        for k in range(1, p.W):
            part = recv.at[r, :, pl.ds(DH, 2 * DH)]
            remote(
                part, part, relay_sem.at[k - 1, j], recv_sem.at[r], me - w + (w + k) % p.W
            ).start()
    for k in range(1, p.W):
        for j in range(p.J):
            r = p.source(j, (w + k) % p.W)
            landed(recv.at[r, :, pl.ds(DH, 2 * DH)], recv_sem.at[r])
    for u in range(p.U):
        end_either(me, u * p.W + mine, send.at[u], recv.at[me], send_sem.at[u], recv_sem.at[me])
    for k in range(1, p.W):
        for j in range(p.J):
            r = p.source(j, w)
            part = recv.at[r, :, pl.ds(DH, 2 * DH)]
            remote(
                part, part, relay_sem.at[k - 1, j], recv_sem.at[r], me - w + (w + k) % p.W
            ).wait_send()


def return_tokens(plan, send, recv, send_sem, recv_sem):
    p = plan
    me = enter(p.R)
    w = me % p.W
    unit = me // p.W
    for j in range(p.J):
        r = p.source(j, w)
        start_either(me, r, send.at[j], recv.at[unit], send_sem.at[j], recv_sem.at[unit])
    for u in range(p.U):
        landed(recv.at[u], recv_sem.at[u])
    for j in range(p.J):
        r = p.source(j, w)
        end_either(me, r, send.at[j], recv.at[unit], send_sem.at[j], recv_sem.at[unit])


def scatter_rows(plan, send, recv, send_sem, recv_sem):
    p = plan
    me = enter(p.R)
    mine = p.worker_of(me)
    slot = p.slot_of(me)
    for u in range(p.U):
        start_either(
            me, u * p.W + mine, send.at[u], recv.at[slot], send_sem.at[u], recv_sem.at[slot]
        )
    for j in range(p.J):
        landed(recv.at[j], recv_sem.at[j])
    for u in range(p.U):
        end_either(
            me, u * p.W + mine, send.at[u], recv.at[slot], send_sem.at[u], recv_sem.at[slot]
        )


def return_grads(plan, dq, dkv, recv, buf, out, send_sem, part_sem, got_sem, recv_sem):
    p = plan
    me = enter(p.R)
    w = me % p.W
    unit = me // p.W

    def give(k, j):
        to = (w + k) % p.W
        r = p.source(j, to)
        return remote(
            dkv.at[r],
            buf.at[k - 1, j],
            part_sem.at[k - 1, j],
            got_sem.at[k - 1, j],
            me - w + to,
        )

    for j in range(p.J):
        for k in range(1, p.W):
            give(k, j).start()
    for j in range(p.J):
        r = p.source(j, w)
        total = dkv[r].astype(F32)
        for k in range(1, p.W):
            landed(buf.at[k - 1, j], got_sem.at[k - 1, j])
            total = total + buf[k - 1, j].astype(F32)
        out[j, :, 0:DH, :] = dq[j]
        out[j, :, DH : 3 * DH, :] = total.astype(B16)
        start_either(me, r, out.at[j], recv.at[unit], send_sem.at[j], recv_sem.at[unit])
    for u in range(p.U):
        landed(recv.at[u], recv_sem.at[u])
    for j in range(p.J):
        r = p.source(j, w)
        end_either(me, r, out.at[j], recv.at[unit], send_sem.at[j], recv_sem.at[unit])
        for k in range(1, p.W):
            give(k, j).wait_send()


def comm_call(kernel, out, args, scratch, collective, name, space=pl.ANY):
    return pl.pallas_call(
        kernel,
        out_shape=jax.ShapeDtypeStruct(out, B16),
        in_specs=[pl.BlockSpec(memory_space=space)] * len(args),
        out_specs=pl.BlockSpec(memory_space=space),
        scratch_shapes=list(scratch),
        compiler_params=pltpu.CompilerParams(
            collective_id=collective, has_side_effects=True, vmem_limit_bytes=40 * 2**20
        ),
        name=name,
    )(*args)


def project_kernel(plan, hidden, gain, wq, wk, wv, a1_ref, send):
    p = plan
    x = hidden[...].reshape(p.S * p.T, D).astype(F32)
    a1 = (x * scale_of(x) * gain[0:1, :]).astype(B16)
    a1_ref[...] = a1
    for n, weight in enumerate((wq, wk, wv)):
        rows = dot(a1, mat(weight))
        for s in range(p.S):
            turned = jnp.transpose(rows[s * p.T : (s + 1) * p.T]).astype(B16)
            for i in range(H):
                send[s * p.G + i // p.HG, i % p.HG, n * DH : (n + 1) * DH, :] = turned[
                    i * DH : (i + 1) * DH
                ]


def bias_tiles(plan, w, line, tiles):
    p = plan
    far = line[:, 2 * p.T - 1 : 2 * p.T]
    near = pltpu.roll(jnp.broadcast_to(line, (p.T, 2 * p.T)), 0, 1, stride=1, stride_axis=0)
    key = lax.broadcasted_iota(jnp.int32, (p.T, p.T), 0)
    query = lax.broadcasted_iota(jnp.int32, (p.T, p.T), 1)
    same = jnp.where(query >= key, near[:, : p.T], HIDE)
    next_ = near[:, p.T :]
    farb = jnp.broadcast_to(far, (p.T, p.T))
    tiles[0] = jnp.broadcast_to(far, (p.CK, 2 * p.T))
    for a in range(2):
        ahead = w if a == 0 else 2 * p.W - 1 - w
        for b in range(2 * p.W):
            diff = ahead - b
            tile = jnp.where(
                diff == 0, same, jnp.where(diff == 1, next_, jnp.where(diff < 0, HIDE, farb))
            )
            tiles[2, b * p.T : (b + 1) * p.T, a * p.T : (a + 1) * p.T] = tile
            back = diff + 2 * p.W
            tiles[1, b * p.T : (b + 1) * p.T, a * p.T : (a + 1) * p.T] = jnp.where(
                back == 1, next_, farb
            )


def block_pair(plan, ref, pair, w, h):
    p = plan
    return jnp.concatenate(
        [ref[p.source_in(pair, late, w), h, 0:DH, :] for late in range(2)], axis=1
    )


def in_two(count, body, carry, between):
    if between is None:
        return lax.fori_loop(0, count, body, carry)
    carry = lax.fori_loop(0, count - 1, body, carry)
    between()
    return lax.fori_loop(count - 1, count, body, carry)


def line_of(p, block, head):
    return block[pl.ds(3 + head, 1), 0 : 2 * p.T]


def attend_head(p, w, h, line, recv, o_ref, of_ref, rl, kn, vt, tiles, between=None):
    bias_tiles(p, w, line, tiles)
    for r in range(p.R):
        kn[r * p.T : (r + 1) * p.T, :] = jnp.transpose(
            recv[r, h, DH : 2 * DH, :].astype(F32)
        ).astype(B16)
        vt[0:DH, r * p.T : (r + 1) * p.T] = recv[r, h, 2 * DH : 3 * DH, :]
    vt[DH : DH + ONES, :] = jnp.ones((ONES, p.L), B16)

    def one_pair(pair, carry):
        qt = block_pair(p, recv, pair, w, h)

        def step(i, acc):
            start = pl.multiple_of(i * p.CK, p.CK)
            e = jnp.exp(dot(kn[pl.ds(start, p.CK), :], qt) + tiles[jnp.maximum(i - pair + 2, 0)])
            return acc + dot(vt[:, pl.ds(start, p.CK)], e.astype(B16))

        acc = lax.fori_loop(0, pair + 1, step, jnp.zeros((DH + ONES, 2 * p.T), F32))
        scale = 1.0 / acc[DH : DH + 1]
        of = acc[:DH] * scale
        rl[pair] = scale
        for a in range(2):
            part = of[:, a * p.T : (a + 1) * p.T]
            of_ref[2 * pair + a, h] = part
            o_ref[2 * pair + a, h] = part.astype(B16)
        return carry

    in_two(p.NP, one_pair, 0, between)


def attend_scratch(p):
    return [
        pltpu.VMEM((p.L, DH), B16),
        pltpu.VMEM((DH + ONES, p.L), B16),
        pltpu.VMEM((3, p.CK, 2 * p.T), F32),
    ]


def attend_kernel(plan, recv, block, o_ref, of_ref, rl_ref, *scratch):
    p = plan
    me = lax.axis_index("rep")
    w = me % p.W
    group = (me // p.W) % p.G
    h = pl.program_id(0)
    line = line_of(p, block, group * p.HG + h)
    attend_head(p, w, h, line, recv, o_ref, of_ref, rl_ref.at[h], *scratch)


def back_head(
    p,
    w,
    h,
    line,
    recv,
    dout,
    of_ref,
    rl,
    dq_ref,
    dkv_ref,
    kn,
    vn,
    kt,
    dk,
    dv,
    tiles,
    near,
    between=None,
):
    bias_tiles(p, w, line, tiles)
    for r in range(p.R):
        kn[r * p.T : (r + 1) * p.T, :] = jnp.transpose(
            recv[r, h, DH : 2 * DH, :].astype(F32)
        ).astype(B16)
        vn[r * p.T : (r + 1) * p.T, :] = jnp.transpose(
            recv[r, h, 2 * DH : 3 * DH, :].astype(F32)
        ).astype(B16)
        kt[0:DH, r * p.T : (r + 1) * p.T] = recv[r, h, DH : 2 * DH, :]
    kt[DH : DH + ONES, :] = jnp.ones((ONES, p.L), B16)
    dk[...] = jnp.zeros_like(dk)
    dv[...] = jnp.zeros_like(dv)
    near[...] = jnp.zeros_like(near)

    def one_pair(pair, total):
        qt = block_pair(p, recv, pair, w, h)
        dot_rows = jnp.concatenate([dout[2 * pair + a, h] for a in range(2)], axis=1)
        of = jnp.concatenate([of_ref[2 * pair + a, h] for a in range(2)], axis=1)
        delta = jnp.sum(dot_rows.astype(F32) * of, axis=0, keepdims=True)
        scale = rl[pair]
        qn = jnp.transpose(qt.astype(F32)).astype(B16)
        don = jnp.transpose(dot_rows.astype(F32)).astype(B16)

        def step(i, acc):
            start = pl.multiple_of(i * p.CK, p.CK)
            kind = jnp.maximum(i - pair + 2, 0)
            keys = pl.ds(start, p.CK)
            prob = jnp.exp(dot(kn[keys, :], qt) + tiles[kind]) * scale
            ds = (prob * (dot(vn[keys, :], dot_rows) - delta)).astype(B16)
            near[kind] += ds.astype(F32)
            dk[keys, :] += dot(ds, qn)
            dv[keys, :] += dot(prob.astype(B16), don)
            return acc + dot(kt[:, keys], ds)

        acc = lax.fori_loop(0, pair + 1, step, jnp.zeros((DH + ONES, 2 * p.T), F32))
        for a in range(2):
            dq_ref[2 * pair + a, h] = acc[:DH, a * p.T : (a + 1) * p.T].astype(B16)
        return total + acc[DH : DH + 1]

    total = in_two(p.NP, one_pair, jnp.zeros((1, 2 * p.T), F32), between)
    for r in range(p.R):
        dkv_ref[r, h, 0:DH, :] = jnp.transpose(dk[r * p.T : (r + 1) * p.T, :]).astype(B16)
        dkv_ref[r, h, DH : 2 * DH, :] = jnp.transpose(dv[r * p.T : (r + 1) * p.T, :]).astype(B16)
    same = jnp.zeros((p.T, p.T), F32)
    next_ = jnp.zeros((p.T, p.T), F32)
    for a in range(2):
        ahead = w if a == 0 else 2 * p.W - 1 - w
        for b in range(2 * p.W):
            diff = ahead - b
            spot = (slice(b * p.T, (b + 1) * p.T), slice(a * p.T, (a + 1) * p.T))
            tile = near[(2, *spot)]
            same = same + jnp.where(diff == 0, tile, 0.0)
            next_ = next_ + jnp.where(diff == 1, tile, 0.0)
            next_ = next_ + jnp.where(diff + 2 * p.W == 1, near[(1, *spot)], 0.0)
    both = jnp.concatenate([same, next_], axis=1)
    key = lax.broadcasted_iota(jnp.int32, (p.T, p.T), 0)
    other = lax.broadcasted_iota(jnp.int32, (p.T, p.T), 1)
    swap = (key + other == p.T - 1).astype(F32)
    turned = lax.dot_general(
        swap,
        both,
        (((1,), (0,)), ((), ())),
        precision=lax.Precision.HIGHEST,
        preferred_element_type=F32,
    )
    turned = pltpu.roll(turned, p.T + 1, 1, stride=1, stride_axis=0)
    by_distance = jnp.sum(turned, axis=0, keepdims=True)
    rest = jnp.sum(total) - jnp.sum(both)
    place = lax.broadcasted_iota(jnp.int32, (1, 2 * p.T), 1)
    return by_distance + jnp.where(place == 2 * p.T - 1, rest, 0.0)


def back_scratch(p):
    return [
        pltpu.VMEM((p.L, DH), B16),
        pltpu.VMEM((p.L, DH), B16),
        pltpu.VMEM((DH + ONES, p.L), B16),
        pltpu.VMEM((p.L, DH), F32),
        pltpu.VMEM((p.L, DH), F32),
        pltpu.VMEM((3, p.CK, 2 * p.T), F32),
        pltpu.VMEM((3, p.CK, 2 * p.T), F32),
    ]


def attend_back_kernel(plan, recv, block, dout, of_ref, rl_ref, dq_ref, dkv_ref, line_ref, *scratch):
    p = plan
    me = lax.axis_index("rep")
    w = me % p.W
    group = (me // p.W) % p.G
    h = pl.program_id(0)
    line_ref[h] = back_head(
        p,
        w,
        h,
        line_of(p, block, group * p.HG + h),
        recv,
        dout,
        of_ref,
        rl_ref.at[h],
        dq_ref,
        dkv_ref,
        *scratch,
    )


def encode_kernel(enc, wk, wv, kn, kt, vn, vt):
    encode_one(enc, wk, kn, kt)
    encode_one(enc, wv, vn, vt)


def encode_one(enc, weight, natural, turned):
    value = dot(mat(enc), mat(weight))
    natural[...] = value.astype(B16)
    flipped = jnp.transpose(value).astype(B16)
    if len(turned.shape) == 2:
        turned[...] = flipped
        return
    for i in range(H // 2):
        turned[i, 0 : 2 * DH, :] = flipped[2 * i * DH : 2 * (i + 1) * DH]
        turned[i, 2 * DH : 2 * DH + ONES, :] = jnp.ones((ONES, turned.shape[2]), B16)


def apart(pair, axis, other):
    twice = jnp.concatenate([pair, pair], axis=axis)
    half = (pair.shape[axis], pair.shape[other] // 2)
    one = lax.broadcasted_iota(jnp.int32, twice.shape, axis) < half[0]
    two = lax.broadcasted_iota(jnp.int32, twice.shape, other) < half[1]
    return jnp.where(one == two, twice, jnp.zeros_like(twice))


def rows_of(units, s, seqs):
    groups = units.shape[0] // seqs
    return units[s * groups : (s + 1) * groups].reshape(-1, units.shape[-1])


def cross_kernel(
    seqs,
    hidden,
    ot,
    wo,
    gain,
    wcq,
    wco,
    kn,
    vt,
    x1_ref,
    x2_ref,
    a2_ref,
    qt_ref,
    of_ref,
    rl_ref,
    pause=lambda: None,
):
    toks = hidden.shape[1]
    span = kn.shape[0] // seqs
    x = hidden[...].reshape(seqs * toks, D).astype(F32)
    o = jnp.concatenate(
        [jnp.transpose(rows_of(ot, s, seqs).astype(F32)) for s in range(seqs)], axis=0
    ).astype(B16)
    x1 = x + dot(o, mat(wo))
    x1_ref[...] = x1
    a2 = (x1 * scale_of(x1) * gain[1:2, :]).astype(B16)
    a2_ref[...] = a2
    q2 = dot(a2, mat(wcq))
    for s in range(seqs):
        qt_ref[s] = jnp.transpose(q2[s * toks : (s + 1) * toks]).astype(B16)
    pause()

    def heads(i, carry):
        col = pl.multiple_of(2 * i * DH, 2 * DH)
        for s in range(seqs):
            keys = slice(s * span, (s + 1) * span)
            q_pair = apart(qt_ref[s, pl.ds(col, 2 * DH), :], 1, 0)
            e = jnp.exp(dot(kn[keys, pl.ds(col, 2 * DH)], q_pair))
            acc = dot(vt[i, :, keys], e.astype(B16))
            rl = 1.0 / acc[2 * DH : 2 * DH + 1]
            both = acc * rl
            of_ref[s, pl.ds(col, DH), :] = both[:DH, :toks]
            of_ref[s, pl.ds(col + DH, DH), :] = both[DH : 2 * DH, toks:]
            rl_ref[s, i] = rl
        return carry

    lax.fori_loop(0, H // 2, heads, 0)
    pause()
    o2 = jnp.concatenate([jnp.transpose(of_ref[s]) for s in range(seqs)], axis=0).astype(B16)
    x2_ref[...] = x1_ref[...] + dot(o2, mat(wco))


def ffn_products(rows, og, wg, wu, wd, acc, da3):
    gate = dot(rows, wg[...])
    up = dot(rows, wu[...])
    square = gate * gate
    th = jnp.tanh(GELU_A * gate * (1.0 + GELU_B * square))
    half = 0.5 * (1.0 + th)
    value = gate * half
    slope = half + 0.5 * gate * (1.0 - th * th) * (GELU_A * (1.0 + 3.0 * GELU_B * square))
    inner = (value * up).astype(B16)
    acc[...] += dot(inner, wd[...])
    dwd = t_dot(inner, og).astype(B16)
    dinner = dot_t(og, wd[...]).astype(B16).astype(F32)
    dgate = (dinner * up * slope).astype(B16)
    dup = (dinner * value).astype(B16)
    da3[...] += dot_t(dgate, wg[...]) + dot_t(dup, wu[...])
    return t_dot(rows, dgate).astype(B16), t_dot(rows, dup).astype(B16), dwd


def ffn_kernel(
    x2_ref, og_ref, gain, wg, wu, wd, out_ref, dx2_ref, dgain_ref, dwg, dwu, dwd, a3, acc, da3
):
    step = pl.program_id(0)

    @pl.when(step == 0)
    def _():
        x2 = x2_ref[...]
        a3[...] = (x2 * scale_of(x2) * gain[2:3, :]).astype(B16)
        acc[...] = x2
        da3[...] = jnp.zeros_like(da3)

    dwg[...], dwu[...], dwd[...] = ffn_products(a3[...], og_ref[...], wg, wu, wd, acc, da3)

    @pl.when(step == pl.num_programs(0) - 1)
    def _():
        out_ref[...] = acc[...].astype(B16)
        dv, dgain = norm_back(x2_ref[...], gain[2:3, :], da3[...])
        dx2_ref[...] = og_ref[...].astype(F32) + dv
        dgain_ref[...] = dgain


def cross_back_kernel(
    seqs,
    groups,
    dx2_ref,
    x1_ref,
    a2_ref,
    gain,
    qt_ref,
    of_ref,
    rl_ref,
    kn,
    kt,
    vn,
    enc,
    wco,
    wcq,
    wck,
    wcv,
    wo,
    ot,
    dx1_ref,
    dgain_ref,
    dot_ref,
    denc_ref,
    dwco,
    dwcq,
    dwck,
    dwcv,
    dwo,
    dt,
    dqt,
    dk,
    dv,
    need=lambda *refs: None,
    done=lambda ref: None,
):
    toks = qt_ref.shape[2]
    span = kn.shape[0] // seqs
    dx2 = dx2_ref[...]
    dc = dx2.astype(B16)
    o2t = [of_ref[s].astype(B16) for s in range(seqs)]
    total = dot(o2t[0], dc[0:toks])
    for s in range(1, seqs):
        total = total + dot(o2t[s], dc[s * toks : (s + 1) * toks])
    dwco[...] = total.astype(B16)
    done(dwco)
    need(wco)
    do2 = dot_t(dc, mat(wco))
    for s in range(seqs):
        dt[s] = jnp.transpose(do2[s * toks : (s + 1) * toks]).astype(B16)

    need(kn, kt, vn)

    def heads(i, carry):
        col = pl.multiple_of(2 * i * DH, 2 * DH)
        pair = pl.ds(col, 2 * DH)
        for s in range(seqs):
            keys = slice(s * span, (s + 1) * span)
            q_rows, d_rows = qt_ref[s, pair, :], dt[s, pair, :]
            q_pair = apart(jnp.transpose(q_rows.astype(F32)), 0, 1).astype(B16)
            d_pair = apart(jnp.transpose(d_rows.astype(F32)), 0, 1).astype(B16)
            prob = jnp.exp(dot(kn[keys, pair], apart(q_rows, 1, 0))) * rl_ref[s, i]
            terms = d_rows.astype(F32) * of_ref[s, pair, :]
            delta = jnp.concatenate(
                [jnp.sum(terms[n * DH : (n + 1) * DH], axis=0, keepdims=True) for n in range(2)],
                axis=1,
            )
            ds = (prob * (dot(vn[keys, pair], apart(d_rows, 1, 0)) - delta)).astype(B16)
            dq = dot(kt[pair, keys], ds).astype(B16)
            dqt[s, pl.ds(col, DH), :] = dq[:DH, :toks]
            dqt[s, pl.ds(col + DH, DH), :] = dq[DH:, toks:]
            dk[keys, pair] = dot(ds, q_pair).astype(B16)
            dv[keys, pair] = dot(prob.astype(B16), d_pair).astype(B16)
        return carry

    lax.fori_loop(0, H // 2, heads, 0)
    need(enc, wck, wcv, wcq, wo)
    dwck[...] = t_dot(mat(enc), dk[...]).astype(B16)
    done(dwck)
    dwcv[...] = t_dot(mat(enc), dv[...]).astype(B16)
    done(dwcv)
    denc_ref[...] = (dot_t(dk[...], mat(wck)) + dot_t(dv[...], mat(wcv))).astype(B16)
    done(denc_ref)
    dq2 = jnp.concatenate(
        [jnp.transpose(dqt[s].astype(F32)) for s in range(seqs)], axis=0
    ).astype(B16)
    dwcq[...] = t_dot(a2_ref[...], dq2).astype(B16)
    done(dwcq)
    term, dgain = norm_back(x1_ref[...], gain[1:2, :], dot_t(dq2, mat(wcq)))
    dgain_ref[...] = dgain
    dx1 = dx2 + term
    dx1_ref[...] = dx1
    db = dx1.astype(B16)
    total = dot(rows_of(ot, 0, seqs), db[0:toks])
    for s in range(1, seqs):
        total = total + dot(rows_of(ot, s, seqs), db[s * toks : (s + 1) * toks])
    dwo[...] = total.astype(B16)
    done(dwo)
    do = dot_t(db, mat(wo))
    width = D // groups
    for s in range(seqs):
        turned = jnp.transpose(do[s * toks : (s + 1) * toks]).astype(B16)
        for g in range(groups):
            dot_ref[s * groups + g] = turned[g * width : (g + 1) * width].reshape(
                dot_ref.shape[1:]
            )


def cross_back_moves_kernel(kernel, ins, outs, far_ins, far_outs, *refs):
    refs = list(refs)
    take = lambda n: [refs.pop(0) for _ in range(n)]
    args, results, scratch = take(ins), take(outs), take(4)
    near_in, near_out = take(len(far_ins)), take(len(far_outs))
    moves = Moves(refs[0])
    moves.bring([(args[i], near) for i, near in zip(far_ins, near_in)])
    for i, near in zip(far_ins, near_in):
        args[i] = near
    made = {}
    for i, near in zip(far_outs, near_out):
        made[id(near)] = (near, results[i])
        results[i] = near

    def done(ref):
        moves.take(*made[id(ref)])

    kernel(*args, *results, *scratch, need=moves.need, done=done)
    moves.end()


def cross_back_moves_call(kernel, outs, args, scratch):
    near = pl.BlockSpec(memory_space=pltpu.VMEM)
    anywhere = pl.BlockSpec(memory_space=pl.ANY)
    far_ins = [11, 7, 8, 9, 10, 13, 14, 12, 15]
    far_outs = [3, 4, 5, 6, 7, 8]
    scratch = [*scratch]
    scratch += [pltpu.VMEM(args[i].shape, args[i].dtype) for i in far_ins]
    scratch += [pltpu.VMEM(*outs[i]) for i in far_outs]
    scratch += [pltpu.SemaphoreType.DMA((len(far_ins) + len(far_outs),))]
    return pl.pallas_call(
        functools.partial(
            cross_back_moves_kernel, kernel, len(args), len(outs), far_ins, far_outs
        ),
        out_shape=[jax.ShapeDtypeStruct(s, t) for s, t in outs],
        in_specs=[anywhere if i in far_ins else near for i in range(len(args))],
        out_specs=[anywhere if i in far_outs else near for i in range(len(outs))],
        scratch_shapes=scratch,
        compiler_params=pltpu.CompilerParams(vmem_limit_bytes=60 * 2**20),
        name="cross_back",
    )(*args)


def last_kernel(plan, hidden, grads, a1, gain, dx1, wq, wk, wv, dh_ref, dgain_ref, dwq, dwk, dwv):
    dgain_ref[...] = last_products(
        plan, hidden, grads, a1, gain, dx1, wq, wk, wv, dh_ref, dwq, dwk, dwv
    )


def last_products(p, hidden, grads, a1, gain, dx1, wq, wk, wv, dh_ref, dwq, dwk, dwv):
    x = hidden[...].reshape(p.S * p.T, D).astype(F32)
    da1 = jnp.zeros((p.S * p.T, D), F32)
    for n, (weight, dw) in enumerate(((wq, dwq), (wk, dwk), (wv, dwv))):
        rows = []
        for s in range(p.S):
            turned = jnp.concatenate(
                [
                    grads[s * p.G + i // p.HG, i % p.HG, n * DH : (n + 1) * DH, :]
                    for i in range(H)
                ],
                axis=0,
            )
            rows.append(jnp.transpose(turned.astype(F32)))
        d = jnp.concatenate(rows, axis=0).astype(B16)
        dw[...] = t_dot(a1[...], d).astype(B16).reshape(dw.shape)
        da1 = da1 + dot_t(d, mat(weight))
    term, dgain = norm_back(x, gain[0:1, :], da1)
    dh_ref[...] = (dx1[...] + term).astype(B16).reshape(dh_ref.shape)
    return dgain


def gather_rows(part):
    count = lax.axis_size("shard")
    rows, cols = part.shape
    half = rows // 2
    mine = lax.axis_index("shard")
    core = lax.axis_index("rep") % 2
    pairs = [(r, r ^ 1) for r in range(lax.axis_size("rep"))]
    own = lax.dynamic_slice(part, (core * half, 0), (half, cols))
    full = jnp.zeros((count, rows, cols), part.dtype)
    full = lax.dynamic_update_slice(full, part[None], (mine, 0, 0))
    for k in range(1, count):
        got = lax.ppermute(own, "shard", [(i, (i + k) % count) for i in range(count)])
        also = lax.ppermute(got, "rep", pairs)
        owner = (mine - k) % count
        full = lax.dynamic_update_slice(full, got[None], (owner, core * half, 0))
        full = lax.dynamic_update_slice(full, also[None], (owner, (1 - core) * half, 0))
    return full.reshape(count * rows, cols)


def reduce_grads(grads):
    owned = [lax.psum_scatter(g, "shard", scatter_dimension=0, tiled=True) for g in grads]
    summed = lax.psum(tuple(owned), "rep")
    return [s.astype(F32) for s in summed]


class Moves:
    def __init__(self, sems):
        self.sems, self.used, self.coming, self.going = sems, 0, {}, []

    def sem(self):
        self.used += 1
        return self.sems.at[self.used - 1]

    def bring(self, pairs):
        for far, near in pairs:
            sem = self.sem()
            pltpu.make_async_copy(far, near, sem).start()
            self.coming[id(near)] = (near, sem)

    def need(self, *refs):
        for ref in refs:
            if id(ref) in self.coming:
                near, sem = self.coming.pop(id(ref))
                landed(near, sem)

    def take(self, near, far):
        sem = self.sem()
        pltpu.make_async_copy(near, far, sem).start()
        self.going.append((near, sem))

    def end(self):
        for near, sem in self.going:
            landed(near, sem)


BITS = 4
ROW = -1


class Job:
    def __init__(self, result, row, rows, col, cols, order):
        self.result, self.order = result, order
        self.row, self.rows, self.col, self.cols = row, rows, col, cols

    def buffers(self):
        half, rows, lead = self.cols // 2, self.rows, (2,)
        shapes = [(2, rows, half)] * 2
        for axis in self.order:
            if axis == ROW:
                lead = ()
            else:
                rows //= 2
            shapes.append((*lead, rows, half))
        return shapes


def partner(bit):
    me = lax.axis_index("rep")
    half = 2**bit
    mine = (me // half) % 2
    return mine, me + half * (1 - 2 * mine)


def to_rep(src, dst, send, recv, bit):
    return remote(src, dst, send, recv, partner(bit)[1])


def to_row(src, dst, send, recv):
    x = lax.axis_index("shard")
    return pltpu.make_async_remote_copy(
        src_ref=src,
        dst_ref=dst,
        send_sem=send,
        recv_sem=recv,
        device_id={"shard": 1 - x},
        device_id_type=MESH,
    )


def add_into(acc, term, rows):
    step = 16 if rows % 32 else 32

    def body(i, carry):
        at = pl.ds(pl.multiple_of(i * step, step), step)
        acc[at, :] = (acc[at, :].astype(F32) + term[at, :].astype(F32)).astype(B16)
        return carry

    lax.fori_loop(0, rows // step, body, 0)


class JobRun:
    def __init__(self, job, source, result, bufs, sems, index):
        self.job, self.source, self.result = job, source, result
        self.acc, self.core, *self.part = bufs
        self.steps = [(0, 1), (1, FIRST_LAG)] + [(n, LAG) for n in range(2, 10)]
        send, recv, local = sems
        self.send = [send.at[index, i] for i in range(9)]
        self.recv = [recv.at[index, i] for i in range(9)]
        self.local = [local.at[index, i] for i in range(2)]
        self.sent = []
        self.x = lax.axis_index("shard")
        half = job.cols // 2
        core = partner(0)[0]
        self.mine = pl.ds(pl.multiple_of(job.col + core * half, 128), half)
        self.other = pl.ds(pl.multiple_of(job.col + (1 - core) * half, 128), half)
        self.all = pl.ds(job.row, job.rows)
        self.plan, self.back = [], []
        owners, first, count = (0, 1), 0, job.rows
        for axis in job.order:
            if axis == ROW:
                keep = give = (first, count)
                owners, others = (self.x,), (1 - self.x,)
            else:
                count //= 2
                bit = partner(axis)[0]
                keep, give = (first + bit * count, count), (first + (1 - bit) * count, count)
                self.back.insert(0, (axis, (first, 2 * count), give))
                first, others = keep[0], owners
            self.plan.append((axis, owners, keep, others, give))
        self.last = (first, count)

    def span(self, first, count):
        return pl.ds(pl.multiple_of(first, 16), count)

    def out(self, first, count):
        return self.result.at[self.span(self.job.row + first, count), self.mine]

    def held(self, owners, rows):
        at = slice(None) if len(owners) == 2 else owners[0]
        return self.acc.at[at, self.span(*rows)]

    def go(self, n, source, target, axis):
        copy = (to_row if axis == ROW else to_rep)(
            source, target, self.send[n], self.recv[n], *(() if axis == ROW else (axis,))
        )
        copy.start()
        self.sent.append(copy)

    def stage(self, n):
        job = self.job
        if n == 0:
            pltpu.make_async_copy(
                self.source.at[:, self.all, self.mine], self.acc, self.local[0]
            ).start()
            self.go(0, self.source.at[:, self.all, self.other], self.core, 0)
        elif n <= 5:
            if n == 1:
                landed(self.acc, self.local[0])
                landed(self.core, self.recv[0])
                for i in range(2):
                    add_into(self.acc.at[i], self.core.at[i], job.rows)
            else:
                _, owners, keep, _, _ = self.plan[n - 2]
                terms = self.part[n - 2]
                landed(terms, self.recv[n - 1])
                for i, owner in enumerate(owners):
                    add_into(
                        self.held((owner,), keep),
                        terms.at[i] if len(owners) == 2 else terms,
                        keep[1],
                    )
            if n < 5:
                axis, _, _, others, give = self.plan[n - 1]
                self.go(n, self.held(others, give), self.part[n - 1], axis)
            else:
                piece, place = self.held((self.x,), self.last), self.out(*self.last)
                pltpu.make_async_copy(piece, place, self.local[1]).start()
                self.go(5, piece, place, self.back[0][0])
        elif n <= 8:
            if n == 6:
                landed(self.out(*self.last), self.local[1])
            _, rows, came = self.back[n - 6]
            landed(self.out(*came), self.recv[n - 1])
            place = self.out(*rows)
            self.go(n, place, place, self.back[n - 5][0] if n < 8 else 0)
        else:
            landed(self.result.at[self.all, self.other], self.recv[8])
            for copy in self.sent:
                copy.wait_send()


def job_buffers(job):
    return [pltpu.VMEM(shape, B16) for shape in job.buffers()]


class SmallRun:
    steps = [(n, 1) for n in range(BITS + 2)]

    def __init__(self, sums, terms, send, recv):
        self.sums, self.terms, self.send, self.recv = sums, terms, send, recv

    def copy(self, n):
        args = (self.sums.at[n], self.terms.at[n], self.send.at[n], self.recv.at[n])
        return to_row(*args) if n == BITS else to_rep(*args, n)

    def stage(self, n):
        if n > 0:
            landed(self.terms.at[n - 1], self.recv.at[n - 1])
            self.sums[n] = self.sums[n - 1] + self.terms[n - 1]
        if n <= BITS:
            self.copy(n).start()
        else:
            for i in range(BITS + 1):
                self.copy(i).wait_send()


class EncodedRun:
    def __init__(self, source, result, bufs, send, recv, load, lag):
        self.source, self.result, self.send, self.recv, self.load = source, result, send, recv, load
        self.acc, self.terms = bufs[0], bufs[1:]
        self.bits = [partner(b)[0] for b in range(BITS)]
        self.steps = [(0, 1)] + [(n + 1, lag) for n in range(1, BITS + 1)]
        self.sent = []

    def part(self, ref, n, bit):
        at = (slice(None),) * (BITS - n) + (bit,)
        return ref.at[at]

    def go(self, n, source):
        copy = to_rep(source, self.terms[n], self.send.at[n], self.recv.at[n], n)
        copy.start()
        self.sent.append(copy)

    def fixed(self, n):
        return self.acc.at[
            (slice(None),) * (BITS + 1 - n) + tuple(self.bits[b] for b in range(n - 1, 0, -1))
        ]

    def add(self, n):
        left = self.fixed(n + 1)
        terms = self.terms[n]
        lead = left.shape[:-2]
        count = 1
        for d in lead:
            count *= d

        def body(i, carry):
            at, rest = [], i
            for d in reversed(lead):
                at.insert(0, rest % d)
                rest = rest // d
            at = tuple(at)
            left[at] = (left[at].astype(F32) + terms[at].astype(F32)).astype(B16)
            return carry

        lax.fori_loop(0, count, body, 0)

    def stage(self, step):
        if step == 0:
            pltpu.make_async_copy(
                self.part(self.source, 0, self.bits[0]), self.acc, self.load
            ).start()
            self.go(0, self.part(self.source, 0, 1 - self.bits[0]))
            return
        n = step - 1
        if n == 1:
            landed(self.acc, self.load)
        landed(self.terms[n - 1], self.recv.at[n - 1])
        self.add(n - 1)
        if n < BITS:
            self.go(n, self.part(self.fixed(n), n, 1 - self.bits[n]))
        else:
            self.result[...] = self.fixed(BITS)[...]
            for copy in self.sent:
                copy.wait_send()


class Pipeline:
    def __init__(self):
        self.waiting, self.active, self.now = [], [], 0

    def add(self, runs):
        self.waiting += runs

    def tick(self, count=1):
        for _ in range(count):
            if self.waiting:
                self.active.insert(0, [self.waiting.pop(0), 0, self.now])
            early = [e for e in self.active if e[0].steps[e[1]][0] < 2]
            late = [e for e in self.active if e[0].steps[e[1]][0] >= 2]
            for entry in early + late:
                run, at, due = entry
                if due <= self.now:
                    stage, wait = run.steps[at]
                    run.stage(stage)
                    entry[1:] = [at + 1, self.now + wait]
            self.active = [e for e in self.active if e[1] < len(e[0].steps)]
            self.now += 1

    def finish(self):
        while self.waiting or self.active:
            self.tick()


def jobs_of(result, rows, cols, orders):
    wide = cols // 2 if cols > 1024 else cols
    tall = rows // 2 if rows > 512 else rows
    return [
        Job(result, row, tall, col, wide, next(orders))
        for row in range(0, rows, tall)
        for col in range(0, cols, wide)
    ]


EARLY = [(ROW, 1, 2, 3), (2, ROW, 1, 3), (ROW, 1, 2, 3), (ROW, 1, 2, 3)]
LATE = [(ROW, 1, 2, 3)] * 3
SMALL_ROWS = 16
FETCH_LAG = 3
FIRST_LAG = 3
LAG = 2
TICKS = (4, 1, 1, 2)


def tail_kernel(p, jobs, early, arrays, *refs):
    refs = list(refs)
    take = lambda n: [refs.pop(0) for _ in range(n)]
    sources = take(early)
    dot_, denc, *far = take(7)
    lines, rl_ref, hidden, a1, dx1, dgc, dgf = take(7)
    results = take(arrays)
    small, dh_ref, denc_out = take(3)
    dout, dq, dkv, part, out, grads = take(6)
    late = take(3)
    recv, of_ref, wq, wk, wv = held = take(5)
    enc_bufs = take(BITS + 1)
    enc_send, enc_recv, enc_load, move_sems = take(4)
    small_sums, small_terms = take(2)
    back = take(7)
    rows_send, rows_recv, part_sem, got_sem, ret_send, ret_recv = take(6)
    small_send, small_recv = take(2)
    sems = take(3)
    moves = Moves(move_sems)
    moves.bring(zip(far, held))
    sources = sources + late
    runs = []
    for i, job in enumerate(jobs):
        bufs = take(len(job.buffers()))
        runs.append(JobRun(job, sources[job.result], results[job.result], bufs, sems, i))
    ready = len(jobs) - 3
    enc_run = EncodedRun(denc, denc_out, enc_bufs, enc_send, enc_recv, enc_load.at[0], LAG)

    me = lax.axis_index("rep")
    w = me % p.W
    unit = me // p.W
    group = unit % p.G
    mine = p.worker_of(me)
    slot = p.slot_of(me)
    barrier = pltpu.get_barrier_semaphore()
    for k in range(1, p.R):
        pl.semaphore_signal(
            barrier, inc=1, device_id={"rep": (me + k) % p.R}, device_id_type=MESH
        )
    x = lax.axis_index("shard")
    pl.semaphore_signal(barrier, inc=1, device_id={"shard": 1 - x}, device_id_type=MESH)
    pl.semaphore_wait(barrier, p.R)

    pipeline = Pipeline()
    pipeline.add([*runs[:2], enc_run, *runs[2:ready]])
    tick = pipeline.tick
    def outward(u, h):
        to, sem = u * p.W + mine, rows_recv.at[slot, h]
        return me, to, dot_.at[u, h], dout.at[slot, h], rows_send.at[u, h], sem

    def give(k, j, h):
        to = (w + k) % p.W
        return remote(
            dkv.at[p.source(j, to), h],
            part.at[k - 1, j, h],
            part_sem.at[k - 1, j, h],
            got_sem.at[k - 1, j, h],
            me - w + to,
        )

    def returned(j, h):
        r, sem = p.source(j, w), ret_recv.at[unit, h]
        return me, r, out.at[j, h], grads.at[unit, h], ret_send.at[j, h], sem

    def return_all(h):
        for j in range(p.J):
            total = dkv[p.source(j, w), h].astype(F32)
            for k in range(1, p.W):
                landed(part.at[k - 1, j, h], got_sem.at[k - 1, j, h])
                total = total + part[k - 1, j, h].astype(F32)
            out[j, h, 0:DH, :] = dq[j, h]
            out[j, h, DH : 3 * DH, :] = total.astype(B16)
            start_either(*returned(j, h))

    for h in range(p.HG):
        for u in range(p.U):
            start_either(*outward(u, h))
    tick(TICKS[0])
    lines_at = lax.broadcasted_iota(jnp.int32, (SMALL_ROWS, D), 0)
    block = jnp.zeros((SMALL_ROWS, D), F32)
    moves.need(recv, of_ref)
    for h in range(p.HG):
        for j in range(p.J):
            landed(dout.at[j, h], rows_recv.at[j, h])
        between = functools.partial(return_all, h - 1) if h > 0 else None
        sums = back_head(
            p,
            w,
            h,
            line_of(p, lines, group * p.HG + h),
            recv,
            dout,
            of_ref,
            rl_ref.at[h],
            dq,
            dkv,
            *back,
            between=between,
        )
        for j in range(p.J):
            for k in range(1, p.W):
                give(k, j, h).start()
        sums = jnp.concatenate([sums, jnp.zeros((1, D - 2 * p.T), F32)], axis=1)
        block = jnp.where(lines_at == 3 + group * p.HG + h, sums, block)
        tick(TICKS[1])
    tick(TICKS[2])
    return_all(p.HG - 1)
    tick(TICKS[3])
    for u in range(p.U):
        for h in range(p.HG):
            landed(grads.at[u, h], ret_recv.at[u, h])
    moves.need(wq, wk, wv)
    dgain = last_products(p, hidden, grads, a1, lines, dx1, wq, wk, wv, dh_ref, *late)
    for i, row in enumerate((dgain, dgc[...], dgf[...])):
        block = jnp.where(lines_at == i, row, block)
    small_sums[0] = block
    pipeline.add([*runs[ready:], SmallRun(small_sums, small_terms, small_send, small_recv)])
    pipeline.finish()
    small[...] = small_sums[BITS + 1]
    moves.end()
    for h in range(p.HG):
        for u in range(p.U):
            end_either(*outward(u, h))
        for j in range(p.J):
            end_either(*returned(j, h))
            for k in range(1, p.W):
                give(k, j, h).wait_send()


def tail_call(p, early, dot_, denc, far, held, collective):
    half = D // 2
    shapes = [g.shape[1:] for g in early] + [(half, D)] * 3
    turn = itertools.cycle(EARLY)
    jobs = [job for i in range(len(early)) for job in jobs_of(i, *shapes[i], turn)]
    jobs += [Job(len(early) + i, 0, half, 0, D, order) for i, order in enumerate(LATE)]
    sources = early
    piece = denc.shape[0] // (p.S * p.R)
    denc = denc.reshape((p.S,) + (2,) * BITS + (piece, D))
    dma = pltpu.SemaphoreType.DMA
    others = max(p.W - 1, 1)
    scratch = [
        pltpu.VMEM((p.J, p.HG, DH, p.T), B16),
        pltpu.VMEM((p.J, p.HG, DH, p.T), B16),
        pltpu.VMEM((p.R, p.HG, 2 * DH, p.T), B16),
        pltpu.VMEM((others, p.J, p.HG, 2 * DH, p.T), B16),
        pltpu.VMEM((p.J, p.HG, 3 * DH, p.T), B16),
        pltpu.VMEM((p.U, p.HG, 3 * DH, p.T), B16),
    ]
    scratch += [pltpu.VMEM((2, half, D), B16)] * 3
    scratch += [pltpu.VMEM(a.shape, a.dtype) for a in far]
    scratch += [pltpu.VMEM((p.S,) + (2,) * (BITS - 1) + (piece, D), B16)]
    scratch += [
        pltpu.VMEM((p.S,) + (2,) * (BITS - 1 - n) + (piece, D), B16) for n in range(BITS)
    ]
    scratch += [dma((BITS,)), dma((BITS,)), dma((1,)), dma((len(far),))]
    scratch += [
        pltpu.VMEM((BITS + 2, SMALL_ROWS, D), F32),
        pltpu.VMEM((BITS + 1, SMALL_ROWS, D), F32),
    ]
    scratch += back_scratch(p)
    scratch += [
        dma((p.U, p.HG)),
        dma((p.J, p.HG)),
        dma((others, p.J, p.HG)),
        dma((others, p.J, p.HG)),
        dma((p.J, p.HG)),
        dma((p.U, p.HG)),
        dma((BITS + 1,)),
        dma((BITS + 1,)),
        dma((len(jobs), 9)),
        dma((len(jobs), 9)),
        dma((len(jobs), 2)),
    ]
    for job in jobs:
        scratch += job_buffers(job)
    anywhere = pl.BlockSpec(memory_space=pl.ANY)
    near = pl.BlockSpec(memory_space=pltpu.VMEM)
    *sums, small, dh, denc = pl.pallas_call(
        functools.partial(tail_kernel, p, jobs, len(early), len(shapes)),
        out_shape=[jax.ShapeDtypeStruct(s, B16) for s in shapes]
        + [
            jax.ShapeDtypeStruct((SMALL_ROWS, D), F32),
            jax.ShapeDtypeStruct((p.S, p.T, D), B16),
            jax.ShapeDtypeStruct((p.S, piece, D), B16),
        ],
        in_specs=[anywhere] * (len(sources) + 2 + len(far)) + [near] * len(held),
        out_specs=[anywhere] * len(shapes) + [near] * 3,
        scratch_shapes=scratch,
        compiler_params=pltpu.CompilerParams(
            collective_id=collective, has_side_effects=True, vmem_limit_bytes=60 * 2**20
        ),
        name="tail",
    )(*sources, dot_, denc, *far, *held)
    return sums, small, dh, denc


def widen_kernel(count, *refs):
    for i in range(count):
        refs[count + i][...] = refs[i][...].astype(F32)


def widen(mats):
    parts = 2
    blocks = [
        pl.BlockSpec((m.shape[0] // parts, m.shape[1]), lambda i: (i, 0)) for m in mats
    ]
    return pl.pallas_call(
        functools.partial(widen_kernel, len(mats)),
        grid=(parts,),
        out_shape=[jax.ShapeDtypeStruct(m.shape, F32) for m in mats],
        in_specs=blocks,
        out_specs=blocks,
        compiler_params=pltpu.CompilerParams(vmem_limit_bytes=63 * 2**20),
        name="widen",
    )(*mats)


class Fetch:
    def __init__(self, master, staged, out, first, rows, col, cols, stage, own, sems, index, wide):
        self.x = lax.axis_index("shard")
        self.core, self.y = [partner(b)[0] for b in range(2)]
        self.rows, self.staged, self.wide = rows, staged, wide
        self.master = master.at[pl.ds(first, rows), pl.ds(col, cols)]
        self.stage_ref = stage.at[pl.ds(0, rows), pl.ds(0, cols)]
        self.own = own
        self.out, self.first, self.col, self.cols = out, first, col, cols
        load, keep, self.send, self.recv = sems
        self.load, self.keep = load.at[index], keep.at[index]
        self.send = [self.send.at[index, i] for i in range(3)]
        self.recv = [self.recv.at[index, i] for i in range(3)]

    def span(self, core, y=None):
        half = self.rows // 2
        if y is None:
            return core * half, half
        return core * half + y * (half // 2), half // 2

    def place(self, owner, *share):
        first, count = self.span(*share)
        first = pl.multiple_of(self.first + first, 16)
        return self.out.at[owner, pl.ds(first, count), pl.ds(self.col, self.cols)]

    def share(self):
        return (self.core, self.y) if self.wide else (self.core,)

    def read(self):
        pltpu.make_async_copy(self.master, self.stage_ref, self.load).start()

    def kept(self):
        return self.out.at[self.x, pl.ds(self.first, self.rows), pl.ds(self.col, self.cols)]

    def across(self):
        first, count = self.span(*self.share())
        part = self.own.at[pl.ds(pl.multiple_of(first, 16), count)]
        return to_row(part, self.place(self.x, *self.share()), self.send[0], self.recv[0])

    def start(self):
        landed(self.stage_ref, self.load)
        step = 32

        def body(i, carry):
            at = pl.ds(pl.multiple_of(i * step, step), step)
            self.own[at, :] = self.stage_ref[at, :].astype(B16)
            return carry

        lax.fori_loop(0, self.rows // step, body, 0)
        self.across().start()
        if self.staged:
            pltpu.make_async_copy(self.own, self.kept(), self.keep).start()

    def beside(self):
        place = self.place(1 - self.x, self.core, self.y)
        return to_rep(place, place, self.send[2], self.recv[2], 1)

    def over(self):
        place = self.place(1 - self.x, self.core)
        return to_rep(place, place, self.send[1], self.recv[1], 0)

    def relay(self):
        landed(self.place(1 - self.x, *self.share()), self.recv[0])
        if self.wide:
            self.beside().start()
        else:
            self.over().start()

    def relay_more(self):
        if self.wide:
            landed(self.place(1 - self.x, self.core, 1 - self.y), self.recv[2])
            self.over().start()

    def finish(self):
        landed(self.place(1 - self.x, 1 - self.core), self.recv[1])

    def end(self):
        self.across().wait_send()
        self.over().wait_send()
        if self.wide:
            self.beside().wait_send()
        if self.staged:
            landed(self.kept(), self.keep)


def small_block(p, gains, table, buckets, x):
    at = lax.broadcasted_iota(jnp.int32, (SMALL_ROWS, D), 0)
    block = jnp.zeros((SMALL_ROWS, D), F32)
    for i, gain in enumerate(gains):
        part = gain[...].astype(B16).astype(F32).reshape(1, -1)
        none = jnp.zeros_like(part)
        row = jnp.where(
            x == 0,
            jnp.concatenate([part, none], axis=1),
            jnp.concatenate([none, part], axis=1),
        )
        block = jnp.where(at == i, row, block)
    held = table.shape[0]
    bucket = lax.broadcasted_iota(jnp.int32, (held, 2 * p.T), 0) + x * held
    near = buckets[...].reshape(1, -1)[:, : 2 * p.T]
    onehot = (near == bucket).astype(F32).astype(B16)
    lines = t_dot(table[...].astype(B16), onehot)
    lines = jnp.concatenate([lines, jnp.zeros((H, D - 2 * p.T), F32)], axis=1)
    lines = jnp.concatenate(
        [jnp.zeros((3, D), F32), lines, jnp.zeros((SMALL_ROWS - 3 - H, D), F32)], axis=0
    )
    return block + lines


def head_kernel(p, *refs):
    refs = list(refs)
    take = lambda n: [refs.pop(0) for _ in range(n)]
    masters = take(11)
    hidden, encoded, g1, g2, g3, table, buckets = take(7)
    far_mats = take(8)
    wide = take(3)
    far_recv, far_enc, far_kn, far_kt, far_vn = take(5)
    small, a1, of_ref, rl_ref, ot = take(5)
    x1, x2, a2, qt2, of2, rl2 = take(6)
    mats = take(8)
    recv, enc, kn, kt, vn, vt = take(6)
    moves = Moves(take(1)[0])
    send, o_ref, mine_small, their_small = take(4)
    stages = take(4)
    owns = take(6)
    att = take(3)
    fetch_sems = take(4)
    small_send, small_recv, enc_send, enc_recv = take(4)
    tok_send, relay_sem, tok_recv, back_send, back_recv = take(5)

    me = lax.axis_index("rep")
    x = lax.axis_index("shard")
    w = me % p.W
    unit = me // p.W
    group = unit % p.G
    mine = p.worker_of(me)
    bits = [(me // 2**b) % 2 for b in range(BITS)]

    half = D // 2
    jobs = []
    for i in range(8):
        jobs.append((masters[i], mats[i], 0, half, 0, D))
    for i, ref in enumerate(wide):
        rows, cols = ref.shape[1:]
        tall = rows // 2 if rows > 512 else rows
        part = cols // 2 if cols > 1024 else cols
        for row in range(0, rows, tall):
            for col in range(0, cols, part):
                jobs.append((masters[8 + i], ref, row, tall, col, part))
    fetches = []
    for i, (master, out, row, rows, col, cols) in enumerate(jobs):
        staged = i >= 8
        own = owns[i - 8] if staged else out.at[x]
        fetches.append(
            Fetch(
                master,
                staged,
                out,
                row,
                rows,
                col,
                cols,
                stages[i % 4],
                own,
                fetch_sems,
                i,
                3 <= i < 5 or (i > 4 and i % 2 == 0),
            )
        )

    barrier = pltpu.get_barrier_semaphore()
    for k in range(1, p.R):
        pl.semaphore_signal(
            barrier, inc=1, device_id={"rep": (me + k) % p.R}, device_id_type=MESH
        )
    pl.semaphore_signal(barrier, inc=1, device_id={"shard": 1 - x}, device_id_type=MESH)
    for fetch in fetches[:4]:
        fetch.read()
    mine_small[...] = small_block(p, (g1, g2, g3), table, buckets, x)
    enc[:, bits[3], bits[2], bits[1], bits[0]] = encoded[...]
    pl.semaphore_wait(barrier, p.R)

    share = to_row(mine_small, their_small, small_send, small_recv)
    share.start()

    def enc_copy(n):
        at = (slice(None),) * (1 + n) + tuple(bits[b] for b in range(BITS - 1 - n, -1, -1))
        part = enc.at[at]
        return to_rep(part, part, enc_send.at[n], enc_recv.at[n], BITS - 1 - n)

    def enc_landed(n):
        b = [bits[i] for i in range(BITS - 1 - n, -1, -1)]
        b[0] = 1 - b[0]
        landed(enc.at[(slice(None),) * (1 + n) + tuple(b)], enc_recv.at[n])

    started, relayed, more = 0, 0, 0

    def begin(count=1):
        nonlocal started
        for _ in range(count):
            if started < len(fetches):
                fetches[started].start()
                if started + 4 < len(fetches):
                    fetches[started + 4].read()
                started += 1

    def pass_on(count=1):
        nonlocal relayed, more
        for _ in range(count):
            if more < relayed:
                fetches[more].relay_more()
                more += 1
            if relayed < started:
                fetches[relayed].relay()
                relayed += 1

    def slot():
        begin()
        if started - relayed > FETCH_LAG or started == len(fetches):
            pass_on()

    begin(3)
    enc_copy(0).start()
    landed(their_small, small_recv)
    small[...] = mine_small[...] + their_small[...]
    enc_landed(0)
    enc_copy(1).start()
    pass_on(2)
    enc_landed(1)
    enc_copy(2).start()
    pass_on()
    begin(2)
    fetches[2].relay_more()
    more = 3
    for fetch, far in zip(fetches[:3], far_mats):
        fetch.finish()
        moves.take(fetch.out, far)
    project_kernel(p, hidden, small, *mats[:3], a1, send)

    def token(u, h):
        to, sem = u * p.W + mine, tok_recv.at[me, h]
        return me, to, send.at[u, h], recv.at[me, h], tok_send.at[u, h], sem

    def relay(k, j, h):
        r = p.source(j, w)
        part = recv.at[r, h, pl.ds(DH, 2 * DH)]
        to = me - w + (w + k) % p.W
        return remote(part, part, relay_sem.at[k - 1, j, h], tok_recv.at[r, h], to)

    def returned(j, h):
        r, sem = p.source(j, w), back_recv.at[unit, h]
        return me, r, o_ref.at[j, h], ot.at[unit, h], back_send.at[j, h], sem

    def relay_all(h):
        for j in range(p.J):
            r = p.source(j, w)
            landed(recv.at[r, h], tok_recv.at[r, h])
            for k in range(1, p.W):
                relay(k, j, h).start()

    def relayed_all(h):
        for k in range(1, p.W):
            for j in range(p.J):
                r = p.source(j, (w + k) % p.W)
                landed(recv.at[r, h, pl.ds(DH, 2 * DH)], tok_recv.at[r, h])

    def send_all(h):
        for u in range(p.U):
            start_either(*token(u, h))

    send_all(0)
    enc_landed(2)
    enc_copy(3).start()
    begin()
    pass_on(2)
    enc_landed(3)
    moves.take(enc, far_enc)
    fetches[4].relay_more()
    more = 5

    def encode(i, natural, turned):
        fetches[i].finish()
        moves.take(mats[i], far_mats[i])
        encode_one(enc, mats[i], natural, turned)
        slot()

    encode(3, kn, kt)
    if p.HG > 1:
        send_all(1)
    relay_all(0)
    encode(4, vn, vt)
    for h in range(2, p.HG):
        send_all(h)
    for made, far in ((kn, far_kn), (kt, far_kt), (vn, far_vn)):
        moves.take(made, far)
    slot()
    relayed_all(0)
    for h in range(p.HG):
        line = line_of(p, small, group * p.HG + h)
        between = functools.partial(relay_all, h + 1) if h + 1 < p.HG else None
        attend_head(p, w, h, line, recv, o_ref, of_ref, rl_ref.at[h], *att, between=between)
        for j in range(p.J):
            start_either(*returned(j, h))
        slot()
        if h + 1 < p.HG:
            relayed_all(h + 1)
    moves.take(recv, far_recv)
    slot()
    while more < 8:
        pass_on()
    for fetch, far in zip(fetches[5:8], far_mats[5:]):
        fetch.finish()
        moves.take(fetch.out, far)
    for u in range(p.U):
        for h in range(p.HG):
            landed(ot.at[u, h], back_recv.at[u, h])

    pause = slot
    cross_kernel(
        p.S, hidden, ot, mats[5], small, mats[6], mats[7], kn, vt, x1, x2, a2, qt2, of2, rl2, pause
    )
    begin(len(fetches))
    while more < len(fetches):
        pass_on()
    for fetch in fetches[8:]:
        fetch.finish()
    for fetch in fetches:
        fetch.end()
    moves.end()
    share.wait_send()
    for n in range(BITS):
        enc_copy(n).wait_send()
    for h in range(p.HG):
        for u in range(p.U):
            end_either(*token(u, h))
        for j in range(p.J):
            end_either(*returned(j, h))
            for k in range(1, p.W):
                relay(k, j, h).wait_send()


def head_call(p, masters, hidden, encoded, gains, table, buckets, collective):
    half, tokens = D // 2, p.S * p.T
    piece = encoded.shape[1]
    enc_rows = p.S * piece * p.R
    wides = [m.shape for m in masters[8:]]
    near = pl.BlockSpec(memory_space=pltpu.VMEM)
    anywhere = pl.BlockSpec(memory_space=pl.ANY)
    outs = [((2, half, D), B16)] * 8 + [((2, *s), B16) for s in wides]
    inner = [
        ((p.R, p.HG, 3 * DH, p.T), B16),
        ((p.S,) + (2,) * BITS + (piece, D), B16),
        ((enc_rows, D), B16),
        ((D, enc_rows), B16),
        ((enc_rows, D), B16),
    ]
    outs += inner
    inner = [((2, half, D), B16)] * 8 + inner + [((H // 2, 2 * DH + ONES, enc_rows), B16)]
    outs += [
        ((SMALL_ROWS, D), F32),
        ((tokens, D), B16),
        ((p.J, p.HG, DH, p.T), F32),
        ((p.HG, p.NP, 1, 2 * p.T), F32),
        ((p.U, p.HG, DH, p.T), B16),
        ((tokens, D), F32),
        ((tokens, D), F32),
        ((tokens, D), B16),
        ((p.S, D, p.T), B16),
        ((p.S, D, p.T), F32),
        ((p.S, H // 2, 1, 2 * p.T), F32),
    ]
    parts = [(half, D)] * 8
    for rows, cols in wides:
        tall = rows // 2 if rows > 512 else rows
        part = cols // 2 if cols > 1024 else cols
        parts += [(tall, part)] * ((rows // tall) * (cols // part))
    count = len(parts)
    dma = pltpu.SemaphoreType.DMA
    scratch = [pltpu.VMEM(s, t) for s, t in inner] + [dma((13,))]
    scratch += [
        pltpu.VMEM((p.U, p.HG, 3 * DH, p.T), B16),
        pltpu.VMEM((p.J, p.HG, DH, p.T), B16),
        pltpu.VMEM((SMALL_ROWS, D), F32),
        pltpu.VMEM((SMALL_ROWS, D), F32),
    ]
    tallest = max(r for r, _ in parts)
    widest = max(c for _, c in parts)
    scratch += [pltpu.VMEM((tallest, widest), F32)] * 4
    scratch += [pltpu.VMEM(s, B16) for s in parts[8:]]
    scratch += attend_scratch(p)
    scratch += [dma((count,)), dma((count,)), dma((count, 3)), dma((count, 3))]
    scratch += [dma, dma, dma((BITS,)), dma((BITS,))]
    scratch += [
        dma((p.U, p.HG)),
        dma((max(p.W - 1, 1), p.J, p.HG)),
        dma((p.R, p.HG)),
        dma((p.J, p.HG)),
        dma((p.U, p.HG)),
    ]
    return pl.pallas_call(
        functools.partial(head_kernel, p),
        out_shape=[jax.ShapeDtypeStruct(s, t) for s, t in outs],
        in_specs=[anywhere] * 11 + [near] * 7,
        out_specs=[anywhere] * 16 + [near] * 11,
        scratch_shapes=scratch,
        compiler_params=pltpu.CompilerParams(
            collective_id=collective, has_side_effects=True, vmem_limit_bytes=62 * 2**20
        ),
        name="head",
    )(*masters, hidden, encoded, *gains, table, buckets)


def local(
    hidden,
    encoded,
    out_grad,
    self_query,
    self_key,
    self_value,
    self_out,
    cross_query,
    cross_key,
    cross_value,
    cross_out,
    ffn_gate,
    ffn_up,
    ffn_down,
    gain_self,
    gain_cross,
    gain_ffn,
    bias_table,
    buckets,
):
    seqs, toks = hidden.shape[0], hidden.shape[1]
    p = Plan(seqs, toks, lax.axis_size("rep"))
    tokens = seqs * toks
    ff = ffn_gate.shape[1]
    enc_rows = seqs * encoded.shape[1] * p.R
    dma = pltpu.SemaphoreType.DMA

    n_shard = lax.axis_size("shard")
    mine = lax.axis_index("shard")
    part = gain_self.shape[0]
    near = buckets[: 2 * toks]
    onehot = (near[:, None] == jnp.arange(NB, dtype=jnp.int32)[None, :]).astype(B16)
    paired = n_shard == 2 and p.R == 2**BITS and 3 + H <= SMALL_ROWS
    if paired:
        masters = (
            self_query,
            self_key,
            self_value,
            cross_key,
            cross_value,
            self_out,
            cross_query,
            cross_out,
            ffn_gate,
            ffn_up,
            ffn_down,
        )
        gains = [gain_self, gain_cross, gain_ffn]
        got = head_call(
            p, masters, hidden, encoded, gains, bias_table, buckets, 0
        )
        wq, wk, wv, wck, wcv, wo, wcq, wco = got[:8]
        wg, wu, wd = [g.reshape(-1, g.shape[-1]) for g in got[8:11]]
        recv, enc, ckn, ckt, cvn, small, a1, of, rl, ot = got[11:21]
        x1, x2, a2, qt2, of2, rl2 = got[21:]
    else:
        lot = jnp.concatenate(
            [
                jnp.stack([gain_self, gain_cross, gain_ffn]).reshape(-1),
                bias_table.reshape(-1),
            ]
        ).astype(B16)
        lot = lax.all_gather(lot, "shard", axis=0)
        gains = [
            lot[:, i * part : (i + 1) * part].reshape(1, D).astype(F32) for i in range(3)
        ]
        table = lot[:, 3 * part :].reshape(NB, H)
        lines = jnp.einsum("lb,bh->hl", onehot, table, preferred_element_type=F32)
        lines = jnp.pad(lines, ((0, SMALL_ROWS - 3 - H), (0, D - 2 * toks)))
        small = jnp.concatenate([*gains, lines], axis=0)

        wq, wk, wv, wo, wcq, wck, wcv, wco, wg, wu, wd = [
            gather_rows(m.astype(B16))
            for m in (
                self_query,
                self_key,
                self_value,
                self_out,
                cross_query,
                cross_key,
                cross_value,
                cross_out,
                ffn_gate,
                ffn_up,
                ffn_down,
            )
        ]
        enc = lax.all_gather(encoded, "rep", axis=1, tiled=True).reshape(enc_rows, D)

        a1, send = plain_call(
            functools.partial(project_kernel, p),
            [((tokens, D), B16), ((p.U, p.HG, 3 * DH, toks), B16)],
            (hidden, small, wq, wk, wv),
            "project",
        )
        recv = comm_call(
            functools.partial(scatter_tokens, p),
            (p.R, p.HG, 3 * DH, toks),
            (send,),
            [dma((p.U,)), dma((max(p.W - 1, 1), p.J)), dma((p.R,))],
            0,
            "scatter_tokens",
        )
        ckn, ckt, cvn, cvt = plain_call(
            encode_kernel,
            [
                ((enc_rows, D), B16),
                ((D, enc_rows), B16),
                ((enc_rows, D), B16),
                ((H // 2, 2 * DH + ONES, enc_rows), B16),
            ],
            (enc, wck, wcv),
            "encode",
        )
        o, of, rl = pl.pallas_call(
            functools.partial(attend_kernel, p),
            grid=(p.HG,),
            out_shape=[
                jax.ShapeDtypeStruct((p.J, p.HG, DH, toks), B16),
                jax.ShapeDtypeStruct((p.J, p.HG, DH, toks), F32),
                jax.ShapeDtypeStruct((p.HG, p.NP, 1, 2 * toks), F32),
            ],
            in_specs=[whole((p.R, p.HG, 3 * DH, toks)), whole((SMALL_ROWS, D))],
            out_specs=[
                whole((p.J, p.HG, DH, toks)),
                whole((p.J, p.HG, DH, toks)),
                whole((p.HG, p.NP, 1, 2 * toks)),
            ],
            scratch_shapes=attend_scratch(p),
            compiler_params=pltpu.CompilerParams(vmem_limit_bytes=56 * 2**20),
            name="attend",
        )(recv, small)
        ot = comm_call(
            functools.partial(return_tokens, p),
            (p.U, p.HG, DH, toks),
            (o,),
            [dma((p.J,)), dma((p.U,))],
            1,
            "return_tokens",
        )

        x1, x2, a2, qt2, of2, rl2 = plain_call(
            functools.partial(cross_kernel, seqs),
            [
                ((tokens, D), F32),
                ((tokens, D), F32),
                ((tokens, D), B16),
                ((seqs, D, toks), B16),
                ((seqs, D, toks), F32),
                ((seqs, H // 2, 1, 2 * toks), F32),
            ],
            (hidden, ot, wo, small, wcq, wco, ckn, cvt),
            "cross",
        )

    chunk = min(512, ff)
    const = lambda s: pl.BlockSpec(s, lambda i: (0, 0))
    output, dx2, dg_ffn, dwg, dwu, dwd = pl.pallas_call(
        ffn_kernel,
        grid=(ff // chunk,),
        out_shape=[
            jax.ShapeDtypeStruct((tokens, D), B16),
            jax.ShapeDtypeStruct((tokens, D), F32),
            jax.ShapeDtypeStruct((1, D), F32),
            jax.ShapeDtypeStruct((D, ff), B16),
            jax.ShapeDtypeStruct((D, ff), B16),
            jax.ShapeDtypeStruct((ff, D), B16),
        ],
        in_specs=[
            const((tokens, D)),
            const((tokens, D)),
            const((SMALL_ROWS, D)),
            pl.BlockSpec((D, chunk), lambda i: (0, i)),
            pl.BlockSpec((D, chunk), lambda i: (0, i)),
            pl.BlockSpec((chunk, D), lambda i: (i, 0)),
        ],
        out_specs=[
            const((tokens, D)),
            const((tokens, D)),
            const((1, D)),
            pl.BlockSpec((D, chunk), lambda i: (0, i)),
            pl.BlockSpec((D, chunk), lambda i: (0, i)),
            pl.BlockSpec((chunk, D), lambda i: (i, 0)),
        ],
        scratch_shapes=[
            pltpu.VMEM((tokens, D), B16),
            pltpu.VMEM((tokens, D), F32),
            pltpu.VMEM((tokens, D), F32),
        ],
        compiler_params=pltpu.CompilerParams(vmem_limit_bytes=56 * 2**20),
        name="ffn",
    )(x2, out_grad.reshape(tokens, D), small, wg, wu, wd)

    back_outs = [
        ((tokens, D), F32),
        ((1, D), F32),
        ((p.U, p.HG, DH, toks), B16),
        ((enc_rows, D), B16),
    ] + [((D, D), B16)] * 5
    back_args = (dx2, x1, a2, small, qt2, of2, rl2, ckn, ckt, cvn, enc, wco, wcq, wck, wcv, wo, ot)
    back_scratch_ = [
        pltpu.VMEM((seqs, D, toks), B16),
        pltpu.VMEM((seqs, D, toks), B16),
        pltpu.VMEM((enc_rows, D), B16),
        pltpu.VMEM((enc_rows, D), B16),
    ]
    back_kernel = functools.partial(cross_back_kernel, seqs, p.G)
    if paired:
        got = cross_back_moves_call(back_kernel, back_outs, back_args, back_scratch_)
    else:
        got = plain_call(back_kernel, back_outs, back_args, "cross_back", scratch=back_scratch_)
    dx1, dg_cross, dot_, denc, dwco, dwcq, dwck, dwcv, dwo = got
    if paired:
        early = [
            g.reshape(2, g.shape[0] // 2, g.shape[1])
            for g in (dwg, dwu, dwd, dwo, dwcq, dwck, dwcv, dwco)
        ]
        sums, block, hidden_grad, encoded_grad = tail_call(
            p,
            early,
            dot_,
            denc,
            (recv, of, wq, wk, wv),
            (small, rl, hidden, a1, dx1, dg_cross, dg_ffn),
            3,
        )
        dwg, dwu, dwd, dwo, dwcq, dwck, dwcv, dwco, dwq, dwk, dwv = widen(sums)
        mats = [dwq, dwk, dwv, dwo, dwcq, dwck, dwcv, dwco, dwg, dwu, dwd]
        dgains = lax.dynamic_slice(block, (0, mine * part), (3, part))
        by_bucket = jnp.einsum(
            "hl,lb->bh",
            block[3 : 3 + H, : 2 * toks],
            onehot.astype(F32),
            precision=lax.Precision.HIGHEST,
        )
        dtab = lax.dynamic_slice(
            by_bucket, (mine * bias_table.shape[0], 0), bias_table.shape
        )
    else:
        encoded_grad = lax.psum_scatter(
            denc.reshape(seqs, enc_rows // seqs, D), "rep", scatter_dimension=1, tiled=True
        )
        dout = comm_call(
            functools.partial(scatter_rows, p),
            (p.J, p.HG, DH, toks),
            (dot_,),
            [dma((p.U,)), dma((p.J,))],
            2,
            "scatter_rows",
        )
        dq, dkv, line = pl.pallas_call(
            functools.partial(attend_back_kernel, p),
            grid=(p.HG,),
            out_shape=[
                jax.ShapeDtypeStruct((p.J, p.HG, DH, toks), B16),
                jax.ShapeDtypeStruct((p.R, p.HG, 2 * DH, toks), B16),
                jax.ShapeDtypeStruct((p.HG, 1, 2 * toks), F32),
            ],
            in_specs=[
                whole((p.R, p.HG, 3 * DH, toks)),
                whole((SMALL_ROWS, D)),
                whole((p.J, p.HG, DH, toks)),
                whole((p.J, p.HG, DH, toks)),
                whole((p.HG, p.NP, 1, 2 * toks)),
            ],
            out_specs=[
                whole((p.J, p.HG, DH, toks)),
                whole((p.R, p.HG, 2 * DH, toks)),
                whole((p.HG, 1, 2 * toks)),
            ],
            scratch_shapes=back_scratch(p),
            compiler_params=pltpu.CompilerParams(vmem_limit_bytes=56 * 2**20),
            name="attend_back",
        )(recv, small, dout, of, rl)
        grads = comm_call(
            functools.partial(return_grads, p),
            (p.U, p.HG, 3 * DH, toks),
            (dq, dkv),
            [
                pltpu.VMEM((max(p.W - 1, 1), p.J, p.HG, 2 * DH, toks), B16),
                pltpu.VMEM((p.J, p.HG, 3 * DH, toks), B16),
                dma((p.J,)),
                dma((max(p.W - 1, 1), p.J)),
                dma((max(p.W - 1, 1), p.J)),
                dma((p.U,)),
            ],
            3,
            "return_grads",
            space=pltpu.VMEM,
        )
        hidden_grad, dg_self, dwq, dwk, dwv = plain_call(
            functools.partial(last_kernel, p),
            [(hidden.shape, B16), ((1, D), F32)] + [((D, D), B16)] * 3,
            (hidden, grads, a1, small, dx1, wq, wk, wv),
            "last",
        )

        group = (lax.axis_index("rep") // p.W) % p.G
        by_bucket = jnp.einsum(
            "hl,lb->bh", line[:, 0, :], onehot.astype(F32), precision=lax.Precision.HIGHEST
        )
        dtable = lax.dynamic_update_slice(jnp.zeros((NB, H), F32), by_bucket, (0, group * p.HG))

        mats = reduce_grads([dwq, dwk, dwv, dwo, dwcq, dwck, dwcv, dwco, dwg, dwu, dwd])
        lot = jnp.concatenate(
            [g.reshape(n_shard, part) for g in (dg_self, dg_cross, dg_ffn)]
            + [dtable.reshape(n_shard, -1)],
            axis=1,
        )
        size = lot.shape[1]
        lot = lax.psum(lot, ("shard", "rep"))
        lot = lax.dynamic_slice(lot, (mine, 0), (1, size))[0]
        dgains = [lot[i * part : (i + 1) * part] for i in range(3)]
        dtab = lot[3 * part :].reshape(bias_table.shape)
    return (
        output.reshape(hidden.shape),
        hidden_grad,
        encoded_grad,
        *mats,
        *dgains,
        dtab,
    )


def solution(mesh):
    tok = P("shard", "rep", None)
    mat = P("shard", None)
    in_specs = (tok,) * 3 + (mat,) * 11 + (P("shard"),) * 3 + (mat, P())
    out_specs = (tok,) * 3 + (mat,) * 11 + (P("shard"),) * 3 + (mat,)
    return jax.shard_map(local, mesh=mesh, in_specs=in_specs, out_specs=out_specs, check_vma=False)
```

```python
import functools
import itertools

import jax
import jax.numpy as jnp
from jax import lax
from jax.experimental import pallas as pl
from jax.experimental.pallas import tpu as pltpu
from jax.sharding import PartitionSpec as P

D = 768
H = 12
DH = 64
NB = 32
EPS = 1e-06
F32 = jnp.float32
B16 = jnp.bfloat16
ONES = 16
HIDE = -1e30
MESH = pl.DeviceIdType.MESH
GELU_A = 0.7978845608028654
GELU_B = 0.044715


def dot(a, b):
    return lax.dot_general(a, b, (((1,), (0,)), ((), ())), preferred_element_type=F32)


def dot_t(a, b):
    return lax.dot_general(a, b, (((1,), (1,)), ((), ())), preferred_element_type=F32)


def t_dot(a, b):
    return lax.dot_general(a, b, (((0,), (0,)), ((), ())), preferred_element_type=F32)


def mat(ref):
    return ref[...].reshape(-1, ref.shape[-1])


def scale_of(v):
    return lax.rsqrt(jnp.mean(v * v, axis=-1, keepdims=True) + EPS)


def norm_back(v, gain, grad):
    r = scale_of(v)
    n = v * r
    c = grad * gain
    dv = r * (c - n * jnp.mean(c * n, axis=-1, keepdims=True))
    return dv, jnp.sum(grad * n, axis=0, keepdims=True)


def whole(shape):
    return pl.BlockSpec(shape, lambda *_: (0,) * len(shape))


def plain_call(kernel, outs, args, name, scratch=(), vmem=60):
    return pl.pallas_call(
        kernel,
        out_shape=[jax.ShapeDtypeStruct(s, t) for s, t in outs],
        in_specs=[pl.BlockSpec(memory_space=pltpu.VMEM)] * len(args),
        out_specs=[pl.BlockSpec(memory_space=pltpu.VMEM)] * len(outs),
        scratch_shapes=list(scratch),
        compiler_params=pltpu.CompilerParams(vmem_limit_bytes=vmem * 2**20),
        name=name,
    )(*args)


class Plan:
    def __init__(self, seqs, toks, rows):
        self.S, self.T, self.R = seqs, toks, rows
        groups = 1
        for g in range(1, H + 1):
            if H % g == 0 and seqs * g <= rows and rows % (2 * seqs * g) == 0:
                groups = g
        self.G = groups
        self.HG = H // groups
        self.F = self.HG * DH
        self.U = seqs * groups
        self.W = rows // self.U
        self.J = rows // self.W
        self.NP = self.J // 2
        self.CK = 2 * self.W * toks
        self.L = rows * toks

    def worker_of(self, r):
        m = r % (2 * self.W)
        late = m // self.W
        return m * (1 - late) + (2 * self.W - 1 - m) * late

    def slot_of(self, r):
        return 2 * (r // (2 * self.W)) + (r % (2 * self.W)) // self.W

    def source(self, j, w):
        return self.source_in(j // 2, j % 2, w)

    def source_in(self, pair, late, w):
        if late:
            return 2 * self.W * pair + 2 * self.W - 1 - w
        return 2 * self.W * pair + w


def enter(rows):
    me = lax.axis_index("rep")
    barrier = pltpu.get_barrier_semaphore()
    for k in range(1, rows):
        pl.semaphore_signal(
            barrier, inc=1, device_id={"rep": (me + k) % rows}, device_id_type=MESH
        )
    pl.semaphore_wait(barrier, rows - 1)
    return me


def remote(src, dst, send, recv, to):
    return pltpu.make_async_remote_copy(
        src_ref=src,
        dst_ref=dst,
        send_sem=send,
        recv_sem=recv,
        device_id={"rep": to},
        device_id_type=MESH,
    )


def start_either(me, to, src, dst, send, recv):
    @pl.when(to == me)
    def _():
        pltpu.make_async_copy(src, dst, recv).start()

    @pl.when(to != me)
    def _():
        remote(src, dst, send, recv, to).start()


def end_either(me, to, src, dst, send, recv):
    @pl.when(to != me)
    def _():
        remote(src, dst, send, recv, to).wait_send()


def landed(ref, sem):
    pltpu.make_async_copy(ref, ref, sem).wait()


def scatter_tokens(plan, send, recv, send_sem, relay_sem, recv_sem):
    p = plan
    me = enter(p.R)
    w = me % p.W
    mine = p.worker_of(me)
    for u in range(p.U):
        start_either(me, u * p.W + mine, send.at[u], recv.at[me], send_sem.at[u], recv_sem.at[me])
    for j in range(p.J):
        r = p.source(j, w)
        landed(recv.at[r], recv_sem.at[r])
        for k in range(1, p.W):
            part = recv.at[r, :, pl.ds(DH, 2 * DH)]
            remote(
                part, part, relay_sem.at[k - 1, j], recv_sem.at[r], me - w + (w + k) % p.W
            ).start()
    for k in range(1, p.W):
        for j in range(p.J):
            r = p.source(j, (w + k) % p.W)
            landed(recv.at[r, :, pl.ds(DH, 2 * DH)], recv_sem.at[r])
    for u in range(p.U):
        end_either(me, u * p.W + mine, send.at[u], recv.at[me], send_sem.at[u], recv_sem.at[me])
    for k in range(1, p.W):
        for j in range(p.J):
            r = p.source(j, w)
            part = recv.at[r, :, pl.ds(DH, 2 * DH)]
            remote(
                part, part, relay_sem.at[k - 1, j], recv_sem.at[r], me - w + (w + k) % p.W
            ).wait_send()


def return_tokens(plan, send, recv, send_sem, recv_sem):
    p = plan
    me = enter(p.R)
    w = me % p.W
    unit = me // p.W
    for j in range(p.J):
        r = p.source(j, w)
        start_either(me, r, send.at[j], recv.at[unit], send_sem.at[j], recv_sem.at[unit])
    for u in range(p.U):
        landed(recv.at[u], recv_sem.at[u])
    for j in range(p.J):
        r = p.source(j, w)
        end_either(me, r, send.at[j], recv.at[unit], send_sem.at[j], recv_sem.at[unit])


def scatter_rows(plan, send, recv, send_sem, recv_sem):
    p = plan
    me = enter(p.R)
    mine = p.worker_of(me)
    slot = p.slot_of(me)
    for u in range(p.U):
        start_either(
            me, u * p.W + mine, send.at[u], recv.at[slot], send_sem.at[u], recv_sem.at[slot]
        )
    for j in range(p.J):
        landed(recv.at[j], recv_sem.at[j])
    for u in range(p.U):
        end_either(
            me, u * p.W + mine, send.at[u], recv.at[slot], send_sem.at[u], recv_sem.at[slot]
        )


def return_grads(plan, dq, dkv, recv, buf, out, send_sem, part_sem, got_sem, recv_sem):
    p = plan
    me = enter(p.R)
    w = me % p.W
    unit = me // p.W

    def give(k, j):
        to = (w + k) % p.W
        r = p.source(j, to)
        return remote(
            dkv.at[r],
            buf.at[k - 1, j],
            part_sem.at[k - 1, j],
            got_sem.at[k - 1, j],
            me - w + to,
        )

    for j in range(p.J):
        for k in range(1, p.W):
            give(k, j).start()
    for j in range(p.J):
        r = p.source(j, w)
        total = dkv[r].astype(F32)
        for k in range(1, p.W):
            landed(buf.at[k - 1, j], got_sem.at[k - 1, j])
            total = total + buf[k - 1, j].astype(F32)
        out[j, :, 0:DH, :] = dq[j]
        out[j, :, DH : 3 * DH, :] = total.astype(B16)
        start_either(me, r, out.at[j], recv.at[unit], send_sem.at[j], recv_sem.at[unit])
    for u in range(p.U):
        landed(recv.at[u], recv_sem.at[u])
    for j in range(p.J):
        r = p.source(j, w)
        end_either(me, r, out.at[j], recv.at[unit], send_sem.at[j], recv_sem.at[unit])
        for k in range(1, p.W):
            give(k, j).wait_send()


def comm_call(kernel, out, args, scratch, collective, name, space=pl.ANY):
    return pl.pallas_call(
        kernel,
        out_shape=jax.ShapeDtypeStruct(out, B16),
        in_specs=[pl.BlockSpec(memory_space=space)] * len(args),
        out_specs=pl.BlockSpec(memory_space=space),
        scratch_shapes=list(scratch),
        compiler_params=pltpu.CompilerParams(
            collective_id=collective, has_side_effects=True, vmem_limit_bytes=40 * 2**20
        ),
        name=name,
    )(*args)


def project_kernel(plan, hidden, gain, wq, wk, wv, a1_ref, send):
    p = plan
    x = hidden[...].reshape(p.S * p.T, D).astype(F32)
    a1 = (x * scale_of(x) * gain[0:1, :]).astype(B16)
    a1_ref[...] = a1
    for n, weight in enumerate((wq, wk, wv)):
        rows = dot(a1, mat(weight))
        for s in range(p.S):
            turned = jnp.transpose(rows[s * p.T : (s + 1) * p.T]).astype(B16)
            for i in range(H):
                send[s * p.G + i // p.HG, i % p.HG, n * DH : (n + 1) * DH, :] = turned[
                    i * DH : (i + 1) * DH
                ]


def bias_tiles(plan, w, line, tiles):
    p = plan
    far = line[:, 2 * p.T - 1 : 2 * p.T]
    near = pltpu.roll(jnp.broadcast_to(line, (p.T, 2 * p.T)), 0, 1, stride=1, stride_axis=0)
    key = lax.broadcasted_iota(jnp.int32, (p.T, p.T), 0)
    query = lax.broadcasted_iota(jnp.int32, (p.T, p.T), 1)
    same = jnp.where(query >= key, near[:, : p.T], HIDE)
    next_ = near[:, p.T :]
    farb = jnp.broadcast_to(far, (p.T, p.T))
    tiles[0] = jnp.broadcast_to(far, (p.CK, 2 * p.T))
    for a in range(2):
        ahead = w if a == 0 else 2 * p.W - 1 - w
        for b in range(2 * p.W):
            diff = ahead - b
            tile = jnp.where(
                diff == 0, same, jnp.where(diff == 1, next_, jnp.where(diff < 0, HIDE, farb))
            )
            tiles[2, b * p.T : (b + 1) * p.T, a * p.T : (a + 1) * p.T] = tile
            back = diff + 2 * p.W
            tiles[1, b * p.T : (b + 1) * p.T, a * p.T : (a + 1) * p.T] = jnp.where(
                back == 1, next_, farb
            )


def block_pair(plan, ref, pair, w, h):
    p = plan
    return jnp.concatenate(
        [ref[p.source_in(pair, late, w), h, 0:DH, :] for late in range(2)], axis=1
    )


def in_two(count, body, carry, between):
    if between is None:
        return lax.fori_loop(0, count, body, carry)
    carry = lax.fori_loop(0, count - 1, body, carry)
    between()
    return lax.fori_loop(count - 1, count, body, carry)


def line_of(p, block, head):
    return block[pl.ds(3 + head, 1), 0 : 2 * p.T]


def attend_head(p, w, h, line, recv, o_ref, of_ref, rl, kn, vt, tiles, between=None):
    bias_tiles(p, w, line, tiles)
    for r in range(p.R):
        kn[r * p.T : (r + 1) * p.T, :] = jnp.transpose(
            recv[r, h, DH : 2 * DH, :].astype(F32)
        ).astype(B16)
        vt[0:DH, r * p.T : (r + 1) * p.T] = recv[r, h, 2 * DH : 3 * DH, :]
    vt[DH : DH + ONES, :] = jnp.ones((ONES, p.L), B16)

    def one_pair(pair, carry):
        qt = block_pair(p, recv, pair, w, h)

        def step(i, acc):
            start = pl.multiple_of(i * p.CK, p.CK)
            e = jnp.exp(dot(kn[pl.ds(start, p.CK), :], qt) + tiles[jnp.maximum(i - pair + 2, 0)])
            return acc + dot(vt[:, pl.ds(start, p.CK)], e.astype(B16))

        acc = lax.fori_loop(0, pair + 1, step, jnp.zeros((DH + ONES, 2 * p.T), F32))
        scale = 1.0 / acc[DH : DH + 1]
        of = acc[:DH] * scale
        rl[pair] = scale
        for a in range(2):
            part = of[:, a * p.T : (a + 1) * p.T]
            of_ref[2 * pair + a, h] = part
            o_ref[2 * pair + a, h] = part.astype(B16)
        return carry

    in_two(p.NP, one_pair, 0, between)


def attend_scratch(p):
    return [
        pltpu.VMEM((p.L, DH), B16),
        pltpu.VMEM((DH + ONES, p.L), B16),
        pltpu.VMEM((3, p.CK, 2 * p.T), F32),
    ]


def attend_kernel(plan, recv, block, o_ref, of_ref, rl_ref, *scratch):
    p = plan
    me = lax.axis_index("rep")
    w = me % p.W
    group = (me // p.W) % p.G
    h = pl.program_id(0)
    line = line_of(p, block, group * p.HG + h)
    attend_head(p, w, h, line, recv, o_ref, of_ref, rl_ref.at[h], *scratch)


def back_head(
    p,
    w,
    h,
    line,
    recv,
    dout,
    of_ref,
    rl,
    dq_ref,
    dkv_ref,
    kn,
    vn,
    kt,
    dk,
    dv,
    tiles,
    near,
    between=None,
):
    bias_tiles(p, w, line, tiles)
    for r in range(p.R):
        kn[r * p.T : (r + 1) * p.T, :] = jnp.transpose(
            recv[r, h, DH : 2 * DH, :].astype(F32)
        ).astype(B16)
        vn[r * p.T : (r + 1) * p.T, :] = jnp.transpose(
            recv[r, h, 2 * DH : 3 * DH, :].astype(F32)
        ).astype(B16)
        kt[0:DH, r * p.T : (r + 1) * p.T] = recv[r, h, DH : 2 * DH, :]
    kt[DH : DH + ONES, :] = jnp.ones((ONES, p.L), B16)
    dk[...] = jnp.zeros_like(dk)
    dv[...] = jnp.zeros_like(dv)
    near[...] = jnp.zeros_like(near)

    def one_pair(pair, total):
        qt = block_pair(p, recv, pair, w, h)
        dot_rows = jnp.concatenate([dout[2 * pair + a, h] for a in range(2)], axis=1)
        of = jnp.concatenate([of_ref[2 * pair + a, h] for a in range(2)], axis=1)
        delta = jnp.sum(dot_rows.astype(F32) * of, axis=0, keepdims=True)
        scale = rl[pair]
        qn = jnp.transpose(qt.astype(F32)).astype(B16)
        don = jnp.transpose(dot_rows.astype(F32)).astype(B16)

        def step(i, acc):
            start = pl.multiple_of(i * p.CK, p.CK)
            kind = jnp.maximum(i - pair + 2, 0)
            keys = pl.ds(start, p.CK)
            prob = jnp.exp(dot(kn[keys, :], qt) + tiles[kind]) * scale
            ds = (prob * (dot(vn[keys, :], dot_rows) - delta)).astype(B16)
            near[kind] += ds.astype(F32)
            dk[keys, :] += dot(ds, qn)
            dv[keys, :] += dot(prob.astype(B16), don)
            return acc + dot(kt[:, keys], ds)

        acc = lax.fori_loop(0, pair + 1, step, jnp.zeros((DH + ONES, 2 * p.T), F32))
        for a in range(2):
            dq_ref[2 * pair + a, h] = acc[:DH, a * p.T : (a + 1) * p.T].astype(B16)
        return total + acc[DH : DH + 1]

    total = in_two(p.NP, one_pair, jnp.zeros((1, 2 * p.T), F32), between)
    for r in range(p.R):
        dkv_ref[r, h, 0:DH, :] = jnp.transpose(dk[r * p.T : (r + 1) * p.T, :]).astype(B16)
        dkv_ref[r, h, DH : 2 * DH, :] = jnp.transpose(dv[r * p.T : (r + 1) * p.T, :]).astype(B16)
    same = jnp.zeros((p.T, p.T), F32)
    next_ = jnp.zeros((p.T, p.T), F32)
    for a in range(2):
        ahead = w if a == 0 else 2 * p.W - 1 - w
        for b in range(2 * p.W):
            diff = ahead - b
            spot = (slice(b * p.T, (b + 1) * p.T), slice(a * p.T, (a + 1) * p.T))
            tile = near[(2, *spot)]
            same = same + jnp.where(diff == 0, tile, 0.0)
            next_ = next_ + jnp.where(diff == 1, tile, 0.0)
            next_ = next_ + jnp.where(diff + 2 * p.W == 1, near[(1, *spot)], 0.0)
    both = jnp.concatenate([same, next_], axis=1)
    key = lax.broadcasted_iota(jnp.int32, (p.T, p.T), 0)
    other = lax.broadcasted_iota(jnp.int32, (p.T, p.T), 1)
    swap = (key + other == p.T - 1).astype(F32)
    turned = lax.dot_general(
        swap,
        both,
        (((1,), (0,)), ((), ())),
        precision=lax.Precision.HIGHEST,
        preferred_element_type=F32,
    )
    turned = pltpu.roll(turned, p.T + 1, 1, stride=1, stride_axis=0)
    by_distance = jnp.sum(turned, axis=0, keepdims=True)
    rest = jnp.sum(total) - jnp.sum(both)
    place = lax.broadcasted_iota(jnp.int32, (1, 2 * p.T), 1)
    return by_distance + jnp.where(place == 2 * p.T - 1, rest, 0.0)


def back_scratch(p):
    return [
        pltpu.VMEM((p.L, DH), B16),
        pltpu.VMEM((p.L, DH), B16),
        pltpu.VMEM((DH + ONES, p.L), B16),
        pltpu.VMEM((p.L, DH), F32),
        pltpu.VMEM((p.L, DH), F32),
        pltpu.VMEM((3, p.CK, 2 * p.T), F32),
        pltpu.VMEM((3, p.CK, 2 * p.T), F32),
    ]


def attend_back_kernel(plan, recv, block, dout, of_ref, rl_ref, dq_ref, dkv_ref, line_ref, *scratch):
    p = plan
    me = lax.axis_index("rep")
    w = me % p.W
    group = (me // p.W) % p.G
    h = pl.program_id(0)
    line_ref[h] = back_head(
        p,
        w,
        h,
        line_of(p, block, group * p.HG + h),
        recv,
        dout,
        of_ref,
        rl_ref.at[h],
        dq_ref,
        dkv_ref,
        *scratch,
    )


def encode_kernel(enc, wk, wv, kn, kt, vn, vt):
    encode_one(enc, wk, kn, kt)
    encode_one(enc, wv, vn, vt)


def encode_one(enc, weight, natural, turned):
    value = dot(mat(enc), mat(weight))
    natural[...] = value.astype(B16)
    flipped = jnp.transpose(value).astype(B16)
    if len(turned.shape) == 2:
        turned[...] = flipped
        return
    for i in range(H // 2):
        turned[i, 0 : 2 * DH, :] = flipped[2 * i * DH : 2 * (i + 1) * DH]
        turned[i, 2 * DH : 2 * DH + ONES, :] = jnp.ones((ONES, turned.shape[2]), B16)


def apart(pair, axis, other):
    twice = jnp.concatenate([pair, pair], axis=axis)
    half = (pair.shape[axis], pair.shape[other] // 2)
    one = lax.broadcasted_iota(jnp.int32, twice.shape, axis) < half[0]
    two = lax.broadcasted_iota(jnp.int32, twice.shape, other) < half[1]
    return jnp.where(one == two, twice, jnp.zeros_like(twice))


def rows_of(units, s, seqs):
    groups = units.shape[0] // seqs
    return units[s * groups : (s + 1) * groups].reshape(-1, units.shape[-1])


def cross_kernel(
    seqs,
    hidden,
    ot,
    wo,
    gain,
    wcq,
    wco,
    kn,
    vt,
    x1_ref,
    x2_ref,
    a2_ref,
    qt_ref,
    of_ref,
    rl_ref,
    pause=lambda: None,
):
    toks = hidden.shape[1]
    span = kn.shape[0] // seqs
    x = hidden[...].reshape(seqs * toks, D).astype(F32)
    o = jnp.concatenate(
        [jnp.transpose(rows_of(ot, s, seqs).astype(F32)) for s in range(seqs)], axis=0
    ).astype(B16)
    x1 = x + dot(o, mat(wo))
    x1_ref[...] = x1
    a2 = (x1 * scale_of(x1) * gain[1:2, :]).astype(B16)
    a2_ref[...] = a2
    q2 = dot(a2, mat(wcq))
    for s in range(seqs):
        qt_ref[s] = jnp.transpose(q2[s * toks : (s + 1) * toks]).astype(B16)
    pause()

    def heads(i, carry):
        col = pl.multiple_of(2 * i * DH, 2 * DH)
        for s in range(seqs):
            keys = slice(s * span, (s + 1) * span)
            q_pair = apart(qt_ref[s, pl.ds(col, 2 * DH), :], 1, 0)
            e = jnp.exp(dot(kn[keys, pl.ds(col, 2 * DH)], q_pair))
            acc = dot(vt[i, :, keys], e.astype(B16))
            rl = 1.0 / acc[2 * DH : 2 * DH + 1]
            both = acc * rl
            of_ref[s, pl.ds(col, DH), :] = both[:DH, :toks]
            of_ref[s, pl.ds(col + DH, DH), :] = both[DH : 2 * DH, toks:]
            rl_ref[s, i] = rl
        return carry

    lax.fori_loop(0, H // 2, heads, 0)
    pause()
    o2 = jnp.concatenate([jnp.transpose(of_ref[s]) for s in range(seqs)], axis=0).astype(B16)
    x2_ref[...] = x1_ref[...] + dot(o2, mat(wco))


def ffn_products(rows, og, wg, wu, wd, acc, da3):
    gate = dot(rows, wg[...])
    up = dot(rows, wu[...])
    square = gate * gate
    th = jnp.tanh(GELU_A * gate * (1.0 + GELU_B * square))
    half = 0.5 * (1.0 + th)
    value = gate * half
    slope = half + 0.5 * gate * (1.0 - th * th) * (GELU_A * (1.0 + 3.0 * GELU_B * square))
    inner = (value * up).astype(B16)
    acc[...] += dot(inner, wd[...])
    dwd = t_dot(inner, og).astype(B16)
    dinner = dot_t(og, wd[...]).astype(B16).astype(F32)
    dgate = (dinner * up * slope).astype(B16)
    dup = (dinner * value).astype(B16)
    da3[...] += dot_t(dgate, wg[...]) + dot_t(dup, wu[...])
    return t_dot(rows, dgate).astype(B16), t_dot(rows, dup).astype(B16), dwd


def ffn_kernel(
    x2_ref, og_ref, gain, wg, wu, wd, out_ref, dx2_ref, dgain_ref, dwg, dwu, dwd, a3, acc, da3
):
    step = pl.program_id(0)

    @pl.when(step == 0)
    def _():
        x2 = x2_ref[...]
        a3[...] = (x2 * scale_of(x2) * gain[2:3, :]).astype(B16)
        acc[...] = x2
        da3[...] = jnp.zeros_like(da3)

    dwg[...], dwu[...], dwd[...] = ffn_products(a3[...], og_ref[...], wg, wu, wd, acc, da3)

    @pl.when(step == pl.num_programs(0) - 1)
    def _():
        out_ref[...] = acc[...].astype(B16)
        dv, dgain = norm_back(x2_ref[...], gain[2:3, :], da3[...])
        dx2_ref[...] = og_ref[...].astype(F32) + dv
        dgain_ref[...] = dgain


def cross_back_kernel(
    seqs,
    groups,
    dx2_ref,
    x1_ref,
    a2_ref,
    gain,
    qt_ref,
    of_ref,
    rl_ref,
    kn,
    kt,
    vn,
    enc,
    wco,
    wcq,
    wck,
    wcv,
    wo,
    ot,
    dx1_ref,
    dgain_ref,
    dot_ref,
    denc_ref,
    dwco,
    dwcq,
    dwck,
    dwcv,
    dwo,
    dt,
    dqt,
    dk,
    dv,
    need=lambda *refs: None,
    done=lambda ref: None,
):
    toks = qt_ref.shape[2]
    span = kn.shape[0] // seqs
    dx2 = dx2_ref[...]
    dc = dx2.astype(B16)
    o2t = [of_ref[s].astype(B16) for s in range(seqs)]
    total = dot(o2t[0], dc[0:toks])
    for s in range(1, seqs):
        total = total + dot(o2t[s], dc[s * toks : (s + 1) * toks])
    dwco[...] = total.astype(B16)
    done(dwco)
    need(wco)
    do2 = dot_t(dc, mat(wco))
    for s in range(seqs):
        dt[s] = jnp.transpose(do2[s * toks : (s + 1) * toks]).astype(B16)

    need(kn, kt, vn)

    def heads(i, carry):
        col = pl.multiple_of(2 * i * DH, 2 * DH)
        pair = pl.ds(col, 2 * DH)
        for s in range(seqs):
            keys = slice(s * span, (s + 1) * span)
            q_rows, d_rows = qt_ref[s, pair, :], dt[s, pair, :]
            q_pair = apart(jnp.transpose(q_rows.astype(F32)), 0, 1).astype(B16)
            d_pair = apart(jnp.transpose(d_rows.astype(F32)), 0, 1).astype(B16)
            prob = jnp.exp(dot(kn[keys, pair], apart(q_rows, 1, 0))) * rl_ref[s, i]
            terms = d_rows.astype(F32) * of_ref[s, pair, :]
            delta = jnp.concatenate(
                [jnp.sum(terms[n * DH : (n + 1) * DH], axis=0, keepdims=True) for n in range(2)],
                axis=1,
            )
            ds = (prob * (dot(vn[keys, pair], apart(d_rows, 1, 0)) - delta)).astype(B16)
            dq = dot(kt[pair, keys], ds).astype(B16)
            dqt[s, pl.ds(col, DH), :] = dq[:DH, :toks]
            dqt[s, pl.ds(col + DH, DH), :] = dq[DH:, toks:]
            dk[keys, pair] = dot(ds, q_pair).astype(B16)
            dv[keys, pair] = dot(prob.astype(B16), d_pair).astype(B16)
        return carry

    lax.fori_loop(0, H // 2, heads, 0)
    need(enc, wck, wcv, wcq, wo)
    dwck[...] = t_dot(mat(enc), dk[...]).astype(B16)
    done(dwck)
    dwcv[...] = t_dot(mat(enc), dv[...]).astype(B16)
    done(dwcv)
    denc_ref[...] = (dot_t(dk[...], mat(wck)) + dot_t(dv[...], mat(wcv))).astype(B16)
    done(denc_ref)
    dq2 = jnp.concatenate(
        [jnp.transpose(dqt[s].astype(F32)) for s in range(seqs)], axis=0
    ).astype(B16)
    dwcq[...] = t_dot(a2_ref[...], dq2).astype(B16)
    done(dwcq)
    term, dgain = norm_back(x1_ref[...], gain[1:2, :], dot_t(dq2, mat(wcq)))
    dgain_ref[...] = dgain
    dx1 = dx2 + term
    dx1_ref[...] = dx1
    db = dx1.astype(B16)
    total = dot(rows_of(ot, 0, seqs), db[0:toks])
    for s in range(1, seqs):
        total = total + dot(rows_of(ot, s, seqs), db[s * toks : (s + 1) * toks])
    dwo[...] = total.astype(B16)
    done(dwo)
    do = dot_t(db, mat(wo))
    width = D // groups
    for s in range(seqs):
        turned = jnp.transpose(do[s * toks : (s + 1) * toks]).astype(B16)
        for g in range(groups):
            dot_ref[s * groups + g] = turned[g * width : (g + 1) * width].reshape(
                dot_ref.shape[1:]
            )


def cross_back_moves_kernel(kernel, ins, outs, far_ins, far_outs, *refs):
    refs = list(refs)
    take = lambda n: [refs.pop(0) for _ in range(n)]
    args, results, scratch = take(ins), take(outs), take(4)
    near_in, near_out = take(len(far_ins)), take(len(far_outs))
    moves = Moves(refs[0])
    moves.bring([(args[i], near) for i, near in zip(far_ins, near_in)])
    for i, near in zip(far_ins, near_in):
        args[i] = near
    made = {}
    for i, near in zip(far_outs, near_out):
        made[id(near)] = (near, results[i])
        results[i] = near

    def done(ref):
        moves.take(*made[id(ref)])

    kernel(*args, *results, *scratch, need=moves.need, done=done)
    moves.end()


def cross_back_moves_call(kernel, outs, args, scratch):
    near = pl.BlockSpec(memory_space=pltpu.VMEM)
    anywhere = pl.BlockSpec(memory_space=pl.ANY)
    far_ins = [11, 7, 8, 9, 10, 13, 14, 12, 15]
    far_outs = [3, 4, 5, 6, 7, 8]
    scratch = [*scratch]
    scratch += [pltpu.VMEM(args[i].shape, args[i].dtype) for i in far_ins]
    scratch += [pltpu.VMEM(*outs[i]) for i in far_outs]
    scratch += [pltpu.SemaphoreType.DMA((len(far_ins) + len(far_outs),))]
    return pl.pallas_call(
        functools.partial(
            cross_back_moves_kernel, kernel, len(args), len(outs), far_ins, far_outs
        ),
        out_shape=[jax.ShapeDtypeStruct(s, t) for s, t in outs],
        in_specs=[anywhere if i in far_ins else near for i in range(len(args))],
        out_specs=[anywhere if i in far_outs else near for i in range(len(outs))],
        scratch_shapes=scratch,
        compiler_params=pltpu.CompilerParams(vmem_limit_bytes=60 * 2**20),
        name="cross_back",
    )(*args)


def last_kernel(plan, hidden, grads, a1, gain, dx1, wq, wk, wv, dh_ref, dgain_ref, dwq, dwk, dwv):
    dgain_ref[...] = last_products(
        plan, hidden, grads, a1, gain, dx1, wq, wk, wv, dh_ref, dwq, dwk, dwv
    )


def last_products(p, hidden, grads, a1, gain, dx1, wq, wk, wv, dh_ref, dwq, dwk, dwv):
    x = hidden[...].reshape(p.S * p.T, D).astype(F32)
    da1 = jnp.zeros((p.S * p.T, D), F32)
    for n, (weight, dw) in enumerate(((wq, dwq), (wk, dwk), (wv, dwv))):
        rows = []
        for s in range(p.S):
            turned = jnp.concatenate(
                [
                    grads[s * p.G + i // p.HG, i % p.HG, n * DH : (n + 1) * DH, :]
                    for i in range(H)
                ],
                axis=0,
            )
            rows.append(jnp.transpose(turned.astype(F32)))
        d = jnp.concatenate(rows, axis=0).astype(B16)
        dw[...] = t_dot(a1[...], d).astype(B16).reshape(dw.shape)
        da1 = da1 + dot_t(d, mat(weight))
    term, dgain = norm_back(x, gain[0:1, :], da1)
    dh_ref[...] = (dx1[...] + term).astype(B16).reshape(dh_ref.shape)
    return dgain


def gather_rows(part):
    count = lax.axis_size("shard")
    rows, cols = part.shape
    half = rows // 2
    mine = lax.axis_index("shard")
    core = lax.axis_index("rep") % 2
    pairs = [(r, r ^ 1) for r in range(lax.axis_size("rep"))]
    own = lax.dynamic_slice(part, (core * half, 0), (half, cols))
    full = jnp.zeros((count, rows, cols), part.dtype)
    full = lax.dynamic_update_slice(full, part[None], (mine, 0, 0))
    for k in range(1, count):
        got = lax.ppermute(own, "shard", [(i, (i + k) % count) for i in range(count)])
        also = lax.ppermute(got, "rep", pairs)
        owner = (mine - k) % count
        full = lax.dynamic_update_slice(full, got[None], (owner, core * half, 0))
        full = lax.dynamic_update_slice(full, also[None], (owner, (1 - core) * half, 0))
    return full.reshape(count * rows, cols)


def reduce_grads(grads):
    owned = [lax.psum_scatter(g, "shard", scatter_dimension=0, tiled=True) for g in grads]
    summed = lax.psum(tuple(owned), "rep")
    return [s.astype(F32) for s in summed]


class Moves:
    def __init__(self, sems):
        self.sems, self.used, self.coming, self.going = sems, 0, {}, []

    def sem(self):
        self.used += 1
        return self.sems.at[self.used - 1]

    def bring(self, pairs):
        for far, near in pairs:
            sem = self.sem()
            pltpu.make_async_copy(far, near, sem).start()
            self.coming[id(near)] = (near, sem)

    def need(self, *refs):
        for ref in refs:
            if id(ref) in self.coming:
                near, sem = self.coming.pop(id(ref))
                landed(near, sem)

    def take(self, near, far):
        sem = self.sem()
        pltpu.make_async_copy(near, far, sem).start()
        self.going.append((near, sem))

    def end(self):
        for near, sem in self.going:
            landed(near, sem)


BITS = 4
ROW = -1


class Job:
    def __init__(self, result, row, rows, col, cols, order):
        self.result, self.order = result, order
        self.row, self.rows, self.col, self.cols = row, rows, col, cols

    def buffers(self):
        half, rows, lead = self.cols // 2, self.rows, (2,)
        shapes = [(2, rows, half)] * 2
        for axis in self.order:
            if axis == ROW:
                lead = ()
            else:
                rows //= 2
            shapes.append((*lead, rows, half))
        return shapes


def partner(bit):
    me = lax.axis_index("rep")
    half = 2**bit
    mine = (me // half) % 2
    return mine, me + half * (1 - 2 * mine)


def to_rep(src, dst, send, recv, bit):
    return remote(src, dst, send, recv, partner(bit)[1])


def to_row(src, dst, send, recv):
    x = lax.axis_index("shard")
    return pltpu.make_async_remote_copy(
        src_ref=src,
        dst_ref=dst,
        send_sem=send,
        recv_sem=recv,
        device_id={"shard": 1 - x},
        device_id_type=MESH,
    )


def add_into(acc, term, rows):
    step = 16 if rows % 32 else 32

    def body(i, carry):
        at = pl.ds(pl.multiple_of(i * step, step), step)
        acc[at, :] = (acc[at, :].astype(F32) + term[at, :].astype(F32)).astype(B16)
        return carry

    lax.fori_loop(0, rows // step, body, 0)


class JobRun:
    def __init__(self, job, source, result, bufs, sems, index):
        self.job, self.source, self.result = job, source, result
        self.acc, self.core, *self.part = bufs
        self.steps = [(0, 1), (1, FIRST_LAG)] + [(n, LAG) for n in range(2, 10)]
        send, recv, local = sems
        self.send = [send.at[index, i] for i in range(9)]
        self.recv = [recv.at[index, i] for i in range(9)]
        self.local = [local.at[index, i] for i in range(2)]
        self.sent = []
        self.x = lax.axis_index("shard")
        half = job.cols // 2
        core = partner(0)[0]
        self.mine = pl.ds(pl.multiple_of(job.col + core * half, 128), half)
        self.other = pl.ds(pl.multiple_of(job.col + (1 - core) * half, 128), half)
        self.all = pl.ds(job.row, job.rows)
        self.plan, self.back = [], []
        owners, first, count = (0, 1), 0, job.rows
        for axis in job.order:
            if axis == ROW:
                keep = give = (first, count)
                owners, others = (self.x,), (1 - self.x,)
            else:
                count //= 2
                bit = partner(axis)[0]
                keep, give = (first + bit * count, count), (first + (1 - bit) * count, count)
                self.back.insert(0, (axis, (first, 2 * count), give))
                first, others = keep[0], owners
            self.plan.append((axis, owners, keep, others, give))
        self.last = (first, count)

    def span(self, first, count):
        return pl.ds(pl.multiple_of(first, 16), count)

    def out(self, first, count):
        return self.result.at[self.span(self.job.row + first, count), self.mine]

    def held(self, owners, rows):
        at = slice(None) if len(owners) == 2 else owners[0]
        return self.acc.at[at, self.span(*rows)]

    def go(self, n, source, target, axis):
        copy = (to_row if axis == ROW else to_rep)(
            source, target, self.send[n], self.recv[n], *(() if axis == ROW else (axis,))
        )
        copy.start()
        self.sent.append(copy)

    def stage(self, n):
        job = self.job
        if n == 0:
            pltpu.make_async_copy(
                self.source.at[:, self.all, self.mine], self.acc, self.local[0]
            ).start()
            self.go(0, self.source.at[:, self.all, self.other], self.core, 0)
        elif n <= 5:
            if n == 1:
                landed(self.acc, self.local[0])
                landed(self.core, self.recv[0])
                for i in range(2):
                    add_into(self.acc.at[i], self.core.at[i], job.rows)
            else:
                _, owners, keep, _, _ = self.plan[n - 2]
                terms = self.part[n - 2]
                landed(terms, self.recv[n - 1])
                for i, owner in enumerate(owners):
                    add_into(
                        self.held((owner,), keep),
                        terms.at[i] if len(owners) == 2 else terms,
                        keep[1],
                    )
            if n < 5:
                axis, _, _, others, give = self.plan[n - 1]
                self.go(n, self.held(others, give), self.part[n - 1], axis)
            else:
                piece, place = self.held((self.x,), self.last), self.out(*self.last)
                pltpu.make_async_copy(piece, place, self.local[1]).start()
                self.go(5, piece, place, self.back[0][0])
        elif n <= 8:
            if n == 6:
                landed(self.out(*self.last), self.local[1])
            _, rows, came = self.back[n - 6]
            landed(self.out(*came), self.recv[n - 1])
            place = self.out(*rows)
            self.go(n, place, place, self.back[n - 5][0] if n < 8 else 0)
        else:
            landed(self.result.at[self.all, self.other], self.recv[8])
            for copy in self.sent:
                copy.wait_send()


def job_buffers(job):
    return [pltpu.VMEM(shape, B16) for shape in job.buffers()]


class SmallRun:
    steps = [(n, 1) for n in range(BITS + 2)]

    def __init__(self, sums, terms, send, recv):
        self.sums, self.terms, self.send, self.recv = sums, terms, send, recv

    def copy(self, n):
        args = (self.sums.at[n], self.terms.at[n], self.send.at[n], self.recv.at[n])
        return to_row(*args) if n == BITS else to_rep(*args, n)

    def stage(self, n):
        if n > 0:
            landed(self.terms.at[n - 1], self.recv.at[n - 1])
            self.sums[n] = self.sums[n - 1] + self.terms[n - 1]
        if n <= BITS:
            self.copy(n).start()
        else:
            for i in range(BITS + 1):
                self.copy(i).wait_send()


class EncodedRun:
    def __init__(self, source, result, bufs, send, recv, load, lag):
        self.source, self.result, self.send, self.recv, self.load = source, result, send, recv, load
        self.acc, self.terms = bufs[0], bufs[1:]
        self.bits = [partner(b)[0] for b in range(BITS)]
        self.steps = [(0, 1)] + [(n + 1, lag) for n in range(1, BITS + 1)]
        self.sent = []

    def part(self, ref, n, bit):
        at = (slice(None),) * (BITS - n) + (bit,)
        return ref.at[at]

    def go(self, n, source):
        copy = to_rep(source, self.terms[n], self.send.at[n], self.recv.at[n], n)
        copy.start()
        self.sent.append(copy)

    def fixed(self, n):
        return self.acc.at[
            (slice(None),) * (BITS + 1 - n) + tuple(self.bits[b] for b in range(n - 1, 0, -1))
        ]

    def add(self, n):
        left = self.fixed(n + 1)
        terms = self.terms[n]
        lead = left.shape[:-2]
        count = 1
        for d in lead:
            count *= d

        def body(i, carry):
            at, rest = [], i
            for d in reversed(lead):
                at.insert(0, rest % d)
                rest = rest // d
            at = tuple(at)
            left[at] = (left[at].astype(F32) + terms[at].astype(F32)).astype(B16)
            return carry

        lax.fori_loop(0, count, body, 0)

    def stage(self, step):
        if step == 0:
            pltpu.make_async_copy(
                self.part(self.source, 0, self.bits[0]), self.acc, self.load
            ).start()
            self.go(0, self.part(self.source, 0, 1 - self.bits[0]))
            return
        n = step - 1
        if n == 1:
            landed(self.acc, self.load)
        landed(self.terms[n - 1], self.recv.at[n - 1])
        self.add(n - 1)
        if n < BITS:
            self.go(n, self.part(self.fixed(n), n, 1 - self.bits[n]))
        else:
            self.result[...] = self.fixed(BITS)[...]
            for copy in self.sent:
                copy.wait_send()


class Pipeline:
    def __init__(self):
        self.waiting, self.active, self.now = [], [], 0

    def add(self, runs):
        self.waiting += runs

    def tick(self, count=1):
        for _ in range(count):
            if self.waiting:
                self.active.insert(0, [self.waiting.pop(0), 0, self.now])
            early = [e for e in self.active if e[0].steps[e[1]][0] < 2]
            late = [e for e in self.active if e[0].steps[e[1]][0] >= 2]
            for entry in early + late:
                run, at, due = entry
                if due <= self.now:
                    stage, wait = run.steps[at]
                    run.stage(stage)
                    entry[1:] = [at + 1, self.now + wait]
            self.active = [e for e in self.active if e[1] < len(e[0].steps)]
            self.now += 1

    def finish(self):
        while self.waiting or self.active:
            self.tick()


def jobs_of(result, rows, cols, orders):
    wide = cols // 2 if cols > 1024 else cols
    tall = rows // 2 if rows > 512 else rows
    return [
        Job(result, row, tall, col, wide, next(orders))
        for row in range(0, rows, tall)
        for col in range(0, cols, wide)
    ]


EARLY = [(ROW, 1, 2, 3), (2, ROW, 1, 3), (ROW, 1, 2, 3), (ROW, 1, 2, 3)]
LATE = [(ROW, 1, 2, 3)] * 3
SMALL_ROWS = 16
FETCH_LAG = 5
FIRST_LAG = 3
LAG = 2
TICKS = (4, 1, 1, 2)


def tail_kernel(p, jobs, early, arrays, *refs):
    refs = list(refs)
    take = lambda n: [refs.pop(0) for _ in range(n)]
    sources = take(early)
    dot_, denc, *far = take(7)
    lines, rl_ref, hidden, a1, dx1, dgc, dgf = take(7)
    results = take(arrays)
    small, dh_ref, denc_out = take(3)
    dout, dq, dkv, part, out, grads = take(6)
    late = take(3)
    recv, of_ref, wq, wk, wv = held = take(5)
    enc_bufs = take(BITS + 1)
    enc_send, enc_recv, enc_load, move_sems = take(4)
    small_sums, small_terms = take(2)
    back = take(7)
    rows_send, rows_recv, part_sem, got_sem, ret_send, ret_recv = take(6)
    small_send, small_recv = take(2)
    sems = take(3)
    moves = Moves(move_sems)
    moves.bring(zip(far, held))
    sources = sources + late
    runs = []
    for i, job in enumerate(jobs):
        bufs = take(len(job.buffers()))
        runs.append(JobRun(job, sources[job.result], results[job.result], bufs, sems, i))
    ready = len(jobs) - 3
    enc_run = EncodedRun(denc, denc_out, enc_bufs, enc_send, enc_recv, enc_load.at[0], LAG)

    me = lax.axis_index("rep")
    w = me % p.W
    unit = me // p.W
    group = unit % p.G
    mine = p.worker_of(me)
    slot = p.slot_of(me)
    barrier = pltpu.get_barrier_semaphore()
    for k in range(1, p.R):
        pl.semaphore_signal(
            barrier, inc=1, device_id={"rep": (me + k) % p.R}, device_id_type=MESH
        )
    x = lax.axis_index("shard")
    pl.semaphore_signal(barrier, inc=1, device_id={"shard": 1 - x}, device_id_type=MESH)
    pl.semaphore_wait(barrier, p.R)

    pipeline = Pipeline()
    pipeline.add([*runs[:2], enc_run, *runs[2:ready]])
    tick = pipeline.tick
    def outward(u, h):
        to, sem = u * p.W + mine, rows_recv.at[slot, h]
        return me, to, dot_.at[u, h], dout.at[slot, h], rows_send.at[u, h], sem

    def give(k, j, h):
        to = (w + k) % p.W
        return remote(
            dkv.at[p.source(j, to), h],
            part.at[k - 1, j, h],
            part_sem.at[k - 1, j, h],
            got_sem.at[k - 1, j, h],
            me - w + to,
        )

    def returned(j, h):
        r, sem = p.source(j, w), ret_recv.at[unit, h]
        return me, r, out.at[j, h], grads.at[unit, h], ret_send.at[j, h], sem

    def return_all(h):
        for j in range(p.J):
            total = dkv[p.source(j, w), h].astype(F32)
            for k in range(1, p.W):
                landed(part.at[k - 1, j, h], got_sem.at[k - 1, j, h])
                total = total + part[k - 1, j, h].astype(F32)
            out[j, h, 0:DH, :] = dq[j, h]
            out[j, h, DH : 3 * DH, :] = total.astype(B16)
            start_either(*returned(j, h))

    for h in range(p.HG):
        for u in range(p.U):
            start_either(*outward(u, h))
    tick(TICKS[0])
    lines_at = lax.broadcasted_iota(jnp.int32, (SMALL_ROWS, D), 0)
    block = jnp.zeros((SMALL_ROWS, D), F32)
    moves.need(recv, of_ref)
    for h in range(p.HG):
        for j in range(p.J):
            landed(dout.at[j, h], rows_recv.at[j, h])
        between = functools.partial(return_all, h - 1) if h > 0 else None
        sums = back_head(
            p,
            w,
            h,
            line_of(p, lines, group * p.HG + h),
            recv,
            dout,
            of_ref,
            rl_ref.at[h],
            dq,
            dkv,
            *back,
            between=between,
        )
        for j in range(p.J):
            for k in range(1, p.W):
                give(k, j, h).start()
        sums = jnp.concatenate([sums, jnp.zeros((1, D - 2 * p.T), F32)], axis=1)
        block = jnp.where(lines_at == 3 + group * p.HG + h, sums, block)
        tick(TICKS[1])
    tick(TICKS[2])
    return_all(p.HG - 1)
    tick(TICKS[3])
    for u in range(p.U):
        for h in range(p.HG):
            landed(grads.at[u, h], ret_recv.at[u, h])
    moves.need(wq, wk, wv)
    dgain = last_products(p, hidden, grads, a1, lines, dx1, wq, wk, wv, dh_ref, *late)
    for i, row in enumerate((dgain, dgc[...], dgf[...])):
        block = jnp.where(lines_at == i, row, block)
    small_sums[0] = block
    pipeline.add([*runs[ready:], SmallRun(small_sums, small_terms, small_send, small_recv)])
    pipeline.finish()
    small[...] = small_sums[BITS + 1]
    moves.end()
    for h in range(p.HG):
        for u in range(p.U):
            end_either(*outward(u, h))
        for j in range(p.J):
            end_either(*returned(j, h))
            for k in range(1, p.W):
                give(k, j, h).wait_send()


def tail_call(p, early, dot_, denc, far, held, collective):
    half = D // 2
    shapes = [g.shape[1:] for g in early] + [(half, D)] * 3
    turn = itertools.cycle(EARLY)
    jobs = [job for i in range(len(early)) for job in jobs_of(i, *shapes[i], turn)]
    jobs += [Job(len(early) + i, 0, half, 0, D, order) for i, order in enumerate(LATE)]
    sources = early
    piece = denc.shape[0] // (p.S * p.R)
    denc = denc.reshape((p.S,) + (2,) * BITS + (piece, D))
    dma = pltpu.SemaphoreType.DMA
    others = max(p.W - 1, 1)
    scratch = [
        pltpu.VMEM((p.J, p.HG, DH, p.T), B16),
        pltpu.VMEM((p.J, p.HG, DH, p.T), B16),
        pltpu.VMEM((p.R, p.HG, 2 * DH, p.T), B16),
        pltpu.VMEM((others, p.J, p.HG, 2 * DH, p.T), B16),
        pltpu.VMEM((p.J, p.HG, 3 * DH, p.T), B16),
        pltpu.VMEM((p.U, p.HG, 3 * DH, p.T), B16),
    ]
    scratch += [pltpu.VMEM((2, half, D), B16)] * 3
    scratch += [pltpu.VMEM(a.shape, a.dtype) for a in far]
    scratch += [pltpu.VMEM((p.S,) + (2,) * (BITS - 1) + (piece, D), B16)]
    scratch += [
        pltpu.VMEM((p.S,) + (2,) * (BITS - 1 - n) + (piece, D), B16) for n in range(BITS)
    ]
    scratch += [dma((BITS,)), dma((BITS,)), dma((1,)), dma((len(far),))]
    scratch += [
        pltpu.VMEM((BITS + 2, SMALL_ROWS, D), F32),
        pltpu.VMEM((BITS + 1, SMALL_ROWS, D), F32),
    ]
    scratch += back_scratch(p)
    scratch += [
        dma((p.U, p.HG)),
        dma((p.J, p.HG)),
        dma((others, p.J, p.HG)),
        dma((others, p.J, p.HG)),
        dma((p.J, p.HG)),
        dma((p.U, p.HG)),
        dma((BITS + 1,)),
        dma((BITS + 1,)),
        dma((len(jobs), 9)),
        dma((len(jobs), 9)),
        dma((len(jobs), 2)),
    ]
    for job in jobs:
        scratch += job_buffers(job)
    anywhere = pl.BlockSpec(memory_space=pl.ANY)
    near = pl.BlockSpec(memory_space=pltpu.VMEM)
    *sums, small, dh, denc = pl.pallas_call(
        functools.partial(tail_kernel, p, jobs, len(early), len(shapes)),
        out_shape=[jax.ShapeDtypeStruct(s, B16) for s in shapes]
        + [
            jax.ShapeDtypeStruct((SMALL_ROWS, D), F32),
            jax.ShapeDtypeStruct((p.S, p.T, D), B16),
            jax.ShapeDtypeStruct((p.S, piece, D), B16),
        ],
        in_specs=[anywhere] * (len(sources) + 2 + len(far)) + [near] * len(held),
        out_specs=[anywhere] * len(shapes) + [near] * 3,
        scratch_shapes=scratch,
        compiler_params=pltpu.CompilerParams(
            collective_id=collective, has_side_effects=True, vmem_limit_bytes=60 * 2**20
        ),
        name="tail",
    )(*sources, dot_, denc, *far, *held)
    return sums, small, dh, denc


def widen_kernel(count, *refs):
    for i in range(count):
        refs[count + i][...] = refs[i][...].astype(F32)


def widen(mats):
    parts = 2
    blocks = [
        pl.BlockSpec((m.shape[0] // parts, m.shape[1]), lambda i: (i, 0)) for m in mats
    ]
    return pl.pallas_call(
        functools.partial(widen_kernel, len(mats)),
        grid=(parts,),
        out_shape=[jax.ShapeDtypeStruct(m.shape, F32) for m in mats],
        in_specs=blocks,
        out_specs=blocks,
        compiler_params=pltpu.CompilerParams(vmem_limit_bytes=63 * 2**20),
        name="widen",
    )(*mats)


class Fetch:
    def __init__(self, master, staged, out, first, rows, col, cols, stage, own, sems, index, wide):
        self.x = lax.axis_index("shard")
        self.core, self.y = [partner(b)[0] for b in range(2)]
        self.rows, self.staged, self.wide = rows, staged, wide
        self.master = master.at[pl.ds(first, rows), pl.ds(col, cols)]
        self.stage_ref = stage.at[pl.ds(0, rows), pl.ds(0, cols)]
        self.own = own
        self.out, self.first, self.col, self.cols = out, first, col, cols
        load, keep, self.send, self.recv = sems
        self.load, self.keep = load.at[index], keep.at[index]
        self.send = [self.send.at[index, i] for i in range(3)]
        self.recv = [self.recv.at[index, i] for i in range(3)]

    def span(self, core, y=None):
        half = self.rows // 2
        if y is None:
            return core * half, half
        return core * half + y * (half // 2), half // 2

    def place(self, owner, *share):
        first, count = self.span(*share)
        first = pl.multiple_of(self.first + first, 16)
        return self.out.at[owner, pl.ds(first, count), pl.ds(self.col, self.cols)]

    def share(self):
        return (self.core, self.y) if self.wide else (self.core,)

    def read(self):
        pltpu.make_async_copy(self.master, self.stage_ref, self.load).start()

    def kept(self):
        return self.out.at[self.x, pl.ds(self.first, self.rows), pl.ds(self.col, self.cols)]

    def across(self):
        first, count = self.span(*self.share())
        part = self.own.at[pl.ds(pl.multiple_of(first, 16), count)]
        return to_row(part, self.place(self.x, *self.share()), self.send[0], self.recv[0])

    def start(self):
        landed(self.stage_ref, self.load)
        step = 32

        def body(i, carry):
            at = pl.ds(pl.multiple_of(i * step, step), step)
            self.own[at, :] = self.stage_ref[at, :].astype(B16)
            return carry

        lax.fori_loop(0, self.rows // step, body, 0)
        self.across().start()
        if self.staged:
            pltpu.make_async_copy(self.own, self.kept(), self.keep).start()

    def beside(self):
        place = self.place(1 - self.x, self.core, self.y)
        return to_rep(place, place, self.send[2], self.recv[2], 1)

    def over(self):
        place = self.place(1 - self.x, self.core)
        return to_rep(place, place, self.send[1], self.recv[1], 0)

    def relay(self):
        landed(self.place(1 - self.x, *self.share()), self.recv[0])
        if self.wide:
            self.beside().start()
        else:
            self.over().start()

    def relay_more(self):
        if self.wide:
            landed(self.place(1 - self.x, self.core, 1 - self.y), self.recv[2])
            self.over().start()

    def finish(self):
        landed(self.place(1 - self.x, 1 - self.core), self.recv[1])

    def end(self):
        self.across().wait_send()
        self.over().wait_send()
        if self.wide:
            self.beside().wait_send()
        if self.staged:
            landed(self.kept(), self.keep)


def small_block(p, gains, table, buckets, x):
    at = lax.broadcasted_iota(jnp.int32, (SMALL_ROWS, D), 0)
    block = jnp.zeros((SMALL_ROWS, D), F32)
    for i, gain in enumerate(gains):
        part = gain[...].astype(B16).astype(F32).reshape(1, -1)
        none = jnp.zeros_like(part)
        row = jnp.where(
            x == 0,
            jnp.concatenate([part, none], axis=1),
            jnp.concatenate([none, part], axis=1),
        )
        block = jnp.where(at == i, row, block)
    held = table.shape[0]
    bucket = lax.broadcasted_iota(jnp.int32, (held, 2 * p.T), 0) + x * held
    near = buckets[...].reshape(1, -1)[:, : 2 * p.T]
    onehot = (near == bucket).astype(F32).astype(B16)
    lines = t_dot(table[...].astype(B16), onehot)
    lines = jnp.concatenate([lines, jnp.zeros((H, D - 2 * p.T), F32)], axis=1)
    lines = jnp.concatenate(
        [jnp.zeros((3, D), F32), lines, jnp.zeros((SMALL_ROWS - 3 - H, D), F32)], axis=0
    )
    return block + lines


def head_kernel(p, *refs):
    refs = list(refs)
    take = lambda n: [refs.pop(0) for _ in range(n)]
    masters = take(11)
    hidden, encoded, g1, g2, g3, table, buckets = take(7)
    far_mats = take(8)
    wide = take(3)
    far_recv, far_enc, far_kn, far_kt, far_vn = take(5)
    small, a1, of_ref, rl_ref, ot = take(5)
    x1, x2, a2, qt2, of2, rl2 = take(6)
    mats = take(8)
    recv, enc, kn, kt, vn, vt = take(6)
    moves = Moves(take(1)[0])
    send, o_ref, mine_small, their_small = take(4)
    stages = take(4)
    owns = take(6)
    att = take(3)
    fetch_sems = take(4)
    small_send, small_recv, enc_send, enc_recv = take(4)
    tok_send, relay_sem, tok_recv, back_send, back_recv = take(5)

    me = lax.axis_index("rep")
    x = lax.axis_index("shard")
    w = me % p.W
    unit = me // p.W
    group = unit % p.G
    mine = p.worker_of(me)
    bits = [(me // 2**b) % 2 for b in range(BITS)]

    half = D // 2
    jobs = []
    for i in range(8):
        jobs.append((masters[i], mats[i], 0, half, 0, D))
    for i, ref in enumerate(wide):
        rows, cols = ref.shape[1:]
        tall = rows // 2 if rows > 512 else rows
        part = cols // 2 if cols > 1024 else cols
        for row in range(0, rows, tall):
            for col in range(0, cols, part):
                jobs.append((masters[8 + i], ref, row, tall, col, part))
    fetches = []
    for i, (master, out, row, rows, col, cols) in enumerate(jobs):
        staged = i >= 8
        own = owns[i - 8] if staged else out.at[x]
        fetches.append(
            Fetch(
                master,
                staged,
                out,
                row,
                rows,
                col,
                cols,
                stages[i % 4],
                own,
                fetch_sems,
                i,
                3 <= i < 5 or (i > 4 and i % 2 == 0),
            )
        )

    barrier = pltpu.get_barrier_semaphore()
    for k in range(1, p.R):
        pl.semaphore_signal(
            barrier, inc=1, device_id={"rep": (me + k) % p.R}, device_id_type=MESH
        )
    pl.semaphore_signal(barrier, inc=1, device_id={"shard": 1 - x}, device_id_type=MESH)
    for fetch in fetches[:4]:
        fetch.read()
    mine_small[...] = small_block(p, (g1, g2, g3), table, buckets, x)
    enc[:, bits[3], bits[2], bits[1], bits[0]] = encoded[...]
    pl.semaphore_wait(barrier, p.R)

    share = to_row(mine_small, their_small, small_send, small_recv)
    share.start()

    def enc_copy(n):
        at = (slice(None),) * (1 + n) + tuple(bits[b] for b in range(BITS - 1 - n, -1, -1))
        part = enc.at[at]
        return to_rep(part, part, enc_send.at[n], enc_recv.at[n], BITS - 1 - n)

    def enc_landed(n):
        b = [bits[i] for i in range(BITS - 1 - n, -1, -1)]
        b[0] = 1 - b[0]
        landed(enc.at[(slice(None),) * (1 + n) + tuple(b)], enc_recv.at[n])

    started, relayed, more = 0, 0, 0

    def begin(count=1):
        nonlocal started
        for _ in range(count):
            if started < len(fetches):
                fetches[started].start()
                if started + 4 < len(fetches):
                    fetches[started + 4].read()
                started += 1

    def pass_on(count=1):
        nonlocal relayed, more
        for _ in range(count):
            if more < relayed:
                fetches[more].relay_more()
                more += 1
            if relayed < started:
                fetches[relayed].relay()
                relayed += 1

    def slot():
        begin(2)
        if started - relayed > FETCH_LAG or started == len(fetches):
            pass_on()

    begin(3)
    enc_copy(0).start()
    landed(their_small, small_recv)
    small[...] = mine_small[...] + their_small[...]
    enc_landed(0)
    enc_copy(1).start()
    pass_on(2)
    enc_landed(1)
    enc_copy(2).start()
    pass_on()
    begin(2)
    fetches[2].relay_more()
    more = 3
    for fetch, far in zip(fetches[:3], far_mats):
        fetch.finish()
        moves.take(fetch.out, far)
    project_kernel(p, hidden, small, *mats[:3], a1, send)

    def token(u, h):
        to, sem = u * p.W + mine, tok_recv.at[me, h]
        return me, to, send.at[u, h], recv.at[me, h], tok_send.at[u, h], sem

    def relay(k, j, h):
        r = p.source(j, w)
        part = recv.at[r, h, pl.ds(DH, 2 * DH)]
        to = me - w + (w + k) % p.W
        return remote(part, part, relay_sem.at[k - 1, j, h], tok_recv.at[r, h], to)

    def returned(j, h):
        r, sem = p.source(j, w), back_recv.at[unit, h]
        return me, r, o_ref.at[j, h], ot.at[unit, h], back_send.at[j, h], sem

    def relay_all(h):
        for j in range(p.J):
            r = p.source(j, w)
            landed(recv.at[r, h], tok_recv.at[r, h])
            for k in range(1, p.W):
                relay(k, j, h).start()

    def relayed_all(h):
        for k in range(1, p.W):
            for j in range(p.J):
                r = p.source(j, (w + k) % p.W)
                landed(recv.at[r, h, pl.ds(DH, 2 * DH)], tok_recv.at[r, h])

    def send_all(h):
        for u in range(p.U):
            start_either(*token(u, h))

    send_all(0)
    enc_landed(2)
    enc_copy(3).start()
    begin()
    pass_on(2)
    enc_landed(3)
    moves.take(enc, far_enc)
    fetches[4].relay_more()
    more = 5

    def encode(i, natural, turned):
        fetches[i].finish()
        moves.take(mats[i], far_mats[i])
        encode_one(enc, mats[i], natural, turned)
        slot()

    encode(3, kn, kt)
    if p.HG > 1:
        send_all(1)
    relay_all(0)
    encode(4, vn, vt)
    for h in range(2, p.HG):
        send_all(h)
    for made, far in ((kn, far_kn), (kt, far_kt), (vn, far_vn)):
        moves.take(made, far)
    slot()
    relayed_all(0)
    for h in range(p.HG):
        line = line_of(p, small, group * p.HG + h)
        between = functools.partial(relay_all, h + 1) if h + 1 < p.HG else None
        attend_head(p, w, h, line, recv, o_ref, of_ref, rl_ref.at[h], *att, between=between)
        for j in range(p.J):
            start_either(*returned(j, h))
        slot()
        if h + 1 < p.HG:
            relayed_all(h + 1)
    moves.take(recv, far_recv)
    slot()
    while more < 8:
        pass_on()
    for fetch, far in zip(fetches[5:8], far_mats[5:]):
        fetch.finish()
        moves.take(fetch.out, far)
    for u in range(p.U):
        for h in range(p.HG):
            landed(ot.at[u, h], back_recv.at[u, h])

    pause = slot
    cross_kernel(
        p.S, hidden, ot, mats[5], small, mats[6], mats[7], kn, vt, x1, x2, a2, qt2, of2, rl2, pause
    )
    begin(len(fetches))
    while more < len(fetches):
        pass_on()
    for fetch in fetches[8:]:
        fetch.finish()
    for fetch in fetches:
        fetch.end()
    moves.end()
    share.wait_send()
    for n in range(BITS):
        enc_copy(n).wait_send()
    for h in range(p.HG):
        for u in range(p.U):
            end_either(*token(u, h))
        for j in range(p.J):
            end_either(*returned(j, h))
            for k in range(1, p.W):
                relay(k, j, h).wait_send()


def head_call(p, masters, hidden, encoded, gains, table, buckets, collective):
    half, tokens = D // 2, p.S * p.T
    piece = encoded.shape[1]
    enc_rows = p.S * piece * p.R
    wides = [m.shape for m in masters[8:]]
    near = pl.BlockSpec(memory_space=pltpu.VMEM)
    anywhere = pl.BlockSpec(memory_space=pl.ANY)
    outs = [((2, half, D), B16)] * 8 + [((2, *s), B16) for s in wides]
    inner = [
        ((p.R, p.HG, 3 * DH, p.T), B16),
        ((p.S,) + (2,) * BITS + (piece, D), B16),
        ((enc_rows, D), B16),
        ((D, enc_rows), B16),
        ((enc_rows, D), B16),
    ]
    outs += inner
    inner = [((2, half, D), B16)] * 8 + inner + [((H // 2, 2 * DH + ONES, enc_rows), B16)]
    outs += [
        ((SMALL_ROWS, D), F32),
        ((tokens, D), B16),
        ((p.J, p.HG, DH, p.T), F32),
        ((p.HG, p.NP, 1, 2 * p.T), F32),
        ((p.U, p.HG, DH, p.T), B16),
        ((tokens, D), F32),
        ((tokens, D), F32),
        ((tokens, D), B16),
        ((p.S, D, p.T), B16),
        ((p.S, D, p.T), F32),
        ((p.S, H // 2, 1, 2 * p.T), F32),
    ]
    parts = [(half, D)] * 8
    for rows, cols in wides:
        tall = rows // 2 if rows > 512 else rows
        part = cols // 2 if cols > 1024 else cols
        parts += [(tall, part)] * ((rows // tall) * (cols // part))
    count = len(parts)
    dma = pltpu.SemaphoreType.DMA
    scratch = [pltpu.VMEM(s, t) for s, t in inner] + [dma((13,))]
    scratch += [
        pltpu.VMEM((p.U, p.HG, 3 * DH, p.T), B16),
        pltpu.VMEM((p.J, p.HG, DH, p.T), B16),
        pltpu.VMEM((SMALL_ROWS, D), F32),
        pltpu.VMEM((SMALL_ROWS, D), F32),
    ]
    tallest = max(r for r, _ in parts)
    widest = max(c for _, c in parts)
    scratch += [pltpu.VMEM((tallest, widest), F32)] * 4
    scratch += [pltpu.VMEM(s, B16) for s in parts[8:]]
    scratch += attend_scratch(p)
    scratch += [dma((count,)), dma((count,)), dma((count, 3)), dma((count, 3))]
    scratch += [dma, dma, dma((BITS,)), dma((BITS,))]
    scratch += [
        dma((p.U, p.HG)),
        dma((max(p.W - 1, 1), p.J, p.HG)),
        dma((p.R, p.HG)),
        dma((p.J, p.HG)),
        dma((p.U, p.HG)),
    ]
    return pl.pallas_call(
        functools.partial(head_kernel, p),
        out_shape=[jax.ShapeDtypeStruct(s, t) for s, t in outs],
        in_specs=[anywhere] * 11 + [near] * 7,
        out_specs=[anywhere] * 16 + [near] * 11,
        scratch_shapes=scratch,
        compiler_params=pltpu.CompilerParams(
            collective_id=collective, has_side_effects=True, vmem_limit_bytes=62 * 2**20
        ),
        name="head",
    )(*masters, hidden, encoded, *gains, table, buckets)


def local(
    hidden,
    encoded,
    out_grad,
    self_query,
    self_key,
    self_value,
    self_out,
    cross_query,
    cross_key,
    cross_value,
    cross_out,
    ffn_gate,
    ffn_up,
    ffn_down,
    gain_self,
    gain_cross,
    gain_ffn,
    bias_table,
    buckets,
):
    seqs, toks = hidden.shape[0], hidden.shape[1]
    p = Plan(seqs, toks, lax.axis_size("rep"))
    tokens = seqs * toks
    ff = ffn_gate.shape[1]
    enc_rows = seqs * encoded.shape[1] * p.R
    dma = pltpu.SemaphoreType.DMA

    n_shard = lax.axis_size("shard")
    mine = lax.axis_index("shard")
    part = gain_self.shape[0]
    near = buckets[: 2 * toks]
    onehot = (near[:, None] == jnp.arange(NB, dtype=jnp.int32)[None, :]).astype(B16)
    paired = n_shard == 2 and p.R == 2**BITS and 3 + H <= SMALL_ROWS
    if paired:
        masters = (
            self_query,
            self_key,
            self_value,
            cross_key,
            cross_value,
            self_out,
            cross_query,
            cross_out,
            ffn_gate,
            ffn_up,
            ffn_down,
        )
        gains = [gain_self, gain_cross, gain_ffn]
        got = head_call(
            p, masters, hidden, encoded, gains, bias_table, buckets, 0
        )
        wq, wk, wv, wck, wcv, wo, wcq, wco = got[:8]
        wg, wu, wd = [g.reshape(-1, g.shape[-1]) for g in got[8:11]]
        recv, enc, ckn, ckt, cvn, small, a1, of, rl, ot = got[11:21]
        x1, x2, a2, qt2, of2, rl2 = got[21:]
    else:
        lot = jnp.concatenate(
            [
                jnp.stack([gain_self, gain_cross, gain_ffn]).reshape(-1),
                bias_table.reshape(-1),
            ]
        ).astype(B16)
        lot = lax.all_gather(lot, "shard", axis=0)
        gains = [
            lot[:, i * part : (i + 1) * part].reshape(1, D).astype(F32) for i in range(3)
        ]
        table = lot[:, 3 * part :].reshape(NB, H)
        lines = jnp.einsum("lb,bh->hl", onehot, table, preferred_element_type=F32)
        lines = jnp.pad(lines, ((0, SMALL_ROWS - 3 - H), (0, D - 2 * toks)))
        small = jnp.concatenate([*gains, lines], axis=0)

        wq, wk, wv, wo, wcq, wck, wcv, wco, wg, wu, wd = [
            gather_rows(m.astype(B16))
            for m in (
                self_query,
                self_key,
                self_value,
                self_out,
                cross_query,
                cross_key,
                cross_value,
                cross_out,
                ffn_gate,
                ffn_up,
                ffn_down,
            )
        ]
        enc = lax.all_gather(encoded, "rep", axis=1, tiled=True).reshape(enc_rows, D)

        a1, send = plain_call(
            functools.partial(project_kernel, p),
            [((tokens, D), B16), ((p.U, p.HG, 3 * DH, toks), B16)],
            (hidden, small, wq, wk, wv),
            "project",
        )
        recv = comm_call(
            functools.partial(scatter_tokens, p),
            (p.R, p.HG, 3 * DH, toks),
            (send,),
            [dma((p.U,)), dma((max(p.W - 1, 1), p.J)), dma((p.R,))],
            0,
            "scatter_tokens",
        )
        ckn, ckt, cvn, cvt = plain_call(
            encode_kernel,
            [
                ((enc_rows, D), B16),
                ((D, enc_rows), B16),
                ((enc_rows, D), B16),
                ((H // 2, 2 * DH + ONES, enc_rows), B16),
            ],
            (enc, wck, wcv),
            "encode",
        )
        o, of, rl = pl.pallas_call(
            functools.partial(attend_kernel, p),
            grid=(p.HG,),
            out_shape=[
                jax.ShapeDtypeStruct((p.J, p.HG, DH, toks), B16),
                jax.ShapeDtypeStruct((p.J, p.HG, DH, toks), F32),
                jax.ShapeDtypeStruct((p.HG, p.NP, 1, 2 * toks), F32),
            ],
            in_specs=[whole((p.R, p.HG, 3 * DH, toks)), whole((SMALL_ROWS, D))],
            out_specs=[
                whole((p.J, p.HG, DH, toks)),
                whole((p.J, p.HG, DH, toks)),
                whole((p.HG, p.NP, 1, 2 * toks)),
            ],
            scratch_shapes=attend_scratch(p),
            compiler_params=pltpu.CompilerParams(vmem_limit_bytes=56 * 2**20),
            name="attend",
        )(recv, small)
        ot = comm_call(
            functools.partial(return_tokens, p),
            (p.U, p.HG, DH, toks),
            (o,),
            [dma((p.J,)), dma((p.U,))],
            1,
            "return_tokens",
        )

        x1, x2, a2, qt2, of2, rl2 = plain_call(
            functools.partial(cross_kernel, seqs),
            [
                ((tokens, D), F32),
                ((tokens, D), F32),
                ((tokens, D), B16),
                ((seqs, D, toks), B16),
                ((seqs, D, toks), F32),
                ((seqs, H // 2, 1, 2 * toks), F32),
            ],
            (hidden, ot, wo, small, wcq, wco, ckn, cvt),
            "cross",
        )

    chunk = min(512, ff)
    const = lambda s: pl.BlockSpec(s, lambda i: (0, 0))
    output, dx2, dg_ffn, dwg, dwu, dwd = pl.pallas_call(
        ffn_kernel,
        grid=(ff // chunk,),
        out_shape=[
            jax.ShapeDtypeStruct((tokens, D), B16),
            jax.ShapeDtypeStruct((tokens, D), F32),
            jax.ShapeDtypeStruct((1, D), F32),
            jax.ShapeDtypeStruct((D, ff), B16),
            jax.ShapeDtypeStruct((D, ff), B16),
            jax.ShapeDtypeStruct((ff, D), B16),
        ],
        in_specs=[
            const((tokens, D)),
            const((tokens, D)),
            const((SMALL_ROWS, D)),
            pl.BlockSpec((D, chunk), lambda i: (0, i)),
            pl.BlockSpec((D, chunk), lambda i: (0, i)),
            pl.BlockSpec((chunk, D), lambda i: (i, 0)),
        ],
        out_specs=[
            const((tokens, D)),
            const((tokens, D)),
            const((1, D)),
            pl.BlockSpec((D, chunk), lambda i: (0, i)),
            pl.BlockSpec((D, chunk), lambda i: (0, i)),
            pl.BlockSpec((chunk, D), lambda i: (i, 0)),
        ],
        scratch_shapes=[
            pltpu.VMEM((tokens, D), B16),
            pltpu.VMEM((tokens, D), F32),
            pltpu.VMEM((tokens, D), F32),
        ],
        compiler_params=pltpu.CompilerParams(vmem_limit_bytes=56 * 2**20),
        name="ffn",
    )(x2, out_grad.reshape(tokens, D), small, wg, wu, wd)

    back_outs = [
        ((tokens, D), F32),
        ((1, D), F32),
        ((p.U, p.HG, DH, toks), B16),
        ((enc_rows, D), B16),
    ] + [((D, D), B16)] * 5
    back_args = (dx2, x1, a2, small, qt2, of2, rl2, ckn, ckt, cvn, enc, wco, wcq, wck, wcv, wo, ot)
    back_scratch_ = [
        pltpu.VMEM((seqs, D, toks), B16),
        pltpu.VMEM((seqs, D, toks), B16),
        pltpu.VMEM((enc_rows, D), B16),
        pltpu.VMEM((enc_rows, D), B16),
    ]
    back_kernel = functools.partial(cross_back_kernel, seqs, p.G)
    if paired:
        got = cross_back_moves_call(back_kernel, back_outs, back_args, back_scratch_)
    else:
        got = plain_call(back_kernel, back_outs, back_args, "cross_back", scratch=back_scratch_)
    dx1, dg_cross, dot_, denc, dwco, dwcq, dwck, dwcv, dwo = got
    if paired:
        early = [
            g.reshape(2, g.shape[0] // 2, g.shape[1])
            for g in (dwg, dwu, dwd, dwo, dwcq, dwck, dwcv, dwco)
        ]
        sums, block, hidden_grad, encoded_grad = tail_call(
            p,
            early,
            dot_,
            denc,
            (recv, of, wq, wk, wv),
            (small, rl, hidden, a1, dx1, dg_cross, dg_ffn),
            3,
        )
        dwg, dwu, dwd, dwo, dwcq, dwck, dwcv, dwco, dwq, dwk, dwv = widen(sums)
        mats = [dwq, dwk, dwv, dwo, dwcq, dwck, dwcv, dwco, dwg, dwu, dwd]
        dgains = lax.dynamic_slice(block, (0, mine * part), (3, part))
        by_bucket = jnp.einsum(
            "hl,lb->bh",
            block[3 : 3 + H, : 2 * toks],
            onehot.astype(F32),
            precision=lax.Precision.HIGHEST,
        )
        dtab = lax.dynamic_slice(
            by_bucket, (mine * bias_table.shape[0], 0), bias_table.shape
        )
    else:
        encoded_grad = lax.psum_scatter(
            denc.reshape(seqs, enc_rows // seqs, D), "rep", scatter_dimension=1, tiled=True
        )
        dout = comm_call(
            functools.partial(scatter_rows, p),
            (p.J, p.HG, DH, toks),
            (dot_,),
            [dma((p.U,)), dma((p.J,))],
            2,
            "scatter_rows",
        )
        dq, dkv, line = pl.pallas_call(
            functools.partial(attend_back_kernel, p),
            grid=(p.HG,),
            out_shape=[
                jax.ShapeDtypeStruct((p.J, p.HG, DH, toks), B16),
                jax.ShapeDtypeStruct((p.R, p.HG, 2 * DH, toks), B16),
                jax.ShapeDtypeStruct((p.HG, 1, 2 * toks), F32),
            ],
            in_specs=[
                whole((p.R, p.HG, 3 * DH, toks)),
                whole((SMALL_ROWS, D)),
                whole((p.J, p.HG, DH, toks)),
                whole((p.J, p.HG, DH, toks)),
                whole((p.HG, p.NP, 1, 2 * toks)),
            ],
            out_specs=[
                whole((p.J, p.HG, DH, toks)),
                whole((p.R, p.HG, 2 * DH, toks)),
                whole((p.HG, 1, 2 * toks)),
            ],
            scratch_shapes=back_scratch(p),
            compiler_params=pltpu.CompilerParams(vmem_limit_bytes=56 * 2**20),
            name="attend_back",
        )(recv, small, dout, of, rl)
        grads = comm_call(
            functools.partial(return_grads, p),
            (p.U, p.HG, 3 * DH, toks),
            (dq, dkv),
            [
                pltpu.VMEM((max(p.W - 1, 1), p.J, p.HG, 2 * DH, toks), B16),
                pltpu.VMEM((p.J, p.HG, 3 * DH, toks), B16),
                dma((p.J,)),
                dma((max(p.W - 1, 1), p.J)),
                dma((max(p.W - 1, 1), p.J)),
                dma((p.U,)),
            ],
            3,
            "return_grads",
            space=pltpu.VMEM,
        )
        hidden_grad, dg_self, dwq, dwk, dwv = plain_call(
            functools.partial(last_kernel, p),
            [(hidden.shape, B16), ((1, D), F32)] + [((D, D), B16)] * 3,
            (hidden, grads, a1, small, dx1, wq, wk, wv),
            "last",
        )

        group = (lax.axis_index("rep") // p.W) % p.G
        by_bucket = jnp.einsum(
            "hl,lb->bh", line[:, 0, :], onehot.astype(F32), precision=lax.Precision.HIGHEST
        )
        dtable = lax.dynamic_update_slice(jnp.zeros((NB, H), F32), by_bucket, (0, group * p.HG))

        mats = reduce_grads([dwq, dwk, dwv, dwo, dwcq, dwck, dwcv, dwco, dwg, dwu, dwd])
        lot = jnp.concatenate(
            [g.reshape(n_shard, part) for g in (dg_self, dg_cross, dg_ffn)]
            + [dtable.reshape(n_shard, -1)],
            axis=1,
        )
        size = lot.shape[1]
        lot = lax.psum(lot, ("shard", "rep"))
        lot = lax.dynamic_slice(lot, (mine, 0), (1, size))[0]
        dgains = [lot[i * part : (i + 1) * part] for i in range(3)]
        dtab = lot[3 * part :].reshape(bias_table.shape)
    return (
        output.reshape(hidden.shape),
        hidden_grad,
        encoded_grad,
        *mats,
        *dgains,
        dtab,
    )


def solution(mesh):
    tok = P("shard", "rep", None)
    mat = P("shard", None)
    in_specs = (tok,) * 3 + (mat,) * 11 + (P("shard"),) * 3 + (mat, P())
    out_specs = (tok,) * 3 + (mat,) * 11 + (P("shard"),) * 3 + (mat,)
    return jax.shard_map(local, mesh=mesh, in_specs=in_specs, out_specs=out_specs, check_vma=False)
```
